32 devices in a mesh: dp: 8 (over y, x, core), ctx: 4 (over z).
Axes of the slice: x: 2, y: 2, z: 4, core: 2. Of those that a mesh axis runs over, the one named last changes fastest.
Arguments:
- layer_in: bfloat16 [8, 1024, 1536], P('dp', 'ctx'), may hold values from -6 to 6
- seg_ids: int32 [8, 1024], P('dp'), may hold values from 0 to 1, as said below
- route_ids: int32 [8, 1024, 6], P('dp', 'ctx'), may hold values from 0 to 31, all different within a row; in each aligned block of 256 rows (0 to 255, 256 to 511, ..., all dimensions but the last counted through in order) at most 60 rows name the same one
- out_grad: bfloat16 [8, 1024, 1536], P('dp', 'ctx'), may hold values from -6 to 6
- norm_in: bfloat16 [1536], P(('dp', 'ctx')), may hold values from 0.5 to 1.5
- w_in: bfloat16 [1536, 6448], P(('dp', 'ctx')), may hold values from -0.15625 to 0.15625
- conv_w: bfloat16 [4, 3328], P(None, ('dp', 'ctx')), may hold values from -3 to 3
- conv_b: bfloat16 [3328], P(('dp', 'ctx')), may hold values from -2 to 2
- dt_bias: float32 [48], replicated, may hold values from -1 to 1
- a_log: float32 [48], replicated, may hold values from -7 to -2
- d_skip: float32 [48], replicated, may hold values from 0.5 to 1.5
- norm_gate: bfloat16 [3072], P(('dp', 'ctx')), may hold values from 0.5 to 1.5
- w_out: bfloat16 [3072, 1536], P(('dp', 'ctx')), may hold values from -0.109375 to 0.109375
- norm_mid: bfloat16 [1536], P(('dp', 'ctx')), may hold values from 0.5 to 1.5
- w_router: bfloat16 [1536, 32], P(('dp', 'ctx')), may hold values from -0.078125 to 0.078125
- w_sgate: bfloat16 [1536, 1024], P(('dp', 'ctx')), may hold values from -0.15625 to 0.15625
- w_sup: bfloat16 [1536, 1024], P(('dp', 'ctx')), may hold values from -0.15625 to 0.15625
- w_sdown: bfloat16 [1024, 1536], P(('dp', 'ctx')), may hold values from -0.1875 to 0.1875
- e_gate: bfloat16 [32, 1536, 512], P('dp', 'ctx'), may hold values from -0.15625 to 0.15625
- e_up: bfloat16 [32, 1536, 512], P('dp', 'ctx'), may hold values from -0.15625 to 0.15625
- e_down: bfloat16 [32, 512, 1536], P('dp', None, 'ctx'), may hold values from -0.25 to 0.25
Outputs:
- layer_out: bfloat16 [8, 1024, 1536], P('dp', 'ctx')
- grad_in: float32 [8, 1024, 1536], P('dp', 'ctx')
- grad_norm_in: float32 [1536], P(('dp', 'ctx'))
- grad_w_in: float32 [1536, 6448], P(('dp', 'ctx'))
- grad_conv_w: float32 [4, 3328], P(None, ('dp', 'ctx'))
- grad_conv_b: float32 [3328], P(('dp', 'ctx'))
- grad_dt_bias: float32 [48], replicated
- grad_a_log: float32 [48], replicated
- grad_d_skip: float32 [48], replicated
- grad_norm_gate: float32 [3072], P(('dp', 'ctx'))
- grad_w_out: float32 [3072, 1536], P(('dp', 'ctx'))
- grad_norm_mid: float32 [1536], P(('dp', 'ctx'))
- grad_w_router: float32 [1536, 32], P(('dp', 'ctx'))
- grad_w_sgate: float32 [1536, 1024], P(('dp', 'ctx'))
- grad_w_sup: float32 [1536, 1024], P(('dp', 'ctx'))
- grad_w_sdown: float32 [1024, 1536], P(('dp', 'ctx'))
- grad_e_gate: float32 [32, 1536, 512], P('dp', 'ctx')
- grad_e_up: float32 [32, 1536, 512], P('dp', 'ctx')
- grad_e_down: float32 [32, 512, 1536], P('dp', None, 'ctx')
The draws below stay inside these ranges and needn't reach their ends.
Inputs may be any that keep to these rules, and one draw needn't show every extreme that they name: `seg_ids`: within a sequence the numbers start at 0 and rise by one at the first token of each further document; at most one document starts in each aligned span of 64 tokens, and none in the first span. In every group of 1 sequence that one index of dp holds, one sequence has exactly two documents, the second starting in its last aligned span of 64 tokens and after the first of its last 256 tokens; if 1 > 1 another sequence starts a document in every span after the first. `route_ids`: the 6 routes of a token differ. In each aligned block of 256 tokens (one sequence's tokens on one index of ctx), no expert is named by more than 60 routes, a bound that some block reaches.
All inputs are finite; a program needn't handle non-finite values.
Results may differ from the reference program's by a relative error of at most 0.015.
Values may be sent and summed in bfloat16 or wider, within the bound.
A program may use at most 320 MiB of HBM per device.

```python
import math
import jax
import jax.numpy as jnp
import numpy as np
from jax import lax

D = 1536
HEADS = 48
HEAD = 64
STATE = 128
KC = 4
FE = 512
FS = 1024
TOP = 6
SEQ_LEN = 1024
SEQ_DEV = 1
DI = 3072
CONV = 3328
PROJ = 6448
EXPERTS = 32
SEQS = 8
CH = 256
CAP = 60
N_CTX = 4


def draw_seg_ids(key, part):
    key = jax.random.fold_in(key, 11)
    key_on, key_at, key_pick, key_end = jax.random.split(key, 4)
    span_count = SEQ_LEN // 64
    group_count = SEQS // SEQ_DEV
    active = jax.random.randint(key_on, (SEQS, span_count), 0, 2) == 1
    offsets = jax.random.randint(key_at, (SEQS, span_count), 0, 64)
    chosen = jax.random.randint(key_pick, (group_count, 1), 0, SEQ_DEV)
    member = (jnp.arange(SEQS) % SEQ_DEV).reshape(group_count, SEQ_DEV)
    single = (member == chosen).reshape(SEQS, 1)
    if SEQ_DEV > 1:
        filled = (member == (chosen + 1) % SEQ_DEV).reshape(SEQS, 1)
        active = active | filled
    active = active & jnp.logical_not(single)
    active = active & (jnp.arange(span_count) > 0)[None, :]
    places = jnp.arange(span_count)[None, :] * 64 + offsets
    hits = (jnp.arange(SEQ_LEN)[None, None, :] == places[:, :, None]) & active[:, :, None]
    boundary = jnp.sum(hits.astype(jnp.int32), axis=1)
    back_steps = jax.random.randint(key_end, (group_count, 1), 0, min(CH, 64) - 1)
    last_start = SEQ_LEN - 1 - jnp.broadcast_to(back_steps, (group_count, SEQ_DEV)).reshape(SEQS, 1)
    extra = (jnp.arange(SEQ_LEN)[None, :] == last_start) & single
    boundary = boundary + extra.astype(jnp.int32)
    return jnp.cumsum(boundary, axis=1).astype(jnp.int32)


def block_levels(own_key, shape, cuts, least, top_value):
    factor_of, own = 1.0, jax.random.fold_in(own_key, 6)
    for position, parts in cuts:
        draws = jnp.exp(jax.random.uniform(jax.random.fold_in(own, position), (parts,), jnp.float32, least / len(cuts), top_value / len(cuts)))
        factor_of = factor_of * jnp.repeat(draws, shape[position] // parts).reshape([-1 if axis == position else 1 for axis in range(len(shape))])
    return factor_of


def assign_block(key, own, number, rows, amount, top, bound, slope):
    sequence = jax.random.permutation(key, amount)
    crowded, usual = load_shares(amount, rows * top, bound, slope, True), load_shares(amount, rows * top, bound, slope, False)
    places = jnp.arange(amount)

    def named(tallies, turn):
        used = int((tallies > 0).sum())
        fixed = max(1, used // 4)
        passed = fixed + (places - fixed + turn * (used - fixed)) % max(1, amount - fixed)
        return jnp.zeros((amount,), jnp.int32).at[sequence[jnp.where(places < fixed, places, passed)]].set(jnp.asarray(tallies, jnp.int32))

    tallies = jnp.where(number % 4 == 0, named(crowded, number // 4), named(usual, number - number // 4 - 1))
    mixed = jax.random.permutation(jax.random.fold_in(own, 3), amount)
    giver, taker = mixed[0:amount // 2 * 2:2], mixed[1:amount // 2 * 2:2]
    margin = jnp.minimum(tallies[giver] - 1, bound - tallies[taker]) // 2
    margin = jnp.where((giver == sequence[0]) | (taker == sequence[0]) | (tallies[taker] == 0), 0, jnp.maximum(margin, 0))
    passed = jax.random.randint(jax.random.fold_in(own, 4), (amount // 2,), 0, 1 << 20) % (margin + 1)
    tallies = tallies.at[giver].add(-passed).at[taker].add(passed)
    items = jnp.searchsorted(jnp.cumsum(tallies), jnp.arange(rows * top), side="right").astype(jnp.int32)
    listing = items.reshape(top, rows).T
    listing = listing[jax.random.permutation(jax.random.fold_in(own, 1), rows)]
    turn = jax.random.randint(jax.random.fold_in(own, 2), (rows, 1), 0, top)
    return jnp.take_along_axis(listing, (jnp.arange(top)[None, :] + turn) % top, axis=1)


def load_shares(number_of, total, most, slope, full):
    weights = [(1 << 20) // math.isqrt(rank ** slope) + 1 for rank in range(1, number_of + 1)]
    largest = most if full else min(most, max(-(-total // number_of), total * weights[0] // sum(weights)))
    least = 1 if total - largest >= number_of - 1 else 0
    counts, spare = [largest] + [least] * (number_of - 1), total - largest - least * (number_of - 1)
    while spare > 0:
        movable = [i for i in range(1, number_of) if counts[i] < largest] or [i for i in range(1, number_of) if counts[i] < most]
        mass, budget = sum([weights[i] for i in movable]), spare
        for i in movable:
            addition = min(most - counts[i], max(1, budget * weights[i] // mass), spare)
            counts[i] = counts[i] + addition
            spare = spare - addition
    return np.array(counts)


def noise(key, shape, width, most, cuts=(), kind=jnp.bfloat16):
    drawn = width * jax.random.normal(key, shape, jnp.float32)
    if cuts:
        drawn = drawn * block_levels(key, shape, cuts, -0.22, 0.18)
    return jnp.clip(drawn, -most, most).astype(kind)


def setup_inputs(seed: int = 0) -> dict:
    keys = jax.random.split(jax.random.key(seed), 22)
    layer_in = noise(keys[0], (SEQS, SEQ_LEN, D), 1.0, 6.0, ((0, 8), (1, 4)))
    seg_ids = draw_seg_ids(jax.random.fold_in(keys[21], 71), 0)
    route_ids_keys = jax.random.split(jax.random.fold_in(keys[2], 1), SEQS * SEQ_LEN // CH)
    route_ids_turns = jax.random.permutation(jax.random.fold_in(keys[2], 3), SEQS * SEQ_LEN // CH)
    route_ids = jax.vmap(lambda own, number: assign_block(jax.random.fold_in(keys[2], 2), own, number, CH, EXPERTS, TOP, CAP, 0))(route_ids_keys, route_ids_turns).reshape((SEQS, SEQ_LEN, TOP))
    out_grad = noise(keys[3], (SEQS, SEQ_LEN, D), 1.0, 6.0, ((0, 8), (1, 4)))
    norm_in = jnp.clip(1.0 + 0.1 * jax.random.normal(keys[4], (D,), jnp.float32), 0.5, 1.5).astype(jnp.bfloat16)
    w_in = noise(keys[5], (D, PROJ), D ** -0.5, 0.15625, ((0, 32),))
    conv_w = noise(keys[6], (KC, CONV), 0.5, 3.0, ((1, 32),))
    conv_b = noise(keys[7], (CONV,), 0.3, 2.0, ((0, 32),))
    dt_bias = jnp.clip(jax.random.uniform(keys[8], (HEADS,), jnp.float32, -1.0, 1.0), -1.0, 1.0)
    a_log = jnp.clip(jax.random.uniform(keys[9], (HEADS,), jnp.float32, -7.0, -2.0), -7.0, -2.0)
    d_skip = jnp.clip(jax.random.uniform(keys[10], (HEADS,), jnp.float32, 0.5, 1.5), 0.5, 1.5)
    norm_gate = jnp.clip(1.0 + 0.1 * jax.random.normal(keys[11], (DI,), jnp.float32), 0.5, 1.5).astype(jnp.bfloat16)
    w_out = noise(keys[12], (DI, D), DI ** -0.5, 0.109375, ((0, 32),))
    norm_mid = jnp.clip(1.0 + 0.1 * jax.random.normal(keys[13], (D,), jnp.float32), 0.5, 1.5).astype(jnp.bfloat16)
    w_router = noise(keys[14], (D, EXPERTS), (4 * D) ** -0.5, 0.078125, ((0, 32),))
    w_sgate = noise(keys[15], (D, FS), D ** -0.5, 0.15625, ((0, 32),))
    w_sup = noise(keys[16], (D, FS), D ** -0.5, 0.15625, ((0, 32),))
    w_sdown = noise(keys[17], (FS, D), FS ** -0.5, 0.1875, ((0, 32),))
    e_gate = noise(keys[18], (EXPERTS, D, FE), D ** -0.5, 0.15625, ((0, 8), (1, 4)))
    e_up = noise(keys[19], (EXPERTS, D, FE), D ** -0.5, 0.15625, ((0, 8), (1, 4)))
    e_down = noise(keys[20], (EXPERTS, FE, D), FE ** -0.5, 0.25, ((0, 8), (2, 4)))
    return dict(layer_in=layer_in, seg_ids=seg_ids, route_ids=route_ids, out_grad=out_grad, norm_in=norm_in, w_in=w_in, conv_w=conv_w, conv_b=conv_b, dt_bias=dt_bias, a_log=a_log, d_skip=d_skip, norm_gate=norm_gate, w_out=w_out, norm_mid=norm_mid, w_router=w_router, w_sgate=w_sgate, w_sup=w_sup, w_sdown=w_sdown, e_gate=e_gate, e_up=e_up, e_down=e_down)


@jax.custom_vjp
def low(v):
    return lax.optimization_barrier(v.astype(jnp.bfloat16)).astype(jnp.float32)

@jax.custom_vjp
def low_back(v):
    return v

def low_keep(v):
    return (low(v), None)

def low_pass(kept, grad):
    return (grad,)

def back_keep(v):
    return (v, None)

def back_low(kept, grad):
    return (low(grad),)
low.defvjp(low_keep, low_pass)
low_back.defvjp(back_keep, back_low)

def normalize(value):
    return value * lax.rsqrt(lax.optimization_barrier(jnp.mean(value * value, axis=-1, keepdims=True)) + 1e-05)

def gate_norm(y_heads, z_part, gain):
    joined = y_heads.reshape(z_part.shape) * jax.nn.silu(z_part)
    return normalize(joined) * gain

def conv_apply(padded, weight, bias, seg_pad):
    tap_count = weight.shape[0]
    length = padded.shape[1] - tap_count + 1
    current = seg_pad[:, tap_count - 1:]
    summed = bias + jnp.zeros(padded[:, tap_count - 1:].shape, jnp.float32)
    for offset in range(tap_count):
        matches = (seg_pad[:, offset:offset + length] == current).astype(jnp.float32)
        summed = summed + weight[offset] * padded[:, offset:offset + length] * matches[..., None]
    return jax.nn.silu(summed)

def split_blocks(value, count):
    shaped = value.reshape((value.shape[0], count, value.shape[1] // count) + value.shape[2:])
    return jnp.moveaxis(shaped, 1, 0)

def block_step(carried_in, pieces):
    memory, previous = carried_in
    x_heads, b_mat, c_mat, dt_pos, decay, segment_ids = pieces
    cumul = jnp.cumsum(decay, axis=1)
    places = jnp.arange(segment_ids.shape[1])
    causal = places[:, None] >= places[None, :]
    linked = ((segment_ids[:, :, None] == segment_ids[:, None, :]) & causal[None])[..., None]
    spread = cumul[:, :, None, :] - cumul[:, None, :, :]
    weights = jnp.where(linked, jnp.exp(jnp.where(linked, spread, 0.0)), 0.0)
    inner = jnp.einsum('gtn,gsn->gts', c_mat, b_mat, precision=lax.Precision.HIGHEST)
    weights = weights * inner[..., None] * dt_pos[:, None, :, :]
    output = jnp.einsum('gtsh,gshp->gthp', weights, x_heads, precision=lax.Precision.HIGHEST)
    keeps = (segment_ids == previous[:, None]).astype(jnp.float32)
    reach = jnp.exp(cumul) * keeps[..., None]
    output = output + jnp.einsum('gtn,ghpn->gthp', c_mat, memory, precision=lax.Precision.HIGHEST) * reach[..., None]
    latest = segment_ids[:, -1]
    tails = jnp.exp(cumul[:, -1:, :] - cumul) * (segment_ids == latest[:, None]).astype(jnp.float32)[..., None] * dt_pos
    through = jnp.exp(cumul[:, -1, :]) * (latest == previous).astype(jnp.float32)[:, None]
    memory = memory * through[..., None, None] + jnp.einsum('gsh,gshp,gsn->ghpn', tails, x_heads, b_mat, precision=lax.Precision.HIGHEST)
    return ((memory, latest), output)

def scan_blocks(x_heads, b_mat, c_mat, dt_pos, decay, segment_ids, memory, previous):
    length = segment_ids.shape[1]
    count = length // min(128, length)
    inputs = tuple((split_blocks(value, count) for value in (x_heads, b_mat, c_mat, dt_pos, decay, segment_ids)))
    (memory, latest), outputs = lax.scan(jax.checkpoint(block_step), (memory, previous), inputs)
    return (jnp.moveaxis(outputs, 0, 1).reshape(x_heads.shape), memory)

def route_slots(flat_routes, expert_count, capacity):
    blocks = flat_routes.shape[0]
    onehot = (flat_routes[..., None] == jnp.arange(expert_count, dtype=jnp.int32)).astype(jnp.int32)
    ranks = lax.optimization_barrier(jnp.sum((jnp.cumsum(onehot, axis=1) - onehot) * onehot, axis=-1))
    spots = flat_routes * (blocks * capacity) + jnp.arange(blocks, dtype=jnp.int32)[:, None] * capacity + ranks
    return spots.astype(jnp.int32)

def layer_forward(inputs, segments, routes, norm_in, w_in, conv_w, conv_b, dt_bias, a_log, d_skip, norm_gate, w_out, norm_mid, w_router, w_sgate, w_sup, w_sdown, e_gate, e_up, e_down):
    seq_count = inputs.shape[0]
    normed = low(normalize(inputs) * norm_in)
    projected = low_back(jnp.einsum('gld,dp->glp', normed, w_in, precision=lax.Precision.HIGHEST))
    z_part = projected[..., :DI]
    xbc_part = projected[..., DI:DI + CONV]
    dt_raw = projected[..., DI + CONV:]
    seg_pad = jnp.concatenate([jnp.full((seq_count, KC - 1), -1, jnp.int32), segments], axis=1)
    padded = jnp.concatenate([jnp.zeros((seq_count, KC - 1, CONV), jnp.float32), xbc_part], axis=1)
    conv_out = conv_apply(padded, conv_w, conv_b, seg_pad)
    x_heads = conv_out[..., :DI].reshape(seq_count, SEQ_LEN, HEADS, HEAD)
    b_mat = conv_out[..., DI:DI + STATE]
    c_mat = conv_out[..., DI + STATE:]
    dt_pos = jax.nn.softplus(dt_raw + dt_bias)
    decay = -jnp.exp(a_log) * dt_pos
    start_state = jnp.zeros((seq_count, HEADS, HEAD, STATE), jnp.float32)
    before = jnp.full((seq_count,), -1, jnp.int32)
    mixed_heads, final_state = scan_blocks(x_heads, b_mat, c_mat, dt_pos, decay, segments, start_state, before)
    y_heads = mixed_heads + d_skip[:, None] * x_heads
    gated = low(gate_norm(y_heads, z_part, norm_gate))
    mixed = low_back(jnp.einsum('gli,id->gld', gated, w_out, precision=lax.Precision.HIGHEST))
    resid_mid = inputs + mixed
    normed_mid = low(normalize(resid_mid) * norm_mid)
    logits = low_back(jnp.einsum('gld,de->gle', normed_mid, w_router, precision=lax.Precision.HIGHEST))
    gates = jax.nn.softmax(jnp.take_along_axis(logits, routes, axis=-1), axis=-1)
    shared_gate = low_back(jnp.einsum('gld,df->glf', normed_mid, w_sgate, precision=lax.Precision.HIGHEST))
    shared_up = low_back(jnp.einsum('gld,df->glf', normed_mid, w_sup, precision=lax.Precision.HIGHEST))
    shared_act = low(jax.nn.silu(shared_gate) * shared_up)
    shared_out = low_back(jnp.einsum('glf,fd->gld', shared_act, w_sdown, precision=lax.Precision.HIGHEST))
    flat_routes = routes.reshape(seq_count * N_CTX, CH * TOP)
    slot_ids = route_slots(flat_routes, EXPERTS, CAP)
    block_count = slot_ids.shape[0]
    assigned = jnp.arange(slot_ids.size, dtype=jnp.int32)
    owners = jnp.full((EXPERTS * block_count * CAP,), slot_ids.size, jnp.int32).at[slot_ids.reshape(-1)].set(assigned)
    rows_pad = jnp.concatenate([normed_mid.reshape(-1, D), jnp.zeros((1, D), jnp.float32)], axis=0)
    dispatched = low_back(rows_pad[owners // TOP].reshape(EXPERTS, block_count * CAP, D))
    hidden_gate = low_back(jnp.einsum('erd,edf->erf', dispatched, e_gate, precision=lax.Precision.HIGHEST))
    hidden_up = low_back(jnp.einsum('erd,edf->erf', dispatched, e_up, precision=lax.Precision.HIGHEST))
    hidden_act = low(jax.nn.silu(hidden_gate) * hidden_up)
    expert_out = low(low_back(jnp.einsum('erf,efd->erd', hidden_act, e_down, precision=lax.Precision.HIGHEST)))
    picked = expert_out.reshape(-1, D)[slot_ids.reshape(seq_count, SEQ_LEN, TOP)]
    routed = lax.optimization_barrier(jnp.sum(gates[..., None] * picked, axis=2))
    return resid_mid + shared_out + routed

def reference(layer_in, seg_ids, route_ids, out_grad, norm_in, w_in, conv_w, conv_b, dt_bias, a_log, d_skip, norm_gate, w_out, norm_mid, w_router, w_sgate, w_sup, w_sdown, e_gate, e_up, e_down):
    params = tuple((value.astype(jnp.float32) for value in (norm_in, w_in, conv_w, conv_b, dt_bias, a_log, d_skip, norm_gate, w_out, norm_mid, w_router, w_sgate, w_sup, w_sdown, e_gate, e_up, e_down)))
    group_count = SEQS // SEQ_DEV

    def regroup(value):
        return value.reshape((group_count, SEQ_DEV) + value.shape[1:])

    def one_group(totals, pieces):
        group_in, group_seg, group_route, group_grad = pieces

        def forward_of(inputs, *weights):
            return layer_forward(inputs, group_seg, group_route, *weights)
        result, pull = jax.vjp(forward_of, group_in.astype(jnp.float32), *params)
        gradient = pull(group_grad.astype(jnp.float32))
        totals = tuple((summed + piece for summed, piece in zip(totals, gradient[1:])))
        return (totals, (result.astype(jnp.bfloat16), gradient[0]))
    start = tuple((jnp.zeros(value.shape, jnp.float32) for value in params))
    totals, (outputs, grad_inputs) = lax.scan(one_group, start, (regroup(layer_in), regroup(seg_ids), regroup(route_ids), regroup(out_grad)))
    return (outputs.reshape(layer_in.shape), grad_inputs.reshape(layer_in.shape), totals[0], totals[1], totals[2], totals[3], totals[4], totals[5], totals[6], totals[7], totals[8], totals[9], totals[10], totals[11], totals[12], totals[13], totals[14], totals[15], totals[16])
```

```python
from functools import partial

import jax
import jax.numpy as jnp
from jax import lax
from jax.experimental import pallas as pl
from jax.experimental.pallas import tpu as pltpu
from jax.sharding import PartitionSpec as P

HEADS = 48
HEAD = 64
STATE = 128
TOP = 6
EXP_DEV = 4
DI = 3072
CONV = 3328
PROJ = 6448


def from_behind(value, axis, steps):
    count = lax.axis_size(axis)
    leading, last = (max(0, -steps), min(count, count - steps))
    return lax.ppermute(value, axis, [(source, source + steps) for source in range(leading, last)])


def carried_in_2(x, axis, combine, identity):
    count, mine = (lax.axis_size(axis), lax.axis_index(axis))
    everything = jax.tree.map(
        lambda part, kind: lax.all_gather(part.astype(kind), axis), x, (jnp.bfloat16, jnp.bfloat16)
    )
    start = jax.tree.map(
        lambda part, zero: jnp.broadcast_to(jnp.asarray(zero, part.dtype), part.shape), x, identity
    )

    def lap(k, before):
        reached = k < mine
        new = combine(
            before, jax.tree.map(lambda part, own: part[k].astype(own.dtype), everything, x)
        )
        return jax.tree.map(lambda a, b: jnp.where(reached, a, b), new, before)

    return lax.fori_loop(0, count, lap, start)


def carried_in_3(x, axis, combine, identity):
    count, mine = (lax.axis_size(axis), lax.axis_index(axis))
    everything = jax.tree.map(
        lambda part, kind: lax.all_gather(part.astype(kind), axis),
        x,
        jax.tree.map(lambda a: jnp.bfloat16 if a.dtype == jnp.float32 else a.dtype, x),
    )
    start = jax.tree.map(
        lambda part, zero: jnp.broadcast_to(jnp.asarray(zero, part.dtype), part.shape), x, identity
    )

    def lap(k, before):
        at = count - 1 - k
        reached = at > mine
        new = combine(
            before, jax.tree.map(lambda part, own: part[at].astype(own.dtype), everything, x)
        )
        return jax.tree.map(lambda a, b: jnp.where(reached, a, b), new, before)

    return lax.fori_loop(0, count, lap, start)


def for_sending(x):
    return jax.tree.map(lambda a: a.astype(jnp.bfloat16) if a.dtype == jnp.float32 else a, x)


def normalize(value):
    return value * lax.rsqrt(jnp.mean(value * value, axis=-1, keepdims=True) + 1e-05)


def scaled_norm(value, gain):
    return normalize(value) * gain


def gate_norm(y_heads, z_part, gain):
    joined = y_heads.reshape(z_part.shape) * jax.nn.silu(z_part)
    return normalize(joined) * gain


def silu_slope(value):
    squashed = jax.nn.sigmoid(value)
    return squashed * (1.0 + value * (1.0 - squashed))


def conv_apply(padded, weight, bias, seg_pad):
    tap_count = weight.shape[0]
    length = padded.shape[1] - tap_count + 1
    current = seg_pad[:, tap_count - 1 :]
    summed = bias + jnp.zeros(padded[:, tap_count - 1 :].shape, jnp.float32)
    for offset in range(tap_count):
        matches = (seg_pad[:, offset : offset + length] == current).astype(jnp.float32)
        summed = summed + weight[offset] * padded[:, offset : offset + length] * matches[..., None]
    return jax.nn.silu(summed)


def split_blocks(value, count):
    shaped = value.reshape((value.shape[0], count, value.shape[1] // count) + value.shape[2:])
    return jnp.moveaxis(shaped, 1, 0)


def block_step(carried_in, pieces):
    memory, previous = carried_in
    x_heads, b_mat, c_mat, dt_pos, decay, segment_ids = pieces
    cumul = jnp.cumsum(decay, axis=1)
    places = jnp.arange(segment_ids.shape[1])
    causal = places[:, None] >= places[None, :]
    linked = ((segment_ids[:, :, None] == segment_ids[:, None, :]) & causal[None])[..., None]
    spread = cumul[:, :, None, :] - cumul[:, None, :, :]
    weights = jnp.where(linked, jnp.exp(jnp.where(linked, spread, 0.0)), 0.0)
    inner = jnp.einsum("gtn,gsn->gts", c_mat, b_mat, precision=lax.Precision.HIGHEST)
    weights = weights * inner[..., None] * dt_pos[:, None, :, :]
    output = jnp.einsum("gtsh,gshp->gthp", weights, x_heads, precision=lax.Precision.HIGHEST)
    keeps = (segment_ids == previous[:, None]).astype(jnp.float32)
    reach = jnp.exp(cumul) * keeps[..., None]
    output = (
        output
        + jnp.einsum("gtn,ghpn->gthp", c_mat, memory, precision=lax.Precision.HIGHEST)
        * reach[..., None]
    )
    latest = segment_ids[:, -1]
    tails = (
        jnp.exp(cumul[:, -1:, :] - cumul)
        * (segment_ids == latest[:, None]).astype(jnp.float32)[..., None]
        * dt_pos
    )
    through = jnp.exp(cumul[:, -1, :]) * (latest == previous).astype(jnp.float32)[:, None]
    memory = memory * through[..., None, None] + jnp.einsum(
        "gsh,gshp,gsn->ghpn", tails, x_heads, b_mat, precision=lax.Precision.HIGHEST
    )
    return ((memory, latest), output)


def scan_blocks(x_heads, b_mat, c_mat, dt_pos, decay, segment_ids, memory, previous):
    length = segment_ids.shape[1]
    count = length // min(128, length)
    inputs = tuple(
        (
            split_blocks(value, count)
            for value in (x_heads, b_mat, c_mat, dt_pos, decay, segment_ids)
        )
    )
    (memory, latest), outputs = lax.scan(jax.checkpoint(block_step), (memory, previous), inputs)
    return (jnp.moveaxis(outputs, 0, 1).reshape(x_heads.shape), memory)


def part_local(x_heads, b_mat, c_mat, dt_raw, dt_bias, a_log, d_skip, segment_ids, previous):
    dt_pos = jax.nn.softplus(dt_raw + dt_bias)
    decay = -jnp.exp(a_log) * dt_pos
    zero_state = jnp.zeros((x_heads.shape[0], HEADS, HEAD, STATE), jnp.float32)
    mixed_heads, final_state = scan_blocks(
        x_heads, b_mat, c_mat, dt_pos, decay, segment_ids, zero_state, previous
    )
    y_local = mixed_heads + d_skip[:, None] * x_heads
    through = (
        jnp.exp(jnp.sum(decay, axis=1))
        * (segment_ids[:, -1] == previous).astype(jnp.float32)[:, None]
    )
    return (y_local, final_state, through)


def part_carry(c_mat, dt_raw, dt_bias, a_log, state_in, segment_ids, previous):
    dt_pos = jax.nn.softplus(dt_raw + dt_bias)
    cumul = jnp.cumsum(-jnp.exp(a_log) * dt_pos, axis=1)
    keeps = (segment_ids == previous[:, None]).astype(jnp.float32)
    reach = jnp.exp(cumul) * keeps[..., None]
    return (
        jnp.einsum("gtn,ghpn->gthp", c_mat, state_in, precision=lax.Precision.HIGHEST)
        * reach[..., None]
    )


def carry_forward(earlier, later):
    return (earlier[0] * later[0], later[0][..., None, None] * earlier[1] + later[1])


def carry_backward(earlier, later):
    return (earlier[0] * later[0], later[1] + later[0][..., None, None] * earlier[1])


def route_slots(flat_routes, expert_count, capacity):
    blocks = flat_routes.shape[0]
    onehot = (flat_routes[..., None] == jnp.arange(expert_count, dtype=jnp.int32)).astype(jnp.int32)
    ranks = jnp.sum((jnp.cumsum(onehot, axis=1) - onehot) * onehot, axis=-1)
    spots = (
        flat_routes * (blocks * capacity)
        + jnp.arange(blocks, dtype=jnp.int32)[:, None] * capacity
        + ranks
    )
    return spots


def times_rows(left, right):
    return lax.dot_general(
        left, right, (((0,), (0,)), ((), ())), preferred_element_type=jnp.float32
    )


def times_back(left, right):
    return lax.dot_general(
        left, right, (((1,), (1,)), ((), ())), preferred_element_type=jnp.float32
    )


def on_device_general(
    layer_in,
    seg_ids,
    route_ids,
    out_grad,
    norm_in,
    w_in,
    conv_w,
    conv_b,
    dt_bias,
    a_log,
    d_skip,
    norm_gate,
    w_out,
    norm_mid,
    w_router,
    w_sgate,
    w_sup,
    w_sdown,
    e_gate,
    e_up,
    e_down,
):
    seq_count, row_count, d_model = layer_in.shape
    token_count = seq_count * row_count
    tap_count = conv_w.shape[0]
    ctx_place = lax.axis_index("ctx")
    expert_count = EXP_DEV * lax.axis_size("dp")
    capacity = row_count * TOP * 5 // (expert_count * 4)
    dense_set = (
        lax.all_gather(norm_in, ("dp", "ctx"), axis=0, tiled=True),
        lax.all_gather(w_in, ("dp", "ctx"), axis=0, tiled=True),
        lax.all_gather(conv_w, ("dp", "ctx"), axis=1, tiled=True),
        lax.all_gather(conv_b, ("dp", "ctx"), axis=0, tiled=True),
        lax.all_gather(norm_gate, ("dp", "ctx"), axis=0, tiled=True),
        lax.all_gather(w_out, ("dp", "ctx"), axis=0, tiled=True),
        lax.all_gather(norm_mid, ("dp", "ctx"), axis=0, tiled=True),
        lax.all_gather(w_router, ("dp", "ctx"), axis=0, tiled=True),
        lax.all_gather(w_sgate, ("dp", "ctx"), axis=0, tiled=True),
        lax.all_gather(w_sup, ("dp", "ctx"), axis=0, tiled=True),
        lax.all_gather(w_sdown, ("dp", "ctx"), axis=0, tiled=True),
    )
    (
        gain_in,
        weight_in,
        conv_weight,
        conv_bias,
        gain_gate,
        weight_out,
        gain_mid,
        router_weight,
        sgate_weight,
        sup_weight,
        sdown_weight,
    ) = dense_set
    expert_gate, expert_up, expert_down = (
        lax.all_gather(e_gate, "ctx", axis=1, tiled=True),
        lax.all_gather(e_up, "ctx", axis=1, tiled=True),
        lax.all_gather(e_down, "ctx", axis=2, tiled=True),
    )
    input_f = layer_in.astype(jnp.float32)
    normed_f, pull_in = jax.vjp(scaled_norm, input_f, gain_in.astype(jnp.float32))
    normed = normed_f.astype(jnp.bfloat16).reshape(token_count, d_model)
    projected = jnp.dot(normed, weight_in, preferred_element_type=jnp.float32).reshape(
        seq_count, row_count, PROJ
    )
    z_part = projected[..., :DI]
    xbc_part = projected[..., DI : DI + CONV]
    dt_raw = projected[..., DI + CONV :]
    edge_rows = from_behind(
        xbc_part[:, row_count - tap_count + 1 :, :].astype(jnp.bfloat16), "ctx", 1
    ).astype(jnp.float32)
    seg_pad = jnp.concatenate(
        [jnp.full((seq_count, tap_count - 1), -1, jnp.int32), seg_ids], axis=1
    )
    seg_window = lax.dynamic_slice_in_dim(
        seg_pad, ctx_place * row_count, row_count + tap_count - 1, 1
    )
    seg_now = seg_window[:, tap_count - 1 :]
    seg_before = seg_window[:, tap_count - 2]
    padded = jnp.concatenate([edge_rows, xbc_part], axis=1)
    conv_out, pull_conv = jax.vjp(
        partial(conv_apply, seg_pad=seg_window),
        padded,
        conv_weight.astype(jnp.float32),
        conv_bias.astype(jnp.float32),
    )
    x_heads = conv_out[..., :DI].reshape(seq_count, row_count, HEADS, HEAD)
    b_mat = conv_out[..., DI : DI + STATE]
    c_mat = conv_out[..., DI + STATE :]
    local_piece = partial(part_local, segment_ids=seg_now, previous=seg_before)
    (y_local, state_out, through), pull_local = jax.vjp(
        local_piece, x_heads, b_mat, c_mat, dt_raw, dt_bias, a_log, d_skip
    )
    carried = carried_in_2(
        (through, state_out),
        "ctx",
        carry_forward,
        (jnp.ones_like(through), jnp.zeros_like(state_out)),
    )
    state_in = carried[1]
    carry_piece = partial(part_carry, segment_ids=seg_now, previous=seg_before)
    y_carry, pull_carry = jax.vjp(carry_piece, c_mat, dt_raw, dt_bias, a_log, state_in)
    gated_f, pull_gate = jax.vjp(
        gate_norm, y_local + y_carry, z_part, gain_gate.astype(jnp.float32)
    )
    gated = gated_f.astype(jnp.bfloat16).reshape(token_count, DI)
    mixed = jnp.dot(gated, weight_out, preferred_element_type=jnp.float32)
    resid_mid = input_f.reshape(token_count, d_model) + mixed
    normed_mid_f, pull_mid = jax.vjp(scaled_norm, resid_mid, gain_mid.astype(jnp.float32))
    normed_mid = normed_mid_f.astype(jnp.bfloat16)
    logits = jnp.dot(normed_mid, router_weight, preferred_element_type=jnp.float32)
    route_flat = route_ids.reshape(token_count, TOP)
    gates = jax.nn.softmax(jnp.take_along_axis(logits, route_flat, axis=1), axis=-1)
    shared_gate = jnp.dot(normed_mid, sgate_weight, preferred_element_type=jnp.float32)
    shared_up = jnp.dot(normed_mid, sup_weight, preferred_element_type=jnp.float32)
    shared_act = (jax.nn.silu(shared_gate) * shared_up).astype(jnp.bfloat16)
    shared_out = jnp.dot(shared_act, sdown_weight, preferred_element_type=jnp.float32)
    slot_ids = route_slots(route_ids.reshape(seq_count, row_count * TOP), expert_count, capacity)
    assigned = jnp.arange(token_count * TOP, dtype=jnp.int32)
    owners = (
        jnp.full((expert_count * seq_count * capacity,), token_count * TOP, jnp.int32)
        .at[slot_ids.reshape(-1)]
        .set(assigned)
    )
    token_of = owners // TOP
    rows_pad = jnp.concatenate([normed_mid, jnp.zeros((1, d_model), jnp.bfloat16)], axis=0)
    outgoing = rows_pad[token_of].reshape(expert_count, seq_count * capacity, d_model)
    incoming = lax.all_to_all(outgoing, "dp", split_axis=0, concat_axis=1, tiled=True)
    hidden_gate = jnp.einsum(
        "erd,edf->erf", incoming, expert_gate, preferred_element_type=jnp.float32
    )
    hidden_up = jnp.einsum("erd,edf->erf", incoming, expert_up, preferred_element_type=jnp.float32)
    hidden_act = (jax.nn.silu(hidden_gate) * hidden_up).astype(jnp.bfloat16)
    expert_out = jnp.einsum(
        "erf,efd->erd", hidden_act, expert_down, preferred_element_type=jnp.float32
    ).astype(jnp.bfloat16)
    returned = lax.all_to_all(expert_out, "dp", split_axis=1, concat_axis=0, tiled=True)
    slot_flat = slot_ids.reshape(token_count, TOP)
    picked = returned.reshape(-1, d_model)[slot_flat]
    routed = jnp.sum(gates[..., None] * picked, axis=1)
    layer_out = (
        (resid_mid + shared_out + routed)
        .astype(jnp.bfloat16)
        .reshape(seq_count, row_count, d_model)
    )
    grad_top = out_grad.astype(jnp.float32).reshape(token_count, d_model)
    grad_gates = jnp.sum(picked * grad_top[:, None, :], axis=-1)
    grad_pick = gates * (grad_gates - jnp.sum(gates * grad_gates, axis=-1, keepdims=True))
    expert_ids = jnp.arange(expert_count, dtype=jnp.int32)
    grad_logits = jnp.sum(
        grad_pick[..., None] * (route_flat[..., None] == expert_ids).astype(jnp.float32), axis=1
    ).astype(jnp.bfloat16)
    gates_pad = jnp.concatenate([gates.reshape(-1), jnp.zeros((1,), jnp.float32)])
    grad_pad = jnp.concatenate([grad_top, jnp.zeros((1, d_model), jnp.float32)], axis=0)
    grad_slots = (
        (gates_pad[owners][:, None] * grad_pad[token_of])
        .astype(jnp.bfloat16)
        .reshape(expert_count, seq_count * capacity, d_model)
    )
    grad_arrived = lax.all_to_all(grad_slots, "dp", split_axis=0, concat_axis=1, tiled=True)
    grad_act = jnp.einsum(
        "erd,efd->erf", grad_arrived, expert_down, preferred_element_type=jnp.float32
    )
    grad_e_down = jnp.einsum(
        "erf,erd->efd", hidden_act, grad_arrived, preferred_element_type=jnp.float32
    )
    grad_hgate = (grad_act * hidden_up * silu_slope(hidden_gate)).astype(jnp.bfloat16)
    grad_hup = (grad_act * jax.nn.silu(hidden_gate)).astype(jnp.bfloat16)
    grad_e_gate = jnp.einsum(
        "erd,erf->edf", incoming, grad_hgate, preferred_element_type=jnp.float32
    )
    grad_e_up = jnp.einsum("erd,erf->edf", incoming, grad_hup, preferred_element_type=jnp.float32)
    grad_incoming = jnp.einsum(
        "erf,edf->erd", grad_hgate, expert_gate, preferred_element_type=jnp.float32
    )
    grad_incoming = (
        grad_incoming
        + jnp.einsum("erf,edf->erd", grad_hup, expert_up, preferred_element_type=jnp.float32)
    ).astype(jnp.bfloat16)
    grad_returned = lax.all_to_all(grad_incoming, "dp", split_axis=1, concat_axis=0, tiled=True)
    grad_routed = jnp.sum(grad_returned.reshape(-1, d_model)[slot_flat], axis=1, dtype=jnp.float32)
    dense_set = (
        lax.all_gather(norm_in, ("dp", "ctx"), axis=0, tiled=True),
        lax.all_gather(w_in, ("dp", "ctx"), axis=0, tiled=True),
        lax.all_gather(conv_w, ("dp", "ctx"), axis=1, tiled=True),
        lax.all_gather(conv_b, ("dp", "ctx"), axis=0, tiled=True),
        lax.all_gather(norm_gate, ("dp", "ctx"), axis=0, tiled=True),
        lax.all_gather(w_out, ("dp", "ctx"), axis=0, tiled=True),
        lax.all_gather(norm_mid, ("dp", "ctx"), axis=0, tiled=True),
        lax.all_gather(w_router, ("dp", "ctx"), axis=0, tiled=True),
        lax.all_gather(w_sgate, ("dp", "ctx"), axis=0, tiled=True),
        lax.all_gather(w_sup, ("dp", "ctx"), axis=0, tiled=True),
        lax.all_gather(w_sdown, ("dp", "ctx"), axis=0, tiled=True),
    )
    (
        gain_in,
        weight_in,
        conv_weight,
        conv_bias,
        gain_gate,
        weight_out,
        gain_mid,
        router_weight,
        sgate_weight,
        sup_weight,
        sdown_weight,
    ) = dense_set
    grad_w_router = times_rows(normed_mid, grad_logits)
    grad_shared_out = grad_top.astype(jnp.bfloat16)
    grad_w_sdown = times_rows(shared_act, grad_shared_out)
    grad_shared_act = times_back(grad_shared_out, sdown_weight)
    grad_sgate = (grad_shared_act * shared_up * silu_slope(shared_gate)).astype(jnp.bfloat16)
    grad_sup = (grad_shared_act * jax.nn.silu(shared_gate)).astype(jnp.bfloat16)
    grad_w_sgate = times_rows(normed_mid, grad_sgate)
    grad_w_sup = times_rows(normed_mid, grad_sup)
    grad_mid = (
        grad_routed
        + times_back(grad_logits, router_weight)
        + times_back(grad_sgate, sgate_weight)
        + times_back(grad_sup, sup_weight)
    )
    grad_resid_part, grad_gain_mid = pull_mid(grad_mid)
    grad_resid = grad_top + grad_resid_part
    grad_mixed = grad_resid.astype(jnp.bfloat16)
    grad_w_out = times_rows(gated, grad_mixed)
    grad_gated = times_back(grad_mixed, weight_out).reshape(seq_count, row_count, DI)
    grad_y, grad_z, grad_gain_gate = pull_gate(grad_gated)
    grad_cmat_carry, grad_dt_carry, grad_bias_carry, grad_alog_carry, grad_state_in = pull_carry(
        grad_y
    )
    back_scan = carried_in_3(
        (through, grad_state_in),
        "ctx",
        carry_backward,
        (jnp.ones_like(through), jnp.zeros_like(grad_state_in)),
    )
    grad_state_out = back_scan[1]
    grad_through = jnp.sum(state_in * grad_state_out, axis=(2, 3))
    (
        grad_xheads,
        grad_bmat,
        grad_cmat,
        grad_dt_local,
        grad_bias_local,
        grad_alog_local,
        grad_dskip,
    ) = pull_local((grad_y, grad_state_out, grad_through))
    grad_conv_out = jnp.concatenate(
        [grad_xheads.reshape(seq_count, row_count, DI), grad_bmat, grad_cmat + grad_cmat_carry],
        axis=-1,
    )
    grad_padded, grad_conv_w, grad_conv_b = pull_conv(grad_conv_out)
    edge_grad = from_behind(for_sending(grad_padded[:, : tap_count - 1, :]), "ctx", -1)
    grad_xbc = grad_padded[:, tap_count - 1 :, :]
    grad_xbc = jnp.concatenate(
        [
            grad_xbc[:, : row_count - tap_count + 1],
            grad_xbc[:, row_count - tap_count + 1 :] + edge_grad,
        ],
        axis=1,
    )
    grad_proj = (
        jnp.concatenate([grad_z, grad_xbc, grad_dt_local + grad_dt_carry], axis=-1)
        .astype(jnp.bfloat16)
        .reshape(token_count, PROJ)
    )
    grad_w_in = times_rows(normed, grad_proj)
    grad_normed = times_back(grad_proj, weight_in).reshape(seq_count, row_count, d_model)
    grad_input_part, grad_gain_in = pull_in(grad_normed)
    grad_in = grad_resid.reshape(seq_count, row_count, d_model) + grad_input_part
    dense_grads = (
        lax.psum_scatter(grad_gain_in, ("dp", "ctx"), scatter_dimension=0, tiled=True),
        lax.psum_scatter(grad_w_in, ("dp", "ctx"), scatter_dimension=0, tiled=True),
        lax.psum_scatter(grad_conv_w, ("dp", "ctx"), scatter_dimension=1, tiled=True),
        lax.psum_scatter(grad_conv_b, ("dp", "ctx"), scatter_dimension=0, tiled=True),
        lax.psum_scatter(grad_gain_gate, ("dp", "ctx"), scatter_dimension=0, tiled=True),
        lax.psum_scatter(grad_w_out, ("dp", "ctx"), scatter_dimension=0, tiled=True),
        lax.psum_scatter(grad_gain_mid, ("dp", "ctx"), scatter_dimension=0, tiled=True),
        lax.psum_scatter(grad_w_router, ("dp", "ctx"), scatter_dimension=0, tiled=True),
        lax.psum_scatter(grad_w_sgate, ("dp", "ctx"), scatter_dimension=0, tiled=True),
        lax.psum_scatter(grad_w_sup, ("dp", "ctx"), scatter_dimension=0, tiled=True),
        lax.psum_scatter(grad_w_sdown, ("dp", "ctx"), scatter_dimension=0, tiled=True),
    )
    expert_grads = (
        lax.psum_scatter(
            grad_e_gate.astype(jnp.bfloat16), "ctx", scatter_dimension=1, tiled=True
        ).astype(jnp.float32),
        lax.psum_scatter(
            grad_e_up.astype(jnp.bfloat16), "ctx", scatter_dimension=1, tiled=True
        ).astype(jnp.float32),
        lax.psum_scatter(
            grad_e_down.astype(jnp.bfloat16), "ctx", scatter_dimension=2, tiled=True
        ).astype(jnp.float32),
    )
    head_grads = lax.psum(
        (grad_bias_local + grad_bias_carry, grad_alog_local + grad_alog_carry, grad_dskip),
        ("dp", "ctx"),
    )
    return (
        layer_out,
        grad_in,
        dense_grads[0],
        dense_grads[1],
        dense_grads[2],
        dense_grads[3],
        head_grads[0],
        head_grads[1],
        head_grads[2],
        dense_grads[4],
        dense_grads[5],
        dense_grads[6],
        dense_grads[7],
        dense_grads[8],
        dense_grads[9],
        dense_grads[10],
        expert_grads[0],
        expert_grads[1],
        expert_grads[2],
    )


GROUP = 8
WIDE = GROUP * HEAD
VMEM_MOST = 56 * 1024 * 1024


def spread_rows(rows):
    count, width = rows.shape
    return jnp.broadcast_to(rows[:, None, :], (count, HEAD, width)).reshape(count * HEAD, width)


def head_sums(value):
    return jnp.sum(value.reshape(GROUP, HEAD, value.shape[-1]), axis=1)


def mul_nn(left, right):
    return lax.dot_general(
        left, right, (((1,), (0,)), ((), ())), preferred_element_type=jnp.float32
    )


def mul_nt(left, right):
    return lax.dot_general(
        left, right, (((1,), (1,)), ((), ())), preferred_element_type=jnp.float32
    )


def mul_tn(left, right):
    return lax.dot_general(
        left, right, (((0,), (0,)), ((), ())), preferred_element_type=jnp.float32
    )


def half(value):
    return value.astype(jnp.bfloat16)


def call_steps(kernel, steps, ins, in_specs, outs, out_specs, scratch=(), flops=1 << 30):
    return pl.pallas_call(
        kernel,
        grid=(steps,),
        in_specs=in_specs,
        out_specs=out_specs,
        out_shape=outs,
        scratch_shapes=list(scratch),
        cost_estimate=pl.CostEstimate(flops=flops, bytes_accessed=8 << 20, transcendentals=0),
        compiler_params=pltpu.CompilerParams(
            vmem_limit_bytes=VMEM_MOST, dimension_semantics=("arbitrary",)
        ),
    )(*ins)


def block(shape, index):
    return pl.BlockSpec(shape, index)


def whole(array):
    return pl.BlockSpec(array.shape, lambda i: (0,) * array.ndim)


def f32_out(*shape):
    return jax.ShapeDtypeStruct(shape, jnp.float32)


def bf16_out(*shape):
    return jax.ShapeDtypeStruct(shape, jnp.bfloat16)


def conv_steps(x, taps, masks):
    total = taps[:, 4:5] + taps[:, 3:4] * x * masks[0:1]
    for back in (1, 2, 3):
        total = total + taps[:, 3 - back : 4 - back] * pltpu.roll(x, back, 1) * masks[back : back + 1]
    return total


def conv_kernel(x_ref, taps_ref, masks_ref, pre_ref):
    tokens = pre_ref.shape[1]
    pre_ref[...] = conv_steps(x_ref[...], taps_ref[...], masks_ref[...])[:, :tokens]


def conv_adjoint(grad_pre, x, taps, masks):
    width = x.shape[1]
    grad_x = jnp.zeros_like(x)
    columns = []
    for back in (3, 2, 1, 0):
        part = grad_pre * masks[back : back + 1]
        moved = x if back == 0 else pltpu.roll(x, back, 1)
        columns.append(jnp.sum(part * moved, axis=1, keepdims=True))
        tap = taps[:, 3 - back : 4 - back]
        grad_x = grad_x + tap * (part if back == 0 else pltpu.roll(part, width - back, 1))
    columns.append(jnp.sum(grad_pre, axis=1, keepdims=True))
    lane = lax.broadcasted_iota(jnp.int32, (x.shape[0], 8), 1)
    packed = jnp.zeros((x.shape[0], 8), jnp.float32)
    for place, column in enumerate(columns):
        packed = jnp.where(lane == place, column, packed)
    return grad_x, packed


def conv_back_kernel(grad_ref, pre_ref, x_ref, taps_ref, masks_ref, grad_x_ref, taps_out_ref):
    grad_pre = grad_ref[...] * silu_slope(pre_ref[...])
    rest = x_ref.shape[1] - grad_pre.shape[1]
    grad_pre = jnp.concatenate([grad_pre, jnp.zeros((grad_pre.shape[0], rest), jnp.float32)], axis=1)
    grad_x, packed = conv_adjoint(grad_pre, x_ref[...], taps_ref[...], masks_ref[...])
    grad_x_ref[...] = grad_x.astype(grad_x_ref.dtype)
    taps_out_ref[...] = packed


def link_mask(seg_row, seg_col):
    count = seg_row.shape[1]
    source = lax.broadcasted_iota(jnp.int32, (count, count), 0)
    target = lax.broadcasted_iota(jnp.int32, (count, count), 1)
    linked = jnp.logical_and(source <= target, seg_row == seg_col)
    return jnp.where(linked, 0.0, -1e30)


def state_kernel(x_ref, taps_ref, masks_ref, bc_ref, dt_ref, cum_ref, flags_ref, pre_ref, state_ref):
    tokens = pre_ref.shape[1]
    pre = conv_steps(x_ref[...], taps_ref[...], masks_ref[...])[:, :tokens]
    pre_ref[...] = pre
    b_t = half(jax.nn.silu(bc_ref[:STATE, :]))
    cum = cum_ref[...]
    tail = jnp.exp(cum[:, tokens - 1 :] - cum) * flags_ref[1:2, :] * dt_ref[...]
    scaled = half(jax.nn.silu(pre) * spread_rows(tail))
    state_ref[...] = half(mul_nt(scaled, b_t))


def inner_kernel(
    pre_ref, bc_ref, dt_ref, cum_ref, cum_col_ref, skip_ref, flags_ref, seg_col_ref, y_ref, mask_s, inner_s
):
    @pl.when(pl.program_id(0) == 0)
    def _():
        mask_s[...] = link_mask(flags_ref[2:3, :], seg_col_ref[:, 0:1])
        bc = half(jax.nn.silu(bc_ref[...]))
        inner_s[...] = mul_tn(bc[:STATE], bc[STATE:])

    x = jax.nn.silu(pre_ref[...])
    scaled = half(x * spread_rows(dt_ref[...]))
    cum, cum_col = cum_ref[...], cum_col_ref[0]
    for head in range(GROUP):
        rows = slice(head * HEAD, (head + 1) * HEAD)
        spread = cum[head : head + 1, :] - cum_col[:, head : head + 1] + mask_s[...]
        weights = half(jnp.exp(spread) * inner_s[...])
        y_ref[rows, :] = mul_nn(scaled[rows], weights) + x[rows] * skip_ref[head : head + 1, :]


def join_kernel(
    y_ref, state_ref, bc_ref, cum_ref, z_ref, gain_ref, flags_ref, y_out_ref, gated_ref, sums_ref, u_s, sum_s
):
    step, groups = pl.program_id(0), u_s.shape[0]

    @pl.when(step == 0)
    def _():
        sum_s[...] = jnp.zeros_like(sum_s)

    @pl.when(step < groups)
    def _():
        c_t = half(jax.nn.silu(bc_ref[STATE:, :]))
        reach = jnp.exp(cum_ref[...]) * flags_ref[0:1, :]
        y = y_ref[...] + mul_nn(state_ref[...], c_t) * spread_rows(reach)
        y_out_ref[...] = y
        u = y * jax.nn.silu(z_ref[...])
        u_s[step] = u
        sum_s[...] += jnp.sum(u * u, axis=0, keepdims=True)

    @pl.when(step >= groups)
    def _():
        scale = lax.rsqrt(sum_s[0:1, :] * (1.0 / DI) + 1e-05)
        gated_ref[...] = half(u_s[step - groups] * scale * gain_ref[:, 0:1])
        sums_ref[...] = jnp.broadcast_to(scale, sums_ref.shape)


def gate_back_kernel(
    y_ref, z_ref, grad_ref, gain_ref, rows_ref, bc_ref, cum_ref, flags_ref, grad_y_ref, grad_z_ref, grad_state_ref
):
    y, z, gain = y_ref[...], z_ref[...], gain_ref[:, 0:1]
    squashed = jax.nn.sigmoid(z)
    u = y * z * squashed
    grad_u = gain * rows_ref[0:1, :] * grad_ref[...] - u * rows_ref[1:2, :]
    grad_y = grad_u * z * squashed
    grad_y_ref[...] = grad_y
    grad_z_ref[...] = half(grad_u * y * (squashed * (1.0 + z * (1.0 - squashed))))
    c_t = half(jax.nn.silu(bc_ref[STATE:, :]))
    reach = jnp.exp(cum_ref[...]) * flags_ref[0:1, :]
    grad_state_ref[...] = half(mul_nt(half(grad_y * spread_rows(reach)), c_t))


def inner_back_kernel(
    pre_ref, grad_y_ref, bc_ref, dt_ref, cum_ref, cum_col_ref, flags_ref, seg_col_ref,
    grad_x_ref, grad_cum_ref, grad_skip_ref, grad_bc_ref, mask_s, inner_s, total_s,
):
    step = pl.program_id(0)

    @pl.when(step == 0)
    def _():
        mask_s[...] = link_mask(flags_ref[2:3, :], seg_col_ref[:, 0:1])
        bc = half(jax.nn.silu(bc_ref[...]))
        inner_s[...] = mul_tn(bc[:STATE], bc[STATE:])
        total_s[...] = jnp.zeros_like(total_s)

    x = jax.nn.silu(pre_ref[...])
    grad_y = grad_y_ref[...]
    grad_skip_ref[...] = head_sums(x * grad_y)
    scaled = half(x * spread_rows(dt_ref[...]))
    grad_half = half(grad_y)
    cum, cum_col = cum_ref[...], cum_col_ref[0]
    ones = jnp.ones((8, cum.shape[1]), jnp.bfloat16)
    for head in range(GROUP):
        rows = slice(head * HEAD, (head + 1) * HEAD)
        decay = jnp.exp(cum[head : head + 1, :] - cum_col[:, head : head + 1] + mask_s[...])
        weights = decay * inner_s[...]
        grad_x_ref[rows, :] = mul_nt(grad_half[rows], half(weights))
        grad_weights = mul_tn(scaled[rows], grad_half[rows])
        total_s[...] += grad_weights * decay
        moved = half(grad_weights * weights)
        sums = mul_nn(ones, moved) - mul_nt(ones, moved)
        grad_cum_ref[head : head + 1, :] = sums[0:1]

    @pl.when(step == pl.num_programs(0) - 1)
    def _():
        bc = half(jax.nn.silu(bc_ref[...]))
        total = half(total_s[...])
        grad_bc_ref[:STATE, :] = mul_nt(bc[STATE:], total)
        grad_bc_ref[STATE:, :] = mul_nn(bc[:STATE], total)


def join_back_kernel(
    grad_in_ref, grad_y_ref, pre_ref, x_ref, taps_ref, masks_ref, state_ref, grad_state_ref,
    bc_ref, dt_ref, cum_ref, skip_ref, flags_ref,
    grad_x_ref, taps_out_ref, grad_dt_ref, grad_cum_ref, grad_last_ref, grad_bc_ref,
):
    step = pl.program_id(0)

    @pl.when(step == 0)
    def _():
        grad_bc_ref[...] = jnp.zeros_like(grad_bc_ref)

    bc = half(jax.nn.silu(bc_ref[...]))
    b_t, c_t = bc[:STATE], bc[STATE:]
    pre, grad_y, cum, dt = pre_ref[...], grad_y_ref[...], cum_ref[...], dt_ref[...]
    tokens = pre.shape[1]
    state, grad_state = state_ref[...], grad_state_ref[...]
    x = jax.nn.silu(pre)
    reached = grad_y * spread_rows(jnp.exp(cum) * flags_ref[0:1, :])
    grad_cum = head_sums(reached * mul_nn(state, c_t))
    grad_bc_ref[STATE:, :] += mul_tn(state, half(reached))
    tail = spread_rows(jnp.exp(cum[:, tokens - 1 :] - cum) * flags_ref[1:2, :])
    dt_wide = spread_rows(dt)
    scaled = x * dt_wide
    from_state = mul_nn(grad_state, b_t) * tail
    grad_bc_ref[:STATE, :] += mul_tn(grad_state, half(scaled * tail))
    tails = head_sums(scaled * from_state)
    grad_cum_ref[...] = grad_cum - tails
    last = jnp.sum(tails, axis=1, keepdims=True)
    through = jnp.sum(
        head_sums(state.astype(jnp.float32) * grad_state.astype(jnp.float32)), axis=1, keepdims=True
    )
    lane = lax.broadcasted_iota(jnp.int32, (GROUP, 128), 1)
    grad_last_ref[...] = jnp.where(lane == 0, last, jnp.where(lane == 1, through, 0.0))
    grad_scaled = grad_in_ref[...] + from_state
    grad_dt_ref[...] = head_sums(grad_scaled * x)
    grad_pre = (grad_scaled * dt_wide + grad_y * spread_rows(skip_ref[...])) * silu_slope(pre)
    rest = x_ref.shape[1] - tokens
    grad_pre = jnp.concatenate([grad_pre, jnp.zeros((grad_pre.shape[0], rest), jnp.float32)], axis=1)
    grad_x, packed = conv_adjoint(grad_pre, x_ref[...], taps_ref[...], masks_ref[...])
    grad_x_ref[...] = half(grad_x)
    taps_out_ref[...] = packed


def mixer_rows(dt_raw, dt_bias, a_log, d_skip, seg_window, taps):
    tokens = dt_raw.shape[1]
    dt = jax.nn.softplus(dt_raw + dt_bias[:, None])
    decay = -jnp.exp(a_log)[:, None] * dt
    upper = jnp.triu(jnp.ones((tokens, tokens), jnp.float32))
    cum = jnp.dot(decay, upper, precision=lax.Precision.HIGHEST)
    cum_col = jnp.swapaxes(cum.reshape(-1, GROUP, tokens), 1, 2)
    seg_now = seg_window[taps - 1 :]
    before = seg_window[taps - 2]
    reach = (seg_now == before).astype(jnp.float32)
    tail = (seg_now == seg_now[-1]).astype(jnp.float32)
    none = jnp.zeros((5, tokens), jnp.float32)
    flags = jnp.concatenate([jnp.stack([reach, tail, seg_now.astype(jnp.float32)]), none])
    seg_col = jnp.broadcast_to(seg_now.astype(jnp.float32)[:, None], (tokens, 8))
    masks = [
        (seg_window[taps - 1 - back : taps - 1 - back + tokens] == seg_now).astype(jnp.float32)
        for back in range(taps)
    ]
    masks = jnp.pad(jnp.stack(masks), ((0, 8 - taps), (0, 128)))
    through = jnp.exp(cum[:, -1]) * (seg_now[-1] == before).astype(jnp.float32)
    skip = jnp.broadcast_to(d_skip[:, None], dt.shape)
    return dt, decay, cum, cum_col, flags, seg_col, masks, through, skip


def mixer_forward_states(proj, taps, masks, dt, cum, flags):
    tokens, groups = dt.shape[1], HEADS // GROUP
    wide = proj.shape[1]
    bc_pre = call_steps(
        conv_kernel, 1, (proj, taps, masks),
        [block((2 * STATE, wide), lambda i: (DI // STATE, 0)),
         block((2 * STATE, 8), lambda i: (DI // (2 * STATE), 0)), whole(masks)],
        f32_out(2 * STATE, tokens), block((2 * STATE, tokens), lambda i: (0, 0)),
    )
    rows = block((GROUP, tokens), lambda i: (i, 0))
    pre, state = call_steps(
        state_kernel, groups, (proj, taps, masks, bc_pre, dt, cum, flags),
        [block((WIDE, wide), lambda i: (i + groups, 0)), block((WIDE, 8), lambda i: (i, 0)), whole(masks),
         whole(bc_pre), rows, rows, whole(flags)],
        [f32_out(DI, tokens), bf16_out(DI, STATE)],
        [block((WIDE, tokens), lambda i: (i, 0)), block((WIDE, STATE), lambda i: (i, 0))],
    )
    return bc_pre, pre, state


def mixer_forward_inner(pre, bc_pre, dt, cum, cum_col, skip, flags, seg_col):
    tokens, groups = dt.shape[1], HEADS // GROUP
    rows = block((GROUP, tokens), lambda i: (i, 0))
    wide = block((WIDE, tokens), lambda i: (i, 0))
    square = pltpu.VMEM((tokens, tokens), jnp.float32)
    return call_steps(
        inner_kernel, groups, (pre, bc_pre, dt, cum, cum_col, skip, flags, seg_col),
        [wide, whole(bc_pre), rows, rows, block((1, tokens, GROUP), lambda i: (i, 0, 0)), rows,
         whole(flags), whole(seg_col)],
        f32_out(DI, tokens), wide, (square, square), flops=30 << 30,
    )


def mixer_forward_join(y, state_in, bc_pre, cum, proj, gain_col, flags):
    tokens, groups = y.shape[1], HEADS // GROUP
    first = lambda i: (jnp.minimum(i, groups - 1), 0)
    second = lambda i: (jnp.maximum(i - groups, 0), 0)
    return call_steps(
        join_kernel, 2 * groups, (y, state_in, bc_pre, cum, proj, gain_col, flags),
        [block((WIDE, tokens), first), block((WIDE, STATE), first), whole(bc_pre),
         block((GROUP, tokens), first), block((WIDE, tokens), first), block((WIDE, 8), second), whole(flags)],
        [f32_out(DI, tokens), bf16_out(DI, tokens), f32_out(8, tokens)],
        [block((WIDE, tokens), first), block((WIDE, tokens), second), block((8, tokens), lambda i: (0, 0))],
        (pltpu.VMEM((groups, WIDE, tokens), jnp.float32), pltpu.VMEM((8, tokens), jnp.float32)),
    )


def mixer_back_gate(y, proj, grad_gated, gain_col, gate_rows, bc_pre, cum, flags):
    tokens, groups = y.shape[1], HEADS // GROUP
    wide = block((WIDE, tokens), lambda i: (i, 0))
    return call_steps(
        gate_back_kernel, groups, (y, proj, grad_gated, gain_col, gate_rows, bc_pre, cum, flags),
        [wide, wide, wide, block((WIDE, 8), lambda i: (i, 0)), whole(gate_rows), whole(bc_pre),
         block((GROUP, tokens), lambda i: (i, 0)), whole(flags)],
        [f32_out(DI, tokens), bf16_out(DI, tokens), bf16_out(DI, STATE)],
        [wide, wide, block((WIDE, STATE), lambda i: (i, 0))],
    )


def mixer_back_inner(pre, grad_y, bc_pre, dt, cum, cum_col, flags, seg_col):
    tokens, groups = dt.shape[1], HEADS // GROUP
    rows = block((GROUP, tokens), lambda i: (i, 0))
    wide = block((WIDE, tokens), lambda i: (i, 0))
    square = pltpu.VMEM((tokens, tokens), jnp.float32)
    return call_steps(
        inner_back_kernel, groups, (pre, grad_y, bc_pre, dt, cum, cum_col, flags, seg_col),
        [wide, wide, whole(bc_pre), rows, rows, block((1, tokens, GROUP), lambda i: (i, 0, 0)),
         whole(flags), whole(seg_col)],
        [f32_out(DI, tokens), f32_out(HEADS, tokens), f32_out(HEADS, tokens), f32_out(2 * STATE, tokens)],
        [wide, rows, rows, block((2 * STATE, tokens), lambda i: (0, 0))],
        (square, square, square), flops=50 << 30,
    )


def mixer_back_join(grad_scaled, grad_y, pre, proj, taps, masks, state_in, grad_state, bc_pre, dt, cum, skip, flags):
    tokens, groups = dt.shape[1], HEADS // GROUP
    rows = block((GROUP, tokens), lambda i: (i, 0))
    wide = block((WIDE, tokens), lambda i: (i, 0))
    longer = block((WIDE, proj.shape[1]), lambda i: (i, 0))
    later = block((WIDE, proj.shape[1]), lambda i: (i + groups, 0))
    states = block((WIDE, STATE), lambda i: (i, 0))
    narrow = block((WIDE, 8), lambda i: (i, 0))
    return call_steps(
        join_back_kernel, groups,
        (grad_scaled, grad_y, pre, proj, taps, masks, state_in, grad_state, bc_pre, dt, cum, skip, flags),
        [wide, wide, wide, later, narrow, whole(masks), states, states, whole(bc_pre), rows, rows, rows,
         whole(flags)],
        [bf16_out(DI, proj.shape[1]), f32_out(DI, 8), f32_out(HEADS, tokens), f32_out(HEADS, tokens),
         f32_out(HEADS, 128), f32_out(2 * STATE, tokens)],
        [longer, narrow, rows, rows, block((GROUP, 128), lambda i: (i, 0)),
         block((2 * STATE, tokens), lambda i: (0, 0))],
    )


def mixer_back_conv(grad_bc, bc_pre, proj, taps, masks):
    place = DI // (2 * STATE)
    wide = proj.shape[1]
    return call_steps(
        conv_back_kernel, 1, (grad_bc, bc_pre, proj, taps, masks),
        [whole(grad_bc), whole(bc_pre), block((2 * STATE, wide), lambda i: (2 * place, 0)),
         block((2 * STATE, 8), lambda i: (place, 0)), whole(masks)],
        [bf16_out(2 * STATE, wide), f32_out(2 * STATE, 8)],
        [block((2 * STATE, wide), lambda i: (0, 0)), block((2 * STATE, 8), lambda i: (0, 0))],
    )


def cut(array_index, rows, columns, row_step, column_step):
    found = []
    for row in range(0, rows, row_step):
        for column in range(0, columns, column_step):
            found.append(
                (array_index, row, min(row_step, rows - row), column, min(column_step, columns - column))
            )
    return found


def places(lined):
    dp, z = lax.axis_index("dp"), lax.axis_index("ctx")
    y, x, core = lax.div(dp, 4), lax.rem(lax.div(dp, 2), 2), lax.rem(dp, 2)
    others = {
        "x": (dp + 2 - 4 * x, z),
        "y": (dp + 4 - 8 * y, z),
        "core": (dp + 1 - 2 * core, z),
    }
    for away in (1, 2, 3) if lined else ():
        others[away] = (dp, lax.rem(z + away, 4))
    return y, x, core, z, others


def greet(others):
    barrier = pltpu.get_barrier_semaphore()
    for device in others.values():
        pl.semaphore_signal(
            barrier, inc=1, device_id=device, device_id_type=pl.DeviceIdType.MESH
        )
    pl.semaphore_wait(barrier, len(others))


def send(source, target, sems, piece, leg, device):
    return pltpu.make_async_remote_copy(
        src_ref=source,
        dst_ref=target,
        send_sem=sems[0].at[piece, leg],
        recv_sem=sems[1].at[piece, leg],
        device_id=device,
        device_id_type=pl.DeviceIdType.MESH,
    )


def gather_kernel(pieces, ahead, count, lined, *refs):
    ins, outs, (sent, came, kept) = refs[:count], refs[count : 2 * count], refs[2 * count :]
    y, x, core, z, others = places(lined)
    greet(others)
    sems = (sent, came)
    started = []

    def legs(number):
        array, row, rows, column, columns = pieces[number]
        area = (pl.ds(row, rows), pl.ds(column, columns))
        out = outs[array]
        first, second = ("x", "y") if number % 2 == 0 else ("y", "x")
        rest = ((slice(None),) if lined else ()) + area
        own = ins[array].at[area]
        mine = out.at[(y, x, core) + ((z,) if lined else ()) + area]
        line = out.at[(y, x, core) + rest]
        if first == "x":
            plane = out.at[(y, slice(None), core) + rest]
        else:
            plane = out.at[(slice(None), x, core) + rest]
        every = out.at[(slice(None), slice(None), core) + rest]
        return {
            "keep": lambda: pltpu.make_async_copy(own, mine, kept.at[number]),
            "line": lambda: [
                send(own, mine, sems, number, away - 1, others[away])
                for away in ((1, 2, 3) if lined else ())
            ],
            "first": lambda: send(line if lined else own, line, sems, number, 3, others[first]),
            "second": lambda: send(plane, plane, sems, number, 4, others[second]),
            "core": lambda: send(every, every, sems, number, 5, others["core"]),
        }

    def begin(number):
        if number < len(pieces):
            leg = legs(number)
            leg["keep"]().start()
            for copy in leg["line"]():
                copy.start()

    def advance(number, stage):
        if not 0 <= number < len(pieces):
            return
        leg = legs(number)
        if stage == 0:
            leg["keep"]().wait()
            for copy in leg["line"]():
                copy.wait_recv()
            leg["first"]().start()
        elif stage == 1:
            leg["first"]().wait_recv()
            leg["second"]().start()
        elif stage == 2:
            leg["second"]().wait_recv()
            leg["core"]().start()
        else:
            leg["core"]().wait_recv()

    for number in range(2 * ahead):
        begin(number)
    pairs = -(-len(pieces) // 2)
    for turn in range(pairs + 3):
        for stage in range(4):
            for number in (2 * (turn - stage), 2 * (turn - stage) + 1):
                advance(number, stage)
                if stage == 0 and number < len(pieces):
                    begin(number + 2 * ahead)
    for number in range(len(pieces)):
        leg = legs(number)
        for copy in leg["line"]() + [leg["first"](), leg["second"](), leg["core"]()]:
            copy.wait_send()


def pallas_gather(parts, steps, name_id, lined=True, ahead=2):
    pieces = []
    for index, (part, (row_step, column_step)) in enumerate(zip(parts, steps)):
        pieces += cut(index, part.shape[0], part.shape[1], row_step, column_step)
    count = len(parts)
    lead = (2, 2, 2, 4) if lined else (2, 2, 2)
    anywhere = pl.BlockSpec(memory_space=pl.ANY)
    outs = pl.pallas_call(
        partial(gather_kernel, pieces, ahead, count, lined),
        in_specs=[anywhere] * count,
        out_specs=[anywhere] * count,
        out_shape=[jax.ShapeDtypeStruct(lead + part.shape, part.dtype) for part in parts],
        scratch_shapes=[
            pltpu.SemaphoreType.DMA((len(pieces), 6)),
            pltpu.SemaphoreType.DMA((len(pieces), 6)),
            pltpu.SemaphoreType.DMA((len(pieces),)),
        ],
        compiler_params=pltpu.CompilerParams(collective_id=name_id, has_side_effects=True),
    )(*parts)
    return [out.reshape((-1,) + part.shape) for out, part in zip(outs, parts)]


def reduce_kernel(pieces, ahead, count, lined, *refs):
    ins, outs = refs[:count], refs[count : 2 * count]
    sent, came, kept, put = refs[2 * count : 2 * count + 4]
    room = refs[2 * count + 4 :]
    y, x, core, z, others = places(lined)
    greet(others)
    sems = (sent, came)
    amount = len(pieces)

    def held(number):
        return room[6 * number : 6 * number + 6]

    def legs(number):
        array, row, rows, column, columns = pieces[number]
        area = (pl.ds(row, rows), pl.ds(column, columns))
        total, from_core, from_first, from_second, from_line, result = held(number)
        every = (slice(None), slice(None))
        rest = ((slice(None),) if lined else ()) + area
        side = number % 2 == 0
        return {
            "load": lambda: pltpu.make_async_copy(
                ins[array].at[every + (core,) + rest], total, kept.at[number]
            ),
            "core": lambda: send(
                ins[array].at[every + (1 - core,) + rest],
                from_core, sems, number, 0, others["core"],
            ),
            "first": lambda: send(
                total.at[:, 1 - x] if side else total.at[1 - y],
                from_first, sems, number, 1, others["x" if side else "y"],
            ),
            "second": lambda: send(
                total.at[1 - y, x] if side else total.at[y, 1 - x],
                from_second, sems, number, 2, others["y" if side else "x"],
            ),
            "line": lambda: [
                send(
                    total.at[y, x, lax.rem(z + away, 4)], from_line.at[away - 1],
                    sems, number, 2 + away, others[away],
                )
                for away in ((1, 2, 3) if lined else ())
            ],
            "store": lambda: pltpu.make_async_copy(result, outs[array].at[area], put.at[number]),
        }

    def begin(number):
        if number < amount:
            leg = legs(number)
            leg["load"]().start()
            leg["core"]().start()

    def advance(number, stage):
        if not 0 <= number < amount:
            return
        leg = legs(number)
        total, from_core, from_first, from_second, from_line, result = held(number)
        deep = 4 if lined else 1

        def place(at, *lead):
            return lead + ((lax.rem(at, deep),) if lined else ())

        if stage == 0:
            leg["load"]().wait()
            leg["core"]().wait_recv()

            @pl.loop(0, 4 * deep)
            def _(at):
                here = place(at, lax.div(at, 2 * deep), lax.rem(lax.div(at, deep), 2))
                total[here] = total[here] + from_core[here]

            leg["first"]().start()
        elif stage == 1:
            leg["first"]().wait_recv()

            @pl.loop(0, 2 * deep)
            def _(at):
                outer = lax.div(at, deep)
                here = place(at, outer, x) if number % 2 == 0 else place(at, y, outer)
                total[here] = total[here] + from_first[place(at, outer)]

            leg["second"]().start()
        elif stage == 2:
            leg["second"]().wait_recv()
            if lined:

                @pl.loop(0, 4)
                def _(at):
                    total[y, x, at] = total[y, x, at] + from_second[at]

                for copy in leg["line"]():
                    copy.start()
            else:
                result[...] = total[y, x].astype(jnp.float32) + from_second[...].astype(jnp.float32)
                leg["store"]().start()
        elif lined:
            for copy in leg["line"]():
                copy.wait_recv()
            summed = total[y, x, z].astype(jnp.float32)
            for away in range(3):
                summed = summed + from_line[away].astype(jnp.float32)
            result[...] = summed
            leg["store"]().start()

    for number in range(2 * ahead):
        begin(number)
    pairs = -(-amount // 2)
    for turn in range(pairs + 3):
        for stage in range(4):
            for number in (2 * (turn - stage), 2 * (turn - stage) + 1):
                advance(number, stage)
                if stage == 0 and number >= 0:
                    begin(number + 2 * ahead)
    for number in range(amount):
        leg = legs(number)
        for copy in [leg["core"](), leg["first"](), leg["second"]()] + leg["line"]():
            copy.wait_send()
        leg["store"]().wait()


def pallas_reduce(parts, steps, name_id, lined=True, ahead=2):
    shapes = [part.shape[1:] for part in parts]
    pieces = []
    for index, (shape, (row_step, column_step)) in enumerate(zip(shapes, steps)):
        pieces += cut(index, shape[0], shape[1], row_step, column_step)
    count, amount = len(parts), len(pieces)
    anywhere = pl.BlockSpec(memory_space=pl.ANY)
    room = []
    for array, _, rows, _, columns in pieces:
        kind = parts[array].dtype
        deep = (4,) if lined else ()
        for lead in ((2, 2) + deep, (2, 2) + deep, (2,) + deep, deep, (3,) if lined else (1,)):
            room.append(pltpu.VMEM(lead + (rows, columns), kind))
        room.append(pltpu.VMEM((rows, columns), jnp.float32))
    return pl.pallas_call(
        partial(reduce_kernel, pieces, ahead, count, lined),
        in_specs=[anywhere] * count,
        out_specs=[anywhere] * count,
        out_shape=[jax.ShapeDtypeStruct(shape, jnp.float32) for shape in shapes],
        scratch_shapes=[
            pltpu.SemaphoreType.DMA((amount, 6)),
            pltpu.SemaphoreType.DMA((amount, 6)),
            pltpu.SemaphoreType.DMA((amount,)),
            pltpu.SemaphoreType.DMA((amount,)),
        ] + room,
        compiler_params=pltpu.CompilerParams(
            collective_id=name_id, has_side_effects=True, vmem_limit_bytes=VMEM_MOST
        ),
        )(*[part.reshape((2, 2, 2) + ((4,) if lined else ()) + shape) for part, shape in zip(parts, shapes)])


def chained_states(local, through, step):
    count = lax.axis_size("ctx")
    total, factor = None, None
    rows = jnp.pad(through[:, None], ((0, 0), (0, 127)))
    for away in range(1, count):
        arrived = from_behind(local, "ctx", step * away).astype(jnp.float32)
        if factor is not None:
            arrived = (arrived.reshape(HEADS, HEAD, STATE) * factor[:, None, None]).reshape(DI, STATE)
        total = arrived if total is None else total + arrived
        if away < count - 1:
            passed = from_behind(rows, "ctx", step * away)[:, 0]
            factor = passed if factor is None else factor * passed
    return half(total)


BOTH = ("dp", "ctx")


def after(values, *earlier):
    return lax.optimization_barrier((values, earlier))[0]


def two_parts(value):
    high = value.astype(jnp.bfloat16)
    low = (value - high.astype(jnp.float32)).astype(jnp.bfloat16)
    return high, low


def route_table(routes, expert_count):
    named = jnp.any(
        routes[:, :, None] == jnp.arange(expert_count, dtype=jnp.int32), axis=1
    )
    rows = routes.shape[0]
    earlier = jnp.tril(jnp.ones((rows, rows), jnp.bfloat16), -1)
    ranks = jnp.dot(earlier, named.astype(jnp.bfloat16), preferred_element_type=jnp.float32)
    return named, jnp.where(named, ranks, -1.0)


def on_device(
    layer_in,
    seg_ids,
    route_ids,
    out_grad,
    norm_in,
    w_in,
    conv_w,
    conv_b,
    dt_bias,
    a_log,
    d_skip,
    norm_gate,
    w_out,
    norm_mid,
    w_router,
    w_sgate,
    w_sup,
    w_sdown,
    e_gate,
    e_up,
    e_down,
):
    f32, bf16 = jnp.float32, jnp.bfloat16
    row_count, d_model = layer_in.shape[1:]
    devices = lax.axis_size("dp") * lax.axis_size("ctx")
    ctx_place = lax.axis_index("ctx")
    first_expert = lax.axis_index("dp") * EXP_DEV
    blocks = lax.axis_size("dp")
    expert_count = EXP_DEV * blocks
    capacity = row_count * TOP * 5 // (expert_count * 4)
    slots = -(-capacity // 64) * 64
    tap_count = conv_w.shape[0]
    halo = 8

    small_parts = (norm_in, conv_w, conv_b, norm_gate, norm_mid, w_router)
    small_flat = jnp.concatenate([part.reshape(-1) for part in small_parts])
    small_flat = jnp.pad(small_flat, (0, 4096 - small_flat.shape[0])).reshape(32, 128)
    w_in_all, small_all = pallas_gather([w_in, small_flat], [(16, 1664), (32, 128)], 1)
    small_all = small_all.reshape(devices, 4096)
    taken, pieces = 0, []
    for part in small_parts:
        pieces.append(small_all[:, taken : taken + part.size])
        taken += part.size
    gain_in = pieces[0].reshape(-1).astype(f32)
    conv_weight = jnp.moveaxis(pieces[1].reshape(devices, tap_count, -1), 0, 1).reshape(tap_count, CONV).astype(f32)
    conv_bias = pieces[2].reshape(-1).astype(f32)
    gain_gate = pieces[3].reshape(-1).astype(f32)
    gain_mid = pieces[4].reshape(-1).astype(f32)
    router_weight = pieces[5].reshape(d_model, expert_count)
    weight_in = w_in_all.reshape(d_model, PROJ)
    expert_gate = lax.all_gather(e_gate, "ctx", axis=1, tiled=True)
    expert_up = lax.all_gather(e_up, "ctx", axis=1, tiled=True)
    expert_down = lax.all_gather(e_down, "ctx", axis=2, tiled=True)
    named, ranks = route_table(route_ids[0], expert_count)

    own_in = layer_in[0]
    edge_in = from_behind(own_in[row_count - halo :], "ctx", 1)
    input_f = jnp.concatenate(
        [own_in, jnp.zeros((128 - halo, d_model), bf16), edge_in], axis=0
    ).astype(f32)
    normed = scaled_norm(input_f, gain_in).astype(bf16)
    projected = lax.dot_general(
        weight_in, normed, (((0,), (1,)), ((), ())), preferred_element_type=f32
    )
    seg_pad = jnp.concatenate([jnp.full((tap_count - 1,), -1, jnp.int32), seg_ids[0]])
    seg_window = lax.dynamic_slice_in_dim(
        seg_pad, ctx_place * row_count, row_count + tap_count - 1, 0
    )
    taps = jnp.concatenate(
        [conv_weight.T, conv_bias[:, None], jnp.zeros((CONV, 7 - tap_count), f32)], axis=1
    )
    dt_raw = projected[DI + CONV :, :row_count]
    dt_pos, decay, cumul, cumul_col, flags, seg_col, masks, through, skip_rows = mixer_rows(
        dt_raw, dt_bias, a_log, d_skip, seg_window, tap_count
    )
    bc_pre, pre, state_out = mixer_forward_states(projected, taps, masks, dt_pos, cumul, flags)
    state_in = chained_states(state_out, through, 1)
    w_out_all, sgate_all, sup_all, sdown_all = pallas_gather(
        after([w_out, w_sgate, w_sup, w_sdown], state_out),
        [(16, 1536), (16, 1024), (16, 1024), (16, 1536)],
        2,
    )
    weight_out = w_out_all.reshape(DI, d_model)
    sgate_weight = sgate_all.reshape(d_model, -1)
    sup_weight = sup_all.reshape(d_model, -1)
    sdown_weight = sdown_all.reshape(-1, d_model)
    y_inner = mixer_forward_inner(pre, bc_pre, dt_pos, cumul, cumul_col, skip_rows, flags, seg_col)
    gain_col = jnp.broadcast_to(gain_gate[:, None], (DI, 8))
    y_heads, gated, gate_scale = mixer_forward_join(
        after(y_inner, weight_out), state_in, bc_pre, cumul, projected, gain_col, flags
    )

    mixed = times_rows(gated, weight_out)
    resid_mid = own_in.astype(f32) + mixed
    normed_mid_f, pull_mid = jax.vjp(scaled_norm, resid_mid, gain_mid)
    normed_mid = normed_mid_f.astype(bf16)
    logits = jnp.dot(normed_mid, router_weight, preferred_element_type=f32)
    top_logit = jnp.max(jnp.where(named, logits, -jnp.inf), axis=-1, keepdims=True)
    powers = jnp.where(named, jnp.exp(jnp.where(named, logits - top_logit, 0.0)), 0.0)
    gates = powers / jnp.sum(powers, axis=-1, keepdims=True)
    gate_high, gate_low = two_parts(gates)
    side = jnp.concatenate(
        [gate_high, gate_low, ranks.astype(bf16), jnp.zeros((row_count, 128 - 3 * expert_count), bf16)],
        axis=1,
    )
    token_rows, grad_rows, side_all = pallas_gather(
        [normed_mid, out_grad[0], side], [(16, 1536), (16, 1536), (128, 128)], 3, lined=False, ahead=4
    )
    shared_gate = jnp.dot(normed_mid, sgate_weight, preferred_element_type=f32)
    shared_up = jnp.dot(normed_mid, sup_weight, preferred_element_type=f32)
    shared_act = (jax.nn.silu(shared_gate) * shared_up).astype(bf16)
    shared_out = jnp.dot(shared_act, sdown_weight, preferred_element_type=f32)

    mine_of = partial(lax.dynamic_slice_in_dim, slice_size=EXP_DEV, axis=2)
    my_gate = mine_of(side_all, first_expert).astype(f32) + mine_of(
        side_all, first_expert + expert_count
    ).astype(f32)
    my_rank = mine_of(side_all, first_expert + 2 * expert_count).astype(f32)
    my_gate, my_rank = jnp.swapaxes(my_gate, 1, 2), jnp.swapaxes(my_rank, 1, 2)
    chosen = my_rank[:, :, None, :] == jnp.arange(slots, dtype=f32)[None, None, :, None]
    select = chosen.astype(bf16)
    slot_gate = jnp.sum(jnp.where(chosen, my_gate[:, :, None, :], 0.0), axis=-1)
    gate_col = jnp.swapaxes(slot_gate, 0, 1).reshape(EXP_DEV, blocks * slots, 1)

    def to_slots(rows):
        taken = jnp.einsum("best,btd->ebsd", select, rows, preferred_element_type=f32)
        return taken.astype(bf16).reshape(EXP_DEV, blocks * slots, -1)

    def to_tokens(rows):
        rows = rows.reshape(EXP_DEV, blocks, slots, -1)
        return jnp.einsum("best,ebsd->btd", select, rows, preferred_element_type=f32).astype(bf16)

    def each(spec, left, right):
        return jnp.einsum(spec, left, right, preferred_element_type=f32)

    slot_in = to_slots(token_rows)
    slot_grad = to_slots(grad_rows)
    hidden_gate = each("erd,edf->erf", slot_in, expert_gate)
    hidden_up = each("erd,edf->erf", slot_in, expert_up)
    hidden_act = (jax.nn.silu(hidden_gate) * hidden_up).astype(bf16)
    expert_out = each("erf,efd->erd", hidden_act, expert_down).astype(bf16)
    slot_dgate = jnp.sum(slot_grad.astype(f32) * expert_out.astype(f32), axis=-1)
    grad_out_slots = (gate_col * slot_grad).astype(bf16)
    grad_act = each("erd,efd->erf", grad_out_slots, expert_down)
    grad_e_down = each("erf,erd->efd", hidden_act, grad_out_slots)
    grad_hgate = (grad_act * hidden_up * silu_slope(hidden_gate)).astype(bf16)
    grad_hup = (grad_act * jax.nn.silu(hidden_gate)).astype(bf16)
    grad_slots = (
        each("erf,edf->erd", grad_hgate, expert_gate) + each("erf,edf->erd", grad_hup, expert_up)
    ).astype(bf16)
    slot_dgate = jnp.swapaxes(slot_dgate.reshape(EXP_DEV, blocks, slots), 0, 1)
    token_dgate = jnp.sum(jnp.where(chosen, slot_dgate[..., None], 0.0), axis=2)
    held = jnp.arange(EXP_DEV, dtype=jnp.int32)[:, None] + first_expert
    dgate_table = jnp.sum(
        token_dgate[..., None] * (jnp.arange(expert_count) == held).astype(f32)[:, None, :], axis=1
    )
    dgate_high, dgate_low = two_parts(dgate_table)
    back_side = jnp.concatenate(
        [dgate_high, dgate_low, jnp.zeros((blocks, row_count, 128 - 2 * expert_count), bf16)], axis=-1
    )
    back_rows, routed, back_side = pallas_reduce(
        [to_tokens(grad_slots), to_tokens((gate_col * expert_out).astype(bf16)), back_side],
        [(32, 1536), (32, 1536), (128, 128)],
        4,
        lined=False,
    )
    grad_e_gate = each("erd,erf->edf", slot_in, grad_hgate)
    grad_e_up = each("erd,erf->edf", slot_in, grad_hup)

    def to_owner(grad, axis):
        sent = lax.psum_scatter(grad.astype(bf16), "ctx", scatter_dimension=axis + 1, tiled=True)
        return sent.astype(f32)

    expert_grads = (to_owner(grad_e_gate, 0), to_owner(grad_e_up, 0), to_owner(grad_e_down, 1))

    layer_out = (resid_mid + shared_out + routed).astype(bf16)[None]
    grad_top = out_grad[0].astype(f32)
    grad_shared_out = out_grad[0]
    grad_w_sdown = times_rows(shared_act, grad_shared_out)
    grad_shared_act = times_back(grad_shared_out, sdown_weight)
    grad_sgate = (grad_shared_act * shared_up * silu_slope(shared_gate)).astype(bf16)
    grad_sup = (grad_shared_act * jax.nn.silu(shared_gate)).astype(bf16)
    grad_w_sgate = times_rows(normed_mid, grad_sgate)
    grad_w_sup = times_rows(normed_mid, grad_sup)
    grad_mid_shared = times_back(grad_sgate, sgate_weight) + times_back(grad_sup, sup_weight)
    grad_gates = back_side[:, :expert_count] + back_side[:, expert_count : 2 * expert_count]
    grad_pick = gates * (grad_gates - jnp.sum(gates * grad_gates, axis=-1, keepdims=True))
    grad_logits = grad_pick.astype(bf16)
    grad_w_router = times_rows(normed_mid, grad_logits)
    grad_mid = (
        back_rows + grad_mid_shared + times_back(grad_logits, router_weight)
    )
    grad_resid_part, grad_gain_mid = pull_mid(grad_mid)
    grad_resid = grad_top + grad_resid_part
    grad_mixed = grad_resid.astype(bf16)

    def owned(grad):
        return grad.astype(bf16).reshape(devices, -1, grad.shape[-1])

    grad_w_out = jnp.dot(gated, grad_mixed, preferred_element_type=f32)
    grad_gated = times_back(weight_out, grad_mixed)
    scaled_u = y_heads * jax.nn.silu(projected[:DI, :row_count])
    scale_row = gate_scale[:1]
    along = jnp.sum(grad_gated * gain_gate[:, None] * scaled_u, axis=0, keepdims=True)
    grad_gain_gate = jnp.sum(grad_gated * scaled_u * scale_row, axis=1)
    gate_rows = jnp.concatenate(
        [scale_row, scale_row * scale_row * scale_row * along * (1.0 / DI), jnp.zeros((6, row_count), f32)]
    )
    grad_y, grad_z, grad_state_local = mixer_back_gate(
        y_heads, projected, grad_gated, gain_col, gate_rows, bc_pre, cumul, flags
    )
    grad_state_out = chained_states(grad_state_local, through, -1)
    sum_out, sum_sgate, sum_sup, sum_sdown = pallas_reduce(
        after(
            [owned(grad_w_out), owned(grad_w_sgate), owned(grad_w_sup), owned(grad_w_sdown)],
            grad_state_local,
        ),
        [(16, 1536), (16, 1024), (16, 1024), (16, 1536)],
        5,
    )
    grad_scaled, grad_cum_inner, grad_skip, grad_bc_inner = mixer_back_inner(
        pre, grad_y, bc_pre, dt_pos, cumul, cumul_col, flags, seg_col
    )
    grad_x, grad_taps_x, grad_dt, grad_cum_join, grad_last, grad_bc_join = mixer_back_join(
        after(grad_scaled, sum_out), grad_y, pre, projected, taps, masks, state_in, grad_state_out,
        bc_pre, dt_pos, cumul, skip_rows, flags,
    )
    grad_bc, grad_taps_bc = mixer_back_conv(
        grad_bc_inner + grad_bc_join, bc_pre, projected, taps, masks
    )
    grad_cum = grad_cum_inner + grad_cum_join
    grad_last = grad_last[:, 0] + through * grad_last[:, 1]
    lower = jnp.tril(jnp.ones((row_count, row_count), f32))
    grad_decay = jnp.dot(grad_cum, lower, precision=lax.Precision.HIGHEST) + grad_last[:, None]
    grad_dt = grad_dt - jnp.exp(a_log)[:, None] * grad_decay
    grad_raw = grad_dt * jax.nn.sigmoid(dt_raw + dt_bias[:, None])
    grad_taps = jnp.concatenate([grad_taps_x, grad_taps_bc])
    grad_conv_w, grad_conv_b = grad_taps[:, :tap_count].T, grad_taps[:, tap_count]
    head_sums_all = jnp.concatenate(
        [jnp.sum(grad_raw, axis=1), jnp.sum(decay * grad_decay, axis=1), jnp.sum(grad_skip, axis=1)]
    )
    grad_proj = jnp.concatenate(
        [
            jnp.pad(grad_z, ((0, 0), (0, 128))),
            grad_x,
            grad_bc,
            jnp.pad(grad_raw.astype(bf16), ((0, 0), (0, 128))),
        ]
    )
    grad_w_in = lax.dot_general(
        normed, grad_proj, (((0,), (1,)), ((), ())), preferred_element_type=f32
    )
    grad_normed = lax.dot_general(
        grad_proj, weight_in, (((0,), (1,)), ((), ())), preferred_element_type=f32
    )
    edge_grad = from_behind(grad_normed[row_count + 128 - halo :], "ctx", -1)
    grad_normed = jnp.concatenate(
        [grad_normed[: row_count - halo], grad_normed[row_count - halo : row_count] + edge_grad],
        axis=0,
    )
    _, pull_in = jax.vjp(scaled_norm, own_in.astype(f32), gain_in)
    grad_input_part, grad_gain_in = pull_in(grad_normed)
    grad_in = (grad_resid + grad_input_part)[None]

    small_grads = jnp.concatenate(
        [
            grad_gain_in.reshape(devices, -1),
            jnp.moveaxis(grad_conv_w.reshape(tap_count, devices, -1), 1, 0).reshape(devices, -1),
            grad_conv_b.reshape(devices, -1),
            grad_gain_gate.reshape(devices, -1),
            grad_gain_mid.reshape(devices, -1),
            grad_w_router.reshape(devices, -1),
            jnp.broadcast_to(head_sums_all, (devices, 3 * HEADS)),
        ],
        axis=1,
    )
    small_grads = jnp.pad(small_grads, ((0, 0), (0, 3072 - small_grads.shape[1])))
    sum_in, sum_small = pallas_reduce(
        [owned(grad_w_in), small_grads.reshape(devices, 24, 128)], [(16, 1664), (24, 128)], 6
    )
    sum_small = sum_small.reshape(-1)
    taken, mine = 0, []
    for part in small_parts:
        mine.append(sum_small[taken : taken + part.size].reshape(part.shape))
        taken += part.size
    return (
        layer_out,
        grad_in,
        mine[0],
        sum_in,
        mine[1],
        mine[2],
        sum_small[taken : taken + HEADS],
        sum_small[taken + HEADS : taken + 2 * HEADS],
        sum_small[taken + 2 * HEADS : taken + 3 * HEADS],
        mine[3],
        sum_out,
        mine[4],
        mine[5],
        sum_sgate,
        sum_sup,
        sum_sdown,
        expert_grads[0],
        expert_grads[1],
        expert_grads[2],
    )


def solution(mesh):
    in_specs = (
        P("dp", "ctx", None),
        P("dp", None),
        P("dp", "ctx", None),
        P("dp", "ctx", None),
        P(("dp", "ctx")),
        P(("dp", "ctx"), None),
        P(None, ("dp", "ctx")),
        P(("dp", "ctx")),
        P(),
        P(),
        P(),
        P(("dp", "ctx")),
        P(("dp", "ctx"), None),
        P(("dp", "ctx")),
        P(("dp", "ctx"), None),
        P(("dp", "ctx"), None),
        P(("dp", "ctx"), None),
        P(("dp", "ctx"), None),
        P("dp", "ctx", None),
        P("dp", "ctx", None),
        P("dp", None, "ctx"),
    )
    out_specs = (
        P("dp", "ctx", None),
        P("dp", "ctx", None),
        P(("dp", "ctx")),
        P(("dp", "ctx"), None),
        P(None, ("dp", "ctx")),
        P(("dp", "ctx")),
        P(),
        P(),
        P(),
        P(("dp", "ctx")),
        P(("dp", "ctx"), None),
        P(("dp", "ctx")),
        P(("dp", "ctx"), None),
        P(("dp", "ctx"), None),
        P(("dp", "ctx"), None),
        P(("dp", "ctx"), None),
        P("dp", "ctx", None),
        P("dp", "ctx", None),
        P("dp", None, "ctx"),
    )
    one_each = mesh.shape["ctx"] == EXP_DEV and mesh.shape["dp"] == 8
    return jax.shard_map(
        on_device if one_each else on_device_general, mesh=mesh, in_specs=in_specs, out_specs=out_specs, check_vma=False
    )
```

```python
from functools import partial

import jax
import jax.numpy as jnp
from jax import lax
from jax.experimental import pallas as pl
from jax.experimental.pallas import tpu as pltpu
from jax.sharding import PartitionSpec as P

HEADS = 48
HEAD = 64
STATE = 128
TOP = 6
EXP_DEV = 4
DI = 3072
CONV = 3328
PROJ = 6448


def from_behind(value, axis, steps):
    count = lax.axis_size(axis)
    leading, last = (max(0, -steps), min(count, count - steps))
    return lax.ppermute(value, axis, [(source, source + steps) for source in range(leading, last)])


def carried_in_2(x, axis, combine, identity):
    count, mine = (lax.axis_size(axis), lax.axis_index(axis))
    everything = jax.tree.map(
        lambda part, kind: lax.all_gather(part.astype(kind), axis), x, (jnp.bfloat16, jnp.bfloat16)
    )
    start = jax.tree.map(
        lambda part, zero: jnp.broadcast_to(jnp.asarray(zero, part.dtype), part.shape), x, identity
    )

    def lap(k, before):
        reached = k < mine
        new = combine(
            before, jax.tree.map(lambda part, own: part[k].astype(own.dtype), everything, x)
        )
        return jax.tree.map(lambda a, b: jnp.where(reached, a, b), new, before)

    return lax.fori_loop(0, count, lap, start)


def carried_in_3(x, axis, combine, identity):
    count, mine = (lax.axis_size(axis), lax.axis_index(axis))
    everything = jax.tree.map(
        lambda part, kind: lax.all_gather(part.astype(kind), axis),
        x,
        jax.tree.map(lambda a: jnp.bfloat16 if a.dtype == jnp.float32 else a.dtype, x),
    )
    start = jax.tree.map(
        lambda part, zero: jnp.broadcast_to(jnp.asarray(zero, part.dtype), part.shape), x, identity
    )

    def lap(k, before):
        at = count - 1 - k
        reached = at > mine
        new = combine(
            before, jax.tree.map(lambda part, own: part[at].astype(own.dtype), everything, x)
        )
        return jax.tree.map(lambda a, b: jnp.where(reached, a, b), new, before)

    return lax.fori_loop(0, count, lap, start)


def for_sending(x):
    return jax.tree.map(lambda a: a.astype(jnp.bfloat16) if a.dtype == jnp.float32 else a, x)


def normalize(value):
    return value * lax.rsqrt(jnp.mean(value * value, axis=-1, keepdims=True) + 1e-05)


def scaled_norm(value, gain):
    return normalize(value) * gain


def gate_norm(y_heads, z_part, gain):
    joined = y_heads.reshape(z_part.shape) * jax.nn.silu(z_part)
    return normalize(joined) * gain


def silu_slope(value):
    squashed = jax.nn.sigmoid(value)
    return squashed * (1.0 + value * (1.0 - squashed))


def conv_apply(padded, weight, bias, seg_pad):
    tap_count = weight.shape[0]
    length = padded.shape[1] - tap_count + 1
    current = seg_pad[:, tap_count - 1 :]
    summed = bias + jnp.zeros(padded[:, tap_count - 1 :].shape, jnp.float32)
    for offset in range(tap_count):
        matches = (seg_pad[:, offset : offset + length] == current).astype(jnp.float32)
        summed = summed + weight[offset] * padded[:, offset : offset + length] * matches[..., None]
    return jax.nn.silu(summed)


def split_blocks(value, count):
    shaped = value.reshape((value.shape[0], count, value.shape[1] // count) + value.shape[2:])
    return jnp.moveaxis(shaped, 1, 0)


def block_step(carried_in, pieces):
    memory, previous = carried_in
    x_heads, b_mat, c_mat, dt_pos, decay, segment_ids = pieces
    cumul = jnp.cumsum(decay, axis=1)
    places = jnp.arange(segment_ids.shape[1])
    causal = places[:, None] >= places[None, :]
    linked = ((segment_ids[:, :, None] == segment_ids[:, None, :]) & causal[None])[..., None]
    spread = cumul[:, :, None, :] - cumul[:, None, :, :]
    weights = jnp.where(linked, jnp.exp(jnp.where(linked, spread, 0.0)), 0.0)
    inner = jnp.einsum("gtn,gsn->gts", c_mat, b_mat, precision=lax.Precision.HIGHEST)
    weights = weights * inner[..., None] * dt_pos[:, None, :, :]
    output = jnp.einsum("gtsh,gshp->gthp", weights, x_heads, precision=lax.Precision.HIGHEST)
    keeps = (segment_ids == previous[:, None]).astype(jnp.float32)
    reach = jnp.exp(cumul) * keeps[..., None]
    output = (
        output
        + jnp.einsum("gtn,ghpn->gthp", c_mat, memory, precision=lax.Precision.HIGHEST)
        * reach[..., None]
    )
    latest = segment_ids[:, -1]
    tails = (
        jnp.exp(cumul[:, -1:, :] - cumul)
        * (segment_ids == latest[:, None]).astype(jnp.float32)[..., None]
        * dt_pos
    )
    through = jnp.exp(cumul[:, -1, :]) * (latest == previous).astype(jnp.float32)[:, None]
    memory = memory * through[..., None, None] + jnp.einsum(
        "gsh,gshp,gsn->ghpn", tails, x_heads, b_mat, precision=lax.Precision.HIGHEST
    )
    return ((memory, latest), output)


def scan_blocks(x_heads, b_mat, c_mat, dt_pos, decay, segment_ids, memory, previous):
    length = segment_ids.shape[1]
    count = length // min(128, length)
    inputs = tuple(
        (
            split_blocks(value, count)
            for value in (x_heads, b_mat, c_mat, dt_pos, decay, segment_ids)
        )
    )
    (memory, latest), outputs = lax.scan(jax.checkpoint(block_step), (memory, previous), inputs)
    return (jnp.moveaxis(outputs, 0, 1).reshape(x_heads.shape), memory)


def part_local(x_heads, b_mat, c_mat, dt_raw, dt_bias, a_log, d_skip, segment_ids, previous):
    dt_pos = jax.nn.softplus(dt_raw + dt_bias)
    decay = -jnp.exp(a_log) * dt_pos
    zero_state = jnp.zeros((x_heads.shape[0], HEADS, HEAD, STATE), jnp.float32)
    mixed_heads, final_state = scan_blocks(
        x_heads, b_mat, c_mat, dt_pos, decay, segment_ids, zero_state, previous
    )
    y_local = mixed_heads + d_skip[:, None] * x_heads
    through = (
        jnp.exp(jnp.sum(decay, axis=1))
        * (segment_ids[:, -1] == previous).astype(jnp.float32)[:, None]
    )
    return (y_local, final_state, through)


def part_carry(c_mat, dt_raw, dt_bias, a_log, state_in, segment_ids, previous):
    dt_pos = jax.nn.softplus(dt_raw + dt_bias)
    cumul = jnp.cumsum(-jnp.exp(a_log) * dt_pos, axis=1)
    keeps = (segment_ids == previous[:, None]).astype(jnp.float32)
    reach = jnp.exp(cumul) * keeps[..., None]
    return (
        jnp.einsum("gtn,ghpn->gthp", c_mat, state_in, precision=lax.Precision.HIGHEST)
        * reach[..., None]
    )


def carry_forward(earlier, later):
    return (earlier[0] * later[0], later[0][..., None, None] * earlier[1] + later[1])


def carry_backward(earlier, later):
    return (earlier[0] * later[0], later[1] + later[0][..., None, None] * earlier[1])


def route_slots(flat_routes, expert_count, capacity):
    blocks = flat_routes.shape[0]
    onehot = (flat_routes[..., None] == jnp.arange(expert_count, dtype=jnp.int32)).astype(jnp.int32)
    ranks = jnp.sum((jnp.cumsum(onehot, axis=1) - onehot) * onehot, axis=-1)
    spots = (
        flat_routes * (blocks * capacity)
        + jnp.arange(blocks, dtype=jnp.int32)[:, None] * capacity
        + ranks
    )
    return spots


def times_rows(left, right):
    return lax.dot_general(
        left, right, (((0,), (0,)), ((), ())), preferred_element_type=jnp.float32
    )


def times_back(left, right):
    return lax.dot_general(
        left, right, (((1,), (1,)), ((), ())), preferred_element_type=jnp.float32
    )


def on_device_general(
    layer_in,
    seg_ids,
    route_ids,
    out_grad,
    norm_in,
    w_in,
    conv_w,
    conv_b,
    dt_bias,
    a_log,
    d_skip,
    norm_gate,
    w_out,
    norm_mid,
    w_router,
    w_sgate,
    w_sup,
    w_sdown,
    e_gate,
    e_up,
    e_down,
):
    seq_count, row_count, d_model = layer_in.shape
    token_count = seq_count * row_count
    tap_count = conv_w.shape[0]
    ctx_place = lax.axis_index("ctx")
    expert_count = EXP_DEV * lax.axis_size("dp")
    capacity = row_count * TOP * 5 // (expert_count * 4)
    dense_set = (
        lax.all_gather(norm_in, ("dp", "ctx"), axis=0, tiled=True),
        lax.all_gather(w_in, ("dp", "ctx"), axis=0, tiled=True),
        lax.all_gather(conv_w, ("dp", "ctx"), axis=1, tiled=True),
        lax.all_gather(conv_b, ("dp", "ctx"), axis=0, tiled=True),
        lax.all_gather(norm_gate, ("dp", "ctx"), axis=0, tiled=True),
        lax.all_gather(w_out, ("dp", "ctx"), axis=0, tiled=True),
        lax.all_gather(norm_mid, ("dp", "ctx"), axis=0, tiled=True),
        lax.all_gather(w_router, ("dp", "ctx"), axis=0, tiled=True),
        lax.all_gather(w_sgate, ("dp", "ctx"), axis=0, tiled=True),
        lax.all_gather(w_sup, ("dp", "ctx"), axis=0, tiled=True),
        lax.all_gather(w_sdown, ("dp", "ctx"), axis=0, tiled=True),
    )
    (
        gain_in,
        weight_in,
        conv_weight,
        conv_bias,
        gain_gate,
        weight_out,
        gain_mid,
        router_weight,
        sgate_weight,
        sup_weight,
        sdown_weight,
    ) = dense_set
    expert_gate, expert_up, expert_down = (
        lax.all_gather(e_gate, "ctx", axis=1, tiled=True),
        lax.all_gather(e_up, "ctx", axis=1, tiled=True),
        lax.all_gather(e_down, "ctx", axis=2, tiled=True),
    )
    input_f = layer_in.astype(jnp.float32)
    normed_f, pull_in = jax.vjp(scaled_norm, input_f, gain_in.astype(jnp.float32))
    normed = normed_f.astype(jnp.bfloat16).reshape(token_count, d_model)
    projected = jnp.dot(normed, weight_in, preferred_element_type=jnp.float32).reshape(
        seq_count, row_count, PROJ
    )
    z_part = projected[..., :DI]
    xbc_part = projected[..., DI : DI + CONV]
    dt_raw = projected[..., DI + CONV :]
    edge_rows = from_behind(
        xbc_part[:, row_count - tap_count + 1 :, :].astype(jnp.bfloat16), "ctx", 1
    ).astype(jnp.float32)
    seg_pad = jnp.concatenate(
        [jnp.full((seq_count, tap_count - 1), -1, jnp.int32), seg_ids], axis=1
    )
    seg_window = lax.dynamic_slice_in_dim(
        seg_pad, ctx_place * row_count, row_count + tap_count - 1, 1
    )
    seg_now = seg_window[:, tap_count - 1 :]
    seg_before = seg_window[:, tap_count - 2]
    padded = jnp.concatenate([edge_rows, xbc_part], axis=1)
    conv_out, pull_conv = jax.vjp(
        partial(conv_apply, seg_pad=seg_window),
        padded,
        conv_weight.astype(jnp.float32),
        conv_bias.astype(jnp.float32),
    )
    x_heads = conv_out[..., :DI].reshape(seq_count, row_count, HEADS, HEAD)
    b_mat = conv_out[..., DI : DI + STATE]
    c_mat = conv_out[..., DI + STATE :]
    local_piece = partial(part_local, segment_ids=seg_now, previous=seg_before)
    (y_local, state_out, through), pull_local = jax.vjp(
        local_piece, x_heads, b_mat, c_mat, dt_raw, dt_bias, a_log, d_skip
    )
    carried = carried_in_2(
        (through, state_out),
        "ctx",
        carry_forward,
        (jnp.ones_like(through), jnp.zeros_like(state_out)),
    )
    state_in = carried[1]
    carry_piece = partial(part_carry, segment_ids=seg_now, previous=seg_before)
    y_carry, pull_carry = jax.vjp(carry_piece, c_mat, dt_raw, dt_bias, a_log, state_in)
    gated_f, pull_gate = jax.vjp(
        gate_norm, y_local + y_carry, z_part, gain_gate.astype(jnp.float32)
    )
    gated = gated_f.astype(jnp.bfloat16).reshape(token_count, DI)
    mixed = jnp.dot(gated, weight_out, preferred_element_type=jnp.float32)
    resid_mid = input_f.reshape(token_count, d_model) + mixed
    normed_mid_f, pull_mid = jax.vjp(scaled_norm, resid_mid, gain_mid.astype(jnp.float32))
    normed_mid = normed_mid_f.astype(jnp.bfloat16)
    logits = jnp.dot(normed_mid, router_weight, preferred_element_type=jnp.float32)
    route_flat = route_ids.reshape(token_count, TOP)
    gates = jax.nn.softmax(jnp.take_along_axis(logits, route_flat, axis=1), axis=-1)
    shared_gate = jnp.dot(normed_mid, sgate_weight, preferred_element_type=jnp.float32)
    shared_up = jnp.dot(normed_mid, sup_weight, preferred_element_type=jnp.float32)
    shared_act = (jax.nn.silu(shared_gate) * shared_up).astype(jnp.bfloat16)
    shared_out = jnp.dot(shared_act, sdown_weight, preferred_element_type=jnp.float32)
    slot_ids = route_slots(route_ids.reshape(seq_count, row_count * TOP), expert_count, capacity)
    assigned = jnp.arange(token_count * TOP, dtype=jnp.int32)
    owners = (
        jnp.full((expert_count * seq_count * capacity,), token_count * TOP, jnp.int32)
        .at[slot_ids.reshape(-1)]
        .set(assigned)
    )
    token_of = owners // TOP
    rows_pad = jnp.concatenate([normed_mid, jnp.zeros((1, d_model), jnp.bfloat16)], axis=0)
    outgoing = rows_pad[token_of].reshape(expert_count, seq_count * capacity, d_model)
    incoming = lax.all_to_all(outgoing, "dp", split_axis=0, concat_axis=1, tiled=True)
    hidden_gate = jnp.einsum(
        "erd,edf->erf", incoming, expert_gate, preferred_element_type=jnp.float32
    )
    hidden_up = jnp.einsum("erd,edf->erf", incoming, expert_up, preferred_element_type=jnp.float32)
    hidden_act = (jax.nn.silu(hidden_gate) * hidden_up).astype(jnp.bfloat16)
    expert_out = jnp.einsum(
        "erf,efd->erd", hidden_act, expert_down, preferred_element_type=jnp.float32
    ).astype(jnp.bfloat16)
    returned = lax.all_to_all(expert_out, "dp", split_axis=1, concat_axis=0, tiled=True)
    slot_flat = slot_ids.reshape(token_count, TOP)
    picked = returned.reshape(-1, d_model)[slot_flat]
    routed = jnp.sum(gates[..., None] * picked, axis=1)
    layer_out = (
        (resid_mid + shared_out + routed)
        .astype(jnp.bfloat16)
        .reshape(seq_count, row_count, d_model)
    )
    grad_top = out_grad.astype(jnp.float32).reshape(token_count, d_model)
    grad_gates = jnp.sum(picked * grad_top[:, None, :], axis=-1)
    grad_pick = gates * (grad_gates - jnp.sum(gates * grad_gates, axis=-1, keepdims=True))
    expert_ids = jnp.arange(expert_count, dtype=jnp.int32)
    grad_logits = jnp.sum(
        grad_pick[..., None] * (route_flat[..., None] == expert_ids).astype(jnp.float32), axis=1
    ).astype(jnp.bfloat16)
    gates_pad = jnp.concatenate([gates.reshape(-1), jnp.zeros((1,), jnp.float32)])
    grad_pad = jnp.concatenate([grad_top, jnp.zeros((1, d_model), jnp.float32)], axis=0)
    grad_slots = (
        (gates_pad[owners][:, None] * grad_pad[token_of])
        .astype(jnp.bfloat16)
        .reshape(expert_count, seq_count * capacity, d_model)
    )
    grad_arrived = lax.all_to_all(grad_slots, "dp", split_axis=0, concat_axis=1, tiled=True)
    grad_act = jnp.einsum(
        "erd,efd->erf", grad_arrived, expert_down, preferred_element_type=jnp.float32
    )
    grad_e_down = jnp.einsum(
        "erf,erd->efd", hidden_act, grad_arrived, preferred_element_type=jnp.float32
    )
    grad_hgate = (grad_act * hidden_up * silu_slope(hidden_gate)).astype(jnp.bfloat16)
    grad_hup = (grad_act * jax.nn.silu(hidden_gate)).astype(jnp.bfloat16)
    grad_e_gate = jnp.einsum(
        "erd,erf->edf", incoming, grad_hgate, preferred_element_type=jnp.float32
    )
    grad_e_up = jnp.einsum("erd,erf->edf", incoming, grad_hup, preferred_element_type=jnp.float32)
    grad_incoming = jnp.einsum(
        "erf,edf->erd", grad_hgate, expert_gate, preferred_element_type=jnp.float32
    )
    grad_incoming = (
        grad_incoming
        + jnp.einsum("erf,edf->erd", grad_hup, expert_up, preferred_element_type=jnp.float32)
    ).astype(jnp.bfloat16)
    grad_returned = lax.all_to_all(grad_incoming, "dp", split_axis=1, concat_axis=0, tiled=True)
    grad_routed = jnp.sum(grad_returned.reshape(-1, d_model)[slot_flat], axis=1, dtype=jnp.float32)
    dense_set = (
        lax.all_gather(norm_in, ("dp", "ctx"), axis=0, tiled=True),
        lax.all_gather(w_in, ("dp", "ctx"), axis=0, tiled=True),
        lax.all_gather(conv_w, ("dp", "ctx"), axis=1, tiled=True),
        lax.all_gather(conv_b, ("dp", "ctx"), axis=0, tiled=True),
        lax.all_gather(norm_gate, ("dp", "ctx"), axis=0, tiled=True),
        lax.all_gather(w_out, ("dp", "ctx"), axis=0, tiled=True),
        lax.all_gather(norm_mid, ("dp", "ctx"), axis=0, tiled=True),
        lax.all_gather(w_router, ("dp", "ctx"), axis=0, tiled=True),
        lax.all_gather(w_sgate, ("dp", "ctx"), axis=0, tiled=True),
        lax.all_gather(w_sup, ("dp", "ctx"), axis=0, tiled=True),
        lax.all_gather(w_sdown, ("dp", "ctx"), axis=0, tiled=True),
    )
    (
        gain_in,
        weight_in,
        conv_weight,
        conv_bias,
        gain_gate,
        weight_out,
        gain_mid,
        router_weight,
        sgate_weight,
        sup_weight,
        sdown_weight,
    ) = dense_set
    grad_w_router = times_rows(normed_mid, grad_logits)
    grad_shared_out = grad_top.astype(jnp.bfloat16)
    grad_w_sdown = times_rows(shared_act, grad_shared_out)
    grad_shared_act = times_back(grad_shared_out, sdown_weight)
    grad_sgate = (grad_shared_act * shared_up * silu_slope(shared_gate)).astype(jnp.bfloat16)
    grad_sup = (grad_shared_act * jax.nn.silu(shared_gate)).astype(jnp.bfloat16)
    grad_w_sgate = times_rows(normed_mid, grad_sgate)
    grad_w_sup = times_rows(normed_mid, grad_sup)
    grad_mid = (
        grad_routed
        + times_back(grad_logits, router_weight)
        + times_back(grad_sgate, sgate_weight)
        + times_back(grad_sup, sup_weight)
    )
    grad_resid_part, grad_gain_mid = pull_mid(grad_mid)
    grad_resid = grad_top + grad_resid_part
    grad_mixed = grad_resid.astype(jnp.bfloat16)
    grad_w_out = times_rows(gated, grad_mixed)
    grad_gated = times_back(grad_mixed, weight_out).reshape(seq_count, row_count, DI)
    grad_y, grad_z, grad_gain_gate = pull_gate(grad_gated)
    grad_cmat_carry, grad_dt_carry, grad_bias_carry, grad_alog_carry, grad_state_in = pull_carry(
        grad_y
    )
    back_scan = carried_in_3(
        (through, grad_state_in),
        "ctx",
        carry_backward,
        (jnp.ones_like(through), jnp.zeros_like(grad_state_in)),
    )
    grad_state_out = back_scan[1]
    grad_through = jnp.sum(state_in * grad_state_out, axis=(2, 3))
    (
        grad_xheads,
        grad_bmat,
        grad_cmat,
        grad_dt_local,
        grad_bias_local,
        grad_alog_local,
        grad_dskip,
    ) = pull_local((grad_y, grad_state_out, grad_through))
    grad_conv_out = jnp.concatenate(
        [grad_xheads.reshape(seq_count, row_count, DI), grad_bmat, grad_cmat + grad_cmat_carry],
        axis=-1,
    )
    grad_padded, grad_conv_w, grad_conv_b = pull_conv(grad_conv_out)
    edge_grad = from_behind(for_sending(grad_padded[:, : tap_count - 1, :]), "ctx", -1)
    grad_xbc = grad_padded[:, tap_count - 1 :, :]
    grad_xbc = jnp.concatenate(
        [
            grad_xbc[:, : row_count - tap_count + 1],
            grad_xbc[:, row_count - tap_count + 1 :] + edge_grad,
        ],
        axis=1,
    )
    grad_proj = (
        jnp.concatenate([grad_z, grad_xbc, grad_dt_local + grad_dt_carry], axis=-1)
        .astype(jnp.bfloat16)
        .reshape(token_count, PROJ)
    )
    grad_w_in = times_rows(normed, grad_proj)
    grad_normed = times_back(grad_proj, weight_in).reshape(seq_count, row_count, d_model)
    grad_input_part, grad_gain_in = pull_in(grad_normed)
    grad_in = grad_resid.reshape(seq_count, row_count, d_model) + grad_input_part
    dense_grads = (
        lax.psum_scatter(grad_gain_in, ("dp", "ctx"), scatter_dimension=0, tiled=True),
        lax.psum_scatter(grad_w_in, ("dp", "ctx"), scatter_dimension=0, tiled=True),
        lax.psum_scatter(grad_conv_w, ("dp", "ctx"), scatter_dimension=1, tiled=True),
        lax.psum_scatter(grad_conv_b, ("dp", "ctx"), scatter_dimension=0, tiled=True),
        lax.psum_scatter(grad_gain_gate, ("dp", "ctx"), scatter_dimension=0, tiled=True),
        lax.psum_scatter(grad_w_out, ("dp", "ctx"), scatter_dimension=0, tiled=True),
        lax.psum_scatter(grad_gain_mid, ("dp", "ctx"), scatter_dimension=0, tiled=True),
        lax.psum_scatter(grad_w_router, ("dp", "ctx"), scatter_dimension=0, tiled=True),
        lax.psum_scatter(grad_w_sgate, ("dp", "ctx"), scatter_dimension=0, tiled=True),
        lax.psum_scatter(grad_w_sup, ("dp", "ctx"), scatter_dimension=0, tiled=True),
        lax.psum_scatter(grad_w_sdown, ("dp", "ctx"), scatter_dimension=0, tiled=True),
    )
    expert_grads = (
        lax.psum_scatter(
            grad_e_gate.astype(jnp.bfloat16), "ctx", scatter_dimension=1, tiled=True
        ).astype(jnp.float32),
        lax.psum_scatter(
            grad_e_up.astype(jnp.bfloat16), "ctx", scatter_dimension=1, tiled=True
        ).astype(jnp.float32),
        lax.psum_scatter(
            grad_e_down.astype(jnp.bfloat16), "ctx", scatter_dimension=2, tiled=True
        ).astype(jnp.float32),
    )
    head_grads = lax.psum(
        (grad_bias_local + grad_bias_carry, grad_alog_local + grad_alog_carry, grad_dskip),
        ("dp", "ctx"),
    )
    return (
        layer_out,
        grad_in,
        dense_grads[0],
        dense_grads[1],
        dense_grads[2],
        dense_grads[3],
        head_grads[0],
        head_grads[1],
        head_grads[2],
        dense_grads[4],
        dense_grads[5],
        dense_grads[6],
        dense_grads[7],
        dense_grads[8],
        dense_grads[9],
        dense_grads[10],
        expert_grads[0],
        expert_grads[1],
        expert_grads[2],
    )


GROUP = 8
WIDE = GROUP * HEAD
VMEM_MOST = 56 * 1024 * 1024
BRIEF = pl.CostEstimate(flops=1024, bytes_accessed=1024, transcendentals=0)


def spread_rows(rows):
    count, width = rows.shape
    return jnp.broadcast_to(rows[:, None, :], (count, HEAD, width)).reshape(count * HEAD, width)


def head_sums(value):
    return jnp.sum(value.reshape(GROUP, HEAD, value.shape[-1]), axis=1)


def mul_nn(left, right):
    return lax.dot_general(
        left, right, (((1,), (0,)), ((), ())), preferred_element_type=jnp.float32
    )


def mul_nt(left, right):
    return lax.dot_general(
        left, right, (((1,), (1,)), ((), ())), preferred_element_type=jnp.float32
    )


def mul_tn(left, right):
    return lax.dot_general(
        left, right, (((0,), (0,)), ((), ())), preferred_element_type=jnp.float32
    )


def half(value):
    return value.astype(jnp.bfloat16)


def call_steps(kernel, steps, ins, in_specs, outs, out_specs, scratch=(), name_id=None):
    return pl.pallas_call(
        kernel,
        grid=(steps,),
        in_specs=in_specs,
        out_specs=out_specs,
        out_shape=outs,
        scratch_shapes=list(scratch),
        cost_estimate=BRIEF,
        compiler_params=pltpu.CompilerParams(
            vmem_limit_bytes=VMEM_MOST,
            dimension_semantics=("arbitrary",),
            collective_id=name_id,
            has_side_effects=name_id is not None,
        ),
    )(*ins)


def block(shape, index):
    return pl.BlockSpec(shape, index)


def whole(array):
    return pl.BlockSpec(array.shape, lambda i: (0,) * array.ndim)


def f32_out(*shape):
    return jax.ShapeDtypeStruct(shape, jnp.float32)


def bf16_out(*shape):
    return jax.ShapeDtypeStruct(shape, jnp.bfloat16)


def conv_steps(x, taps, masks):
    total = taps[:, 4:5] + taps[:, 3:4] * x * masks[0:1]
    for back in (1, 2, 3):
        total = total + taps[:, 3 - back : 4 - back] * pltpu.roll(x, back, 1) * masks[back : back + 1]
    return total


def conv_kernel(x_ref, taps_ref, masks_ref, pre_ref):
    tokens = pre_ref.shape[1]
    pre_ref[...] = conv_steps(x_ref[...], taps_ref[...], masks_ref[...])[:, :tokens]


def conv_adjoint(grad_pre, x, taps, masks):
    width = x.shape[1]
    grad_x = jnp.zeros_like(x)
    columns = []
    for back in (3, 2, 1, 0):
        part = grad_pre * masks[back : back + 1]
        moved = x if back == 0 else pltpu.roll(x, back, 1)
        columns.append(jnp.sum(part * moved, axis=1, keepdims=True))
        tap = taps[:, 3 - back : 4 - back]
        grad_x = grad_x + tap * (part if back == 0 else pltpu.roll(part, width - back, 1))
    columns.append(jnp.sum(grad_pre, axis=1, keepdims=True))
    lane = lax.broadcasted_iota(jnp.int32, (x.shape[0], 8), 1)
    packed = jnp.zeros((x.shape[0], 8), jnp.float32)
    for place, column in enumerate(columns):
        packed = jnp.where(lane == place, column, packed)
    return grad_x, packed


def conv_back_kernel(grad_ref, pre_ref, x_ref, taps_ref, masks_ref, grad_x_ref, taps_out_ref):
    grad_pre = grad_ref[...] * silu_slope(pre_ref[...])
    rest = x_ref.shape[1] - grad_pre.shape[1]
    grad_pre = jnp.concatenate([grad_pre, jnp.zeros((grad_pre.shape[0], rest), jnp.float32)], axis=1)
    grad_x, packed = conv_adjoint(grad_pre, x_ref[...], taps_ref[...], masks_ref[...])
    grad_x_ref[...] = grad_x.astype(grad_x_ref.dtype)
    taps_out_ref[...] = packed


def link_mask(seg_row, seg_col):
    count = seg_row.shape[1]
    source = lax.broadcasted_iota(jnp.int32, (count, count), 0)
    target = lax.broadcasted_iota(jnp.int32, (count, count), 1)
    linked = jnp.logical_and(source <= target, seg_row == seg_col)
    return jnp.where(linked, 0.0, -1e30)


def state_kernel(x_ref, taps_ref, masks_ref, bc_ref, dt_ref, cum_ref, flags_ref, pre_ref, state_ref):
    tokens = pre_ref.shape[1]
    pre = conv_steps(x_ref[...], taps_ref[...], masks_ref[...])[:, :tokens]
    pre_ref[...] = pre
    b_t = half(jax.nn.silu(bc_ref[:STATE, :]))
    cum = cum_ref[...]
    tail = jnp.exp(cum[:, tokens - 1 :] - cum) * flags_ref[1:2, :] * dt_ref[...]
    scaled = half(jax.nn.silu(pre) * spread_rows(tail))
    state_ref[...] = half(mul_nt(scaled, b_t))


def gate_back_kernel(
    y_ref, z_ref, grad_ref, gain_ref, rows_ref, bc_ref, cum_ref, flags_ref, grad_y_ref, grad_z_ref, grad_state_ref
):
    y, z, gain = y_ref[...], z_ref[...], gain_ref[:, 0:1]
    squashed = jax.nn.sigmoid(z)
    u = y * z * squashed
    grad_u = gain * rows_ref[0:1, :] * grad_ref[...] - u * rows_ref[1:2, :]
    grad_y = grad_u * z * squashed
    grad_y_ref[...] = grad_y
    grad_z_ref[...] = half(grad_u * y * (squashed * (1.0 + z * (1.0 - squashed))))
    c_t = half(jax.nn.silu(bc_ref[STATE:, :]))
    reach = jnp.exp(cum_ref[...]) * flags_ref[0:1, :]
    grad_state_ref[...] = half(mul_nt(half(grad_y * spread_rows(reach)), c_t))


def inner_back_kernel(
    local_ref, passed_ref, pre_ref, grad_y_ref, bc_ref, dt_ref, cum_ref, cum_col_ref, flags_ref, seg_col_ref,
    grad_x_ref, grad_state_ref, grad_cum_ref, grad_skip_ref, grad_bc_ref, mask_s, inner_s, total_s, *chain,
):
    step = pl.program_id(0)
    first, last, device = chain_places(step, False)

    @pl.when(step == 0)
    def _():
        mask_s[...] = link_mask(flags_ref[2:3, :], seg_col_ref[:, 0:1])
        bc = half(jax.nn.silu(bc_ref[...]))
        inner_s[...] = mul_tn(bc[:STATE], bc[STATE:])
        total_s[...] = jnp.zeros_like(total_s)

    grad_state_ref[...] = chain_step(step, first, last, device, local_ref, passed_ref, *chain)
    x = jax.nn.silu(pre_ref[...])
    grad_y = grad_y_ref[...]
    grad_skip_ref[...] = head_sums(x * grad_y)
    scaled = half(x * spread_rows(dt_ref[...]))
    grad_half = half(grad_y)
    cum, cum_col = cum_ref[...], cum_col_ref[0]
    ones = jnp.ones((8, cum.shape[1]), jnp.bfloat16)
    for head in range(GROUP):
        rows = slice(head * HEAD, (head + 1) * HEAD)
        decay = jnp.exp(cum[head : head + 1, :] - cum_col[:, head : head + 1] + mask_s[...])
        weights = decay * inner_s[...]
        grad_x_ref[rows, :] = mul_nt(grad_half[rows], half(weights))
        grad_weights = mul_tn(scaled[rows], grad_half[rows])
        total_s[...] += grad_weights * decay
        moved = half(grad_weights * weights)
        sums = mul_nn(ones, moved) - mul_nt(ones, moved)
        grad_cum_ref[head : head + 1, :] = sums[0:1]

    @pl.when(step == pl.num_programs(0) - 1)
    def _():
        bc = half(jax.nn.silu(bc_ref[...]))
        total = half(total_s[...])
        grad_bc_ref[:STATE, :] = mul_nt(bc[STATE:], total)
        grad_bc_ref[STATE:, :] = mul_nn(bc[:STATE], total)
        chain_end(chain[0].shape[0], last, device, *chain)


def join_back_kernel(
    grad_in_ref, grad_y_ref, pre_ref, x_ref, taps_ref, masks_ref, state_ref, grad_state_ref,
    bc_ref, dt_ref, cum_ref, skip_ref, flags_ref,
    grad_x_ref, taps_out_ref, grad_dt_ref, grad_cum_ref, grad_last_ref, grad_bc_ref,
):
    step = pl.program_id(0)

    @pl.when(step == 0)
    def _():
        grad_bc_ref[...] = jnp.zeros_like(grad_bc_ref)

    bc = half(jax.nn.silu(bc_ref[...]))
    b_t, c_t = bc[:STATE], bc[STATE:]
    pre, grad_y, cum, dt = pre_ref[...], grad_y_ref[...], cum_ref[...], dt_ref[...]
    tokens = pre.shape[1]
    state, grad_state = state_ref[...], grad_state_ref[...]
    x = jax.nn.silu(pre)
    reached = grad_y * spread_rows(jnp.exp(cum) * flags_ref[0:1, :])
    grad_cum = head_sums(reached * mul_nn(state, c_t))
    grad_bc_ref[STATE:, :] += mul_tn(state, half(reached))
    tail = spread_rows(jnp.exp(cum[:, tokens - 1 :] - cum) * flags_ref[1:2, :])
    dt_wide = spread_rows(dt)
    scaled = x * dt_wide
    from_state = mul_nn(grad_state, b_t) * tail
    grad_bc_ref[:STATE, :] += mul_tn(grad_state, half(scaled * tail))
    tails = head_sums(scaled * from_state)
    grad_cum_ref[...] = grad_cum - tails
    last = jnp.sum(tails, axis=1, keepdims=True)
    through = jnp.sum(
        head_sums(state.astype(jnp.float32) * grad_state.astype(jnp.float32)), axis=1, keepdims=True
    )
    lane = lax.broadcasted_iota(jnp.int32, (GROUP, 128), 1)
    grad_last_ref[...] = jnp.where(lane == 0, last, jnp.where(lane == 1, through, 0.0))
    grad_scaled = grad_in_ref[...] + from_state
    grad_dt_ref[...] = head_sums(grad_scaled * x)
    grad_pre = (grad_scaled * dt_wide + grad_y * spread_rows(skip_ref[...])) * silu_slope(pre)
    rest = x_ref.shape[1] - tokens
    grad_pre = jnp.concatenate([grad_pre, jnp.zeros((grad_pre.shape[0], rest), jnp.float32)], axis=1)
    grad_x, packed = conv_adjoint(grad_pre, x_ref[...], taps_ref[...], masks_ref[...])
    grad_x_ref[...] = half(grad_x)
    taps_out_ref[...] = packed


def mixer_rows(dt_raw, dt_bias, a_log, d_skip, seg_window, taps):
    tokens = dt_raw.shape[1]
    dt = jax.nn.softplus(dt_raw + dt_bias[:, None])
    decay = -jnp.exp(a_log)[:, None] * dt
    upper = jnp.triu(jnp.ones((tokens, tokens), jnp.float32))
    cum = jnp.dot(decay, upper, precision=lax.Precision.HIGHEST)
    cum_col = jnp.swapaxes(cum.reshape(-1, GROUP, tokens), 1, 2)
    seg_now = seg_window[taps - 1 :]
    before = seg_window[taps - 2]
    reach = (seg_now == before).astype(jnp.float32)
    tail = (seg_now == seg_now[-1]).astype(jnp.float32)
    none = jnp.zeros((5, tokens), jnp.float32)
    flags = jnp.concatenate([jnp.stack([reach, tail, seg_now.astype(jnp.float32)]), none])
    seg_col = jnp.broadcast_to(seg_now.astype(jnp.float32)[:, None], (tokens, 8))
    masks = [
        (seg_window[taps - 1 - back : taps - 1 - back + tokens] == seg_now).astype(jnp.float32)
        for back in range(taps)
    ]
    masks = jnp.pad(jnp.stack(masks), ((0, 8 - taps), (0, 128)))
    through = jnp.exp(cum[:, -1]) * (seg_now[-1] == before).astype(jnp.float32)
    skip = jnp.broadcast_to(d_skip[:, None], dt.shape)
    return dt, decay, cum, cum_col, flags, seg_col, masks, through, skip


def mixer_forward_states(proj, taps, masks, dt, cum, flags):
    tokens, groups = dt.shape[1], HEADS // GROUP
    wide = proj.shape[1]
    bc_pre = call_steps(
        conv_kernel, 1, (proj, taps, masks),
        [block((2 * STATE, wide), lambda i: (DI // STATE, 0)),
         block((2 * STATE, 8), lambda i: (DI // (2 * STATE), 0)), whole(masks)],
        f32_out(2 * STATE, tokens), block((2 * STATE, tokens), lambda i: (0, 0)),
    )
    rows = block((GROUP, tokens), lambda i: (i, 0))
    pre, state = call_steps(
        state_kernel, groups, (proj, taps, masks, bc_pre, dt, cum, flags),
        [block((WIDE, wide), lambda i: (i + groups, 0)), block((WIDE, 8), lambda i: (i, 0)), whole(masks),
         whole(bc_pre), rows, rows, whole(flags)],
        [f32_out(DI, tokens), bf16_out(DI, STATE)],
        [block((WIDE, tokens), lambda i: (i, 0)), block((WIDE, STATE), lambda i: (i, 0))],
    )
    return bc_pre, pre, state


def mixer_back_gate(y, proj, grad_gated, gain_col, gate_rows, bc_pre, cum, flags):
    tokens, groups = y.shape[1], HEADS // GROUP
    wide = block((WIDE, tokens), lambda i: (i, 0))
    return call_steps(
        gate_back_kernel, groups, (y, proj, grad_gated, gain_col, gate_rows, bc_pre, cum, flags),
        [wide, wide, wide, block((WIDE, 8), lambda i: (i, 0)), whole(gate_rows), whole(bc_pre),
         block((GROUP, tokens), lambda i: (i, 0)), whole(flags)],
        [f32_out(DI, tokens), bf16_out(DI, tokens), bf16_out(DI, STATE)],
        [wide, wide, block((WIDE, STATE), lambda i: (i, 0))],
    )


def mixer_back_inner(local, passed, pre, grad_y, bc_pre, dt, cum, cum_col, flags, seg_col, name_id):
    tokens, groups = dt.shape[1], HEADS // GROUP
    rows = block((GROUP, tokens), lambda i: (i, 0))
    wide = block((WIDE, tokens), lambda i: (i, 0))
    states = block((WIDE, STATE), lambda i: (i, 0))
    square = pltpu.VMEM((tokens, tokens), jnp.float32)
    return call_steps(
        inner_back_kernel, groups, (local, passed, pre, grad_y, bc_pre, dt, cum, cum_col, flags, seg_col),
        [states, block((WIDE, 8), lambda i: (i, 0)), wide, wide, whole(bc_pre), rows, rows, block((1, tokens, GROUP), lambda i: (i, 0, 0)),
         whole(flags), whole(seg_col)],
        [f32_out(DI, tokens), bf16_out(DI, STATE), f32_out(HEADS, tokens), f32_out(HEADS, tokens),
         f32_out(2 * STATE, tokens)],
        [wide, states, rows, rows, block((2 * STATE, tokens), lambda i: (0, 0))],
        (square, square, square) + chain_room(groups), name_id=name_id,
    )


def mixer_back_join(grad_scaled, grad_y, pre, proj, taps, masks, state_in, grad_state, bc_pre, dt, cum, skip, flags):
    tokens, groups = dt.shape[1], HEADS // GROUP
    rows = block((GROUP, tokens), lambda i: (i, 0))
    wide = block((WIDE, tokens), lambda i: (i, 0))
    longer = block((WIDE, proj.shape[1]), lambda i: (i, 0))
    later = block((WIDE, proj.shape[1]), lambda i: (i + groups, 0))
    states = block((WIDE, STATE), lambda i: (i, 0))
    narrow = block((WIDE, 8), lambda i: (i, 0))
    return call_steps(
        join_back_kernel, groups,
        (grad_scaled, grad_y, pre, proj, taps, masks, state_in, grad_state, bc_pre, dt, cum, skip, flags),
        [wide, wide, wide, later, narrow, whole(masks), states, states, whole(bc_pre), rows, rows, rows,
         whole(flags)],
        [bf16_out(DI, proj.shape[1]), f32_out(DI, 8), f32_out(HEADS, tokens), f32_out(HEADS, tokens),
         f32_out(HEADS, 128), f32_out(2 * STATE, tokens)],
        [longer, narrow, rows, rows, block((GROUP, 128), lambda i: (i, 0)),
         block((2 * STATE, tokens), lambda i: (0, 0))],
    )


def mixer_back_conv(grad_bc, bc_pre, proj, taps, masks):
    place = DI // (2 * STATE)
    wide = proj.shape[1]
    return call_steps(
        conv_back_kernel, 1, (grad_bc, bc_pre, proj, taps, masks),
        [whole(grad_bc), whole(bc_pre), block((2 * STATE, wide), lambda i: (2 * place, 0)),
         block((2 * STATE, 8), lambda i: (place, 0)), whole(masks)],
        [bf16_out(2 * STATE, wide), f32_out(2 * STATE, 8)],
        [block((2 * STATE, wide), lambda i: (0, 0)), block((2 * STATE, 8), lambda i: (0, 0))],
    )


def cut(array_index, rows, columns, row_step, column_step):
    found = []
    for row in range(0, rows, row_step):
        for column in range(0, columns, column_step):
            found.append(
                (array_index, row, min(row_step, rows - row), column, min(column_step, columns - column))
            )
    return found


def flipped(z, bits):
    if bits & 1:
        z = z + 1 - 2 * lax.rem(z, 2)
    return lax.rem(z + (bits & 2), 4)


def places(line):
    dp, z = lax.axis_index("dp"), lax.axis_index("ctx")
    y, x, core = lax.div(dp, 4), lax.rem(lax.div(dp, 2), 2), lax.rem(dp, 2)
    others = {
        "x": (dp + 2 - 4 * x, z),
        "y": (dp + 4 - 8 * y, z),
        "core": (dp + 1 - 2 * core, z),
    }
    for away in line:
        others[away] = (dp, lax.rem(z + away, 4))
    others["beside"] = (dp, flipped(z, 1))
    return y, x, core, z, others


def moved(moves, refs_in, refs_out, z, others, sems):
    copies = []
    for at, (source, target, take, put, bits) in enumerate(moves):
        source, target = refs_in[source], refs_out[target]
        source, target = source.at[take(z)], target.at[put(z)]
        copies.append(
            pltpu.make_async_remote_copy(
                src_ref=source,
                dst_ref=target,
                send_sem=sems[0].at[at],
                recv_sem=sems[1].at[at],
                device_id=others["beside" if bits == 1 else 2],
                device_id_type=pl.DeviceIdType.MESH,
            )
        )
    return copies


def greet(others):
    barrier = pltpu.get_barrier_semaphore()
    for device in others.values():
        pl.semaphore_signal(
            barrier, inc=1, device_id=device, device_id_type=pl.DeviceIdType.MESH
        )
    pl.semaphore_wait(barrier, len(others))


def send(source, target, sems, piece, leg, device):
    return pltpu.make_async_remote_copy(
        src_ref=source,
        dst_ref=target,
        send_sem=sems[0].at[piece, leg],
        recv_sem=sems[1].at[piece, leg],
        device_id=device,
        device_id_type=pl.DeviceIdType.MESH,
    )


def gather_kernel(pieces, ahead, count, line, moves, sizes, *refs):
    ins, more_in = refs[:count], refs[count : count + sizes[0]]
    refs = refs[count + sizes[0] :]
    outs, more_out = refs[:count], refs[count : count + sizes[1]]
    sent, came, kept, *more_sems = refs[count + sizes[1] :]
    y, x, core, z, others = places(line)
    deep = len(line) + 1
    slot = z if deep == 4 else lax.div(z, 2)
    greet(others)
    sems = (sent, came)

    def extra():
        return moved(moves, more_in if sizes[2] else more_out, more_out, z, others, more_sems) if moves else []

    def extra_turn(turn, turns):
        share = -(-len(moves) // turns)
        if turn < turns:
            for copy in extra()[share * turn : share * (turn + 1)]:
                copy.start()

    def legs(number):
        array, row, rows, column, columns = pieces[number]
        area = (pl.ds(row, rows), pl.ds(column, columns))
        out = outs[array]
        first, second = ("x", "y") if number % 2 == 0 else ("y", "x")
        rest = ((slice(None),) if line else ()) + area
        own = ins[array].at[area]
        mine = out.at[(y, x, core) + ((slot,) if line else ()) + area]
        lane = out.at[(y, x, core) + rest]
        if first == "x":
            plane = out.at[(y, slice(None), core) + rest]
        else:
            plane = out.at[(slice(None), x, core) + rest]
        every = out.at[(slice(None), slice(None), core) + rest]
        return {
            "keep": lambda: pltpu.make_async_copy(own, mine, kept.at[number]),
            "line": lambda: [
                send(own, mine, sems, number, away - 1, others[away])
                for away in line
            ],
            "first": lambda: send(lane if line else own, lane, sems, number, 3, others[first]),
            "second": lambda: send(plane, plane, sems, number, 4, others[second]),
            "core": lambda: send(every, every, sems, number, 5, others["core"]),
        }

    def begin(number):
        if number < len(pieces):
            leg = legs(number)
            leg["keep"]().start()
            for copy in leg["line"]():
                copy.start()

    def advance(number, stage):
        if not 0 <= number < len(pieces):
            return
        leg = legs(number)
        if stage == 0:
            leg["keep"]().wait()
            for copy in leg["line"]():
                copy.wait_recv()
            leg["first"]().start()
        elif stage == 1:
            leg["first"]().wait_recv()
            leg["second"]().start()
        elif stage == 2:
            leg["second"]().wait_recv()
            leg["core"]().start()
        else:
            leg["core"]().wait_recv()

    for number in range(2 * ahead):
        begin(number)
    pairs = -(-len(pieces) // 2)
    for turn in range(pairs + 3):
        extra_turn(turn, pairs)
        for stage in range(4):
            for number in (2 * (turn - stage), 2 * (turn - stage) + 1):
                advance(number, stage)
                if stage == 0 and number < len(pieces):
                    begin(number + 2 * ahead)
    for number in range(len(pieces)):
        leg = legs(number)
        for copy in leg["line"]() + [leg["first"](), leg["second"](), leg["core"]()]:
            copy.wait_send()
    for copy in extra():
        copy.wait()


def move_room(moves):
    if not moves:
        return []
    return [pltpu.SemaphoreType.DMA((len(moves),))] * 2


def pallas_gather(parts, steps, name_id, line=(1, 2, 3), ahead=2, more=(), more_shapes=(), moves=()):
    pieces = []
    for index, (part, (row_step, column_step)) in enumerate(zip(parts, steps)):
        pieces += cut(index, part.shape[0], part.shape[1], row_step, column_step)
    count = len(parts)
    made = more_shapes or [part.shape for part in more]
    lead = (2, 2, 2) + ((len(line) + 1,) if line else ())
    anywhere = pl.BlockSpec(memory_space=pl.ANY)
    outs = pl.pallas_call(
        partial(gather_kernel, pieces, ahead, count, line, moves, (len(more), len(made), bool(more_shapes))),
        in_specs=[anywhere] * (count + len(more)),
        out_specs=[anywhere] * (count + len(made)),
        out_shape=[jax.ShapeDtypeStruct(lead + part.shape, part.dtype) for part in parts]
        + [bf16_out(*shape) for shape in made],
        scratch_shapes=[
            pltpu.SemaphoreType.DMA((len(pieces), 6)),
            pltpu.SemaphoreType.DMA((len(pieces), 6)),
            pltpu.SemaphoreType.DMA((len(pieces),)),
        ]
        + move_room(moves),
        input_output_aliases={} if more_shapes else {count + at: count + at for at in range(len(more))},
        cost_estimate=BRIEF,
        compiler_params=pltpu.CompilerParams(collective_id=name_id, has_side_effects=True),
    )(*parts, *more)
    return [out.reshape((-1,) + part.shape) for out, part in zip(outs, parts)] + list(outs[count:])


def reduce_kernel(pieces, ahead, count, lines, moves, sizes, *refs):
    ins, more_in = refs[:count], refs[count : count + sizes[0]]
    refs = refs[count + sizes[0] :]
    outs, more_out = refs[:count], refs[count : count + sizes[1]]
    sent, came, kept, put = refs[count + sizes[1] : count + sizes[1] + 4]
    room = refs[count + sizes[1] + 4 :]
    if moves:
        more_sems, room = room[:2], room[2:]
    y, x, core, z, others = places(max(lines, key=len))
    greet(others)
    sems = (sent, came)
    amount = len(pieces)

    def extra():
        return moved(moves, more_in, more_out, z, others, more_sems) if moves else []

    def extra_turn(turn, turns):
        share = -(-len(moves) // turns)
        if turn < turns:
            for copy in extra()[share * turn : share * (turn + 1)]:
                copy.start()

    def held(number):
        return room[6 * number : 6 * number + 6]

    def legs(number):
        array, row, rows, column, columns = pieces[number]
        area = (pl.ds(row, rows), pl.ds(column, columns))
        total, from_core, from_first, from_second, from_line, result = held(number)
        every = (slice(None), slice(None))
        line = lines[array]
        deep = len(line) + 1
        slot = z if deep == 4 else lax.div(z, 2)
        rest = ((slice(None),) if line else ()) + area
        side = number % 2 == 0
        return {
            "load": lambda: pltpu.make_async_copy(
                ins[array].at[every + (core,) + rest], total, kept.at[number]
            ),
            "core": lambda: send(
                ins[array].at[every + (1 - core,) + rest],
                from_core, sems, number, 0, others["core"],
            ),
            "first": lambda: send(
                total.at[:, 1 - x] if side else total.at[1 - y],
                from_first, sems, number, 1, others["x" if side else "y"],
            ),
            "second": lambda: send(
                total.at[1 - y, x] if side else total.at[y, 1 - x],
                from_second, sems, number, 2, others["y" if side else "x"],
            ),
            "line": lambda: [
                send(
                    total.at[y, x, lax.rem(z + away, 4) if deep == 4 else 1 - slot],
                    from_line.at[away - line[0]], sems, number, 2 + away, others[away],
                )
                for away in line
            ],
            "store": lambda: pltpu.make_async_copy(result, outs[array].at[area], put.at[number]),
        }

    def begin(number):
        if number < amount:
            leg = legs(number)
            leg["load"]().start()
            leg["core"]().start()

    def advance(number, stage):
        if not 0 <= number < amount:
            return
        leg = legs(number)
        total, from_core, from_first, from_second, from_line, result = held(number)
        line = lines[pieces[number][0]]
        deep = len(line) + 1
        slot = z if deep == 4 else lax.div(z, 2)

        def place(at, *lead):
            return lead + ((lax.rem(at, deep),) if line else ())

        if stage == 0:
            leg["load"]().wait()
            leg["core"]().wait_recv()

            @pl.loop(0, 4 * deep)
            def _(at):
                here = place(at, lax.div(at, 2 * deep), lax.rem(lax.div(at, deep), 2))
                total[here] = total[here] + from_core[here]

            leg["first"]().start()
        elif stage == 1:
            leg["first"]().wait_recv()

            @pl.loop(0, 2 * deep)
            def _(at):
                outer = lax.div(at, deep)
                here = place(at, outer, x) if number % 2 == 0 else place(at, y, outer)
                total[here] = total[here] + from_first[place(at, outer)]

            leg["second"]().start()
        elif stage == 2:
            leg["second"]().wait_recv()
            if line:

                @pl.loop(0, deep)
                def _(at):
                    total[y, x, at] = total[y, x, at] + from_second[at]

                for copy in leg["line"]():
                    copy.start()
            else:
                result[...] = total[y, x].astype(jnp.float32) + from_second[...].astype(jnp.float32)
                leg["store"]().start()
        elif line:
            for copy in leg["line"]():
                copy.wait_recv()
            summed = total[y, x, slot].astype(jnp.float32)
            for away in range(len(line)):
                summed = summed + from_line[away].astype(jnp.float32)
            result[...] = summed
            leg["store"]().start()

    for number in range(2 * ahead):
        begin(number)
    pairs = -(-amount // 2)
    for turn in range(pairs + 3):
        extra_turn(turn, pairs)
        for stage in range(4):
            for number in (2 * (turn - stage), 2 * (turn - stage) + 1):
                advance(number, stage)
                if stage == 0 and number >= 0:
                    begin(number + 2 * ahead)
    for number in range(amount):
        leg = legs(number)
        for copy in [leg["core"](), leg["first"](), leg["second"]()] + leg["line"]():
            copy.wait_send()
        leg["store"]().wait()
    for copy in extra():
        copy.wait()


def pallas_reduce(parts, steps, name_id, lines=None, ahead=2, more=(), more_shapes=(), moves=()):
    lines = lines or [(1, 2, 3)] * len(parts)
    shapes = [part.shape[1:] for part in parts]
    pieces = []
    for index, (shape, (row_step, column_step)) in enumerate(zip(shapes, steps)):
        pieces += cut(index, shape[0], shape[1], row_step, column_step)
    count, amount = len(parts), len(pieces)
    anywhere = pl.BlockSpec(memory_space=pl.ANY)
    room = []
    for array, _, rows, _, columns in pieces:
        kind, line = parts[array].dtype, lines[array]
        deep = (len(line) + 1,) if line else ()
        for lead in ((2, 2) + deep, (2, 2) + deep, (2,) + deep, deep, (max(len(line), 1),)):
            room.append(pltpu.VMEM(lead + (rows, columns), kind))
        room.append(pltpu.VMEM((rows, columns), jnp.float32))
    return pl.pallas_call(
        partial(reduce_kernel, pieces, ahead, count, lines, moves, (len(more), len(more_shapes))),
        in_specs=[anywhere] * (count + len(more)),
        out_specs=[anywhere] * (count + len(more_shapes)),
        out_shape=[jax.ShapeDtypeStruct(shape, jnp.float32) for shape in shapes]
        + [bf16_out(*shape) for shape in more_shapes],
        scratch_shapes=[
            pltpu.SemaphoreType.DMA((amount, 6)),
            pltpu.SemaphoreType.DMA((amount, 6)),
            pltpu.SemaphoreType.DMA((amount,)),
            pltpu.SemaphoreType.DMA((amount,)),
        ]
        + move_room(moves)
        + room,
        cost_estimate=BRIEF,
        compiler_params=pltpu.CompilerParams(
            collective_id=name_id, has_side_effects=True, vmem_limit_bytes=VMEM_MOST
        ),
        )(*[part.reshape((2, 2, 2) + ((len(line) + 1,) if line else ()) + shape) for part, shape, line in zip(parts, shapes, lines)], *more)


def proj_back_kernel(normed_ref, weight_ref, grad_ref, grad_weight_ref, grad_normed_ref):
    step, width = pl.program_id(0), weight_ref.shape[1]
    last = pl.num_programs(0) - 1
    grad = grad_ref[...]
    grad_weight_ref[...] = half(mul_nt(normed_ref[...], grad))

    @pl.when(step == 0)
    def _():
        grad_normed_ref[...] = jnp.zeros_like(grad_normed_ref)

    @pl.when(step < last)
    def _():
        grad_normed_ref[...] += mul_nn(weight_ref[...], grad)

    @pl.when(step == last)
    def _():
        left = PROJ - last * width
        lane = lax.broadcasted_iota(jnp.int32, weight_ref.shape, 1)
        row = lax.broadcasted_iota(jnp.int32, grad.shape, 0)
        weight = jnp.where(lane < left, weight_ref[...], jnp.zeros_like(weight_ref))
        grad_normed_ref[...] += mul_nn(weight, jnp.where(row < left, grad, jnp.zeros_like(grad)))


def proj_back(normed_t, weight, grad_t):
    features, tokens = normed_t.shape
    width = 512
    return call_steps(
        proj_back_kernel, -(-PROJ // width), (normed_t, weight, grad_t),
        [whole(normed_t), block((features, width), lambda i: (0, i)), block((width, tokens), lambda i: (i, 0))],
        [bf16_out(features, PROJ), f32_out(features, tokens)],
        [block((features, width), lambda i: (0, i)), block((features, tokens), lambda i: (0, 0))],

    )


def hop(group, leaving, arrived, sent, came, device):
    return pltpu.make_async_remote_copy(
        src_ref=leaving.at[group],
        dst_ref=arrived.at[group],
        send_sem=sent.at[group],
        recv_sem=came.at[group],
        device_id=device,
        device_id_type=pl.DeviceIdType.MESH,
    )


def chain_places(step, forward):
    dp, z = lax.axis_index("dp"), lax.axis_index("ctx")
    others = {"left": (dp, lax.rem(z + 3, 4)), "right": (dp, lax.rem(z + 1, 4))}

    @pl.when(step == 0)
    def _():
        greet(others)

    if forward:
        return z == 0, z == 3, others["right"]
    return z == 3, z == 0, others["left"]


def chain_step(step, first, last, device, local_ref, passed_ref, leaving, arrived, sent, came):
    @pl.when(first)
    def _():
        arrived[step] = jnp.zeros(arrived.shape[1:], arrived.dtype)

    @pl.when(jnp.logical_not(first))
    def _():
        hop(step, leaving, arrived, sent, came, device).wait_recv()

    here = arrived[step]
    leaving[step] = half(here.astype(jnp.float32) * passed_ref[:, 0:1] + local_ref[...].astype(jnp.float32))

    @pl.when(jnp.logical_not(last))
    def _():
        hop(step, leaving, arrived, sent, came, device).start()

    return here


def chain_end(groups, last, device, leaving, arrived, sent, came):
    @pl.when(jnp.logical_not(last))
    def _():
        for group in range(groups):
            hop(group, leaving, arrived, sent, came, device).wait_send()


def chain_room(groups):
    slots = pltpu.VMEM((groups, WIDE, STATE), jnp.bfloat16)
    sems = pltpu.SemaphoreType.DMA((groups,))
    return (slots, slots, sems, sems)


def forward_kernel(
    local_ref, passed_ref, pre_ref, bc_ref, dt_ref, cum_ref, cum_col_ref, skip_ref, flags_ref, seg_col_ref,
    z_ref, gain_ref, y_ref, state_ref, gated_ref, scale_ref, mask_s, inner_s, u_s, sum_s, *chain,
):
    step, groups = pl.program_id(0), u_s.shape[0]
    first, last, device = chain_places(step, True)

    @pl.when(step == 0)
    def _():
        mask_s[...] = link_mask(flags_ref[2:3, :], seg_col_ref[:, 0:1])
        bc = half(jax.nn.silu(bc_ref[...]))
        inner_s[...] = mul_tn(bc[:STATE], bc[STATE:])
        sum_s[...] = jnp.zeros_like(sum_s)

    @pl.when(step < groups)
    def _():
        here = chain_step(step, first, last, device, local_ref, passed_ref, *chain)
        state_ref[...] = here
        cum, cum_col = cum_ref[...], cum_col_ref[0]
        c_t = half(jax.nn.silu(bc_ref[STATE:, :]))
        x = jax.nn.silu(pre_ref[...])
        scaled = half(x * spread_rows(dt_ref[...]))
        reach = jnp.exp(cum) * flags_ref[0:1, :]
        y_ref[...] = mul_nn(here, c_t) * spread_rows(reach) + x * spread_rows(skip_ref[...])
        for head in range(GROUP):
            rows = slice(head * HEAD, (head + 1) * HEAD)
            spread = cum[head : head + 1, :] - cum_col[:, head : head + 1] + mask_s[...]
            y_ref[rows, :] += mul_nn(scaled[rows], half(jnp.exp(spread) * inner_s[...]))
        u = y_ref[...] * jax.nn.silu(z_ref[...])
        u_s[step] = u
        sum_s[...] += jnp.sum(u * u, axis=0, keepdims=True)

    @pl.when(step >= groups)
    def _():
        scale = lax.rsqrt(sum_s[0:1, :] * (1.0 / DI) + 1e-05)
        gated_ref[...] = half(u_s[step - groups] * scale * gain_ref[:, 0:1])
        scale_ref[...] = jnp.broadcast_to(scale, scale_ref.shape)

    @pl.when(step == 2 * groups - 1)
    def _():
        chain_end(groups, last, device, *chain)


def mixer_forward(local, passed, pre, bc_pre, dt, cum, cum_col, skip, flags, seg_col, proj, gain_col, name_id):
    tokens, groups = dt.shape[1], HEADS // GROUP
    first = lambda i: (jnp.minimum(i, groups - 1), 0)
    second = lambda i: (jnp.maximum(i - groups, 0), 0)
    rows, wide = block((GROUP, tokens), first), block((WIDE, tokens), first)
    states = block((WIDE, STATE), first)
    square = pltpu.VMEM((tokens, tokens), jnp.float32)
    return call_steps(
        forward_kernel, 2 * groups,
        (local, passed, pre, bc_pre, dt, cum, cum_col, skip, flags, seg_col, proj, gain_col),
        [states, block((WIDE, 8), first), wide, whole(bc_pre), rows, rows,
         block((1, tokens, GROUP), lambda i: (jnp.minimum(i, groups - 1), 0, 0)), rows, whole(flags),
         whole(seg_col), wide, block((WIDE, 8), second)],
        [f32_out(DI, tokens), bf16_out(DI, STATE), bf16_out(DI, tokens), f32_out(8, tokens)],
        [wide, states, block((WIDE, tokens), second), block((8, tokens), lambda i: (0, 0))],
        (square, square, pltpu.VMEM((groups, WIDE, tokens), jnp.float32), pltpu.VMEM((8, tokens), jnp.float32))
        + chain_room(groups),
        name_id=name_id,
    )


BOTH = ("dp", "ctx")


def nothing(value):
    first = value[(0,) * value.ndim].astype(jnp.float32)
    return jnp.minimum(jnp.abs(first), 0.0)


def no_step(value):
    return nothing(value).astype(jnp.int32)


def two_parts(value):
    high = value.astype(jnp.bfloat16)
    low = (value - high.astype(jnp.float32)).astype(jnp.bfloat16)
    return high, low


def route_table(routes, expert_count):
    named = jnp.any(
        routes[:, :, None] == jnp.arange(expert_count, dtype=jnp.int32), axis=1
    )
    rows = routes.shape[0]
    earlier = jnp.tril(jnp.ones((rows, rows), jnp.bfloat16), -1)
    ranks = jnp.dot(earlier, named.astype(jnp.bfloat16), preferred_element_type=jnp.float32)
    return named, jnp.where(named, ranks, -1.0)


def swap(value, bits):
    count = lax.axis_size("ctx")
    return lax.ppermute(value, "ctx", [(source, source ^ bits) for source in range(count)])


def held_experts(shard, other):
    held = EXP_DEV // 2
    half_at = lax.div(lax.axis_index("ctx"), 2)
    return lax.dynamic_slice_in_dim(shard, held * (1 - half_at if other else half_at), held, 0)


STRIP = 64


def quarter(axis, width, bits, start):
    def at(z):
        first = flipped(z, bits) * width
        if axis == 1:
            return (slice(None), pl.ds(pl.multiple_of(first + start, STRIP), STRIP))
        return (slice(None), pl.ds(start, STRIP), pl.ds(pl.multiple_of(first, 128), width))

    return at


def strip(start, *lead):
    return lambda z: lead + (slice(None), pl.ds(start, STRIP))


def strips(rows):
    return range(0, rows, STRIP)


def with_quarter(whole, own, axis):
    place = lax.axis_index("ctx") * own.shape[axis]
    return lax.dynamic_update_slice_in_dim(whole, own, place, axis)


def own_quarter(whole, axis, bits):
    width = whole.shape[axis] // 4
    return lax.dynamic_slice_in_dim(whole, flipped(lax.axis_index("ctx"), bits) * width, width, axis)


def expert_owners(near, far):
    far = far.astype(jnp.float32)
    low = lax.div(lax.axis_index("ctx"), 2) == 0
    return jnp.concatenate([jnp.where(low, near, far), jnp.where(low, far, near)], axis=0)


TILE = 4


def experts_kernel(
    rank_ref, gate_ref, rows_ref, grads_ref, first_ref, down_ref,
    routed_ref, back_ref, dgate_ref, grad_first_ref, grad_down_ref,
    x_s, g_s, sum_first_s, sum_down_s, ready_s, sem,
):
    tile, expert = pl.program_id(0), pl.program_id(1)
    last = pl.num_programs(0) - 1
    hidden = down_ref.shape[1]
    slots = x_s.shape[0] // TILE
    tokens = rank_ref.shape[2]
    chosen, gates = [], []
    number = lax.broadcasted_iota(jnp.int32, (slots, tokens), 0).astype(jnp.float32)
    for at in range(TILE):
        rows = pl.ds(at * slots, slots)
        own = rank_ref[at, pl.ds(expert, 1), :] == number
        chosen.append(own)
        gates.append(jnp.sum(jnp.where(own, gate_ref[at, pl.ds(expert, 1), :], 0.0), axis=1, keepdims=True))
        picker = half(own.astype(jnp.float32))
        x_s[rows, :] = half(mul_nn(picker, rows_ref[at]))
        g_s[rows, :] = half(mul_nn(picker, grads_ref[at]))
    gate = jnp.concatenate(gates, axis=0)
    x, grad = x_s[...], g_s[...].astype(jnp.float32)
    both = mul_nn(x, first_ref[0])
    hg, hu = both[:, :hidden], both[:, hidden:]
    squashed = jax.nn.sigmoid(hg)
    act = half(hg * squashed * hu)
    out = half(mul_nn(act, down_ref[0]))
    out_f = out.astype(jnp.float32)
    dgate = jnp.sum(grad * out_f, axis=1, keepdims=True)
    routed = half(gate * out_f)
    grad_out = half(gate * grad)
    grad_act = mul_nt(grad_out, down_ref[0])
    grad_hg = half(grad_act * hu * (squashed * (1.0 + hg * (1.0 - squashed))))
    grad_hu = half(grad_act * hg * squashed)
    grad_both = jnp.concatenate([grad_hg, grad_hu], axis=1)
    back = half(mul_nt(grad_both, first_ref[0]))

    @pl.when(tile == 0)
    def _():
        sum_first_s[expert] = jnp.zeros(sum_first_s.shape[1:], jnp.float32)
        sum_down_s[expert] = jnp.zeros(sum_down_s.shape[1:], jnp.float32)

    @pl.loop(0, x_s.shape[1] // 256)
    def _(at):
        some = pl.ds(pl.multiple_of(at * 256, 256), 256)
        sum_first_s[expert, some, :] += mul_tn(x_s[:, some], grad_both)

    sum_down_s[expert] += mul_tn(act, grad_out)
    for at in range(TILE):
        rows = slice(at * slots, (at + 1) * slots)
        picker = half(chosen[at].astype(jnp.float32))
        routed_part, back_part = half(mul_tn(picker, routed[rows])), half(mul_tn(picker, back[rows]))

        @pl.when(expert == 0)
        def _():
            routed_ref[at] = routed_part
            back_ref[at] = back_part

        @pl.when(expert > 0)
        def _():
            routed_ref[at] = routed_ref[at] + routed_part
            back_ref[at] = back_ref[at] + back_part

        dgate_ref[at, pl.ds(expert, 1), :] = jnp.sum(
            jnp.where(chosen[at], dgate[rows], 0.0), axis=0, keepdims=True
        )

    @pl.when(tile == last)
    def _():
        height = ready_s.shape[0]
        for sums, target in ((sum_first_s, grad_first_ref), (sum_down_s, grad_down_ref)):
            width = sums.shape[2]
            for at in range(sums.shape[1] // height):
                some = pl.ds(at * height, height)
                ready_s[:, :width] = half(sums[expert, some, :])
                copy = pltpu.make_async_copy(
                    ready_s.at[:, pl.ds(0, width)], target.at[expert, some, :], sem
                )
                copy.start()
                copy.wait()


def routed_experts(rank, gate, rows, grads, first, down, slots):
    blocks, held, tokens = rank.shape
    features, hidden = first.shape[1], down.shape[1]
    some = lambda t, e: (t, 0, 0)
    table = pl.BlockSpec((TILE, held, tokens), some)
    wide = pl.BlockSpec((TILE, tokens, features), some)
    once = pl.BlockSpec((TILE, tokens, features), some, pipeline_mode=pl.Buffered(1))
    anywhere = pl.BlockSpec(memory_space=pl.ANY)
    return pl.pallas_call(
        experts_kernel,
        grid=(blocks // TILE, held),
        in_specs=[
            table,
            table,
            once,
            once,
            pl.BlockSpec((1, features, 2 * hidden), lambda t, e: (e, 0, 0)),
            pl.BlockSpec((1, hidden, features), lambda t, e: (e, 0, 0)),
        ],
        out_specs=[wide, wide, table, anywhere, anywhere],
        out_shape=[
            bf16_out(blocks, tokens, features),
            bf16_out(blocks, tokens, features),
            f32_out(blocks, held, tokens),
            bf16_out(held, features, 2 * hidden),
            bf16_out(held, hidden, features),
        ],
        scratch_shapes=[
            pltpu.VMEM((TILE * slots, features), jnp.bfloat16),
            pltpu.VMEM((TILE * slots, features), jnp.bfloat16),
            pltpu.VMEM((held, features, 2 * hidden), jnp.float32),
            pltpu.VMEM((held, hidden, features), jnp.float32),
            pltpu.VMEM((256, features), jnp.bfloat16),
            pltpu.SemaphoreType.DMA,
        ],
        cost_estimate=BRIEF,
        compiler_params=pltpu.CompilerParams(
            vmem_limit_bytes=62 * 1024 * 1024, dimension_semantics=("arbitrary", "arbitrary")
        ),
    )(rank, gate, rows, grads, first, down)


def on_device(
    layer_in,
    seg_ids,
    route_ids,
    out_grad,
    norm_in,
    w_in,
    conv_w,
    conv_b,
    dt_bias,
    a_log,
    d_skip,
    norm_gate,
    w_out,
    norm_mid,
    w_router,
    w_sgate,
    w_sup,
    w_sdown,
    e_gate,
    e_up,
    e_down,
):
    f32, bf16 = jnp.float32, jnp.bfloat16
    row_count, d_model = layer_in.shape[1:]
    devices = lax.axis_size("dp") * lax.axis_size("ctx")
    ctx_place = lax.axis_index("ctx")
    held = EXP_DEV // 2
    first_expert = lax.axis_index("dp") * EXP_DEV + lax.div(ctx_place, 2) * held
    blocks = lax.axis_size("dp") * 2
    expert_count = EXP_DEV * lax.axis_size("dp")
    capacity = row_count * TOP * 5 // (expert_count * 4)
    slots = -(-capacity // 64) * 64
    tap_count = conv_w.shape[0]
    halo = 8

    small_parts = (norm_in, conv_w, conv_b, norm_gate, norm_mid, w_router)
    small_flat = jnp.concatenate([part.reshape(-1) for part in small_parts])
    small_flat = jnp.pad(small_flat, (0, 4096 - small_flat.shape[0])).reshape(32, 128)
    edge_rows = layer_in[0, row_count - halo :].reshape(-1, 128)
    gate_up = jnp.concatenate([e_gate, e_up], axis=2)
    width, hidden = e_gate.shape[1:]
    first_strips, down_strips = strips(width), strips(hidden)
    w_in_all, w_out_all, shared_all, sdown_all, small_all, expert_first, expert_down = pallas_gather(
        [
            w_in,
            w_out,
            jnp.concatenate([w_sgate, w_sup], axis=1),
            w_sdown,
            jnp.concatenate([small_flat, edge_rows]),
        ],
        [(16, 1664), (16, 1536), (16, 1024), (16, 1536), (128, 128)],
        1,
        ahead=3,
        more=[held_experts(gate_up, True), held_experts(e_down, True)],
        more_shapes=[(held, d_model, 2 * hidden), (held, hidden, d_model)],
        moves=[
            (part, part, strip(start), quarter(axis, width, 0, start), 2)
            for part, axis, starts in ((0, 1, first_strips), (1, 2, down_strips))
            for start in starts
        ],
    )
    expert_first = with_quarter(expert_first, held_experts(gate_up, False), 1)
    expert_down = with_quarter(expert_down, held_experts(e_down, False), 2)
    edge_all = small_all[:, small_flat.shape[0] :].reshape(devices, halo, d_model)
    small_all = small_all[:, : small_flat.shape[0]].reshape(devices, 4096)
    taken, pieces = 0, []
    for part in small_parts:
        pieces.append(small_all[:, taken : taken + part.size])
        taken += part.size
    gain_in = pieces[0].reshape(-1).astype(f32)
    conv_weight = jnp.moveaxis(pieces[1].reshape(devices, tap_count, -1), 0, 1).reshape(tap_count, CONV).astype(f32)
    conv_bias = pieces[2].reshape(-1).astype(f32)
    gain_gate = pieces[3].reshape(-1).astype(f32)
    gain_mid = pieces[4].reshape(-1).astype(f32)
    router_weight = pieces[5].reshape(d_model, expert_count)
    weight_in = w_in_all.reshape(d_model, PROJ)
    weight_out = w_out_all.reshape(DI, d_model)
    shared_weight = shared_all.reshape(d_model, -1)
    sdown_weight = sdown_all.reshape(-1, d_model)
    named, ranks = route_table(route_ids[0], expert_count)

    own_in = layer_in[0]
    place = lax.axis_index("dp") * lax.axis_size("ctx") + ctx_place
    edge_in = lax.dynamic_index_in_dim(edge_all, jnp.maximum(place - 1, 0), 0, keepdims=False)
    edge_in = jnp.where(ctx_place > 0, edge_in, jnp.zeros_like(edge_in))
    input_f = jnp.concatenate(
        [own_in, jnp.zeros((128 - halo, d_model), bf16), edge_in], axis=0
    ).astype(f32)
    normed = scaled_norm(input_f, gain_in).astype(bf16)
    projected = lax.dot_general(
        weight_in, normed, (((0,), (1,)), ((), ())), preferred_element_type=f32
    )
    seg_pad = jnp.concatenate([jnp.full((tap_count - 1,), -1, jnp.int32), seg_ids[0]])
    seg_window = lax.dynamic_slice_in_dim(
        seg_pad, ctx_place * row_count, row_count + tap_count - 1, 0
    )
    taps = jnp.concatenate(
        [conv_weight.T, conv_bias[:, None], jnp.zeros((CONV, 7 - tap_count), f32)], axis=1
    )
    dt_raw = projected[DI + CONV :, :row_count]
    dt_pos, decay, cumul, cumul_col, flags, seg_col, masks, through, skip_rows = mixer_rows(
        dt_raw, dt_bias, a_log, d_skip, seg_window, tap_count
    )
    bc_pre, pre, state_out = mixer_forward_states(projected, taps, masks, dt_pos, cumul, flags)
    passed = jnp.broadcast_to(jnp.repeat(through, HEAD)[:, None], (DI, 8))
    gain_col = jnp.broadcast_to(gain_gate[:, None], (DI, 8))
    y_heads, state_in, gated, gate_scale = mixer_forward(
        state_out, passed, pre, bc_pre, dt_pos, cumul, cumul_col, skip_rows, flags, seg_col, projected, gain_col, 7
    )

    mixed = times_rows(gated, weight_out)
    resid_mid = own_in.astype(f32) + mixed
    normed_mid_f, pull_mid = jax.vjp(scaled_norm, resid_mid, gain_mid)
    normed_mid = normed_mid_f.astype(bf16)
    logits = jnp.dot(normed_mid, router_weight, preferred_element_type=f32)
    top_logit = jnp.max(jnp.where(named, logits, -jnp.inf), axis=-1, keepdims=True)
    powers = jnp.where(named, jnp.exp(jnp.where(named, logits - top_logit, 0.0)), 0.0)
    gates = powers / jnp.sum(powers, axis=-1, keepdims=True)
    gate_high, gate_low = two_parts(gates)
    side = jnp.concatenate(
        [gate_high, gate_low, ranks.astype(bf16), jnp.zeros((row_count, 128 - 3 * expert_count), bf16)],
        axis=1,
    )
    token_rows, grad_rows, side_all, expert_first, expert_down = pallas_gather(
        [normed_mid, out_grad[0], side],
        [(16, 1536), (16, 1536), (128, 128)],
        3,
        line=(2,),
        ahead=4,
        more=[expert_first, expert_down],
        moves=[
            (part, part, quarter(axis, width, 2 * far, start), quarter(axis, width, 2 * far, start), 1)
            for far in (0, 1)
            for part, axis, starts in ((0, 1, first_strips), (1, 2, down_strips))
            for start in starts
        ],
    )
    shared_hidden = jnp.dot(normed_mid, shared_weight, preferred_element_type=f32)
    shared_gate, shared_up = jnp.split(shared_hidden, 2, axis=1)
    shared_act = (jax.nn.silu(shared_gate) * shared_up).astype(bf16)
    shared_out = jnp.dot(shared_act, sdown_weight, preferred_element_type=f32)

    def owned(grad):
        return grad.astype(bf16).reshape(devices, -1, grad.shape[-1])

    mine_of = partial(lax.dynamic_slice_in_dim, slice_size=held, axis=2)
    my_gate = mine_of(side_all, first_expert).astype(f32) + mine_of(
        side_all, first_expert + expert_count
    ).astype(f32)
    my_rank = mine_of(side_all, first_expert + 2 * expert_count).astype(f32)
    my_gate, my_rank = jnp.swapaxes(my_gate, 1, 2), jnp.swapaxes(my_rank, 1, 2)
    routed_rows, grad_slot_rows, token_dgate, grad_first, grad_down = routed_experts(
        my_rank, my_gate, token_rows, grad_rows, expert_first, expert_down, slots
    )
    experts = jnp.arange(held, dtype=jnp.int32)[:, None] + first_expert
    dgate_table = jnp.sum(
        token_dgate[..., None] * (jnp.arange(expert_count) == experts).astype(f32)[:, None, :], axis=1
    )
    dgate_high, dgate_low = two_parts(dgate_table)
    back_side = jnp.concatenate(
        [dgate_high, dgate_low, jnp.zeros((blocks, row_count, 128 - 2 * expert_count), bf16)], axis=-1
    )
    grad_shared_out = out_grad[0]
    grad_w_sdown = times_rows(shared_act, grad_shared_out)
    back_rows, routed, back_side, sum_sdown, beside_first, beside_down = pallas_reduce(
        [grad_slot_rows, routed_rows, back_side, owned(grad_w_sdown)],
        [(16, 1536), (16, 1536), (128, 128), (16, 1536)],
        4,
        lines=[(2,), (2,), (2,), (1, 2, 3)],
        more=[grad_first, grad_down],
        more_shapes=[(2, held, width, 2 * hidden), (2, held, hidden, width)],
        moves=[
            (part, part, quarter(axis, width, 2 * far + 1, start), strip(start, far), 1)
            for far in (1, 0)
            for part, axis, starts in ((0, 1, first_strips), (1, 2, down_strips))
            for start in starts
        ],
    )
    far_first, far_down = (
        half(own_quarter(whole, axis, 2).astype(f32) + beside[1].astype(f32))
        for whole, beside, axis in ((grad_first, beside_first, 1), (grad_down, beside_down, 2))
    )
    near_first, near_down = (
        own_quarter(whole, axis, 0).astype(f32) + beside[0].astype(f32)
        for whole, beside, axis in ((grad_first, beside_first, 1), (grad_down, beside_down, 2))
    )

    grad_top = out_grad[0].astype(f32)
    grad_shared_act = times_back(grad_shared_out, sdown_weight)
    grad_sgate = (grad_shared_act * shared_up * silu_slope(shared_gate)).astype(bf16)
    grad_sup = (grad_shared_act * jax.nn.silu(shared_gate)).astype(bf16)
    grad_shared = jnp.concatenate([grad_sgate, grad_sup], axis=1)
    grad_w_shared = times_rows(normed_mid, grad_shared)
    grad_mid_shared = times_back(grad_shared, shared_weight)
    grad_gates = back_side[:, :expert_count] + back_side[:, expert_count : 2 * expert_count]
    grad_pick = gates * (grad_gates - jnp.sum(gates * grad_gates, axis=-1, keepdims=True))
    grad_logits = grad_pick.astype(bf16)
    grad_w_router = times_rows(normed_mid, grad_logits)
    grad_mid = (
        back_rows + grad_mid_shared + times_back(grad_logits, router_weight)
    )
    grad_resid_part, grad_gain_mid = pull_mid(grad_mid)
    grad_resid = grad_top + grad_resid_part
    grad_mixed = grad_resid.astype(bf16)

    grad_w_out = jnp.dot(gated, grad_mixed, preferred_element_type=f32)
    grad_gated = times_back(weight_out, grad_mixed)
    scaled_u = y_heads * jax.nn.silu(projected[:DI, :row_count])
    scale_row = gate_scale[:1]
    along = jnp.sum(grad_gated * gain_gate[:, None] * scaled_u, axis=0, keepdims=True)
    grad_gain_gate = jnp.sum(grad_gated * scaled_u * scale_row, axis=1)
    gate_rows = jnp.concatenate(
        [scale_row, scale_row * scale_row * scale_row * along * (1.0 / DI), jnp.zeros((6, row_count), f32)]
    )
    grad_y, grad_z, grad_state_local = mixer_back_gate(
        y_heads, projected, grad_gated, gain_col, gate_rows, bc_pre, cumul, flags
    )
    grad_scaled, grad_state_out, grad_cum_inner, grad_skip, grad_bc_inner = mixer_back_inner(
        grad_state_local, passed, pre, grad_y, bc_pre, dt_pos, cumul, cumul_col, flags, seg_col, 8
    )
    grad_x, grad_taps_x, grad_dt, grad_cum_join, grad_last, grad_bc_join = mixer_back_join(
        grad_scaled, grad_y, pre, projected, taps, masks, state_in, grad_state_out,
        bc_pre, dt_pos, cumul, skip_rows, flags,
    )
    grad_bc, grad_taps_bc = mixer_back_conv(
        grad_bc_inner + grad_bc_join, bc_pre, projected, taps, masks
    )
    grad_cum = grad_cum_inner + grad_cum_join
    grad_last = grad_last[:, 0] + through * grad_last[:, 1]
    lower = jnp.tril(jnp.ones((row_count, row_count), f32))
    grad_decay = jnp.dot(grad_cum, lower, precision=lax.Precision.HIGHEST) + grad_last[:, None]
    grad_dt = grad_dt - jnp.exp(a_log)[:, None] * grad_decay
    grad_raw = grad_dt * jax.nn.sigmoid(dt_raw + dt_bias[:, None])
    grad_taps = jnp.concatenate([grad_taps_x, grad_taps_bc])
    grad_conv_w, grad_conv_b = grad_taps[:, :tap_count].T, grad_taps[:, tap_count]
    head_sums_all = jnp.concatenate(
        [jnp.sum(grad_raw, axis=1), jnp.sum(decay * grad_decay, axis=1), jnp.sum(grad_skip, axis=1)]
    )
    grad_proj = jnp.concatenate(
        [
            jnp.pad(grad_z, ((0, 0), (0, 128))),
            grad_x,
            grad_bc,
            jnp.pad(grad_raw.astype(bf16), ((0, 0), (0, 128))),
        ]
    )
    normed_t = normed.T
    grad_w_in, grad_normed = proj_back(normed_t, weight_in, grad_proj)
    grad_normed = grad_normed.T
    edge_grad = from_behind(grad_normed[row_count + 128 - halo :], "ctx", -1)
    grad_normed = jnp.concatenate(
        [grad_normed[: row_count - halo], grad_normed[row_count - halo : row_count] + edge_grad],
        axis=0,
    )
    _, pull_in = jax.vjp(scaled_norm, own_in.astype(f32), gain_in)
    grad_input_part, grad_gain_in = pull_in(grad_normed)
    grad_in = (grad_resid + grad_input_part)[None]

    small_grads = jnp.concatenate(
        [
            grad_gain_in.reshape(devices, -1),
            jnp.moveaxis(grad_conv_w.reshape(tap_count, devices, -1), 1, 0).reshape(devices, -1),
            grad_conv_b.reshape(devices, -1),
            grad_gain_gate.reshape(devices, -1),
            grad_gain_mid.reshape(devices, -1),
            grad_w_router.reshape(devices, -1),
            jnp.broadcast_to(head_sums_all, (devices, 3 * HEADS)),
        ],
        axis=1,
    )
    small_grads = jnp.pad(small_grads, ((0, 0), (0, 3072 - small_grads.shape[1])))
    sum_in, sum_out, sum_shared, sum_small, far_first, far_down = pallas_reduce(
        [owned(grad_w_in), owned(grad_w_out), owned(grad_w_shared), small_grads.reshape(devices, 24, 128)],
        [(16, 1664), (16, 1536), (16, 1024), (24, 128)],
        6,
        ahead=3,
        more=[far_first, far_down],
        more_shapes=[far_first.shape, far_down.shape],
        moves=[
            (part, part, strip(start), strip(start), 2)
            for part, starts in ((0, first_strips), (1, down_strips))
            for start in starts
        ],
    )
    layer_out = (resid_mid + shared_out + routed).astype(bf16)[None]
    sum_sgate, sum_sup = jnp.split(sum_shared, 2, axis=1)
    grad_e_gate = expert_owners(near_first[..., :hidden], far_first[..., :hidden])
    grad_e_up = expert_owners(near_first[..., hidden:], far_first[..., hidden:])
    grad_e_down = expert_owners(near_down, far_down)
    sum_small = sum_small.reshape(-1)
    taken, mine = 0, []
    for part in small_parts:
        mine.append(sum_small[taken : taken + part.size].reshape(part.shape))
        taken += part.size
    return (
        layer_out,
        grad_in,
        mine[0],
        sum_in,
        mine[1],
        mine[2],
        sum_small[taken : taken + HEADS],
        sum_small[taken + HEADS : taken + 2 * HEADS],
        sum_small[taken + 2 * HEADS : taken + 3 * HEADS],
        mine[3],
        sum_out,
        mine[4],
        mine[5],
        sum_sgate,
        sum_sup,
        sum_sdown,
        grad_e_gate,
        grad_e_up,
        grad_e_down,
    )


def solution(mesh):
    in_specs = (
        P("dp", "ctx", None),
        P("dp", None),
        P("dp", "ctx", None),
        P("dp", "ctx", None),
        P(("dp", "ctx")),
        P(("dp", "ctx"), None),
        P(None, ("dp", "ctx")),
        P(("dp", "ctx")),
        P(),
        P(),
        P(),
        P(("dp", "ctx")),
        P(("dp", "ctx"), None),
        P(("dp", "ctx")),
        P(("dp", "ctx"), None),
        P(("dp", "ctx"), None),
        P(("dp", "ctx"), None),
        P(("dp", "ctx"), None),
        P("dp", "ctx", None),
        P("dp", "ctx", None),
        P("dp", None, "ctx"),
    )
    out_specs = (
        P("dp", "ctx", None),
        P("dp", "ctx", None),
        P(("dp", "ctx")),
        P(("dp", "ctx"), None),
        P(None, ("dp", "ctx")),
        P(("dp", "ctx")),
        P(),
        P(),
        P(),
        P(("dp", "ctx")),
        P(("dp", "ctx"), None),
        P(("dp", "ctx")),
        P(("dp", "ctx"), None),
        P(("dp", "ctx"), None),
        P(("dp", "ctx"), None),
        P(("dp", "ctx"), None),
        P("dp", "ctx", None),
        P("dp", "ctx", None),
        P("dp", None, "ctx"),
    )
    one_each = mesh.shape["ctx"] == EXP_DEV and mesh.shape["dp"] == 8
    return jax.shard_map(
        on_device if one_each else on_device_general, mesh=mesh, in_specs=in_specs, out_specs=out_specs, check_vma=False
    )
```

```python
from functools import partial

import jax
import jax.numpy as jnp
from jax import lax
from jax.experimental import pallas as pl
from jax.experimental.layout import Layout, with_layout_constraint
from jax.experimental.pallas import tpu as pltpu
from jax.sharding import PartitionSpec as P

HEADS = 48
HEAD = 64
STATE = 128
TOP = 6
EXP_DEV = 4
DI = 3072
CONV = 3328
PROJ = 6448


def from_behind(value, axis, steps):
    count = lax.axis_size(axis)
    leading, last = (max(0, -steps), min(count, count - steps))
    return lax.ppermute(value, axis, [(source, source + steps) for source in range(leading, last)])


def carried_in_2(x, axis, combine, identity):
    count, mine = (lax.axis_size(axis), lax.axis_index(axis))
    everything = jax.tree.map(
        lambda part, kind: lax.all_gather(part.astype(kind), axis), x, (jnp.bfloat16, jnp.bfloat16)
    )
    start = jax.tree.map(
        lambda part, zero: jnp.broadcast_to(jnp.asarray(zero, part.dtype), part.shape), x, identity
    )

    def lap(k, before):
        reached = k < mine
        new = combine(
            before, jax.tree.map(lambda part, own: part[k].astype(own.dtype), everything, x)
        )
        return jax.tree.map(lambda a, b: jnp.where(reached, a, b), new, before)

    return lax.fori_loop(0, count, lap, start)


def carried_in_3(x, axis, combine, identity):
    count, mine = (lax.axis_size(axis), lax.axis_index(axis))
    everything = jax.tree.map(
        lambda part, kind: lax.all_gather(part.astype(kind), axis),
        x,
        jax.tree.map(lambda a: jnp.bfloat16 if a.dtype == jnp.float32 else a.dtype, x),
    )
    start = jax.tree.map(
        lambda part, zero: jnp.broadcast_to(jnp.asarray(zero, part.dtype), part.shape), x, identity
    )

    def lap(k, before):
        at = count - 1 - k
        reached = at > mine
        new = combine(
            before, jax.tree.map(lambda part, own: part[at].astype(own.dtype), everything, x)
        )
        return jax.tree.map(lambda a, b: jnp.where(reached, a, b), new, before)

    return lax.fori_loop(0, count, lap, start)


def for_sending(x):
    return jax.tree.map(lambda a: a.astype(jnp.bfloat16) if a.dtype == jnp.float32 else a, x)


def normalize(value):
    return value * lax.rsqrt(jnp.mean(value * value, axis=-1, keepdims=True) + 1e-05)


def scaled_norm(value, gain):
    return normalize(value) * gain


def gate_norm(y_heads, z_part, gain):
    joined = y_heads.reshape(z_part.shape) * jax.nn.silu(z_part)
    return normalize(joined) * gain


def silu_slope(value):
    squashed = jax.nn.sigmoid(value)
    return squashed * (1.0 + value * (1.0 - squashed))


def conv_apply(padded, weight, bias, seg_pad):
    tap_count = weight.shape[0]
    length = padded.shape[1] - tap_count + 1
    current = seg_pad[:, tap_count - 1 :]
    summed = bias + jnp.zeros(padded[:, tap_count - 1 :].shape, jnp.float32)
    for offset in range(tap_count):
        matches = (seg_pad[:, offset : offset + length] == current).astype(jnp.float32)
        summed = summed + weight[offset] * padded[:, offset : offset + length] * matches[..., None]
    return jax.nn.silu(summed)


def split_blocks(value, count):
    shaped = value.reshape((value.shape[0], count, value.shape[1] // count) + value.shape[2:])
    return jnp.moveaxis(shaped, 1, 0)


def block_step(carried_in, pieces):
    memory, previous = carried_in
    x_heads, b_mat, c_mat, dt_pos, decay, segment_ids = pieces
    cumul = jnp.cumsum(decay, axis=1)
    places = jnp.arange(segment_ids.shape[1])
    causal = places[:, None] >= places[None, :]
    linked = ((segment_ids[:, :, None] == segment_ids[:, None, :]) & causal[None])[..., None]
    spread = cumul[:, :, None, :] - cumul[:, None, :, :]
    weights = jnp.where(linked, jnp.exp(jnp.where(linked, spread, 0.0)), 0.0)
    inner = jnp.einsum("gtn,gsn->gts", c_mat, b_mat, precision=lax.Precision.HIGHEST)
    weights = weights * inner[..., None] * dt_pos[:, None, :, :]
    output = jnp.einsum("gtsh,gshp->gthp", weights, x_heads, precision=lax.Precision.HIGHEST)
    keeps = (segment_ids == previous[:, None]).astype(jnp.float32)
    reach = jnp.exp(cumul) * keeps[..., None]
    output = (
        output
        + jnp.einsum("gtn,ghpn->gthp", c_mat, memory, precision=lax.Precision.HIGHEST)
        * reach[..., None]
    )
    latest = segment_ids[:, -1]
    tails = (
        jnp.exp(cumul[:, -1:, :] - cumul)
        * (segment_ids == latest[:, None]).astype(jnp.float32)[..., None]
        * dt_pos
    )
    through = jnp.exp(cumul[:, -1, :]) * (latest == previous).astype(jnp.float32)[:, None]
    memory = memory * through[..., None, None] + jnp.einsum(
        "gsh,gshp,gsn->ghpn", tails, x_heads, b_mat, precision=lax.Precision.HIGHEST
    )
    return ((memory, latest), output)


def scan_blocks(x_heads, b_mat, c_mat, dt_pos, decay, segment_ids, memory, previous):
    length = segment_ids.shape[1]
    count = length // min(128, length)
    inputs = tuple(
        (
            split_blocks(value, count)
            for value in (x_heads, b_mat, c_mat, dt_pos, decay, segment_ids)
        )
    )
    (memory, latest), outputs = lax.scan(jax.checkpoint(block_step), (memory, previous), inputs)
    return (jnp.moveaxis(outputs, 0, 1).reshape(x_heads.shape), memory)


def part_local(x_heads, b_mat, c_mat, dt_raw, dt_bias, a_log, d_skip, segment_ids, previous):
    dt_pos = jax.nn.softplus(dt_raw + dt_bias)
    decay = -jnp.exp(a_log) * dt_pos
    zero_state = jnp.zeros((x_heads.shape[0], HEADS, HEAD, STATE), jnp.float32)
    mixed_heads, final_state = scan_blocks(
        x_heads, b_mat, c_mat, dt_pos, decay, segment_ids, zero_state, previous
    )
    y_local = mixed_heads + d_skip[:, None] * x_heads
    through = (
        jnp.exp(jnp.sum(decay, axis=1))
        * (segment_ids[:, -1] == previous).astype(jnp.float32)[:, None]
    )
    return (y_local, final_state, through)


def part_carry(c_mat, dt_raw, dt_bias, a_log, state_in, segment_ids, previous):
    dt_pos = jax.nn.softplus(dt_raw + dt_bias)
    cumul = jnp.cumsum(-jnp.exp(a_log) * dt_pos, axis=1)
    keeps = (segment_ids == previous[:, None]).astype(jnp.float32)
    reach = jnp.exp(cumul) * keeps[..., None]
    return (
        jnp.einsum("gtn,ghpn->gthp", c_mat, state_in, precision=lax.Precision.HIGHEST)
        * reach[..., None]
    )


def carry_forward(earlier, later):
    return (earlier[0] * later[0], later[0][..., None, None] * earlier[1] + later[1])


def carry_backward(earlier, later):
    return (earlier[0] * later[0], later[1] + later[0][..., None, None] * earlier[1])


def route_slots(flat_routes, expert_count, capacity):
    blocks = flat_routes.shape[0]
    onehot = (flat_routes[..., None] == jnp.arange(expert_count, dtype=jnp.int32)).astype(jnp.int32)
    ranks = jnp.sum((jnp.cumsum(onehot, axis=1) - onehot) * onehot, axis=-1)
    spots = (
        flat_routes * (blocks * capacity)
        + jnp.arange(blocks, dtype=jnp.int32)[:, None] * capacity
        + ranks
    )
    return spots


def times_rows(left, right):
    return lax.dot_general(
        left, right, (((0,), (0,)), ((), ())), preferred_element_type=jnp.float32
    )


def times_back(left, right):
    return lax.dot_general(
        left, right, (((1,), (1,)), ((), ())), preferred_element_type=jnp.float32
    )


def on_device_general(
    layer_in,
    seg_ids,
    route_ids,
    out_grad,
    norm_in,
    w_in,
    conv_w,
    conv_b,
    dt_bias,
    a_log,
    d_skip,
    norm_gate,
    w_out,
    norm_mid,
    w_router,
    w_sgate,
    w_sup,
    w_sdown,
    e_gate,
    e_up,
    e_down,
):
    seq_count, row_count, d_model = layer_in.shape
    token_count = seq_count * row_count
    tap_count = conv_w.shape[0]
    ctx_place = lax.axis_index("ctx")
    expert_count = EXP_DEV * lax.axis_size("dp")
    capacity = row_count * TOP * 5 // (expert_count * 4)
    dense_set = (
        lax.all_gather(norm_in, ("dp", "ctx"), axis=0, tiled=True),
        lax.all_gather(w_in, ("dp", "ctx"), axis=0, tiled=True),
        lax.all_gather(conv_w, ("dp", "ctx"), axis=1, tiled=True),
        lax.all_gather(conv_b, ("dp", "ctx"), axis=0, tiled=True),
        lax.all_gather(norm_gate, ("dp", "ctx"), axis=0, tiled=True),
        lax.all_gather(w_out, ("dp", "ctx"), axis=0, tiled=True),
        lax.all_gather(norm_mid, ("dp", "ctx"), axis=0, tiled=True),
        lax.all_gather(w_router, ("dp", "ctx"), axis=0, tiled=True),
        lax.all_gather(w_sgate, ("dp", "ctx"), axis=0, tiled=True),
        lax.all_gather(w_sup, ("dp", "ctx"), axis=0, tiled=True),
        lax.all_gather(w_sdown, ("dp", "ctx"), axis=0, tiled=True),
    )
    (
        gain_in,
        weight_in,
        conv_weight,
        conv_bias,
        gain_gate,
        weight_out,
        gain_mid,
        router_weight,
        sgate_weight,
        sup_weight,
        sdown_weight,
    ) = dense_set
    expert_gate, expert_up, expert_down = (
        lax.all_gather(e_gate, "ctx", axis=1, tiled=True),
        lax.all_gather(e_up, "ctx", axis=1, tiled=True),
        lax.all_gather(e_down, "ctx", axis=2, tiled=True),
    )
    input_f = layer_in.astype(jnp.float32)
    normed_f, pull_in = jax.vjp(scaled_norm, input_f, gain_in.astype(jnp.float32))
    normed = normed_f.astype(jnp.bfloat16).reshape(token_count, d_model)
    projected = jnp.dot(normed, weight_in, preferred_element_type=jnp.float32).reshape(
        seq_count, row_count, PROJ
    )
    z_part = projected[..., :DI]
    xbc_part = projected[..., DI : DI + CONV]
    dt_raw = projected[..., DI + CONV :]
    edge_rows = from_behind(
        xbc_part[:, row_count - tap_count + 1 :, :].astype(jnp.bfloat16), "ctx", 1
    ).astype(jnp.float32)
    seg_pad = jnp.concatenate(
        [jnp.full((seq_count, tap_count - 1), -1, jnp.int32), seg_ids], axis=1
    )
    seg_window = lax.dynamic_slice_in_dim(
        seg_pad, ctx_place * row_count, row_count + tap_count - 1, 1
    )
    seg_now = seg_window[:, tap_count - 1 :]
    seg_before = seg_window[:, tap_count - 2]
    padded = jnp.concatenate([edge_rows, xbc_part], axis=1)
    conv_out, pull_conv = jax.vjp(
        partial(conv_apply, seg_pad=seg_window),
        padded,
        conv_weight.astype(jnp.float32),
        conv_bias.astype(jnp.float32),
    )
    x_heads = conv_out[..., :DI].reshape(seq_count, row_count, HEADS, HEAD)
    b_mat = conv_out[..., DI : DI + STATE]
    c_mat = conv_out[..., DI + STATE :]
    local_piece = partial(part_local, segment_ids=seg_now, previous=seg_before)
    (y_local, state_out, through), pull_local = jax.vjp(
        local_piece, x_heads, b_mat, c_mat, dt_raw, dt_bias, a_log, d_skip
    )
    carried = carried_in_2(
        (through, state_out),
        "ctx",
        carry_forward,
        (jnp.ones_like(through), jnp.zeros_like(state_out)),
    )
    state_in = carried[1]
    carry_piece = partial(part_carry, segment_ids=seg_now, previous=seg_before)
    y_carry, pull_carry = jax.vjp(carry_piece, c_mat, dt_raw, dt_bias, a_log, state_in)
    gated_f, pull_gate = jax.vjp(
        gate_norm, y_local + y_carry, z_part, gain_gate.astype(jnp.float32)
    )
    gated = gated_f.astype(jnp.bfloat16).reshape(token_count, DI)
    mixed = jnp.dot(gated, weight_out, preferred_element_type=jnp.float32)
    resid_mid = input_f.reshape(token_count, d_model) + mixed
    normed_mid_f, pull_mid = jax.vjp(scaled_norm, resid_mid, gain_mid.astype(jnp.float32))
    normed_mid = normed_mid_f.astype(jnp.bfloat16)
    logits = jnp.dot(normed_mid, router_weight, preferred_element_type=jnp.float32)
    route_flat = route_ids.reshape(token_count, TOP)
    gates = jax.nn.softmax(jnp.take_along_axis(logits, route_flat, axis=1), axis=-1)
    shared_gate = jnp.dot(normed_mid, sgate_weight, preferred_element_type=jnp.float32)
    shared_up = jnp.dot(normed_mid, sup_weight, preferred_element_type=jnp.float32)
    shared_act = (jax.nn.silu(shared_gate) * shared_up).astype(jnp.bfloat16)
    shared_out = jnp.dot(shared_act, sdown_weight, preferred_element_type=jnp.float32)
    slot_ids = route_slots(route_ids.reshape(seq_count, row_count * TOP), expert_count, capacity)
    assigned = jnp.arange(token_count * TOP, dtype=jnp.int32)
    owners = (
        jnp.full((expert_count * seq_count * capacity,), token_count * TOP, jnp.int32)
        .at[slot_ids.reshape(-1)]
        .set(assigned)
    )
    token_of = owners // TOP
    rows_pad = jnp.concatenate([normed_mid, jnp.zeros((1, d_model), jnp.bfloat16)], axis=0)
    outgoing = rows_pad[token_of].reshape(expert_count, seq_count * capacity, d_model)
    incoming = lax.all_to_all(outgoing, "dp", split_axis=0, concat_axis=1, tiled=True)
    hidden_gate = jnp.einsum(
        "erd,edf->erf", incoming, expert_gate, preferred_element_type=jnp.float32
    )
    hidden_up = jnp.einsum("erd,edf->erf", incoming, expert_up, preferred_element_type=jnp.float32)
    hidden_act = (jax.nn.silu(hidden_gate) * hidden_up).astype(jnp.bfloat16)
    expert_out = jnp.einsum(
        "erf,efd->erd", hidden_act, expert_down, preferred_element_type=jnp.float32
    ).astype(jnp.bfloat16)
    returned = lax.all_to_all(expert_out, "dp", split_axis=1, concat_axis=0, tiled=True)
    slot_flat = slot_ids.reshape(token_count, TOP)
    picked = returned.reshape(-1, d_model)[slot_flat]
    routed = jnp.sum(gates[..., None] * picked, axis=1)
    layer_out = (
        (resid_mid + shared_out + routed)
        .astype(jnp.bfloat16)
        .reshape(seq_count, row_count, d_model)
    )
    grad_top = out_grad.astype(jnp.float32).reshape(token_count, d_model)
    grad_gates = jnp.sum(picked * grad_top[:, None, :], axis=-1)
    grad_pick = gates * (grad_gates - jnp.sum(gates * grad_gates, axis=-1, keepdims=True))
    expert_ids = jnp.arange(expert_count, dtype=jnp.int32)
    grad_logits = jnp.sum(
        grad_pick[..., None] * (route_flat[..., None] == expert_ids).astype(jnp.float32), axis=1
    ).astype(jnp.bfloat16)
    gates_pad = jnp.concatenate([gates.reshape(-1), jnp.zeros((1,), jnp.float32)])
    grad_pad = jnp.concatenate([grad_top, jnp.zeros((1, d_model), jnp.float32)], axis=0)
    grad_slots = (
        (gates_pad[owners][:, None] * grad_pad[token_of])
        .astype(jnp.bfloat16)
        .reshape(expert_count, seq_count * capacity, d_model)
    )
    grad_arrived = lax.all_to_all(grad_slots, "dp", split_axis=0, concat_axis=1, tiled=True)
    grad_act = jnp.einsum(
        "erd,efd->erf", grad_arrived, expert_down, preferred_element_type=jnp.float32
    )
    grad_e_down = jnp.einsum(
        "erf,erd->efd", hidden_act, grad_arrived, preferred_element_type=jnp.float32
    )
    grad_hgate = (grad_act * hidden_up * silu_slope(hidden_gate)).astype(jnp.bfloat16)
    grad_hup = (grad_act * jax.nn.silu(hidden_gate)).astype(jnp.bfloat16)
    grad_e_gate = jnp.einsum(
        "erd,erf->edf", incoming, grad_hgate, preferred_element_type=jnp.float32
    )
    grad_e_up = jnp.einsum("erd,erf->edf", incoming, grad_hup, preferred_element_type=jnp.float32)
    grad_incoming = jnp.einsum(
        "erf,edf->erd", grad_hgate, expert_gate, preferred_element_type=jnp.float32
    )
    grad_incoming = (
        grad_incoming
        + jnp.einsum("erf,edf->erd", grad_hup, expert_up, preferred_element_type=jnp.float32)
    ).astype(jnp.bfloat16)
    grad_returned = lax.all_to_all(grad_incoming, "dp", split_axis=1, concat_axis=0, tiled=True)
    grad_routed = jnp.sum(grad_returned.reshape(-1, d_model)[slot_flat], axis=1, dtype=jnp.float32)
    dense_set = (
        lax.all_gather(norm_in, ("dp", "ctx"), axis=0, tiled=True),
        lax.all_gather(w_in, ("dp", "ctx"), axis=0, tiled=True),
        lax.all_gather(conv_w, ("dp", "ctx"), axis=1, tiled=True),
        lax.all_gather(conv_b, ("dp", "ctx"), axis=0, tiled=True),
        lax.all_gather(norm_gate, ("dp", "ctx"), axis=0, tiled=True),
        lax.all_gather(w_out, ("dp", "ctx"), axis=0, tiled=True),
        lax.all_gather(norm_mid, ("dp", "ctx"), axis=0, tiled=True),
        lax.all_gather(w_router, ("dp", "ctx"), axis=0, tiled=True),
        lax.all_gather(w_sgate, ("dp", "ctx"), axis=0, tiled=True),
        lax.all_gather(w_sup, ("dp", "ctx"), axis=0, tiled=True),
        lax.all_gather(w_sdown, ("dp", "ctx"), axis=0, tiled=True),
    )
    (
        gain_in,
        weight_in,
        conv_weight,
        conv_bias,
        gain_gate,
        weight_out,
        gain_mid,
        router_weight,
        sgate_weight,
        sup_weight,
        sdown_weight,
    ) = dense_set
    grad_w_router = times_rows(normed_mid, grad_logits)
    grad_shared_out = grad_top.astype(jnp.bfloat16)
    grad_w_sdown = times_rows(shared_act, grad_shared_out)
    grad_shared_act = times_back(grad_shared_out, sdown_weight)
    grad_sgate = (grad_shared_act * shared_up * silu_slope(shared_gate)).astype(jnp.bfloat16)
    grad_sup = (grad_shared_act * jax.nn.silu(shared_gate)).astype(jnp.bfloat16)
    grad_w_sgate = times_rows(normed_mid, grad_sgate)
    grad_w_sup = times_rows(normed_mid, grad_sup)
    grad_mid = (
        grad_routed
        + times_back(grad_logits, router_weight)
        + times_back(grad_sgate, sgate_weight)
        + times_back(grad_sup, sup_weight)
    )
    grad_resid_part, grad_gain_mid = pull_mid(grad_mid)
    grad_resid = grad_top + grad_resid_part
    grad_mixed = grad_resid.astype(jnp.bfloat16)
    grad_w_out = times_rows(gated, grad_mixed)
    grad_gated = times_back(grad_mixed, weight_out).reshape(seq_count, row_count, DI)
    grad_y, grad_z, grad_gain_gate = pull_gate(grad_gated)
    grad_cmat_carry, grad_dt_carry, grad_bias_carry, grad_alog_carry, grad_state_in = pull_carry(
        grad_y
    )
    back_scan = carried_in_3(
        (through, grad_state_in),
        "ctx",
        carry_backward,
        (jnp.ones_like(through), jnp.zeros_like(grad_state_in)),
    )
    grad_state_out = back_scan[1]
    grad_through = jnp.sum(state_in * grad_state_out, axis=(2, 3))
    (
        grad_xheads,
        grad_bmat,
        grad_cmat,
        grad_dt_local,
        grad_bias_local,
        grad_alog_local,
        grad_dskip,
    ) = pull_local((grad_y, grad_state_out, grad_through))
    grad_conv_out = jnp.concatenate(
        [grad_xheads.reshape(seq_count, row_count, DI), grad_bmat, grad_cmat + grad_cmat_carry],
        axis=-1,
    )
    grad_padded, grad_conv_w, grad_conv_b = pull_conv(grad_conv_out)
    edge_grad = from_behind(for_sending(grad_padded[:, : tap_count - 1, :]), "ctx", -1)
    grad_xbc = grad_padded[:, tap_count - 1 :, :]
    grad_xbc = jnp.concatenate(
        [
            grad_xbc[:, : row_count - tap_count + 1],
            grad_xbc[:, row_count - tap_count + 1 :] + edge_grad,
        ],
        axis=1,
    )
    grad_proj = (
        jnp.concatenate([grad_z, grad_xbc, grad_dt_local + grad_dt_carry], axis=-1)
        .astype(jnp.bfloat16)
        .reshape(token_count, PROJ)
    )
    grad_w_in = times_rows(normed, grad_proj)
    grad_normed = times_back(grad_proj, weight_in).reshape(seq_count, row_count, d_model)
    grad_input_part, grad_gain_in = pull_in(grad_normed)
    grad_in = grad_resid.reshape(seq_count, row_count, d_model) + grad_input_part
    dense_grads = (
        lax.psum_scatter(grad_gain_in, ("dp", "ctx"), scatter_dimension=0, tiled=True),
        lax.psum_scatter(grad_w_in, ("dp", "ctx"), scatter_dimension=0, tiled=True),
        lax.psum_scatter(grad_conv_w, ("dp", "ctx"), scatter_dimension=1, tiled=True),
        lax.psum_scatter(grad_conv_b, ("dp", "ctx"), scatter_dimension=0, tiled=True),
        lax.psum_scatter(grad_gain_gate, ("dp", "ctx"), scatter_dimension=0, tiled=True),
        lax.psum_scatter(grad_w_out, ("dp", "ctx"), scatter_dimension=0, tiled=True),
        lax.psum_scatter(grad_gain_mid, ("dp", "ctx"), scatter_dimension=0, tiled=True),
        lax.psum_scatter(grad_w_router, ("dp", "ctx"), scatter_dimension=0, tiled=True),
        lax.psum_scatter(grad_w_sgate, ("dp", "ctx"), scatter_dimension=0, tiled=True),
        lax.psum_scatter(grad_w_sup, ("dp", "ctx"), scatter_dimension=0, tiled=True),
        lax.psum_scatter(grad_w_sdown, ("dp", "ctx"), scatter_dimension=0, tiled=True),
    )
    expert_grads = (
        lax.psum_scatter(
            grad_e_gate.astype(jnp.bfloat16), "ctx", scatter_dimension=1, tiled=True
        ).astype(jnp.float32),
        lax.psum_scatter(
            grad_e_up.astype(jnp.bfloat16), "ctx", scatter_dimension=1, tiled=True
        ).astype(jnp.float32),
        lax.psum_scatter(
            grad_e_down.astype(jnp.bfloat16), "ctx", scatter_dimension=2, tiled=True
        ).astype(jnp.float32),
    )
    head_grads = lax.psum(
        (grad_bias_local + grad_bias_carry, grad_alog_local + grad_alog_carry, grad_dskip),
        ("dp", "ctx"),
    )
    return (
        layer_out,
        grad_in,
        dense_grads[0],
        dense_grads[1],
        dense_grads[2],
        dense_grads[3],
        head_grads[0],
        head_grads[1],
        head_grads[2],
        dense_grads[4],
        dense_grads[5],
        dense_grads[6],
        dense_grads[7],
        dense_grads[8],
        dense_grads[9],
        dense_grads[10],
        expert_grads[0],
        expert_grads[1],
        expert_grads[2],
    )


GROUP = 8
WIDE = GROUP * HEAD
VMEM_MOST = 56 * 1024 * 1024
BRIEF = pl.CostEstimate(flops=1024, bytes_accessed=1024, transcendentals=0)


def spread_rows(rows):
    count, width = rows.shape
    return jnp.broadcast_to(rows[:, None, :], (count, HEAD, width)).reshape(count * HEAD, width)


def head_sums(value):
    return jnp.sum(value.reshape(GROUP, HEAD, value.shape[-1]), axis=1)


def mul_nn(left, right):
    return lax.dot_general(
        left, right, (((1,), (0,)), ((), ())), preferred_element_type=jnp.float32
    )


def mul_nt(left, right):
    return lax.dot_general(
        left, right, (((1,), (1,)), ((), ())), preferred_element_type=jnp.float32
    )


def mul_tn(left, right):
    return lax.dot_general(
        left, right, (((0,), (0,)), ((), ())), preferred_element_type=jnp.float32
    )


def half(value):
    return value.astype(jnp.bfloat16)


def call_steps(kernel, steps, ins, in_specs, outs, out_specs, scratch=(), name_id=None, micros=0):
    return pl.pallas_call(
        kernel,
        grid=(steps,),
        in_specs=in_specs,
        out_specs=out_specs,
        out_shape=outs,
        scratch_shapes=list(scratch),
        cost_estimate=pl.CostEstimate(flops=1024 + micros * 10**9, bytes_accessed=1024, transcendentals=0),
        compiler_params=pltpu.CompilerParams(
            vmem_limit_bytes=VMEM_MOST,
            dimension_semantics=("arbitrary",),
            collective_id=name_id,
            has_side_effects=name_id is not None,
        ),
    )(*ins)


def block(shape, index):
    return pl.BlockSpec(shape, index)


def whole(array):
    return pl.BlockSpec(array.shape, lambda i: (0,) * array.ndim)


def f32_out(*shape):
    return jax.ShapeDtypeStruct(shape, jnp.float32)


def bf16_out(*shape):
    return jax.ShapeDtypeStruct(shape, jnp.bfloat16)


def conv_steps(x, taps, masks):
    total = taps[:, 4:5] + taps[:, 3:4] * x * masks[0:1]
    for back in (1, 2, 3):
        total = total + taps[:, 3 - back : 4 - back] * pltpu.roll(x, back, 1) * masks[back : back + 1]
    return total


def conv_kernel(x_ref, taps_ref, masks_ref, pre_ref):
    tokens = pre_ref.shape[1]
    pre_ref[...] = conv_steps(x_ref[...], taps_ref[...], masks_ref[...])[:, :tokens]


def conv_adjoint(grad_pre, x, taps, masks):
    width = x.shape[1]
    grad_x = jnp.zeros_like(x)
    columns = []
    for back in (3, 2, 1, 0):
        part = grad_pre * masks[back : back + 1]
        moved = x if back == 0 else pltpu.roll(x, back, 1)
        columns.append(jnp.sum(part * moved, axis=1, keepdims=True))
        tap = taps[:, 3 - back : 4 - back]
        grad_x = grad_x + tap * (part if back == 0 else pltpu.roll(part, width - back, 1))
    columns.append(jnp.sum(grad_pre, axis=1, keepdims=True))
    lane = lax.broadcasted_iota(jnp.int32, (x.shape[0], 8), 1)
    packed = jnp.zeros((x.shape[0], 8), jnp.float32)
    for place, column in enumerate(columns):
        packed = jnp.where(lane == place, column, packed)
    return grad_x, packed


def conv_back_kernel(grad_ref, pre_ref, x_ref, taps_ref, masks_ref, grad_x_ref, taps_out_ref):
    grad_pre = grad_ref[...] * silu_slope(pre_ref[...])
    rest = x_ref.shape[1] - grad_pre.shape[1]
    grad_pre = jnp.concatenate([grad_pre, jnp.zeros((grad_pre.shape[0], rest), jnp.float32)], axis=1)
    grad_x, packed = conv_adjoint(grad_pre, x_ref[...], taps_ref[...], masks_ref[...])
    grad_x_ref[...] = grad_x.astype(grad_x_ref.dtype)
    taps_out_ref[...] = packed


def link_mask(seg_row, seg_col):
    count = seg_row.shape[1]
    source = lax.broadcasted_iota(jnp.int32, (count, count), 0)
    target = lax.broadcasted_iota(jnp.int32, (count, count), 1)
    linked = jnp.logical_and(source <= target, seg_row == seg_col)
    return jnp.where(linked, 0.0, -1e30)


def state_kernel(x_ref, taps_ref, masks_ref, bc_ref, dt_ref, cum_ref, flags_ref, pre_ref, state_ref):
    tokens = pre_ref.shape[1]
    pre = conv_steps(x_ref[...], taps_ref[...], masks_ref[...])[:, :tokens]
    pre_ref[...] = pre
    b_t = half(jax.nn.silu(bc_ref[:STATE, :]))
    cum = cum_ref[...]
    tail = jnp.exp(cum[:, tokens - 1 :] - cum) * flags_ref[1:2, :] * dt_ref[...]
    scaled = half(jax.nn.silu(pre) * spread_rows(tail))
    state_ref[...] = half(mul_nt(scaled, b_t))


def gate_back_kernel(
    y_ref, z_ref, grad_ref, gain_ref, rows_ref, bc_ref, cum_ref, flags_ref, grad_y_ref, grad_z_ref, grad_state_ref
):
    y, z, gain = y_ref[...], z_ref[...], gain_ref[:, 0:1]
    squashed = jax.nn.sigmoid(z)
    u = y * z * squashed
    grad_u = gain * rows_ref[0:1, :] * grad_ref[...] - u * rows_ref[1:2, :]
    grad_y = grad_u * z * squashed
    grad_y_ref[...] = grad_y
    grad_z_ref[...] = half(grad_u * y * (squashed * (1.0 + z * (1.0 - squashed))))
    c_t = half(jax.nn.silu(bc_ref[STATE:, :]))
    reach = jnp.exp(cum_ref[...]) * flags_ref[0:1, :]
    grad_state_ref[...] = half(mul_nt(half(grad_y * spread_rows(reach)), c_t))


def inner_back_kernel(
    local_ref, passed_ref, pre_ref, grad_y_ref, bc_ref, dt_ref, cum_ref, cum_col_ref, flags_ref, seg_col_ref,
    grad_x_ref, grad_state_ref, grad_cum_ref, grad_skip_ref, grad_bc_ref, mask_s, inner_s, total_s, *chain,
):
    step = pl.program_id(0)
    first, last, device = chain_places(step, False)

    @pl.when(step == 0)
    def _():
        mask_s[...] = link_mask(flags_ref[2:3, :], seg_col_ref[:, 0:1])
        bc = half(jax.nn.silu(bc_ref[...]))
        inner_s[...] = mul_tn(bc[:STATE], bc[STATE:])
        total_s[...] = jnp.zeros_like(total_s)

    grad_state_ref[...] = chain_step(step, first, last, device, local_ref, passed_ref, *chain)
    x = jax.nn.silu(pre_ref[...])
    grad_y = grad_y_ref[...]
    grad_skip_ref[...] = head_sums(x * grad_y)
    scaled = half(x * spread_rows(dt_ref[...]))
    grad_half = half(grad_y)
    cum, cum_col = cum_ref[...], cum_col_ref[0]
    ones = jnp.ones((8, cum.shape[1]), jnp.bfloat16)
    for head in range(GROUP):
        rows = slice(head * HEAD, (head + 1) * HEAD)
        decay = jnp.exp(cum[head : head + 1, :] - cum_col[:, head : head + 1] + mask_s[...])
        weights = decay * inner_s[...]
        grad_x_ref[rows, :] = mul_nt(grad_half[rows], half(weights))
        grad_weights = mul_tn(scaled[rows], grad_half[rows])
        total_s[...] += grad_weights * decay
        moved = half(grad_weights * weights)
        sums = mul_nn(ones, moved) - mul_nt(ones, moved)
        grad_cum_ref[head : head + 1, :] = sums[0:1]

    @pl.when(step == pl.num_programs(0) - 1)
    def _():
        bc = half(jax.nn.silu(bc_ref[...]))
        total = half(total_s[...])
        grad_bc_ref[:STATE, :] = mul_nt(bc[STATE:], total)
        grad_bc_ref[STATE:, :] = mul_nn(bc[:STATE], total)
        chain_end(chain[0].shape[0], last, device, *chain)


def join_back_kernel(
    grad_in_ref, grad_y_ref, pre_ref, x_ref, taps_ref, masks_ref, state_ref, grad_state_ref,
    bc_ref, dt_ref, cum_ref, skip_ref, flags_ref,
    grad_x_ref, taps_out_ref, grad_dt_ref, grad_cum_ref, grad_last_ref, grad_bc_ref,
):
    step = pl.program_id(0)

    @pl.when(step == 0)
    def _():
        grad_bc_ref[...] = jnp.zeros_like(grad_bc_ref)

    bc = half(jax.nn.silu(bc_ref[...]))
    b_t, c_t = bc[:STATE], bc[STATE:]
    pre, grad_y, cum, dt = pre_ref[...], grad_y_ref[...], cum_ref[...], dt_ref[...]
    tokens = pre.shape[1]
    state, grad_state = state_ref[...], grad_state_ref[...]
    x = jax.nn.silu(pre)
    reached = grad_y * spread_rows(jnp.exp(cum) * flags_ref[0:1, :])
    grad_cum = head_sums(reached * mul_nn(state, c_t))
    grad_bc_ref[STATE:, :] += mul_tn(state, half(reached))
    tail = spread_rows(jnp.exp(cum[:, tokens - 1 :] - cum) * flags_ref[1:2, :])
    dt_wide = spread_rows(dt)
    scaled = x * dt_wide
    from_state = mul_nn(grad_state, b_t) * tail
    grad_bc_ref[:STATE, :] += mul_tn(grad_state, half(scaled * tail))
    tails = head_sums(scaled * from_state)
    grad_cum_ref[...] = grad_cum - tails
    last = jnp.sum(tails, axis=1, keepdims=True)
    through = jnp.sum(
        head_sums(state.astype(jnp.float32) * grad_state.astype(jnp.float32)), axis=1, keepdims=True
    )
    lane = lax.broadcasted_iota(jnp.int32, (GROUP, 128), 1)
    grad_last_ref[...] = jnp.where(lane == 0, last, jnp.where(lane == 1, through, 0.0))
    grad_scaled = grad_in_ref[...] + from_state
    grad_dt_ref[...] = head_sums(grad_scaled * x)
    grad_pre = (grad_scaled * dt_wide + grad_y * spread_rows(skip_ref[...])) * silu_slope(pre)
    rest = x_ref.shape[1] - tokens
    grad_pre = jnp.concatenate([grad_pre, jnp.zeros((grad_pre.shape[0], rest), jnp.float32)], axis=1)
    grad_x, packed = conv_adjoint(grad_pre, x_ref[...], taps_ref[...], masks_ref[...])
    grad_x_ref[...] = half(grad_x)
    taps_out_ref[...] = packed


def mixer_rows(dt_raw, dt_bias, a_log, d_skip, seg_window, taps):
    tokens = dt_raw.shape[1]
    dt = jax.nn.softplus(dt_raw + dt_bias[:, None])
    decay = -jnp.exp(a_log)[:, None] * dt
    upper = jnp.triu(jnp.ones((tokens, tokens), jnp.float32))
    cum = jnp.dot(decay, upper, precision=lax.Precision.HIGHEST)
    cum_col = jnp.swapaxes(cum.reshape(-1, GROUP, tokens), 1, 2)
    seg_now = seg_window[taps - 1 :]
    before = seg_window[taps - 2]
    reach = (seg_now == before).astype(jnp.float32)
    tail = (seg_now == seg_now[-1]).astype(jnp.float32)
    none = jnp.zeros((5, tokens), jnp.float32)
    flags = jnp.concatenate([jnp.stack([reach, tail, seg_now.astype(jnp.float32)]), none])
    seg_col = jnp.broadcast_to(seg_now.astype(jnp.float32)[:, None], (tokens, 8))
    masks = [
        (seg_window[taps - 1 - back : taps - 1 - back + tokens] == seg_now).astype(jnp.float32)
        for back in range(taps)
    ]
    masks = jnp.pad(jnp.stack(masks), ((0, 8 - taps), (0, 128)))
    through = jnp.exp(cum[:, -1]) * (seg_now[-1] == before).astype(jnp.float32)
    skip = jnp.broadcast_to(d_skip[:, None], dt.shape)
    return dt, decay, cum, cum_col, flags, seg_col, masks, through, skip


def mixer_forward_states(proj, taps, masks, dt, cum, flags):
    tokens, groups = dt.shape[1], HEADS // GROUP
    wide = proj.shape[1]
    bc_pre = call_steps(
        conv_kernel, 1, (proj, taps, masks),
        [block((2 * STATE, wide), lambda i: (DI // STATE, 0)),
         block((2 * STATE, 8), lambda i: (DI // (2 * STATE), 0)), whole(masks)],
        f32_out(2 * STATE, tokens), block((2 * STATE, tokens), lambda i: (0, 0)),
    )
    rows = block((GROUP, tokens), lambda i: (i, 0))
    pre, state = call_steps(
        state_kernel, groups, (proj, taps, masks, bc_pre, dt, cum, flags),
        [block((WIDE, wide), lambda i: (i + groups, 0)), block((WIDE, 8), lambda i: (i, 0)), whole(masks),
         whole(bc_pre), rows, rows, whole(flags)],
        [f32_out(DI, tokens), bf16_out(DI, STATE)],
        [block((WIDE, tokens), lambda i: (i, 0)), block((WIDE, STATE), lambda i: (i, 0))],
    )
    return bc_pre, pre, state


def mixer_back_gate(y, proj, grad_gated, gain_col, gate_rows, bc_pre, cum, flags):
    tokens, groups = y.shape[1], HEADS // GROUP
    wide = block((WIDE, tokens), lambda i: (i, 0))
    return call_steps(
        gate_back_kernel, groups, (y, proj, grad_gated, gain_col, gate_rows, bc_pre, cum, flags),
        [wide, wide, wide, block((WIDE, 8), lambda i: (i, 0)), whole(gate_rows), whole(bc_pre),
         block((GROUP, tokens), lambda i: (i, 0)), whole(flags)],
        [f32_out(DI, tokens), bf16_out(DI, tokens), bf16_out(DI, STATE)],
        [wide, wide, block((WIDE, STATE), lambda i: (i, 0))], micros=9,
    )


def mixer_back_inner(local, passed, pre, grad_y, bc_pre, dt, cum, cum_col, flags, seg_col, name_id):
    tokens, groups = dt.shape[1], HEADS // GROUP
    rows = block((GROUP, tokens), lambda i: (i, 0))
    wide = block((WIDE, tokens), lambda i: (i, 0))
    states = block((WIDE, STATE), lambda i: (i, 0))
    square = pltpu.VMEM((tokens, tokens), jnp.float32)
    return call_steps(
        inner_back_kernel, groups, (local, passed, pre, grad_y, bc_pre, dt, cum, cum_col, flags, seg_col),
        [states, block((WIDE, 8), lambda i: (i, 0)), wide, wide, whole(bc_pre), rows, rows, block((1, tokens, GROUP), lambda i: (i, 0, 0)),
         whole(flags), whole(seg_col)],
        [f32_out(DI, tokens), bf16_out(DI, STATE), f32_out(HEADS, tokens), f32_out(HEADS, tokens),
         f32_out(2 * STATE, tokens)],
        [wide, states, rows, rows, block((2 * STATE, tokens), lambda i: (0, 0))],
        (square, square, square) + chain_room(groups), name_id=name_id, micros=35,
    )


def mixer_back_join(grad_scaled, grad_y, pre, proj, taps, masks, state_in, grad_state, bc_pre, dt, cum, skip, flags):
    tokens, groups = dt.shape[1], HEADS // GROUP
    rows = block((GROUP, tokens), lambda i: (i, 0))
    wide = block((WIDE, tokens), lambda i: (i, 0))
    longer = block((WIDE, proj.shape[1]), lambda i: (i, 0))
    later = block((WIDE, proj.shape[1]), lambda i: (i + groups, 0))
    states = block((WIDE, STATE), lambda i: (i, 0))
    narrow = block((WIDE, 8), lambda i: (i, 0))
    return call_steps(
        join_back_kernel, groups,
        (grad_scaled, grad_y, pre, proj, taps, masks, state_in, grad_state, bc_pre, dt, cum, skip, flags),
        [wide, wide, wide, later, narrow, whole(masks), states, states, whole(bc_pre), rows, rows, rows,
         whole(flags)],
        [bf16_out(DI, proj.shape[1]), f32_out(DI, 8), f32_out(HEADS, tokens), f32_out(HEADS, tokens),
         f32_out(HEADS, 128), f32_out(2 * STATE, tokens)],
        [longer, narrow, rows, rows, block((GROUP, 128), lambda i: (i, 0)),
         block((2 * STATE, tokens), lambda i: (0, 0))], micros=19,
    )


def mixer_back_conv(grad_bc, bc_pre, proj, taps, masks):
    place = DI // (2 * STATE)
    wide = proj.shape[1]
    return call_steps(
        conv_back_kernel, 1, (grad_bc, bc_pre, proj, taps, masks),
        [whole(grad_bc), whole(bc_pre), block((2 * STATE, wide), lambda i: (2 * place, 0)),
         block((2 * STATE, 8), lambda i: (place, 0)), whole(masks)],
        [bf16_out(2 * STATE, wide), f32_out(2 * STATE, 8)],
        [block((2 * STATE, wide), lambda i: (0, 0)), block((2 * STATE, 8), lambda i: (0, 0))],
    )


def cut(array_index, rows, columns, row_step, column_step):
    found = []
    for row in range(0, rows, row_step):
        for column in range(0, columns, column_step):
            found.append(
                (array_index, row, min(row_step, rows - row), column, min(column_step, columns - column))
            )
    return found


def flipped(z, bits):
    if bits & 1:
        z = z + 1 - 2 * lax.rem(z, 2)
    return lax.rem(z + (bits & 2), 4)


def places(line):
    dp, z = lax.axis_index("dp"), lax.axis_index("ctx")
    y, x, core = lax.div(dp, 4), lax.rem(lax.div(dp, 2), 2), lax.rem(dp, 2)
    others = {
        "x": (dp + 2 - 4 * x, z),
        "y": (dp + 4 - 8 * y, z),
        "core": (dp + 1 - 2 * core, z),
    }
    for away in line:
        others[away] = (dp, lax.rem(z + away, 4))
    others["beside"] = (dp, flipped(z, 1))
    others["across"] = (dp, 3 - z)
    return y, x, core, z, others


def moved(moves, refs_in, refs_out, z, others, sems):
    copies = []
    for at, (source, target, take, put, bits) in enumerate(moves):
        source, target = refs_in[source], refs_out[target]
        source, target = source.at[take(z)], target.at[put(z)]
        copies.append(
            pltpu.make_async_remote_copy(
                src_ref=source,
                dst_ref=target,
                send_sem=sems[0].at[at],
                recv_sem=sems[1].at[at],
                device_id=others["beside" if bits == 1 else 2],
                device_id_type=pl.DeviceIdType.MESH,
            )
        )
    return copies


def greet(others):
    barrier = pltpu.get_barrier_semaphore()
    for device in others.values():
        pl.semaphore_signal(
            barrier, inc=1, device_id=device, device_id_type=pl.DeviceIdType.MESH
        )
    pl.semaphore_wait(barrier, len(others))


def send(source, target, sems, piece, leg, device):
    return pltpu.make_async_remote_copy(
        src_ref=source,
        dst_ref=target,
        send_sem=sems[0].at[piece, leg],
        recv_sem=sems[1].at[piece, leg],
        device_id=device,
        device_id_type=pl.DeviceIdType.MESH,
    )


def gather_kernel(pieces, ahead, count, line, moves, sizes, *refs):
    ins, more_in = refs[:count], refs[count : count + sizes[0]]
    refs = refs[count + sizes[0] :]
    outs, more_out = refs[:count], refs[count : count + sizes[1]]
    sent, came, kept, *more_sems = refs[count + sizes[1] :]
    y, x, core, z, others = places(line)
    deep = len(line) + 1
    slot = z if deep == 4 else lax.div(z, 2)
    inner = jnp.logical_and(z > 0, z < 3)
    greet(others)
    sems = (sent, came)

    def extra():
        return moved(moves, more_in if sizes[2] else more_out, more_out, z, others, more_sems) if moves else []

    def extra_turn(turn, turns):
        share = -(-len(moves) // turns)
        if turn < turns:
            for copy in extra()[share * turn : share * (turn + 1)]:
                copy.start()

    def legs(number):
        array, row, rows, column, columns = pieces[number]
        area = (pl.ds(row, rows), pl.ds(column, columns))
        out = outs[array]
        first, second = ("x", "y") if number % 2 == 0 else ("y", "x")
        rest = ((slice(None),) if line else ()) + area
        own = ins[array].at[area]
        mine = out.at[(y, x, core) + ((slot,) if line else ()) + area]
        lane = out.at[(y, x, core) + rest]
        at_pair = lax.div(z, 2)
        pair = out.at[(y, x, core, pl.ds(2 * at_pair, 2)) + area] if deep == 4 else None
        rest_pair = out.at[(y, x, core, pl.ds(2 - 2 * at_pair, 2)) + area] if deep == 4 else None
        if first == "x":
            plane = out.at[(y, slice(None), core) + rest]
        else:
            plane = out.at[(slice(None), x, core) + rest]
        every = out.at[(slice(None), slice(None), core) + rest]
        return {
            "keep": lambda: pltpu.make_async_copy(own, mine, kept.at[number]),
            "line": lambda: [send(own, mine, sems, number, 0, others["beside" if deep == 4 else 2])],
            "across": lambda: send(pair, pair, sems, number, 1, others["across"]),
            "outward": lambda: send(rest_pair, rest_pair, sems, number, 2, others["beside"]),
            "first": lambda: send(lane if line else own, lane, sems, number, 3, others[first]),
            "second": lambda: send(plane, plane, sems, number, 4, others[second]),
            "core": lambda: send(every, every, sems, number, 5, others["core"]),
        }

    def begin(number):
        if number < len(pieces):
            leg = legs(number)
            leg["keep"]().start()
            for copy in leg["line"]():
                copy.start()

    def advance(number, stage):
        if not 0 <= number < len(pieces):
            return
        leg = legs(number)
        if stage < 2 and deep < 4:
            return
        if stage == 0:
            leg["keep"]().wait()
            leg["line"]()[0].wait_recv()

            @pl.when(inner)
            def _():
                leg["across"]().start()
        elif stage == 1:

            @pl.when(inner)
            def _():
                leg["across"]().wait_recv()
                leg["outward"]().start()
        elif stage == 2:
            if deep == 4:

                @pl.when(jnp.logical_not(inner))
                def _():
                    leg["outward"]().wait_recv()
            else:
                leg["keep"]().wait()
                leg["line"]()[0].wait_recv()
            leg["first"]().start()
        elif stage == 3:
            leg["first"]().wait_recv()
            leg["second"]().start()
        elif stage == 4:
            leg["second"]().wait_recv()
            leg["core"]().start()
        else:
            leg["core"]().wait_recv()

    for number in range(2 * ahead):
        begin(number)
    pairs = -(-len(pieces) // 2)
    early = 0 if deep == 4 else 2
    for turn in range(pairs + 5 - early):
        extra_turn(turn, pairs)
        for stage in range(early, 6):
            for number in (2 * (turn - stage + early), 2 * (turn - stage + early) + 1):
                advance(number, stage)
                if stage == early and number < len(pieces):
                    begin(number + 2 * ahead)
    for number in range(len(pieces)):
        leg = legs(number)
        for copy in leg["line"]() + [leg["first"](), leg["second"](), leg["core"]()]:
            copy.wait_send()
        if deep == 4:

            @pl.when(inner)
            def _():
                leg["across"]().wait_send()
                leg["outward"]().wait_send()
    for copy in extra():
        copy.wait()


def move_room(moves):
    if not moves:
        return []
    return [pltpu.SemaphoreType.DMA((len(moves),))] * 2


def pallas_gather(parts, steps, name_id, line=(1, 2, 3), ahead=2, more=(), more_shapes=(), moves=()):
    pieces = []
    for index, (part, (row_step, column_step)) in enumerate(zip(parts, steps)):
        pieces += cut(index, part.shape[0], part.shape[1], row_step, column_step)
    count = len(parts)
    made = more_shapes or [part.shape for part in more]
    lead = (2, 2, 2) + ((len(line) + 1,) if line else ())
    anywhere = pl.BlockSpec(memory_space=pl.ANY)
    outs = pl.pallas_call(
        partial(gather_kernel, pieces, ahead, count, line, moves, (len(more), len(made), bool(more_shapes))),
        in_specs=[anywhere] * (count + len(more)),
        out_specs=[anywhere] * (count + len(made)),
        out_shape=[jax.ShapeDtypeStruct(lead + part.shape, part.dtype) for part in parts]
        + [bf16_out(*shape) for shape in made],
        scratch_shapes=[
            pltpu.SemaphoreType.DMA((len(pieces), 6)),
            pltpu.SemaphoreType.DMA((len(pieces), 6)),
            pltpu.SemaphoreType.DMA((len(pieces),)),
        ]
        + move_room(moves),
        input_output_aliases={} if more_shapes else {count + at: count + at for at in range(len(more))},
        cost_estimate=BRIEF,
        compiler_params=pltpu.CompilerParams(collective_id=name_id, has_side_effects=True),
    )(*parts, *more)
    return [out.reshape((-1,) + part.shape) for out, part in zip(outs, parts)] + list(outs[count:])


def reduce_kernel(pieces, ahead, count, lines, moves, sizes, *refs):
    ins, more_in = refs[:count], refs[count : count + sizes[0]]
    refs = refs[count + sizes[0] :]
    outs, more_out = refs[:count], refs[count : count + sizes[1]]
    sent, came, kept, put = refs[count + sizes[1] : count + sizes[1] + 4]
    room = refs[count + sizes[1] + 4 :]
    if moves:
        more_sems, room = room[:2], room[2:]
    y, x, core, z, others = places(max(lines, key=len))
    greet(others)
    sems = (sent, came)
    amount = len(pieces)

    def extra():
        return moved(moves, more_in, more_out, z, others, more_sems) if moves else []

    def extra_turn(turn, turns):
        share = -(-len(moves) // turns)
        if turn < turns:
            for copy in extra()[share * turn : share * (turn + 1)]:
                copy.start()

    def held(number):
        return room[6 * number : 6 * number + 6]

    def legs(number):
        array, row, rows, column, columns = pieces[number]
        area = (pl.ds(row, rows), pl.ds(column, columns))
        total, from_core, from_first, from_second, from_line, result = held(number)
        every = (slice(None), slice(None))
        line = lines[array]
        deep = len(line) + 1
        slot = z if deep == 4 else lax.div(z, 2)
        rest = ((slice(None),) if line else ()) + area
        side = number % 2 == 0
        return {
            "load": lambda: pltpu.make_async_copy(
                ins[array].at[every + (core,) + rest], total, kept.at[number]
            ),
            "core": lambda: send(
                ins[array].at[every + (1 - core,) + rest],
                from_core, sems, number, 0, others["core"],
            ),
            "first": lambda: send(
                total.at[:, 1 - x] if side else total.at[1 - y],
                from_first, sems, number, 1, others["x" if side else "y"],
            ),
            "second": lambda: send(
                total.at[1 - y, x] if side else total.at[y, 1 - x],
                from_second, sems, number, 2, others["y" if side else "x"],
            ),
            "line": lambda: [
                send(
                    total.at[y, x, lax.rem(z + away, 4) if deep == 4 else 1 - slot],
                    from_line.at[away - line[0]], sems, number, 2 + away, others[away],
                )
                for away in line
            ],
            "store": lambda: pltpu.make_async_copy(result, outs[array].at[area], put.at[number]),
        }

    def begin(number):
        if number < amount:
            leg = legs(number)
            leg["load"]().start()
            leg["core"]().start()

    def advance(number, stage):
        if not 0 <= number < amount:
            return
        leg = legs(number)
        total, from_core, from_first, from_second, from_line, result = held(number)
        line = lines[pieces[number][0]]
        deep = len(line) + 1
        slot = z if deep == 4 else lax.div(z, 2)

        def place(at, *lead):
            return lead + ((lax.rem(at, deep),) if line else ())

        if stage == 0:
            leg["load"]().wait()
            leg["core"]().wait_recv()

            @pl.loop(0, 4 * deep)
            def _(at):
                here = place(at, lax.div(at, 2 * deep), lax.rem(lax.div(at, deep), 2))
                total[here] = total[here] + from_core[here]

            leg["first"]().start()
        elif stage == 1:
            leg["first"]().wait_recv()

            @pl.loop(0, 2 * deep)
            def _(at):
                outer = lax.div(at, deep)
                here = place(at, outer, x) if number % 2 == 0 else place(at, y, outer)
                total[here] = total[here] + from_first[place(at, outer)]

            leg["second"]().start()
        elif stage == 2:
            leg["second"]().wait_recv()
            if line:

                @pl.loop(0, deep)
                def _(at):
                    total[y, x, at] = total[y, x, at] + from_second[at]

                for copy in leg["line"]():
                    copy.start()
            else:
                result[...] = total[y, x].astype(jnp.float32) + from_second[...].astype(jnp.float32)
                leg["store"]().start()
        elif line:
            for copy in leg["line"]():
                copy.wait_recv()
            summed = total[y, x, slot].astype(jnp.float32)
            for away in range(len(line)):
                summed = summed + from_line[away].astype(jnp.float32)
            result[...] = summed
            leg["store"]().start()

    for number in range(2 * ahead):
        begin(number)
    pairs = -(-amount // 2)
    for turn in range(pairs + 3):
        extra_turn(turn, pairs)
        for stage in range(4):
            for number in (2 * (turn - stage), 2 * (turn - stage) + 1):
                advance(number, stage)
                if stage == 0 and number >= 0:
                    begin(number + 2 * ahead)
    for number in range(amount):
        leg = legs(number)
        for copy in [leg["core"](), leg["first"](), leg["second"]()] + leg["line"]():
            copy.wait_send()
        leg["store"]().wait()
    for copy in extra():
        copy.wait()


def pallas_reduce(parts, steps, name_id, lines=None, ahead=2, more=(), more_shapes=(), moves=(), same=()):
    lines = lines or [(1, 2, 3)] * len(parts)
    shapes = [part.shape[1:] for part in parts]
    pieces = []
    for index, (shape, (row_step, column_step)) in enumerate(zip(shapes, steps)):
        pieces += cut(index, shape[0], shape[1], row_step, column_step)
    count, amount = len(parts), len(pieces)
    anywhere = pl.BlockSpec(memory_space=pl.ANY)
    room = []
    for array, _, rows, _, columns in pieces:
        kind, line = parts[array].dtype, lines[array]
        deep = (len(line) + 1,) if line else ()
        for lead in ((2, 2) + deep, (2, 2) + deep, (2,) + deep, deep, (max(len(line), 1),)):
            room.append(pltpu.VMEM(lead + (rows, columns), kind))
        room.append(pltpu.VMEM((rows, columns), jnp.float32))
    return pl.pallas_call(
        partial(reduce_kernel, pieces, ahead, count, lines, moves, (len(more), len(more_shapes))),
        in_specs=[anywhere] * (count + len(more)),
        out_specs=[anywhere] * (count + len(more_shapes)),
        out_shape=[jax.ShapeDtypeStruct(shape, jnp.float32) for shape in shapes]
        + [bf16_out(*shape) for shape in more_shapes],
        scratch_shapes=[
            pltpu.SemaphoreType.DMA((amount, 6)),
            pltpu.SemaphoreType.DMA((amount, 6)),
            pltpu.SemaphoreType.DMA((amount,)),
            pltpu.SemaphoreType.DMA((amount,)),
        ]
        + move_room(moves)
        + room,
        input_output_aliases={count + at: count + at for at in same},
        cost_estimate=BRIEF,
        compiler_params=pltpu.CompilerParams(
            collective_id=name_id, has_side_effects=True, vmem_limit_bytes=VMEM_MOST
        ),
        )(*[part.reshape((2, 2, 2) + ((len(line) + 1,) if line else ()) + shape) for part, shape, line in zip(parts, shapes, lines)], *more)


def proj_back_kernel(
    normed_ref, weight_ref, grad_z_ref, grad_x_ref, grad_rest_ref, rows_ref,
    grad_weight_ref, grad_normed_ref, came_ref, sent, came,
):
    step, groups = pl.program_id(0), DI // WIDE
    tokens = grad_z_ref.shape[1]
    dp, z = lax.axis_index("dp"), lax.axis_index("ctx")
    far = (dp, lax.rem(z + 2, 4))

    def exchange():
        return pltpu.make_async_remote_copy(
            src_ref=rows_ref,
            dst_ref=came_ref,
            send_sem=sent,
            recv_sem=came,
            device_id=far,
            device_id_type=pl.DeviceIdType.MESH,
        )

    @pl.when(step == 0)
    def _():
        grad_normed_ref[...] = jnp.zeros_like(grad_normed_ref)
        greet({"far": far})
        exchange().start()

    @pl.when(step == 2 * groups)
    def _():
        exchange().wait()

    @pl.when(step < groups)
    def _():
        grad_weight_ref[...] = half(mul_nt(normed_ref[:, :tokens], grad_z_ref[...]))
        grad_normed_ref[:, :tokens] += mul_nn(weight_ref[...], grad_z_ref[...])

    @pl.when(jnp.logical_and(step >= groups, step < 2 * groups))
    def _():
        grad_weight_ref[...] = half(mul_nt(normed_ref[...], grad_x_ref[...]))
        grad_normed_ref[...] += mul_nn(weight_ref[...], grad_x_ref[...])

    @pl.when(step == 2 * groups)
    def _():
        lane = lax.broadcasted_iota(jnp.int32, weight_ref.shape, 1)
        weight = jnp.where(lane < PROJ - 2 * DI, weight_ref[...], jnp.zeros_like(weight_ref))
        grad_weight_ref[...] = half(mul_nt(normed_ref[...], grad_rest_ref[...]))
        grad_normed_ref[...] += mul_nn(weight, grad_rest_ref[...])


def proj_back(normed_t, weight, grad_z, grad_x, grad_rest, rows, name_id):
    features, tokens = normed_t.shape
    groups = DI // WIDE
    return call_steps(
        proj_back_kernel, 2 * groups + 1, (normed_t, weight, grad_z, grad_x, grad_rest, rows),
        [whole(normed_t), block((features, WIDE), lambda i: (0, i)),
         block((WIDE, grad_z.shape[1]), lambda i: (jnp.minimum(i, groups - 1), 0)),
         block((WIDE, tokens), lambda i: (jnp.clip(i - groups, 0, groups - 1), 0)), whole(grad_rest),
         pl.BlockSpec(memory_space=pl.ANY)],
        [bf16_out(features, PROJ), f32_out(features, tokens), bf16_out(*rows.shape)],
        [block((features, WIDE), lambda i: (0, i)), block((features, tokens), lambda i: (0, 0)),
         pl.BlockSpec(memory_space=pl.ANY)],
        (pltpu.SemaphoreType.DMA, pltpu.SemaphoreType.DMA), name_id=name_id, micros=27,
    )


def hop(group, leaving, arrived, sent, came, device):
    return pltpu.make_async_remote_copy(
        src_ref=leaving.at[group],
        dst_ref=arrived.at[group],
        send_sem=sent.at[group],
        recv_sem=came.at[group],
        device_id=device,
        device_id_type=pl.DeviceIdType.MESH,
    )


def chain_places(step, forward):
    dp, z = lax.axis_index("dp"), lax.axis_index("ctx")
    others = {"left": (dp, lax.rem(z + 3, 4)), "right": (dp, lax.rem(z + 1, 4))}

    @pl.when(step == 0)
    def _():
        greet(others)

    if forward:
        return z == 0, z == 3, others["right"]
    return z == 3, z == 0, others["left"]


def chain_step(step, first, last, device, local_ref, passed_ref, leaving, arrived, sent, came):
    @pl.when(first)
    def _():
        arrived[step] = jnp.zeros(arrived.shape[1:], arrived.dtype)

    @pl.when(jnp.logical_not(first))
    def _():
        hop(step, leaving, arrived, sent, came, device).wait_recv()

    here = arrived[step]
    leaving[step] = half(here.astype(jnp.float32) * passed_ref[:, 0:1] + local_ref[...].astype(jnp.float32))

    @pl.when(jnp.logical_not(last))
    def _():
        hop(step, leaving, arrived, sent, came, device).start()

    return here


def chain_end(groups, last, device, leaving, arrived, sent, came):
    @pl.when(jnp.logical_not(last))
    def _():
        for group in range(groups):
            hop(group, leaving, arrived, sent, came, device).wait_send()


def chain_room(groups):
    slots = pltpu.VMEM((groups, WIDE, STATE), jnp.bfloat16)
    sems = pltpu.SemaphoreType.DMA((groups,))
    return (slots, slots, sems, sems)


def forward_kernel(
    local_ref, passed_ref, pre_ref, bc_ref, dt_ref, cum_ref, cum_col_ref, skip_ref, flags_ref, seg_col_ref,
    z_ref, gain_ref, y_ref, state_ref, gated_ref, scale_ref, mask_s, inner_s, u_s, sum_s, *chain,
):
    step, groups = pl.program_id(0), u_s.shape[0]
    first, last, device = chain_places(step, True)

    @pl.when(step == 0)
    def _():
        mask_s[...] = link_mask(flags_ref[2:3, :], seg_col_ref[:, 0:1])
        bc = half(jax.nn.silu(bc_ref[...]))
        inner_s[...] = mul_tn(bc[:STATE], bc[STATE:])
        sum_s[...] = jnp.zeros_like(sum_s)

    @pl.when(step < groups)
    def _():
        here = chain_step(step, first, last, device, local_ref, passed_ref, *chain)
        state_ref[...] = here
        cum, cum_col = cum_ref[...], cum_col_ref[0]
        c_t = half(jax.nn.silu(bc_ref[STATE:, :]))
        x = jax.nn.silu(pre_ref[...])
        scaled = half(x * spread_rows(dt_ref[...]))
        reach = jnp.exp(cum) * flags_ref[0:1, :]
        y_ref[...] = mul_nn(here, c_t) * spread_rows(reach) + x * spread_rows(skip_ref[...])
        for head in range(GROUP):
            rows = slice(head * HEAD, (head + 1) * HEAD)
            spread = cum[head : head + 1, :] - cum_col[:, head : head + 1] + mask_s[...]
            y_ref[rows, :] += mul_nn(scaled[rows], half(jnp.exp(spread) * inner_s[...]))
        u = y_ref[...] * jax.nn.silu(z_ref[...])
        u_s[step] = u
        sum_s[...] += jnp.sum(u * u, axis=0, keepdims=True)

    @pl.when(step >= groups)
    def _():
        scale = lax.rsqrt(sum_s[0:1, :] * (1.0 / DI) + 1e-05)
        gated_ref[...] = half(u_s[step - groups] * scale * gain_ref[:, 0:1])
        scale_ref[...] = jnp.broadcast_to(scale, scale_ref.shape)

    @pl.when(step == 2 * groups - 1)
    def _():
        chain_end(groups, last, device, *chain)


def mixer_forward(local, passed, pre, bc_pre, dt, cum, cum_col, skip, flags, seg_col, proj, gain_col, name_id):
    tokens, groups = dt.shape[1], HEADS // GROUP
    first = lambda i: (jnp.minimum(i, groups - 1), 0)
    second = lambda i: (jnp.maximum(i - groups, 0), 0)
    rows, wide = block((GROUP, tokens), first), block((WIDE, tokens), first)
    states = block((WIDE, STATE), first)
    square = pltpu.VMEM((tokens, tokens), jnp.float32)
    return call_steps(
        forward_kernel, 2 * groups,
        (local, passed, pre, bc_pre, dt, cum, cum_col, skip, flags, seg_col, proj, gain_col),
        [states, block((WIDE, 8), first), wide, whole(bc_pre), rows, rows,
         block((1, tokens, GROUP), lambda i: (jnp.minimum(i, groups - 1), 0, 0)), rows, whole(flags),
         whole(seg_col), wide, block((WIDE, 8), second)],
        [f32_out(DI, tokens), bf16_out(DI, STATE), bf16_out(DI, tokens), f32_out(8, tokens)],
        [wide, states, block((WIDE, tokens), second), block((8, tokens), lambda i: (0, 0))],
        (square, square, pltpu.VMEM((groups, WIDE, tokens), jnp.float32), pltpu.VMEM((8, tokens), jnp.float32))
        + chain_room(groups),
        name_id=name_id,
    )


BOTH = ("dp", "ctx")


def nothing(value):
    first = value[(0,) * value.ndim].astype(jnp.float32)
    return jnp.minimum(jnp.abs(first), 0.0)


def no_step(value):
    return nothing(value).astype(jnp.int32)


def two_parts(value):
    high = value.astype(jnp.bfloat16)
    low = (value - high.astype(jnp.float32)).astype(jnp.bfloat16)
    return high, low


def route_table(routes, expert_count):
    named = jnp.any(
        routes[:, :, None] == jnp.arange(expert_count, dtype=jnp.int32), axis=1
    )
    rows = routes.shape[0]
    earlier = jnp.tril(jnp.ones((rows, rows), jnp.bfloat16), -1)
    ranks = jnp.dot(earlier, named.astype(jnp.bfloat16), preferred_element_type=jnp.float32)
    return named, jnp.where(named, ranks, -1.0)


def swap(value, bits):
    count = lax.axis_size("ctx")
    return lax.ppermute(value, "ctx", [(source, source ^ bits) for source in range(count)])


def other_strip(start):
    def at(z):
        first = EXP_DEV // 2 * (1 - lax.div(z, 2))
        return (pl.ds(first, EXP_DEV // 2), pl.ds(start, STRIP))

    return at


def columns(place, start, size):
    return lambda z: place(z) + (pl.ds(start, size),)


def held_experts(shard, other):
    held = EXP_DEV // 2
    half_at = lax.div(lax.axis_index("ctx"), 2)
    return lax.dynamic_slice_in_dim(shard, held * (1 - half_at if other else half_at), held, 0)


STRIP = 64


def quarter(axis, width, bits, start):
    def at(z):
        first = flipped(z, bits) * width
        if axis == 1:
            return (slice(None), pl.ds(pl.multiple_of(first + start, STRIP), STRIP))
        return (slice(None), pl.ds(start, STRIP), pl.ds(pl.multiple_of(first, 128), width))

    return at


def strip(start, *lead):
    return lambda z: lead + (slice(None), pl.ds(start, STRIP))


def strips(rows):
    return range(0, rows, STRIP)


def with_quarter(whole, own, axis):
    place = lax.axis_index("ctx") * own.shape[axis]
    return lax.dynamic_update_slice_in_dim(whole, own, place, axis)


def own_quarter(whole, axis, bits):
    width = whole.shape[axis] // 4
    return lax.dynamic_slice_in_dim(whole, flipped(lax.axis_index("ctx"), bits) * width, width, axis)


def expert_owners(near, far, late):
    far = far.astype(jnp.float32) + late
    low = lax.div(lax.axis_index("ctx"), 2) == 0
    return jnp.concatenate([jnp.where(low, near, far), jnp.where(low, far, near)], axis=0)


TILE = 4


def experts_kernel(
    rank_ref, gate_ref, rows_ref, grads_ref, first_ref, down_ref,
    routed_ref, back_ref, dgate_ref, grad_first_ref, grad_down_ref,
    x_s, g_s, sum_first_s, sum_down_s, ready_s, sem,
):
    tile, expert = pl.program_id(0), pl.program_id(1)
    last = pl.num_programs(0) - 1
    hidden = down_ref.shape[1]
    slots = x_s.shape[0] // TILE
    tokens = rank_ref.shape[2]
    chosen, gates = [], []
    number = lax.broadcasted_iota(jnp.int32, (slots, tokens), 0).astype(jnp.float32)
    for at in range(TILE):
        rows = pl.ds(at * slots, slots)
        own = rank_ref[at, pl.ds(expert, 1), :] == number
        chosen.append(own)
        gates.append(jnp.sum(jnp.where(own, gate_ref[at, pl.ds(expert, 1), :], 0.0), axis=1, keepdims=True))
        picker = half(own.astype(jnp.float32))
        x_s[rows, :] = half(mul_nn(picker, rows_ref[at]))
        g_s[rows, :] = half(mul_nn(picker, grads_ref[at]))
    gate = jnp.concatenate(gates, axis=0)
    x, grad = x_s[...], g_s[...].astype(jnp.float32)
    both = mul_nn(x, first_ref[0])
    hg, hu = both[:, :hidden], both[:, hidden:]
    squashed = jax.nn.sigmoid(hg)
    act = half(hg * squashed * hu)
    out = half(mul_nn(act, down_ref[0]))
    out_f = out.astype(jnp.float32)
    dgate = jnp.sum(grad * out_f, axis=1, keepdims=True)
    routed = half(gate * out_f)
    grad_out = half(gate * grad)
    grad_act = mul_nt(grad_out, down_ref[0])
    grad_hg = half(grad_act * hu * (squashed * (1.0 + hg * (1.0 - squashed))))
    grad_hu = half(grad_act * hg * squashed)
    grad_both = jnp.concatenate([grad_hg, grad_hu], axis=1)
    back = half(mul_nt(grad_both, first_ref[0]))

    @pl.when(tile == 0)
    def _():
        sum_first_s[expert] = jnp.zeros(sum_first_s.shape[1:], jnp.float32)
        sum_down_s[expert] = jnp.zeros(sum_down_s.shape[1:], jnp.float32)

    @pl.loop(0, x_s.shape[1] // 256)
    def _(at):
        some = pl.ds(pl.multiple_of(at * 256, 256), 256)
        sum_first_s[expert, some, :] += mul_tn(x_s[:, some], grad_both)

    sum_down_s[expert] += mul_tn(act, grad_out)
    for at in range(TILE):
        rows = slice(at * slots, (at + 1) * slots)
        picker = half(chosen[at].astype(jnp.float32))
        routed_part, back_part = half(mul_tn(picker, routed[rows])), half(mul_tn(picker, back[rows]))

        @pl.when(expert == 0)
        def _():
            routed_ref[at] = routed_part
            back_ref[at] = back_part

        @pl.when(expert > 0)
        def _():
            routed_ref[at] = routed_ref[at] + routed_part
            back_ref[at] = back_ref[at] + back_part

        dgate_ref[at, pl.ds(expert, 1), :] = jnp.sum(
            jnp.where(chosen[at], dgate[rows], 0.0), axis=0, keepdims=True
        )

    @pl.when(tile == last)
    def _():
        height = ready_s.shape[0]
        for sums, target in ((sum_first_s, grad_first_ref), (sum_down_s, grad_down_ref)):
            width = sums.shape[2]
            for at in range(sums.shape[1] // height):
                some = pl.ds(at * height, height)
                ready_s[:, :width] = half(sums[expert, some, :])
                copy = pltpu.make_async_copy(
                    ready_s.at[:, pl.ds(0, width)], target.at[expert, some, :], sem
                )
                copy.start()
                copy.wait()


def routed_experts(rank, gate, rows, grads, first, down, slots):
    blocks, held, tokens = rank.shape
    features, hidden = first.shape[1], down.shape[1]
    some = lambda t, e: (t, 0, 0)
    table = pl.BlockSpec((TILE, held, tokens), some)
    wide = pl.BlockSpec((TILE, tokens, features), some)
    once = pl.BlockSpec((TILE, tokens, features), some, pipeline_mode=pl.Buffered(1))
    anywhere = pl.BlockSpec(memory_space=pl.ANY)
    return pl.pallas_call(
        experts_kernel,
        grid=(blocks // TILE, held),
        in_specs=[
            table,
            table,
            once,
            once,
            pl.BlockSpec((1, features, 2 * hidden), lambda t, e: (e, 0, 0)),
            pl.BlockSpec((1, hidden, features), lambda t, e: (e, 0, 0)),
        ],
        out_specs=[wide, wide, table, anywhere, anywhere],
        out_shape=[
            bf16_out(blocks, tokens, features),
            bf16_out(blocks, tokens, features),
            f32_out(blocks, held, tokens),
            bf16_out(held, features, 2 * hidden),
            bf16_out(held, hidden, features),
        ],
        scratch_shapes=[
            pltpu.VMEM((TILE * slots, features), jnp.bfloat16),
            pltpu.VMEM((TILE * slots, features), jnp.bfloat16),
            pltpu.VMEM((held, features, 2 * hidden), jnp.float32),
            pltpu.VMEM((held, hidden, features), jnp.float32),
            pltpu.VMEM((256, features), jnp.bfloat16),
            pltpu.SemaphoreType.DMA,
        ],
        cost_estimate=BRIEF,
        compiler_params=pltpu.CompilerParams(
            vmem_limit_bytes=62 * 1024 * 1024, dimension_semantics=("arbitrary", "arbitrary")
        ),
    )(rank, gate, rows, grads, first, down)


def on_device(
    layer_in,
    seg_ids,
    route_ids,
    out_grad,
    norm_in,
    w_in,
    conv_w,
    conv_b,
    dt_bias,
    a_log,
    d_skip,
    norm_gate,
    w_out,
    norm_mid,
    w_router,
    w_sgate,
    w_sup,
    w_sdown,
    e_gate,
    e_up,
    e_down,
):
    f32, bf16 = jnp.float32, jnp.bfloat16
    row_count, d_model = layer_in.shape[1:]
    devices = lax.axis_size("dp") * lax.axis_size("ctx")
    ctx_place = lax.axis_index("ctx")
    held = EXP_DEV // 2
    first_expert = lax.axis_index("dp") * EXP_DEV + lax.div(ctx_place, 2) * held
    blocks = lax.axis_size("dp") * 2
    expert_count = EXP_DEV * lax.axis_size("dp")
    capacity = row_count * TOP * 5 // (expert_count * 4)
    slots = -(-capacity // 64) * 64
    tap_count = conv_w.shape[0]
    halo = 8

    small_parts = (norm_in, conv_w, conv_b, norm_gate, norm_mid, w_router)
    small_flat = jnp.concatenate([part.reshape(-1) for part in small_parts])
    small_flat = jnp.pad(small_flat, (0, 4096 - small_flat.shape[0])).reshape(32, 128)
    edge_rows = layer_in[0, row_count - halo :].reshape(-1, 128)
    width, hidden = e_gate.shape[1:]
    first_strips, down_strips = strips(width), strips(hidden)
    w_in_all, w_out_all, small_all, expert_first, expert_down = pallas_gather(
        [w_in, w_out, jnp.concatenate([small_flat, edge_rows])],
        [(16, 1664), (16, 1536), (128, 128)],
        1,
        ahead=6,
        more=[e_gate, e_up, e_down],
        more_shapes=[(held, d_model, 2 * hidden), (held, hidden, d_model)],
        moves=[
            (part, 0, other_strip(start), columns(quarter(1, width, 0, start), part * hidden, hidden), 2)
            for start in first_strips
            for part in range(2)
        ]
        + [(2, 1, other_strip(start), quarter(2, width, 0, start), 2) for start in down_strips],
    )
    pair_at = lax.div(ctx_place, 2)
    sent = nothing(w_in_all)
    shared_all = lax.all_gather(
        (jnp.concatenate([w_sgate, w_sup], axis=1).astype(f32) + sent).astype(bf16), BOTH, axis=0
    )
    sdown_all = lax.all_gather((w_sdown.astype(f32) + sent).astype(bf16), BOTH, axis=0)
    own_first = jnp.concatenate([held_experts(e_gate, False), held_experts(e_up, False)], axis=2)
    expert_first = with_quarter(expert_first, own_first, 1)
    expert_down = with_quarter(expert_down, held_experts(e_down, False), 2)
    edge_all = small_all[:, small_flat.shape[0] :].reshape(devices, halo, d_model)
    small_all = small_all[:, : small_flat.shape[0]].reshape(devices, 4096)
    taken, pieces = 0, []
    for part in small_parts:
        pieces.append(small_all[:, taken : taken + part.size])
        taken += part.size
    gain_in = pieces[0].reshape(-1).astype(f32)
    conv_weight = jnp.moveaxis(pieces[1].reshape(devices, tap_count, -1), 0, 1).reshape(tap_count, CONV).astype(f32)
    conv_bias = pieces[2].reshape(-1).astype(f32)
    gain_gate = pieces[3].reshape(-1).astype(f32)
    gain_mid = pieces[4].reshape(-1).astype(f32)
    router_weight = pieces[5].reshape(d_model, expert_count)
    weight_in = w_in_all.reshape(d_model, PROJ)
    weight_out = w_out_all.reshape(DI, d_model)
    shared_weight = shared_all.reshape(d_model, -1)
    sdown_weight = sdown_all.reshape(-1, d_model)
    named, ranks = route_table(route_ids[0], expert_count)

    own_in = layer_in[0]
    place = lax.axis_index("dp") * lax.axis_size("ctx") + ctx_place
    edge_in = lax.dynamic_index_in_dim(edge_all, jnp.maximum(place - 1, 0), 0, keepdims=False)
    edge_in = jnp.where(ctx_place > 0, edge_in, jnp.zeros_like(edge_in))
    input_f = jnp.concatenate(
        [own_in, jnp.zeros((128 - halo, d_model), bf16), edge_in], axis=0
    ).astype(f32)
    normed = scaled_norm(input_f, gain_in).astype(bf16)
    projected = lax.dot_general(
        weight_in, normed, (((0,), (1,)), ((), ())), preferred_element_type=f32
    )
    seg_pad = jnp.concatenate([jnp.full((tap_count - 1,), -1, jnp.int32), seg_ids[0]])
    seg_window = lax.dynamic_slice_in_dim(
        seg_pad, ctx_place * row_count, row_count + tap_count - 1, 0
    )
    taps = jnp.concatenate(
        [conv_weight.T, conv_bias[:, None], jnp.zeros((CONV, 7 - tap_count), f32)], axis=1
    )
    dt_raw = projected[DI + CONV :, :row_count]
    dt_pos, decay, cumul, cumul_col, flags, seg_col, masks, through, skip_rows = mixer_rows(
        dt_raw, dt_bias, a_log, d_skip, seg_window, tap_count
    )
    bc_pre, pre, state_out = mixer_forward_states(projected, taps, masks, dt_pos, cumul, flags)
    passed = jnp.broadcast_to(jnp.repeat(through, HEAD)[:, None], (DI, 8))
    gain_col = jnp.broadcast_to(gain_gate[:, None], (DI, 8))
    y_heads, state_in, gated, gate_scale = mixer_forward(
        state_out, passed, pre, bc_pre, dt_pos, cumul, cumul_col, skip_rows, flags, seg_col, projected, gain_col, 7
    )

    mixed = times_rows(gated, weight_out)
    resid_mid = own_in.astype(f32) + mixed
    normed_mid_f, pull_mid = jax.vjp(scaled_norm, resid_mid, gain_mid)
    normed_mid = normed_mid_f.astype(bf16)
    logits = jnp.dot(normed_mid, router_weight, preferred_element_type=f32)
    top_logit = jnp.max(jnp.where(named, logits, -jnp.inf), axis=-1, keepdims=True)
    powers = jnp.where(named, jnp.exp(jnp.where(named, logits - top_logit, 0.0)), 0.0)
    gates = powers / jnp.sum(powers, axis=-1, keepdims=True)
    gate_high, gate_low = two_parts(gates)
    side = jnp.concatenate(
        [gate_high, gate_low, ranks.astype(bf16), jnp.zeros((row_count, 128 - 3 * expert_count), bf16)],
        axis=1,
    )
    token_rows, grad_rows, side_all, expert_first, expert_down = pallas_gather(
        [normed_mid, out_grad[0], side],
        [(16, 1536), (16, 1536), (128, 128)],
        3,
        line=(2,),
        ahead=4,
        more=[expert_first, expert_down],
        moves=[
            (part, part, quarter(axis, width, 2 * far, start), quarter(axis, width, 2 * far, start), 1)
            for far in (0, 1)
            for part, axis, starts in ((0, 1, first_strips), (1, 2, down_strips))
            for start in starts
        ],
    )
    normed_later = (normed_mid.astype(f32) + nothing(token_rows)).astype(bf16)
    shared_hidden = jnp.dot(normed_later, shared_weight, preferred_element_type=f32)
    shared_gate, shared_up = jnp.split(shared_hidden, 2, axis=1)
    shared_act = (jax.nn.silu(shared_gate) * shared_up).astype(bf16)
    shared_out = jnp.dot(shared_act, sdown_weight, preferred_element_type=f32)

    def owned(grad):
        return grad.astype(bf16).reshape(devices, -1, grad.shape[-1])

    mine_of = partial(lax.dynamic_slice_in_dim, slice_size=held, axis=2)
    my_gate = mine_of(side_all, first_expert).astype(f32) + mine_of(
        side_all, first_expert + expert_count
    ).astype(f32)
    my_rank = mine_of(side_all, first_expert + 2 * expert_count).astype(f32)
    my_gate, my_rank = jnp.swapaxes(my_gate, 1, 2), jnp.swapaxes(my_rank, 1, 2)
    routed_rows, grad_slot_rows, token_dgate, grad_first, grad_down = routed_experts(
        my_rank, my_gate, token_rows, grad_rows, expert_first, expert_down, slots
    )
    experts = jnp.arange(held, dtype=jnp.int32)[:, None] + first_expert
    dgate_table = jnp.sum(
        token_dgate[..., None] * (jnp.arange(expert_count) == experts).astype(f32)[:, None, :], axis=1
    )
    dgate_high, dgate_low = two_parts(dgate_table)
    back_side = jnp.concatenate(
        [dgate_high, dgate_low, jnp.zeros((blocks, row_count, 128 - 2 * expert_count), bf16)], axis=-1
    )
    grad_shared_out = out_grad[0]
    grad_w_sdown = times_rows(shared_act, grad_shared_out)
    grad_shared_act = times_back(grad_shared_out, sdown_weight)
    grad_sgate = (grad_shared_act * shared_up * silu_slope(shared_gate)).astype(bf16)
    grad_sup = (grad_shared_act * jax.nn.silu(shared_gate)).astype(bf16)
    grad_shared = jnp.concatenate([grad_sgate, grad_sup], axis=1)
    grad_w_shared = times_rows(normed_mid, grad_shared)
    back_rows, back_side, sum_sdown, sum_shared, beside_first, beside_down, routed_rows = pallas_reduce(
        [grad_slot_rows, back_side, owned(grad_w_sdown), owned(grad_w_shared)],
        [(16, 1536), (128, 128), (16, 1536), (16, 1024)],
        4,
        lines=[(2,), (2,), (1, 2, 3), (1, 2, 3)],
        more=[grad_first, grad_down, routed_rows],
        more_shapes=[(2, held, width, 2 * hidden), (2, held, hidden, width), routed_rows.shape],
        same=(2,),
        moves=[
            (part, part, quarter(axis, width, 2 * far + 1, start), strip(start, far), 1)
            for far in (1, 0)
            for part, axis, starts in ((0, 1, first_strips), (1, 2, down_strips))
            for start in starts
        ],
    )
    routed = lax.psum_scatter(
        routed_rows.reshape(-1, 2, row_count, d_model), "dp", scatter_dimension=0
    )
    routed = with_layout_constraint(routed, Layout(major_to_minor=(0, 1, 2)))
    routed_own = lax.dynamic_index_in_dim(routed, pair_at, 0, keepdims=False)
    routed_far = lax.dynamic_index_in_dim(routed, 1 - pair_at, 0, keepdims=False)
    near_first, near_down = (
        own_quarter(whole, axis, 0).astype(f32) + beside[0].astype(f32)
        for whole, beside, axis in ((grad_first, beside_first, 1), (grad_down, beside_down, 2))
    )

    grad_top = out_grad[0].astype(f32)
    grad_mid_shared = times_back(grad_shared, shared_weight)
    grad_gates = back_side[:, :expert_count] + back_side[:, expert_count : 2 * expert_count]
    grad_pick = gates * (grad_gates - jnp.sum(gates * grad_gates, axis=-1, keepdims=True))
    grad_logits = grad_pick.astype(bf16)
    grad_w_router = times_rows(normed_mid, grad_logits)
    grad_mid = (
        back_rows + grad_mid_shared + times_back(grad_logits, router_weight)
    )
    grad_resid_part, grad_gain_mid = pull_mid(grad_mid)
    grad_resid = grad_top + grad_resid_part
    grad_mixed = grad_resid.astype(bf16)

    grad_w_out = jnp.dot(gated, grad_mixed, preferred_element_type=f32)
    grad_gated = times_back(weight_out, grad_mixed)
    scaled_u = y_heads * jax.nn.silu(projected[:DI, :row_count])
    scale_row = gate_scale[:1]
    along = jnp.sum(grad_gated * gain_gate[:, None] * scaled_u, axis=0, keepdims=True)
    grad_gain_gate = jnp.sum(grad_gated * scaled_u * scale_row, axis=1)
    gate_rows = jnp.concatenate(
        [scale_row, scale_row * scale_row * scale_row * along * (1.0 / DI), jnp.zeros((6, row_count), f32)]
    )
    grad_y, grad_z, grad_state_local = mixer_back_gate(
        y_heads, projected, grad_gated, gain_col, gate_rows, bc_pre, cumul, flags
    )
    grad_scaled, grad_state_out, grad_cum_inner, grad_skip, grad_bc_inner = mixer_back_inner(
        grad_state_local, passed, pre, grad_y, bc_pre, dt_pos, cumul, cumul_col, flags, seg_col, 8
    )
    far_first, far_down = (
        half(own_quarter(whole, axis, 2).astype(f32) + beside[1].astype(f32))
        for whole, beside, axis in ((grad_first, beside_first, 1), (grad_down, beside_down, 2))
    )
    grad_x, grad_taps_x, grad_dt, grad_cum_join, grad_last, grad_bc_join = mixer_back_join(
        grad_scaled, grad_y, pre, projected, taps, masks, state_in, grad_state_out,
        bc_pre, dt_pos, cumul, skip_rows, flags,
    )
    grad_bc, grad_taps_bc = mixer_back_conv(
        grad_bc_inner + grad_bc_join, bc_pre, projected, taps, masks
    )
    grad_cum = grad_cum_inner + grad_cum_join
    grad_last = grad_last[:, 0] + through * grad_last[:, 1]
    lower = jnp.tril(jnp.ones((row_count, row_count), f32))
    grad_decay = jnp.dot(grad_cum, lower, precision=lax.Precision.HIGHEST) + grad_last[:, None]
    grad_dt = grad_dt - jnp.exp(a_log)[:, None] * grad_decay
    grad_raw = grad_dt * jax.nn.sigmoid(dt_raw + dt_bias[:, None])
    grad_taps = jnp.concatenate([grad_taps_x, grad_taps_bc])
    grad_conv_w, grad_conv_b = grad_taps[:, :tap_count].T, grad_taps[:, tap_count]
    head_sums_all = jnp.concatenate(
        [jnp.sum(grad_raw, axis=1), jnp.sum(decay * grad_decay, axis=1), jnp.sum(grad_skip, axis=1)]
    )
    grad_rest = jnp.concatenate(
        [
            grad_bc,
            jnp.pad(grad_raw.astype(bf16), ((0, WIDE - 2 * STATE - HEADS), (0, 128))),
        ]
    )
    normed_t = normed.T
    grad_w_in, grad_normed, routed_far = proj_back(
        normed_t, weight_in, grad_z, grad_x, grad_rest, routed_far, 9
    )
    grad_normed = grad_normed.T
    edge_grad = from_behind(grad_normed[row_count + 128 - halo :], "ctx", -1)
    grad_normed = jnp.concatenate(
        [grad_normed[: row_count - halo], grad_normed[row_count - halo : row_count] + edge_grad],
        axis=0,
    )
    _, pull_in = jax.vjp(scaled_norm, own_in.astype(f32), gain_in)
    grad_input_part, grad_gain_in = pull_in(grad_normed)
    grad_in = (grad_resid + grad_input_part)[None]

    small_grads = jnp.concatenate(
        [
            grad_gain_in.reshape(devices, -1),
            jnp.moveaxis(grad_conv_w.reshape(tap_count, devices, -1), 1, 0).reshape(devices, -1),
            grad_conv_b.reshape(devices, -1),
            grad_gain_gate.reshape(devices, -1),
            grad_gain_mid.reshape(devices, -1),
            grad_w_router.reshape(devices, -1),
            jnp.broadcast_to(head_sums_all, (devices, 3 * HEADS)),
        ],
        axis=1,
    )
    small_grads = jnp.pad(small_grads, ((0, 0), (0, 3072 - small_grads.shape[1])))
    sum_in, sum_out, sum_small, far_first, far_down = pallas_reduce(
        [owned(grad_w_in), owned(grad_w_out), small_grads.reshape(devices, 24, 128)],
        [(16, 1664), (16, 1536), (24, 128)],
        6,
        ahead=3,
        more=[far_first, far_down],
        more_shapes=[far_first.shape, far_down.shape],
        moves=[
            (part, part, strip(start), strip(start), 2)
            for part, starts in ((0, first_strips), (1, down_strips))
            for start in starts
        ],
    )
    summed = nothing(sum_small)
    layer_out = (resid_mid + shared_out + routed_own.astype(f32) + routed_far.astype(f32) + summed).astype(bf16)[None]
    sum_sgate, sum_sup = jnp.split(sum_shared, 2, axis=1)
    grad_e_gate = expert_owners(near_first[..., :hidden], far_first[..., :hidden], summed)
    grad_e_up = expert_owners(near_first[..., hidden:], far_first[..., hidden:], summed)
    grad_e_down = expert_owners(near_down, far_down, summed)
    sum_small = sum_small.reshape(-1)
    taken, mine = 0, []
    for part in small_parts:
        mine.append(sum_small[taken : taken + part.size].reshape(part.shape))
        taken += part.size
    return (
        layer_out,
        grad_in,
        mine[0],
        sum_in,
        mine[1],
        mine[2],
        sum_small[taken : taken + HEADS],
        sum_small[taken + HEADS : taken + 2 * HEADS],
        sum_small[taken + 2 * HEADS : taken + 3 * HEADS],
        mine[3],
        sum_out,
        mine[4],
        mine[5],
        sum_sgate,
        sum_sup,
        sum_sdown,
        grad_e_gate,
        grad_e_up,
        grad_e_down,
    )


def solution(mesh):
    in_specs = (
        P("dp", "ctx", None),
        P("dp", None),
        P("dp", "ctx", None),
        P("dp", "ctx", None),
        P(("dp", "ctx")),
        P(("dp", "ctx"), None),
        P(None, ("dp", "ctx")),
        P(("dp", "ctx")),
        P(),
        P(),
        P(),
        P(("dp", "ctx")),
        P(("dp", "ctx"), None),
        P(("dp", "ctx")),
        P(("dp", "ctx"), None),
        P(("dp", "ctx"), None),
        P(("dp", "ctx"), None),
        P(("dp", "ctx"), None),
        P("dp", "ctx", None),
        P("dp", "ctx", None),
        P("dp", None, "ctx"),
    )
    out_specs = (
        P("dp", "ctx", None),
        P("dp", "ctx", None),
        P(("dp", "ctx")),
        P(("dp", "ctx"), None),
        P(None, ("dp", "ctx")),
        P(("dp", "ctx")),
        P(),
        P(),
        P(),
        P(("dp", "ctx")),
        P(("dp", "ctx"), None),
        P(("dp", "ctx")),
        P(("dp", "ctx"), None),
        P(("dp", "ctx"), None),
        P(("dp", "ctx"), None),
        P(("dp", "ctx"), None),
        P("dp", "ctx", None),
        P("dp", "ctx", None),
        P("dp", None, "ctx"),
    )
    one_each = mesh.shape["ctx"] == EXP_DEV and mesh.shape["dp"] == 8
    return jax.shard_map(
        on_device if one_each else on_device_general, mesh=mesh, in_specs=in_specs, out_specs=out_specs, check_vma=False
    )
```

```python
from functools import partial

import jax
import jax.numpy as jnp
from jax import lax
from jax.experimental import pallas as pl
from jax.experimental.layout import Layout, with_layout_constraint
from jax.experimental.pallas import tpu as pltpu
from jax.sharding import PartitionSpec as P

HEADS = 48
HEAD = 64
STATE = 128
TOP = 6
EXP_DEV = 4
DI = 3072
CONV = 3328
PROJ = 6448


def from_behind(value, axis, steps):
    count = lax.axis_size(axis)
    leading, last = (max(0, -steps), min(count, count - steps))
    return lax.ppermute(value, axis, [(source, source + steps) for source in range(leading, last)])


def carried_in_2(x, axis, combine, identity):
    count, mine = (lax.axis_size(axis), lax.axis_index(axis))
    everything = jax.tree.map(
        lambda part, kind: lax.all_gather(part.astype(kind), axis), x, (jnp.bfloat16, jnp.bfloat16)
    )
    start = jax.tree.map(
        lambda part, zero: jnp.broadcast_to(jnp.asarray(zero, part.dtype), part.shape), x, identity
    )

    def lap(k, before):
        reached = k < mine
        new = combine(
            before, jax.tree.map(lambda part, own: part[k].astype(own.dtype), everything, x)
        )
        return jax.tree.map(lambda a, b: jnp.where(reached, a, b), new, before)

    return lax.fori_loop(0, count, lap, start)


def carried_in_3(x, axis, combine, identity):
    count, mine = (lax.axis_size(axis), lax.axis_index(axis))
    everything = jax.tree.map(
        lambda part, kind: lax.all_gather(part.astype(kind), axis),
        x,
        jax.tree.map(lambda a: jnp.bfloat16 if a.dtype == jnp.float32 else a.dtype, x),
    )
    start = jax.tree.map(
        lambda part, zero: jnp.broadcast_to(jnp.asarray(zero, part.dtype), part.shape), x, identity
    )

    def lap(k, before):
        at = count - 1 - k
        reached = at > mine
        new = combine(
            before, jax.tree.map(lambda part, own: part[at].astype(own.dtype), everything, x)
        )
        return jax.tree.map(lambda a, b: jnp.where(reached, a, b), new, before)

    return lax.fori_loop(0, count, lap, start)


def for_sending(x):
    return jax.tree.map(lambda a: a.astype(jnp.bfloat16) if a.dtype == jnp.float32 else a, x)


def normalize(value):
    return value * lax.rsqrt(jnp.mean(value * value, axis=-1, keepdims=True) + 1e-05)


def scaled_norm(value, gain):
    return normalize(value) * gain


def gate_norm(y_heads, z_part, gain):
    joined = y_heads.reshape(z_part.shape) * jax.nn.silu(z_part)
    return normalize(joined) * gain


def silu_slope(value):
    squashed = jax.nn.sigmoid(value)
    return squashed * (1.0 + value * (1.0 - squashed))


def conv_apply(padded, weight, bias, seg_pad):
    tap_count = weight.shape[0]
    length = padded.shape[1] - tap_count + 1
    current = seg_pad[:, tap_count - 1 :]
    summed = bias + jnp.zeros(padded[:, tap_count - 1 :].shape, jnp.float32)
    for offset in range(tap_count):
        matches = (seg_pad[:, offset : offset + length] == current).astype(jnp.float32)
        summed = summed + weight[offset] * padded[:, offset : offset + length] * matches[..., None]
    return jax.nn.silu(summed)


def split_blocks(value, count):
    shaped = value.reshape((value.shape[0], count, value.shape[1] // count) + value.shape[2:])
    return jnp.moveaxis(shaped, 1, 0)


def block_step(carried_in, pieces):
    memory, previous = carried_in
    x_heads, b_mat, c_mat, dt_pos, decay, segment_ids = pieces
    cumul = jnp.cumsum(decay, axis=1)
    places = jnp.arange(segment_ids.shape[1])
    causal = places[:, None] >= places[None, :]
    linked = ((segment_ids[:, :, None] == segment_ids[:, None, :]) & causal[None])[..., None]
    spread = cumul[:, :, None, :] - cumul[:, None, :, :]
    weights = jnp.where(linked, jnp.exp(jnp.where(linked, spread, 0.0)), 0.0)
    inner = jnp.einsum("gtn,gsn->gts", c_mat, b_mat, precision=lax.Precision.HIGHEST)
    weights = weights * inner[..., None] * dt_pos[:, None, :, :]
    output = jnp.einsum("gtsh,gshp->gthp", weights, x_heads, precision=lax.Precision.HIGHEST)
    keeps = (segment_ids == previous[:, None]).astype(jnp.float32)
    reach = jnp.exp(cumul) * keeps[..., None]
    output = (
        output
        + jnp.einsum("gtn,ghpn->gthp", c_mat, memory, precision=lax.Precision.HIGHEST)
        * reach[..., None]
    )
    latest = segment_ids[:, -1]
    tails = (
        jnp.exp(cumul[:, -1:, :] - cumul)
        * (segment_ids == latest[:, None]).astype(jnp.float32)[..., None]
        * dt_pos
    )
    through = jnp.exp(cumul[:, -1, :]) * (latest == previous).astype(jnp.float32)[:, None]
    memory = memory * through[..., None, None] + jnp.einsum(
        "gsh,gshp,gsn->ghpn", tails, x_heads, b_mat, precision=lax.Precision.HIGHEST
    )
    return ((memory, latest), output)


def scan_blocks(x_heads, b_mat, c_mat, dt_pos, decay, segment_ids, memory, previous):
    length = segment_ids.shape[1]
    count = length // min(128, length)
    inputs = tuple(
        (
            split_blocks(value, count)
            for value in (x_heads, b_mat, c_mat, dt_pos, decay, segment_ids)
        )
    )
    (memory, latest), outputs = lax.scan(jax.checkpoint(block_step), (memory, previous), inputs)
    return (jnp.moveaxis(outputs, 0, 1).reshape(x_heads.shape), memory)


def part_local(x_heads, b_mat, c_mat, dt_raw, dt_bias, a_log, d_skip, segment_ids, previous):
    dt_pos = jax.nn.softplus(dt_raw + dt_bias)
    decay = -jnp.exp(a_log) * dt_pos
    zero_state = jnp.zeros((x_heads.shape[0], HEADS, HEAD, STATE), jnp.float32)
    mixed_heads, final_state = scan_blocks(
        x_heads, b_mat, c_mat, dt_pos, decay, segment_ids, zero_state, previous
    )
    y_local = mixed_heads + d_skip[:, None] * x_heads
    through = (
        jnp.exp(jnp.sum(decay, axis=1))
        * (segment_ids[:, -1] == previous).astype(jnp.float32)[:, None]
    )
    return (y_local, final_state, through)


def part_carry(c_mat, dt_raw, dt_bias, a_log, state_in, segment_ids, previous):
    dt_pos = jax.nn.softplus(dt_raw + dt_bias)
    cumul = jnp.cumsum(-jnp.exp(a_log) * dt_pos, axis=1)
    keeps = (segment_ids == previous[:, None]).astype(jnp.float32)
    reach = jnp.exp(cumul) * keeps[..., None]
    return (
        jnp.einsum("gtn,ghpn->gthp", c_mat, state_in, precision=lax.Precision.HIGHEST)
        * reach[..., None]
    )


def carry_forward(earlier, later):
    return (earlier[0] * later[0], later[0][..., None, None] * earlier[1] + later[1])


def carry_backward(earlier, later):
    return (earlier[0] * later[0], later[1] + later[0][..., None, None] * earlier[1])


def route_slots(flat_routes, expert_count, capacity):
    blocks = flat_routes.shape[0]
    onehot = (flat_routes[..., None] == jnp.arange(expert_count, dtype=jnp.int32)).astype(jnp.int32)
    ranks = jnp.sum((jnp.cumsum(onehot, axis=1) - onehot) * onehot, axis=-1)
    spots = (
        flat_routes * (blocks * capacity)
        + jnp.arange(blocks, dtype=jnp.int32)[:, None] * capacity
        + ranks
    )
    return spots


def times_rows(left, right):
    return lax.dot_general(
        left, right, (((0,), (0,)), ((), ())), preferred_element_type=jnp.float32
    )


def times_back(left, right):
    return lax.dot_general(
        left, right, (((1,), (1,)), ((), ())), preferred_element_type=jnp.float32
    )


def on_device_general(
    layer_in,
    seg_ids,
    route_ids,
    out_grad,
    norm_in,
    w_in,
    conv_w,
    conv_b,
    dt_bias,
    a_log,
    d_skip,
    norm_gate,
    w_out,
    norm_mid,
    w_router,
    w_sgate,
    w_sup,
    w_sdown,
    e_gate,
    e_up,
    e_down,
):
    seq_count, row_count, d_model = layer_in.shape
    token_count = seq_count * row_count
    tap_count = conv_w.shape[0]
    ctx_place = lax.axis_index("ctx")
    expert_count = EXP_DEV * lax.axis_size("dp")
    capacity = row_count * TOP * 5 // (expert_count * 4)
    dense_set = (
        lax.all_gather(norm_in, ("dp", "ctx"), axis=0, tiled=True),
        lax.all_gather(w_in, ("dp", "ctx"), axis=0, tiled=True),
        lax.all_gather(conv_w, ("dp", "ctx"), axis=1, tiled=True),
        lax.all_gather(conv_b, ("dp", "ctx"), axis=0, tiled=True),
        lax.all_gather(norm_gate, ("dp", "ctx"), axis=0, tiled=True),
        lax.all_gather(w_out, ("dp", "ctx"), axis=0, tiled=True),
        lax.all_gather(norm_mid, ("dp", "ctx"), axis=0, tiled=True),
        lax.all_gather(w_router, ("dp", "ctx"), axis=0, tiled=True),
        lax.all_gather(w_sgate, ("dp", "ctx"), axis=0, tiled=True),
        lax.all_gather(w_sup, ("dp", "ctx"), axis=0, tiled=True),
        lax.all_gather(w_sdown, ("dp", "ctx"), axis=0, tiled=True),
    )
    (
        gain_in,
        weight_in,
        conv_weight,
        conv_bias,
        gain_gate,
        weight_out,
        gain_mid,
        router_weight,
        sgate_weight,
        sup_weight,
        sdown_weight,
    ) = dense_set
    expert_gate, expert_up, expert_down = (
        lax.all_gather(e_gate, "ctx", axis=1, tiled=True),
        lax.all_gather(e_up, "ctx", axis=1, tiled=True),
        lax.all_gather(e_down, "ctx", axis=2, tiled=True),
    )
    input_f = layer_in.astype(jnp.float32)
    normed_f, pull_in = jax.vjp(scaled_norm, input_f, gain_in.astype(jnp.float32))
    normed = normed_f.astype(jnp.bfloat16).reshape(token_count, d_model)
    projected = jnp.dot(normed, weight_in, preferred_element_type=jnp.float32).reshape(
        seq_count, row_count, PROJ
    )
    z_part = projected[..., :DI]
    xbc_part = projected[..., DI : DI + CONV]
    dt_raw = projected[..., DI + CONV :]
    edge_rows = from_behind(
        xbc_part[:, row_count - tap_count + 1 :, :].astype(jnp.bfloat16), "ctx", 1
    ).astype(jnp.float32)
    seg_pad = jnp.concatenate(
        [jnp.full((seq_count, tap_count - 1), -1, jnp.int32), seg_ids], axis=1
    )
    seg_window = lax.dynamic_slice_in_dim(
        seg_pad, ctx_place * row_count, row_count + tap_count - 1, 1
    )
    seg_now = seg_window[:, tap_count - 1 :]
    seg_before = seg_window[:, tap_count - 2]
    padded = jnp.concatenate([edge_rows, xbc_part], axis=1)
    conv_out, pull_conv = jax.vjp(
        partial(conv_apply, seg_pad=seg_window),
        padded,
        conv_weight.astype(jnp.float32),
        conv_bias.astype(jnp.float32),
    )
    x_heads = conv_out[..., :DI].reshape(seq_count, row_count, HEADS, HEAD)
    b_mat = conv_out[..., DI : DI + STATE]
    c_mat = conv_out[..., DI + STATE :]
    local_piece = partial(part_local, segment_ids=seg_now, previous=seg_before)
    (y_local, state_out, through), pull_local = jax.vjp(
        local_piece, x_heads, b_mat, c_mat, dt_raw, dt_bias, a_log, d_skip
    )
    carried = carried_in_2(
        (through, state_out),
        "ctx",
        carry_forward,
        (jnp.ones_like(through), jnp.zeros_like(state_out)),
    )
    state_in = carried[1]
    carry_piece = partial(part_carry, segment_ids=seg_now, previous=seg_before)
    y_carry, pull_carry = jax.vjp(carry_piece, c_mat, dt_raw, dt_bias, a_log, state_in)
    gated_f, pull_gate = jax.vjp(
        gate_norm, y_local + y_carry, z_part, gain_gate.astype(jnp.float32)
    )
    gated = gated_f.astype(jnp.bfloat16).reshape(token_count, DI)
    mixed = jnp.dot(gated, weight_out, preferred_element_type=jnp.float32)
    resid_mid = input_f.reshape(token_count, d_model) + mixed
    normed_mid_f, pull_mid = jax.vjp(scaled_norm, resid_mid, gain_mid.astype(jnp.float32))
    normed_mid = normed_mid_f.astype(jnp.bfloat16)
    logits = jnp.dot(normed_mid, router_weight, preferred_element_type=jnp.float32)
    route_flat = route_ids.reshape(token_count, TOP)
    gates = jax.nn.softmax(jnp.take_along_axis(logits, route_flat, axis=1), axis=-1)
    shared_gate = jnp.dot(normed_mid, sgate_weight, preferred_element_type=jnp.float32)
    shared_up = jnp.dot(normed_mid, sup_weight, preferred_element_type=jnp.float32)
    shared_act = (jax.nn.silu(shared_gate) * shared_up).astype(jnp.bfloat16)
    shared_out = jnp.dot(shared_act, sdown_weight, preferred_element_type=jnp.float32)
    slot_ids = route_slots(route_ids.reshape(seq_count, row_count * TOP), expert_count, capacity)
    assigned = jnp.arange(token_count * TOP, dtype=jnp.int32)
    owners = (
        jnp.full((expert_count * seq_count * capacity,), token_count * TOP, jnp.int32)
        .at[slot_ids.reshape(-1)]
        .set(assigned)
    )
    token_of = owners // TOP
    rows_pad = jnp.concatenate([normed_mid, jnp.zeros((1, d_model), jnp.bfloat16)], axis=0)
    outgoing = rows_pad[token_of].reshape(expert_count, seq_count * capacity, d_model)
    incoming = lax.all_to_all(outgoing, "dp", split_axis=0, concat_axis=1, tiled=True)
    hidden_gate = jnp.einsum(
        "erd,edf->erf", incoming, expert_gate, preferred_element_type=jnp.float32
    )
    hidden_up = jnp.einsum("erd,edf->erf", incoming, expert_up, preferred_element_type=jnp.float32)
    hidden_act = (jax.nn.silu(hidden_gate) * hidden_up).astype(jnp.bfloat16)
    expert_out = jnp.einsum(
        "erf,efd->erd", hidden_act, expert_down, preferred_element_type=jnp.float32
    ).astype(jnp.bfloat16)
    returned = lax.all_to_all(expert_out, "dp", split_axis=1, concat_axis=0, tiled=True)
    slot_flat = slot_ids.reshape(token_count, TOP)
    picked = returned.reshape(-1, d_model)[slot_flat]
    routed = jnp.sum(gates[..., None] * picked, axis=1)
    layer_out = (
        (resid_mid + shared_out + routed)
        .astype(jnp.bfloat16)
        .reshape(seq_count, row_count, d_model)
    )
    grad_top = out_grad.astype(jnp.float32).reshape(token_count, d_model)
    grad_gates = jnp.sum(picked * grad_top[:, None, :], axis=-1)
    grad_pick = gates * (grad_gates - jnp.sum(gates * grad_gates, axis=-1, keepdims=True))
    expert_ids = jnp.arange(expert_count, dtype=jnp.int32)
    grad_logits = jnp.sum(
        grad_pick[..., None] * (route_flat[..., None] == expert_ids).astype(jnp.float32), axis=1
    ).astype(jnp.bfloat16)
    gates_pad = jnp.concatenate([gates.reshape(-1), jnp.zeros((1,), jnp.float32)])
    grad_pad = jnp.concatenate([grad_top, jnp.zeros((1, d_model), jnp.float32)], axis=0)
    grad_slots = (
        (gates_pad[owners][:, None] * grad_pad[token_of])
        .astype(jnp.bfloat16)
        .reshape(expert_count, seq_count * capacity, d_model)
    )
    grad_arrived = lax.all_to_all(grad_slots, "dp", split_axis=0, concat_axis=1, tiled=True)
    grad_act = jnp.einsum(
        "erd,efd->erf", grad_arrived, expert_down, preferred_element_type=jnp.float32
    )
    grad_e_down = jnp.einsum(
        "erf,erd->efd", hidden_act, grad_arrived, preferred_element_type=jnp.float32
    )
    grad_hgate = (grad_act * hidden_up * silu_slope(hidden_gate)).astype(jnp.bfloat16)
    grad_hup = (grad_act * jax.nn.silu(hidden_gate)).astype(jnp.bfloat16)
    grad_e_gate = jnp.einsum(
        "erd,erf->edf", incoming, grad_hgate, preferred_element_type=jnp.float32
    )
    grad_e_up = jnp.einsum("erd,erf->edf", incoming, grad_hup, preferred_element_type=jnp.float32)
    grad_incoming = jnp.einsum(
        "erf,edf->erd", grad_hgate, expert_gate, preferred_element_type=jnp.float32
    )
    grad_incoming = (
        grad_incoming
        + jnp.einsum("erf,edf->erd", grad_hup, expert_up, preferred_element_type=jnp.float32)
    ).astype(jnp.bfloat16)
    grad_returned = lax.all_to_all(grad_incoming, "dp", split_axis=1, concat_axis=0, tiled=True)
    grad_routed = jnp.sum(grad_returned.reshape(-1, d_model)[slot_flat], axis=1, dtype=jnp.float32)
    dense_set = (
        lax.all_gather(norm_in, ("dp", "ctx"), axis=0, tiled=True),
        lax.all_gather(w_in, ("dp", "ctx"), axis=0, tiled=True),
        lax.all_gather(conv_w, ("dp", "ctx"), axis=1, tiled=True),
        lax.all_gather(conv_b, ("dp", "ctx"), axis=0, tiled=True),
        lax.all_gather(norm_gate, ("dp", "ctx"), axis=0, tiled=True),
        lax.all_gather(w_out, ("dp", "ctx"), axis=0, tiled=True),
        lax.all_gather(norm_mid, ("dp", "ctx"), axis=0, tiled=True),
        lax.all_gather(w_router, ("dp", "ctx"), axis=0, tiled=True),
        lax.all_gather(w_sgate, ("dp", "ctx"), axis=0, tiled=True),
        lax.all_gather(w_sup, ("dp", "ctx"), axis=0, tiled=True),
        lax.all_gather(w_sdown, ("dp", "ctx"), axis=0, tiled=True),
    )
    (
        gain_in,
        weight_in,
        conv_weight,
        conv_bias,
        gain_gate,
        weight_out,
        gain_mid,
        router_weight,
        sgate_weight,
        sup_weight,
        sdown_weight,
    ) = dense_set
    grad_w_router = times_rows(normed_mid, grad_logits)
    grad_shared_out = grad_top.astype(jnp.bfloat16)
    grad_w_sdown = times_rows(shared_act, grad_shared_out)
    grad_shared_act = times_back(grad_shared_out, sdown_weight)
    grad_sgate = (grad_shared_act * shared_up * silu_slope(shared_gate)).astype(jnp.bfloat16)
    grad_sup = (grad_shared_act * jax.nn.silu(shared_gate)).astype(jnp.bfloat16)
    grad_w_sgate = times_rows(normed_mid, grad_sgate)
    grad_w_sup = times_rows(normed_mid, grad_sup)
    grad_mid = (
        grad_routed
        + times_back(grad_logits, router_weight)
        + times_back(grad_sgate, sgate_weight)
        + times_back(grad_sup, sup_weight)
    )
    grad_resid_part, grad_gain_mid = pull_mid(grad_mid)
    grad_resid = grad_top + grad_resid_part
    grad_mixed = grad_resid.astype(jnp.bfloat16)
    grad_w_out = times_rows(gated, grad_mixed)
    grad_gated = times_back(grad_mixed, weight_out).reshape(seq_count, row_count, DI)
    grad_y, grad_z, grad_gain_gate = pull_gate(grad_gated)
    grad_cmat_carry, grad_dt_carry, grad_bias_carry, grad_alog_carry, grad_state_in = pull_carry(
        grad_y
    )
    back_scan = carried_in_3(
        (through, grad_state_in),
        "ctx",
        carry_backward,
        (jnp.ones_like(through), jnp.zeros_like(grad_state_in)),
    )
    grad_state_out = back_scan[1]
    grad_through = jnp.sum(state_in * grad_state_out, axis=(2, 3))
    (
        grad_xheads,
        grad_bmat,
        grad_cmat,
        grad_dt_local,
        grad_bias_local,
        grad_alog_local,
        grad_dskip,
    ) = pull_local((grad_y, grad_state_out, grad_through))
    grad_conv_out = jnp.concatenate(
        [grad_xheads.reshape(seq_count, row_count, DI), grad_bmat, grad_cmat + grad_cmat_carry],
        axis=-1,
    )
    grad_padded, grad_conv_w, grad_conv_b = pull_conv(grad_conv_out)
    edge_grad = from_behind(for_sending(grad_padded[:, : tap_count - 1, :]), "ctx", -1)
    grad_xbc = grad_padded[:, tap_count - 1 :, :]
    grad_xbc = jnp.concatenate(
        [
            grad_xbc[:, : row_count - tap_count + 1],
            grad_xbc[:, row_count - tap_count + 1 :] + edge_grad,
        ],
        axis=1,
    )
    grad_proj = (
        jnp.concatenate([grad_z, grad_xbc, grad_dt_local + grad_dt_carry], axis=-1)
        .astype(jnp.bfloat16)
        .reshape(token_count, PROJ)
    )
    grad_w_in = times_rows(normed, grad_proj)
    grad_normed = times_back(grad_proj, weight_in).reshape(seq_count, row_count, d_model)
    grad_input_part, grad_gain_in = pull_in(grad_normed)
    grad_in = grad_resid.reshape(seq_count, row_count, d_model) + grad_input_part
    dense_grads = (
        lax.psum_scatter(grad_gain_in, ("dp", "ctx"), scatter_dimension=0, tiled=True),
        lax.psum_scatter(grad_w_in, ("dp", "ctx"), scatter_dimension=0, tiled=True),
        lax.psum_scatter(grad_conv_w, ("dp", "ctx"), scatter_dimension=1, tiled=True),
        lax.psum_scatter(grad_conv_b, ("dp", "ctx"), scatter_dimension=0, tiled=True),
        lax.psum_scatter(grad_gain_gate, ("dp", "ctx"), scatter_dimension=0, tiled=True),
        lax.psum_scatter(grad_w_out, ("dp", "ctx"), scatter_dimension=0, tiled=True),
        lax.psum_scatter(grad_gain_mid, ("dp", "ctx"), scatter_dimension=0, tiled=True),
        lax.psum_scatter(grad_w_router, ("dp", "ctx"), scatter_dimension=0, tiled=True),
        lax.psum_scatter(grad_w_sgate, ("dp", "ctx"), scatter_dimension=0, tiled=True),
        lax.psum_scatter(grad_w_sup, ("dp", "ctx"), scatter_dimension=0, tiled=True),
        lax.psum_scatter(grad_w_sdown, ("dp", "ctx"), scatter_dimension=0, tiled=True),
    )
    expert_grads = (
        lax.psum_scatter(
            grad_e_gate.astype(jnp.bfloat16), "ctx", scatter_dimension=1, tiled=True
        ).astype(jnp.float32),
        lax.psum_scatter(
            grad_e_up.astype(jnp.bfloat16), "ctx", scatter_dimension=1, tiled=True
        ).astype(jnp.float32),
        lax.psum_scatter(
            grad_e_down.astype(jnp.bfloat16), "ctx", scatter_dimension=2, tiled=True
        ).astype(jnp.float32),
    )
    head_grads = lax.psum(
        (grad_bias_local + grad_bias_carry, grad_alog_local + grad_alog_carry, grad_dskip),
        ("dp", "ctx"),
    )
    return (
        layer_out,
        grad_in,
        dense_grads[0],
        dense_grads[1],
        dense_grads[2],
        dense_grads[3],
        head_grads[0],
        head_grads[1],
        head_grads[2],
        dense_grads[4],
        dense_grads[5],
        dense_grads[6],
        dense_grads[7],
        dense_grads[8],
        dense_grads[9],
        dense_grads[10],
        expert_grads[0],
        expert_grads[1],
        expert_grads[2],
    )


GROUP = 8
WIDE = GROUP * HEAD
VMEM_MOST = 56 * 1024 * 1024
BRIEF = pl.CostEstimate(flops=1024, bytes_accessed=1024, transcendentals=0)


def spread_rows(rows):
    count, width = rows.shape
    return jnp.broadcast_to(rows[:, None, :], (count, HEAD, width)).reshape(count * HEAD, width)


def head_sums(value):
    return jnp.sum(value.reshape(GROUP, HEAD, value.shape[-1]), axis=1)


def mul_nn(left, right):
    return lax.dot_general(
        left, right, (((1,), (0,)), ((), ())), preferred_element_type=jnp.float32
    )


def mul_nt(left, right):
    return lax.dot_general(
        left, right, (((1,), (1,)), ((), ())), preferred_element_type=jnp.float32
    )


def mul_tn(left, right):
    return lax.dot_general(
        left, right, (((0,), (0,)), ((), ())), preferred_element_type=jnp.float32
    )


def half(value):
    return value.astype(jnp.bfloat16)


def call_steps(kernel, steps, ins, in_specs, outs, out_specs, scratch=(), name_id=None, micros=0):
    return pl.pallas_call(
        kernel,
        grid=(steps,),
        in_specs=in_specs,
        out_specs=out_specs,
        out_shape=outs,
        scratch_shapes=list(scratch),
        cost_estimate=pl.CostEstimate(flops=1024 + micros * 10**9, bytes_accessed=1024, transcendentals=0),
        compiler_params=pltpu.CompilerParams(
            vmem_limit_bytes=VMEM_MOST,
            dimension_semantics=("arbitrary",),
            collective_id=name_id,
            has_side_effects=name_id is not None,
        ),
    )(*ins)


def block(shape, index):
    return pl.BlockSpec(shape, index)


def whole(array):
    return pl.BlockSpec(array.shape, lambda i: (0,) * array.ndim)


def f32_out(*shape):
    return jax.ShapeDtypeStruct(shape, jnp.float32)


def bf16_out(*shape):
    return jax.ShapeDtypeStruct(shape, jnp.bfloat16)


def conv_steps(x, taps, masks):
    total = taps[:, 4:5] + taps[:, 3:4] * x * masks[0:1]
    for back in (1, 2, 3):
        total = total + taps[:, 3 - back : 4 - back] * pltpu.roll(x, back, 1) * masks[back : back + 1]
    return total


def conv_kernel(x_ref, taps_ref, masks_ref, pre_ref):
    tokens = pre_ref.shape[1]
    pre_ref[...] = conv_steps(x_ref[...], taps_ref[...], masks_ref[...])[:, :tokens]


def conv_adjoint(grad_pre, x, taps, masks):
    width = x.shape[1]
    grad_x = jnp.zeros_like(x)
    columns = []
    for back in (3, 2, 1, 0):
        part = grad_pre * masks[back : back + 1]
        moved = x if back == 0 else pltpu.roll(x, back, 1)
        columns.append(jnp.sum(part * moved, axis=1, keepdims=True))
        tap = taps[:, 3 - back : 4 - back]
        grad_x = grad_x + tap * (part if back == 0 else pltpu.roll(part, width - back, 1))
    columns.append(jnp.sum(grad_pre, axis=1, keepdims=True))
    lane = lax.broadcasted_iota(jnp.int32, (x.shape[0], 8), 1)
    packed = jnp.zeros((x.shape[0], 8), jnp.float32)
    for place, column in enumerate(columns):
        packed = jnp.where(lane == place, column, packed)
    return grad_x, packed


def conv_back_kernel(grad_ref, pre_ref, x_ref, taps_ref, masks_ref, grad_x_ref, taps_out_ref):
    grad_pre = grad_ref[...] * silu_slope(pre_ref[...])
    rest = x_ref.shape[1] - grad_pre.shape[1]
    grad_pre = jnp.concatenate([grad_pre, jnp.zeros((grad_pre.shape[0], rest), jnp.float32)], axis=1)
    grad_x, packed = conv_adjoint(grad_pre, x_ref[...], taps_ref[...], masks_ref[...])
    grad_x_ref[...] = grad_x.astype(grad_x_ref.dtype)
    taps_out_ref[...] = packed


def link_mask(seg_row, seg_col):
    count = seg_row.shape[1]
    source = lax.broadcasted_iota(jnp.int32, (count, count), 0)
    target = lax.broadcasted_iota(jnp.int32, (count, count), 1)
    linked = jnp.logical_and(source <= target, seg_row == seg_col)
    return jnp.where(linked, 0.0, -1e30)


def state_kernel(x_ref, taps_ref, masks_ref, bc_ref, dt_ref, cum_ref, flags_ref, pre_ref, state_ref):
    tokens = pre_ref.shape[1]
    pre = conv_steps(x_ref[...], taps_ref[...], masks_ref[...])[:, :tokens]
    pre_ref[...] = pre
    b_t = half(jax.nn.silu(bc_ref[:STATE, :]))
    cum = cum_ref[...]
    tail = jnp.exp(cum[:, tokens - 1 :] - cum) * flags_ref[1:2, :] * dt_ref[...]
    scaled = half(jax.nn.silu(pre) * spread_rows(tail))
    state_ref[...] = half(mul_nt(scaled, b_t))


def gate_back_kernel(
    y_ref, z_ref, grad_ref, gain_ref, rows_ref, bc_ref, cum_ref, flags_ref, grad_y_ref, grad_z_ref, grad_state_ref
):
    y, z, gain = y_ref[...], z_ref[...], gain_ref[:, 0:1]
    squashed = jax.nn.sigmoid(z)
    u = y * z * squashed
    grad_u = gain * rows_ref[0:1, :] * grad_ref[...] - u * rows_ref[1:2, :]
    grad_y = grad_u * z * squashed
    grad_y_ref[...] = grad_y
    grad_z_ref[...] = half(grad_u * y * (squashed * (1.0 + z * (1.0 - squashed))))
    c_t = half(jax.nn.silu(bc_ref[STATE:, :]))
    reach = jnp.exp(cum_ref[...]) * flags_ref[0:1, :]
    grad_state_ref[...] = half(mul_nt(half(grad_y * spread_rows(reach)), c_t))


def inner_back_kernel(
    local_ref, passed_ref, pre_ref, grad_y_ref, bc_ref, dt_ref, cum_ref, cum_col_ref, flags_ref, seg_col_ref,
    grad_x_ref, grad_state_ref, grad_cum_ref, grad_skip_ref, grad_bc_ref, mask_s, inner_s, total_s, *chain,
):
    step = pl.program_id(0)
    first, last, device = chain_places(step, False)

    @pl.when(step == 0)
    def _():
        mask_s[...] = link_mask(flags_ref[2:3, :], seg_col_ref[:, 0:1])
        bc = half(jax.nn.silu(bc_ref[...]))
        inner_s[...] = mul_tn(bc[:STATE], bc[STATE:])
        total_s[...] = jnp.zeros_like(total_s)

    grad_state_ref[...] = chain_step(step, first, last, device, local_ref, passed_ref, *chain)
    x = jax.nn.silu(pre_ref[...])
    grad_y = grad_y_ref[...]
    grad_skip_ref[...] = head_sums(x * grad_y)
    scaled = half(x * spread_rows(dt_ref[...]))
    grad_half = half(grad_y)
    cum, cum_col = cum_ref[...], cum_col_ref[0]
    ones = jnp.ones((8, cum.shape[1]), jnp.bfloat16)
    for head in range(GROUP):
        rows = slice(head * HEAD, (head + 1) * HEAD)
        decay = jnp.exp(cum[head : head + 1, :] - cum_col[:, head : head + 1] + mask_s[...])
        weights = decay * inner_s[...]
        grad_x_ref[rows, :] = mul_nt(grad_half[rows], half(weights))
        grad_weights = mul_tn(scaled[rows], grad_half[rows])
        total_s[...] += grad_weights * decay
        moved = half(grad_weights * weights)
        sums = mul_nn(ones, moved) - mul_nt(ones, moved)
        grad_cum_ref[head : head + 1, :] = sums[0:1]

    @pl.when(step == pl.num_programs(0) - 1)
    def _():
        bc = half(jax.nn.silu(bc_ref[...]))
        total = half(total_s[...])
        grad_bc_ref[:STATE, :] = mul_nt(bc[STATE:], total)
        grad_bc_ref[STATE:, :] = mul_nn(bc[:STATE], total)
        chain_end(chain[0].shape[0], last, device, *chain)


def join_back_kernel(
    grad_in_ref, grad_y_ref, pre_ref, x_ref, taps_ref, masks_ref, state_ref, grad_state_ref,
    bc_ref, dt_ref, cum_ref, skip_ref, flags_ref,
    grad_x_ref, taps_out_ref, grad_dt_ref, grad_cum_ref, grad_last_ref, grad_bc_ref,
):
    step = pl.program_id(0)

    @pl.when(step == 0)
    def _():
        grad_bc_ref[...] = jnp.zeros_like(grad_bc_ref)

    bc = half(jax.nn.silu(bc_ref[...]))
    b_t, c_t = bc[:STATE], bc[STATE:]
    pre, grad_y, cum, dt = pre_ref[...], grad_y_ref[...], cum_ref[...], dt_ref[...]
    tokens = pre.shape[1]
    state, grad_state = state_ref[...], grad_state_ref[...]
    x = jax.nn.silu(pre)
    reached = grad_y * spread_rows(jnp.exp(cum) * flags_ref[0:1, :])
    grad_cum = head_sums(reached * mul_nn(state, c_t))
    grad_bc_ref[STATE:, :] += mul_tn(state, half(reached))
    tail = spread_rows(jnp.exp(cum[:, tokens - 1 :] - cum) * flags_ref[1:2, :])
    dt_wide = spread_rows(dt)
    scaled = x * dt_wide
    from_state = mul_nn(grad_state, b_t) * tail
    grad_bc_ref[:STATE, :] += mul_tn(grad_state, half(scaled * tail))
    tails = head_sums(scaled * from_state)
    grad_cum_ref[...] = grad_cum - tails
    last = jnp.sum(tails, axis=1, keepdims=True)
    through = jnp.sum(
        head_sums(state.astype(jnp.float32) * grad_state.astype(jnp.float32)), axis=1, keepdims=True
    )
    lane = lax.broadcasted_iota(jnp.int32, (GROUP, 128), 1)
    grad_last_ref[...] = jnp.where(lane == 0, last, jnp.where(lane == 1, through, 0.0))
    grad_scaled = grad_in_ref[...] + from_state
    grad_dt_ref[...] = head_sums(grad_scaled * x)
    grad_pre = (grad_scaled * dt_wide + grad_y * spread_rows(skip_ref[...])) * silu_slope(pre)
    rest = x_ref.shape[1] - tokens
    grad_pre = jnp.concatenate([grad_pre, jnp.zeros((grad_pre.shape[0], rest), jnp.float32)], axis=1)
    grad_x, packed = conv_adjoint(grad_pre, x_ref[...], taps_ref[...], masks_ref[...])
    grad_x_ref[...] = half(grad_x)
    taps_out_ref[...] = packed


def mixer_rows(dt_raw, dt_bias, a_log, d_skip, seg_window, taps):
    tokens = dt_raw.shape[1]
    dt = jax.nn.softplus(dt_raw + dt_bias[:, None])
    decay = -jnp.exp(a_log)[:, None] * dt
    upper = jnp.triu(jnp.ones((tokens, tokens), jnp.float32))
    cum = jnp.dot(decay, upper, precision=lax.Precision.HIGHEST)
    cum_col = jnp.swapaxes(cum.reshape(-1, GROUP, tokens), 1, 2)
    seg_now = seg_window[taps - 1 :]
    before = seg_window[taps - 2]
    reach = (seg_now == before).astype(jnp.float32)
    tail = (seg_now == seg_now[-1]).astype(jnp.float32)
    none = jnp.zeros((5, tokens), jnp.float32)
    flags = jnp.concatenate([jnp.stack([reach, tail, seg_now.astype(jnp.float32)]), none])
    seg_col = jnp.broadcast_to(seg_now.astype(jnp.float32)[:, None], (tokens, 8))
    masks = [
        (seg_window[taps - 1 - back : taps - 1 - back + tokens] == seg_now).astype(jnp.float32)
        for back in range(taps)
    ]
    masks = jnp.pad(jnp.stack(masks), ((0, 8 - taps), (0, 128)))
    through = jnp.exp(cum[:, -1]) * (seg_now[-1] == before).astype(jnp.float32)
    skip = jnp.broadcast_to(d_skip[:, None], dt.shape)
    return dt, decay, cum, cum_col, flags, seg_col, masks, through, skip


def mixer_forward_states(proj, taps, masks, dt, cum, flags):
    tokens, groups = dt.shape[1], HEADS // GROUP
    wide = proj.shape[1]
    bc_pre = call_steps(
        conv_kernel, 1, (proj, taps, masks),
        [block((2 * STATE, wide), lambda i: (DI // STATE, 0)),
         block((2 * STATE, 8), lambda i: (DI // (2 * STATE), 0)), whole(masks)],
        f32_out(2 * STATE, tokens), block((2 * STATE, tokens), lambda i: (0, 0)),
    )
    rows = block((GROUP, tokens), lambda i: (i, 0))
    pre, state = call_steps(
        state_kernel, groups, (proj, taps, masks, bc_pre, dt, cum, flags),
        [block((WIDE, wide), lambda i: (i + groups, 0)), block((WIDE, 8), lambda i: (i, 0)), whole(masks),
         whole(bc_pre), rows, rows, whole(flags)],
        [f32_out(DI, tokens), bf16_out(DI, STATE)],
        [block((WIDE, tokens), lambda i: (i, 0)), block((WIDE, STATE), lambda i: (i, 0))],
    )
    return bc_pre, pre, state


def mixer_back_gate(y, proj, grad_gated, gain_col, gate_rows, bc_pre, cum, flags):
    tokens, groups = y.shape[1], HEADS // GROUP
    wide = block((WIDE, tokens), lambda i: (i, 0))
    return call_steps(
        gate_back_kernel, groups, (y, proj, grad_gated, gain_col, gate_rows, bc_pre, cum, flags),
        [wide, wide, wide, block((WIDE, 8), lambda i: (i, 0)), whole(gate_rows), whole(bc_pre),
         block((GROUP, tokens), lambda i: (i, 0)), whole(flags)],
        [f32_out(DI, tokens), bf16_out(DI, tokens), bf16_out(DI, STATE)],
        [wide, wide, block((WIDE, STATE), lambda i: (i, 0))], micros=9,
    )


def mixer_back_inner(local, passed, pre, grad_y, bc_pre, dt, cum, cum_col, flags, seg_col, name_id):
    tokens, groups = dt.shape[1], HEADS // GROUP
    rows = block((GROUP, tokens), lambda i: (i, 0))
    wide = block((WIDE, tokens), lambda i: (i, 0))
    states = block((WIDE, STATE), lambda i: (i, 0))
    square = pltpu.VMEM((tokens, tokens), jnp.float32)
    return call_steps(
        inner_back_kernel, groups, (local, passed, pre, grad_y, bc_pre, dt, cum, cum_col, flags, seg_col),
        [states, block((WIDE, 8), lambda i: (i, 0)), wide, wide, whole(bc_pre), rows, rows, block((1, tokens, GROUP), lambda i: (i, 0, 0)),
         whole(flags), whole(seg_col)],
        [f32_out(DI, tokens), bf16_out(DI, STATE), f32_out(HEADS, tokens), f32_out(HEADS, tokens),
         f32_out(2 * STATE, tokens)],
        [wide, states, rows, rows, block((2 * STATE, tokens), lambda i: (0, 0))],
        (square, square, square) + chain_room(groups), name_id=name_id, micros=35,
    )


def mixer_back_join(grad_scaled, grad_y, pre, proj, taps, masks, state_in, grad_state, bc_pre, dt, cum, skip, flags):
    tokens, groups = dt.shape[1], HEADS // GROUP
    rows = block((GROUP, tokens), lambda i: (i, 0))
    wide = block((WIDE, tokens), lambda i: (i, 0))
    longer = block((WIDE, proj.shape[1]), lambda i: (i, 0))
    later = block((WIDE, proj.shape[1]), lambda i: (i + groups, 0))
    states = block((WIDE, STATE), lambda i: (i, 0))
    narrow = block((WIDE, 8), lambda i: (i, 0))
    return call_steps(
        join_back_kernel, groups,
        (grad_scaled, grad_y, pre, proj, taps, masks, state_in, grad_state, bc_pre, dt, cum, skip, flags),
        [wide, wide, wide, later, narrow, whole(masks), states, states, whole(bc_pre), rows, rows, rows,
         whole(flags)],
        [bf16_out(DI, proj.shape[1]), f32_out(DI, 8), f32_out(HEADS, tokens), f32_out(HEADS, tokens),
         f32_out(HEADS, 128), f32_out(2 * STATE, tokens)],
        [longer, narrow, rows, rows, block((GROUP, 128), lambda i: (i, 0)),
         block((2 * STATE, tokens), lambda i: (0, 0))], micros=19,
    )


def mixer_back_conv(grad_bc, bc_pre, proj, taps, masks):
    place = DI // (2 * STATE)
    wide = proj.shape[1]
    return call_steps(
        conv_back_kernel, 1, (grad_bc, bc_pre, proj, taps, masks),
        [whole(grad_bc), whole(bc_pre), block((2 * STATE, wide), lambda i: (2 * place, 0)),
         block((2 * STATE, 8), lambda i: (place, 0)), whole(masks)],
        [bf16_out(2 * STATE, wide), f32_out(2 * STATE, 8)],
        [block((2 * STATE, wide), lambda i: (0, 0)), block((2 * STATE, 8), lambda i: (0, 0))],
    )


def cut(array_index, rows, columns, row_step, column_step):
    found = []
    for row in range(0, rows, row_step):
        for column in range(0, columns, column_step):
            found.append(
                (array_index, row, min(row_step, rows - row), column, min(column_step, columns - column))
            )
    return found


def flipped(z, bits):
    if bits & 1:
        z = z + 1 - 2 * lax.rem(z, 2)
    return lax.rem(z + (bits & 2), 4)


def places(line):
    dp, z = lax.axis_index("dp"), lax.axis_index("ctx")
    y, x, core = lax.div(dp, 4), lax.rem(lax.div(dp, 2), 2), lax.rem(dp, 2)
    others = {
        "x": (dp + 2 - 4 * x, z),
        "y": (dp + 4 - 8 * y, z),
        "core": (dp + 1 - 2 * core, z),
    }
    for away in line:
        others[away] = (dp, lax.rem(z + away, 4))
    others["beside"] = (dp, flipped(z, 1))
    others["across"] = (dp, 3 - z)
    return y, x, core, z, others


def moved(moves, refs_in, refs_out, z, others, sems):
    copies = []
    for at, (source, target, take, put, bits) in enumerate(moves):
        source, target = refs_in[source], refs_out[target]
        source, target = source.at[take(z)], target.at[put(z)]
        copies.append(
            pltpu.make_async_remote_copy(
                src_ref=source,
                dst_ref=target,
                send_sem=sems[0].at[at],
                recv_sem=sems[1].at[at],
                device_id=others["beside" if bits == 1 else 2],
                device_id_type=pl.DeviceIdType.MESH,
            )
        )
    return copies


def greet(others):
    barrier = pltpu.get_barrier_semaphore()
    for device in others.values():
        pl.semaphore_signal(
            barrier, inc=1, device_id=device, device_id_type=pl.DeviceIdType.MESH
        )
    pl.semaphore_wait(barrier, len(others))


def send(source, target, sems, piece, leg, device):
    return pltpu.make_async_remote_copy(
        src_ref=source,
        dst_ref=target,
        send_sem=sems[0].at[piece, leg],
        recv_sem=sems[1].at[piece, leg],
        device_id=device,
        device_id_type=pl.DeviceIdType.MESH,
    )


def gather_kernel(pieces, ahead, count, line, moves, sizes, *refs):
    ins, more_in = refs[:count], refs[count : count + sizes[0]]
    refs = refs[count + sizes[0] :]
    outs, more_out = refs[:count], refs[count : count + sizes[1]]
    sent, came, kept, *more_sems = refs[count + sizes[1] :]
    y, x, core, z, others = places(line)
    deep = len(line) + 1
    slot = z if deep == 4 else lax.div(z, 2)
    inner = jnp.logical_and(z > 0, z < 3)
    greet(others)
    sems = (sent, came)

    def extra():
        return moved(moves, more_in if sizes[2] else more_out, more_out, z, others, more_sems) if moves else []

    def extra_turn(turn, turns):
        share = -(-len(moves) // turns)
        if turn < turns:
            for copy in extra()[share * turn : share * (turn + 1)]:
                copy.start()

    def legs(number):
        array, row, rows, column, columns = pieces[number]
        area = (pl.ds(row, rows), pl.ds(column, columns))
        out = outs[array]
        first, second = ("x", "y") if number % 2 == 0 else ("y", "x")
        rest = ((slice(None),) if line else ()) + area
        own = ins[array].at[area]
        mine = out.at[(y, x, core) + ((slot,) if line else ()) + area]
        lane = out.at[(y, x, core) + rest]
        at_pair = lax.div(z, 2)
        pair = out.at[(y, x, core, pl.ds(2 * at_pair, 2)) + area] if deep == 4 else None
        rest_pair = out.at[(y, x, core, pl.ds(2 - 2 * at_pair, 2)) + area] if deep == 4 else None
        if first == "x":
            plane = out.at[(y, slice(None), core) + rest]
        else:
            plane = out.at[(slice(None), x, core) + rest]
        every = out.at[(slice(None), slice(None), core) + rest]
        return {
            "keep": lambda: pltpu.make_async_copy(own, mine, kept.at[number]),
            "line": lambda: [send(own, mine, sems, number, 0, others["beside" if deep == 4 else 2])],
            "across": lambda: send(pair, pair, sems, number, 1, others["across"]),
            "outward": lambda: send(rest_pair, rest_pair, sems, number, 2, others["beside"]),
            "first": lambda: send(lane if line else own, lane, sems, number, 3, others[first]),
            "second": lambda: send(plane, plane, sems, number, 4, others[second]),
            "core": lambda: send(every, every, sems, number, 5, others["core"]),
        }

    def begin(number):
        if number < len(pieces):
            leg = legs(number)
            leg["keep"]().start()
            for copy in leg["line"]():
                copy.start()

    def advance(number, stage):
        if not 0 <= number < len(pieces):
            return
        leg = legs(number)
        if stage < 2 and deep < 4:
            return
        if stage == 0:
            leg["keep"]().wait()
            leg["line"]()[0].wait_recv()

            @pl.when(inner)
            def _():
                leg["across"]().start()
        elif stage == 1:

            @pl.when(inner)
            def _():
                leg["across"]().wait_recv()
                leg["outward"]().start()
        elif stage == 2:
            if deep == 4:

                @pl.when(jnp.logical_not(inner))
                def _():
                    leg["outward"]().wait_recv()
            else:
                leg["keep"]().wait()
                leg["line"]()[0].wait_recv()
            leg["first"]().start()
        elif stage == 3:
            leg["first"]().wait_recv()
            leg["second"]().start()
        elif stage == 4:
            leg["second"]().wait_recv()
            leg["core"]().start()
        else:
            leg["core"]().wait_recv()

    for number in range(2 * ahead):
        begin(number)
    pairs = -(-len(pieces) // 2)
    early = 0 if deep == 4 else 2
    for turn in range(pairs + 5 - early):
        extra_turn(turn, pairs)
        for stage in range(early, 6):
            for number in (2 * (turn - stage + early), 2 * (turn - stage + early) + 1):
                advance(number, stage)
                if stage == early and number < len(pieces):
                    begin(number + 2 * ahead)
    for number in range(len(pieces)):
        leg = legs(number)
        for copy in leg["line"]() + [leg["first"](), leg["second"](), leg["core"]()]:
            copy.wait_send()
        if deep == 4:

            @pl.when(inner)
            def _():
                leg["across"]().wait_send()
                leg["outward"]().wait_send()
    for copy in extra():
        copy.wait()


def move_room(moves):
    if not moves:
        return []
    return [pltpu.SemaphoreType.DMA((len(moves),))] * 2


def pallas_gather(parts, steps, name_id, line=(1, 2, 3), ahead=2, more=(), more_shapes=(), moves=()):
    pieces = []
    for index, (part, (row_step, column_step)) in enumerate(zip(parts, steps)):
        pieces += cut(index, part.shape[0], part.shape[1], row_step, column_step)
    count = len(parts)
    made = more_shapes or [part.shape for part in more]
    lead = (2, 2, 2) + ((len(line) + 1,) if line else ())
    anywhere = pl.BlockSpec(memory_space=pl.ANY)
    outs = pl.pallas_call(
        partial(gather_kernel, pieces, ahead, count, line, moves, (len(more), len(made), bool(more_shapes))),
        in_specs=[anywhere] * (count + len(more)),
        out_specs=[anywhere] * (count + len(made)),
        out_shape=[jax.ShapeDtypeStruct(lead + part.shape, part.dtype) for part in parts]
        + [bf16_out(*shape) for shape in made],
        scratch_shapes=[
            pltpu.SemaphoreType.DMA((len(pieces), 6)),
            pltpu.SemaphoreType.DMA((len(pieces), 6)),
            pltpu.SemaphoreType.DMA((len(pieces),)),
        ]
        + move_room(moves),
        input_output_aliases={} if more_shapes else {count + at: count + at for at in range(len(more))},
        cost_estimate=BRIEF,
        compiler_params=pltpu.CompilerParams(collective_id=name_id, has_side_effects=True),
    )(*parts, *more)
    return [out.reshape((-1,) + part.shape) for out, part in zip(outs, parts)] + list(outs[count:])


def reduce_kernel(pieces, ahead, count, lines, moves, sizes, *refs):
    ins, more_in = refs[:count], refs[count : count + sizes[0]]
    refs = refs[count + sizes[0] :]
    outs, more_out = refs[:count], refs[count : count + sizes[1]]
    sent, came, kept, put = refs[count + sizes[1] : count + sizes[1] + 4]
    room = refs[count + sizes[1] + 4 :]
    if moves:
        more_sems, room = room[:2], room[2:]
    y, x, core, z, others = places(max(lines, key=len))
    greet(others)
    sems = (sent, came)
    amount = len(pieces)

    def extra():
        return moved(moves, more_in, more_out, z, others, more_sems) if moves else []

    def extra_turn(turn, turns):
        share = -(-len(moves) // turns)
        if turn < turns:
            for copy in extra()[share * turn : share * (turn + 1)]:
                copy.start()

    def held(number):
        return room[6 * number : 6 * number + 6]

    def legs(number):
        array, row, rows, column, columns = pieces[number]
        area = (pl.ds(row, rows), pl.ds(column, columns))
        total, from_core, from_first, from_second, from_line, result = held(number)
        every = (slice(None), slice(None))
        line = lines[array]
        deep = len(line) + 1
        slot = z if deep == 4 else lax.div(z, 2)
        rest = ((slice(None),) if line else ()) + area
        side = number % 2 == 0
        return {
            "load": lambda: pltpu.make_async_copy(
                ins[array].at[every + (core,) + rest], total, kept.at[number]
            ),
            "core": lambda: send(
                ins[array].at[every + (1 - core,) + rest],
                from_core, sems, number, 0, others["core"],
            ),
            "first": lambda: send(
                total.at[:, 1 - x] if side else total.at[1 - y],
                from_first, sems, number, 1, others["x" if side else "y"],
            ),
            "second": lambda: send(
                total.at[1 - y, x] if side else total.at[y, 1 - x],
                from_second, sems, number, 2, others["y" if side else "x"],
            ),
            "line": lambda: [
                send(
                    total.at[y, x, lax.rem(z + away, 4) if deep == 4 else 1 - slot],
                    from_line.at[away - line[0]], sems, number, 2 + away, others[away],
                )
                for away in line
            ],
            "store": lambda: pltpu.make_async_copy(result, outs[array].at[area], put.at[number]),
        }

    def begin(number):
        if number < amount:
            leg = legs(number)
            leg["load"]().start()
            leg["core"]().start()

    def advance(number, stage):
        if not 0 <= number < amount:
            return
        leg = legs(number)
        total, from_core, from_first, from_second, from_line, result = held(number)
        line = lines[pieces[number][0]]
        deep = len(line) + 1
        slot = z if deep == 4 else lax.div(z, 2)

        def place(at, *lead):
            return lead + ((lax.rem(at, deep),) if line else ())

        if stage == 0:
            leg["load"]().wait()
            leg["core"]().wait_recv()

            @pl.loop(0, 4 * deep)
            def _(at):
                here = place(at, lax.div(at, 2 * deep), lax.rem(lax.div(at, deep), 2))
                total[here] = total[here] + from_core[here]

            leg["first"]().start()
        elif stage == 1:
            leg["first"]().wait_recv()

            @pl.loop(0, 2 * deep)
            def _(at):
                outer = lax.div(at, deep)
                here = place(at, outer, x) if number % 2 == 0 else place(at, y, outer)
                total[here] = total[here] + from_first[place(at, outer)]

            leg["second"]().start()
        elif stage == 2:
            leg["second"]().wait_recv()
            if line:

                @pl.loop(0, deep)
                def _(at):
                    total[y, x, at] = total[y, x, at] + from_second[at]

                for copy in leg["line"]():
                    copy.start()
            else:
                result[...] = total[y, x].astype(jnp.float32) + from_second[...].astype(jnp.float32)
                leg["store"]().start()
        elif line:
            for copy in leg["line"]():
                copy.wait_recv()
            summed = total[y, x, slot].astype(jnp.float32)
            for away in range(len(line)):
                summed = summed + from_line[away].astype(jnp.float32)
            result[...] = summed
            leg["store"]().start()

    for number in range(2 * ahead):
        begin(number)
    pairs = -(-amount // 2)
    for turn in range(pairs + 3):
        extra_turn(turn, pairs)
        for stage in range(4):
            for number in (2 * (turn - stage), 2 * (turn - stage) + 1):
                advance(number, stage)
                if stage == 0 and number >= 0:
                    begin(number + 2 * ahead)
    for number in range(amount):
        leg = legs(number)
        for copy in [leg["core"](), leg["first"](), leg["second"]()] + leg["line"]():
            copy.wait_send()
        leg["store"]().wait()
    for copy in extra():
        copy.wait()


def pallas_reduce(parts, steps, name_id, lines=None, ahead=2, more=(), more_shapes=(), moves=(), same=()):
    lines = lines or [(1, 2, 3)] * len(parts)
    shapes = [part.shape[1:] for part in parts]
    pieces = []
    for index, (shape, (row_step, column_step)) in enumerate(zip(shapes, steps)):
        pieces += cut(index, shape[0], shape[1], row_step, column_step)
    count, amount = len(parts), len(pieces)
    anywhere = pl.BlockSpec(memory_space=pl.ANY)
    room = []
    for array, _, rows, _, columns in pieces:
        kind, line = parts[array].dtype, lines[array]
        deep = (len(line) + 1,) if line else ()
        for lead in ((2, 2) + deep, (2, 2) + deep, (2,) + deep, deep, (max(len(line), 1),)):
            room.append(pltpu.VMEM(lead + (rows, columns), kind))
        room.append(pltpu.VMEM((rows, columns), jnp.float32))
    return pl.pallas_call(
        partial(reduce_kernel, pieces, ahead, count, lines, moves, (len(more), len(more_shapes))),
        in_specs=[anywhere] * (count + len(more)),
        out_specs=[anywhere] * (count + len(more_shapes)),
        out_shape=[jax.ShapeDtypeStruct(shape, jnp.float32) for shape in shapes]
        + [bf16_out(*shape) for shape in more_shapes],
        scratch_shapes=[
            pltpu.SemaphoreType.DMA((amount, 6)),
            pltpu.SemaphoreType.DMA((amount, 6)),
            pltpu.SemaphoreType.DMA((amount,)),
            pltpu.SemaphoreType.DMA((amount,)),
        ]
        + move_room(moves)
        + room,
        input_output_aliases={count + at: count + at for at in same},
        cost_estimate=BRIEF,
        compiler_params=pltpu.CompilerParams(
            collective_id=name_id, has_side_effects=True, vmem_limit_bytes=VMEM_MOST
        ),
        )(*[part.reshape((2, 2, 2) + ((len(line) + 1,) if line else ()) + shape) for part, shape, line in zip(parts, shapes, lines)], *more)


def proj_back_kernel(
    normed_ref, weight_ref, grad_z_ref, grad_x_ref, grad_rest_ref, rows_ref,
    grad_weight_ref, grad_normed_ref, came_ref, sent, came,
):
    step, groups = pl.program_id(0), DI // WIDE
    tokens = grad_z_ref.shape[1]
    dp, z = lax.axis_index("dp"), lax.axis_index("ctx")
    far = (dp, lax.rem(z + 2, 4))

    def exchange():
        return pltpu.make_async_remote_copy(
            src_ref=rows_ref,
            dst_ref=came_ref,
            send_sem=sent,
            recv_sem=came,
            device_id=far,
            device_id_type=pl.DeviceIdType.MESH,
        )

    @pl.when(step == 0)
    def _():
        grad_normed_ref[...] = jnp.zeros_like(grad_normed_ref)
        greet({"far": far})
        exchange().start()

    @pl.when(step == 2 * groups)
    def _():
        exchange().wait()

    @pl.when(step < groups)
    def _():
        grad_weight_ref[...] = half(mul_nt(normed_ref[:, :tokens], grad_z_ref[...]))
        grad_normed_ref[:, :tokens] += mul_nn(weight_ref[...], grad_z_ref[...])

    @pl.when(jnp.logical_and(step >= groups, step < 2 * groups))
    def _():
        grad_weight_ref[...] = half(mul_nt(normed_ref[...], grad_x_ref[...]))
        grad_normed_ref[...] += mul_nn(weight_ref[...], grad_x_ref[...])

    @pl.when(step == 2 * groups)
    def _():
        lane = lax.broadcasted_iota(jnp.int32, weight_ref.shape, 1)
        weight = jnp.where(lane < PROJ - 2 * DI, weight_ref[...], jnp.zeros_like(weight_ref))
        grad_weight_ref[...] = half(mul_nt(normed_ref[...], grad_rest_ref[...]))
        grad_normed_ref[...] += mul_nn(weight, grad_rest_ref[...])


def proj_back(normed_t, weight, grad_z, grad_x, grad_rest, rows, name_id):
    features, tokens = normed_t.shape
    groups = DI // WIDE
    return call_steps(
        proj_back_kernel, 2 * groups + 1, (normed_t, weight, grad_z, grad_x, grad_rest, rows),
        [whole(normed_t), block((features, WIDE), lambda i: (0, i)),
         block((WIDE, grad_z.shape[1]), lambda i: (jnp.minimum(i, groups - 1), 0)),
         block((WIDE, tokens), lambda i: (jnp.clip(i - groups, 0, groups - 1), 0)), whole(grad_rest),
         pl.BlockSpec(memory_space=pl.ANY)],
        [bf16_out(features, PROJ), f32_out(features, tokens), bf16_out(*rows.shape)],
        [block((features, WIDE), lambda i: (0, i)), block((features, tokens), lambda i: (0, 0)),
         pl.BlockSpec(memory_space=pl.ANY)],
        (pltpu.SemaphoreType.DMA, pltpu.SemaphoreType.DMA), name_id=name_id, micros=27,
    )


def hop(group, leaving, arrived, sent, came, device):
    return pltpu.make_async_remote_copy(
        src_ref=leaving.at[group],
        dst_ref=arrived.at[group],
        send_sem=sent.at[group],
        recv_sem=came.at[group],
        device_id=device,
        device_id_type=pl.DeviceIdType.MESH,
    )


def chain_places(step, forward):
    dp, z = lax.axis_index("dp"), lax.axis_index("ctx")
    others = {"left": (dp, lax.rem(z + 3, 4)), "right": (dp, lax.rem(z + 1, 4))}

    @pl.when(step == 0)
    def _():
        greet(others)

    if forward:
        return z == 0, z == 3, others["right"]
    return z == 3, z == 0, others["left"]


def chain_step(step, first, last, device, local_ref, passed_ref, leaving, arrived, sent, came):
    @pl.when(first)
    def _():
        arrived[step] = jnp.zeros(arrived.shape[1:], arrived.dtype)

    @pl.when(jnp.logical_not(first))
    def _():
        hop(step, leaving, arrived, sent, came, device).wait_recv()

    here = arrived[step]
    leaving[step] = half(here.astype(jnp.float32) * passed_ref[:, 0:1] + local_ref[...].astype(jnp.float32))

    @pl.when(jnp.logical_not(last))
    def _():
        hop(step, leaving, arrived, sent, came, device).start()

    return here


def chain_end(groups, last, device, leaving, arrived, sent, came):
    @pl.when(jnp.logical_not(last))
    def _():
        for group in range(groups):
            hop(group, leaving, arrived, sent, came, device).wait_send()


def chain_room(groups):
    slots = pltpu.VMEM((groups, WIDE, STATE), jnp.bfloat16)
    sems = pltpu.SemaphoreType.DMA((groups,))
    return (slots, slots, sems, sems)


def forward_kernel(
    local_ref, passed_ref, pre_ref, bc_ref, dt_ref, cum_ref, cum_col_ref, skip_ref, flags_ref, seg_col_ref,
    z_ref, gain_ref, y_ref, state_ref, gated_ref, scale_ref, mask_s, inner_s, u_s, sum_s, *chain,
):
    step, groups = pl.program_id(0), u_s.shape[0]
    first, last, device = chain_places(step, True)

    @pl.when(step == 0)
    def _():
        mask_s[...] = link_mask(flags_ref[2:3, :], seg_col_ref[:, 0:1])
        bc = half(jax.nn.silu(bc_ref[...]))
        inner_s[...] = mul_tn(bc[:STATE], bc[STATE:])
        sum_s[...] = jnp.zeros_like(sum_s)

    @pl.when(step < groups)
    def _():
        here = chain_step(step, first, last, device, local_ref, passed_ref, *chain)
        state_ref[...] = here
        cum, cum_col = cum_ref[...], cum_col_ref[0]
        c_t = half(jax.nn.silu(bc_ref[STATE:, :]))
        x = jax.nn.silu(pre_ref[...])
        scaled = half(x * spread_rows(dt_ref[...]))
        reach = jnp.exp(cum) * flags_ref[0:1, :]
        y_ref[...] = mul_nn(here, c_t) * spread_rows(reach) + x * spread_rows(skip_ref[...])
        for head in range(GROUP):
            rows = slice(head * HEAD, (head + 1) * HEAD)
            spread = cum[head : head + 1, :] - cum_col[:, head : head + 1] + mask_s[...]
            y_ref[rows, :] += mul_nn(scaled[rows], half(jnp.exp(spread) * inner_s[...]))
        u = y_ref[...] * jax.nn.silu(z_ref[...])
        u_s[step] = u
        sum_s[...] += jnp.sum(u * u, axis=0, keepdims=True)

    @pl.when(step >= groups)
    def _():
        scale = lax.rsqrt(sum_s[0:1, :] * (1.0 / DI) + 1e-05)
        gated_ref[...] = half(u_s[step - groups] * scale * gain_ref[:, 0:1])
        scale_ref[...] = jnp.broadcast_to(scale, scale_ref.shape)

    @pl.when(step == 2 * groups - 1)
    def _():
        chain_end(groups, last, device, *chain)


def mixer_forward(local, passed, pre, bc_pre, dt, cum, cum_col, skip, flags, seg_col, proj, gain_col, name_id):
    tokens, groups = dt.shape[1], HEADS // GROUP
    first = lambda i: (jnp.minimum(i, groups - 1), 0)
    second = lambda i: (jnp.maximum(i - groups, 0), 0)
    rows, wide = block((GROUP, tokens), first), block((WIDE, tokens), first)
    states = block((WIDE, STATE), first)
    square = pltpu.VMEM((tokens, tokens), jnp.float32)
    return call_steps(
        forward_kernel, 2 * groups,
        (local, passed, pre, bc_pre, dt, cum, cum_col, skip, flags, seg_col, proj, gain_col),
        [states, block((WIDE, 8), first), wide, whole(bc_pre), rows, rows,
         block((1, tokens, GROUP), lambda i: (jnp.minimum(i, groups - 1), 0, 0)), rows, whole(flags),
         whole(seg_col), wide, block((WIDE, 8), second)],
        [f32_out(DI, tokens), bf16_out(DI, STATE), bf16_out(DI, tokens), f32_out(8, tokens)],
        [wide, states, block((WIDE, tokens), second), block((8, tokens), lambda i: (0, 0))],
        (square, square, pltpu.VMEM((groups, WIDE, tokens), jnp.float32), pltpu.VMEM((8, tokens), jnp.float32))
        + chain_room(groups),
        name_id=name_id,
    )


BOTH = ("dp", "ctx")


def nothing(value):
    first = value[(0,) * value.ndim].astype(jnp.float32)
    return jnp.minimum(jnp.abs(first), 0.0)


def no_step(value):
    return nothing(value).astype(jnp.int32)


def two_parts(value):
    high = value.astype(jnp.bfloat16)
    low = (value - high.astype(jnp.float32)).astype(jnp.bfloat16)
    return high, low


def route_table(routes, expert_count):
    named = jnp.any(
        routes[:, :, None] == jnp.arange(expert_count, dtype=jnp.int32), axis=1
    )
    rows = routes.shape[0]
    earlier = jnp.tril(jnp.ones((rows, rows), jnp.bfloat16), -1)
    ranks = jnp.dot(earlier, named.astype(jnp.bfloat16), preferred_element_type=jnp.float32)
    return named, jnp.where(named, ranks, -1.0)


def swap(value, bits):
    count = lax.axis_size("ctx")
    return lax.ppermute(value, "ctx", [(source, source ^ bits) for source in range(count)])


def half_strip(other, start):
    def at(z):
        own = lax.div(z, 2)
        first = EXP_DEV // 2 * (1 - own if other else own)
        return (pl.ds(first, EXP_DEV // 2), pl.ds(start, STRIP))

    return at


def columns(place, start, size):
    return lambda z: place(z) + (pl.ds(start, size),)


def held_experts(shard, other):
    held = EXP_DEV // 2
    half_at = lax.div(lax.axis_index("ctx"), 2)
    return lax.dynamic_slice_in_dim(shard, held * (1 - half_at if other else half_at), held, 0)


STRIP = 64


def quarter(axis, width, bits, start):
    def at(z):
        first = flipped(z, bits) * width
        if axis == 1:
            return (slice(None), pl.ds(pl.multiple_of(first + start, STRIP), STRIP))
        return (slice(None), pl.ds(start, STRIP), pl.ds(pl.multiple_of(first, 128), width))

    return at


def strip(start, *lead):
    return lambda z: lead + (slice(None), pl.ds(start, STRIP))


def strips(rows):
    return range(0, rows, STRIP)


def with_quarter(whole, own, axis):
    place = lax.axis_index("ctx") * own.shape[axis]
    return lax.dynamic_update_slice_in_dim(whole, own, place, axis)


def own_quarter(whole, axis, bits):
    width = whole.shape[axis] // 4
    return lax.dynamic_slice_in_dim(whole, flipped(lax.axis_index("ctx"), bits) * width, width, axis)


def expert_owners(near, far):
    far = far.astype(jnp.float32)
    low = lax.div(lax.axis_index("ctx"), 2) == 0
    return jnp.concatenate([jnp.where(low, near, far), jnp.where(low, far, near)], axis=0)


TILE = 4


def experts_kernel(
    rank_ref, gate_ref, rows_ref, grads_ref, first_ref, down_ref,
    routed_ref, back_ref, dgate_ref, grad_first_ref, grad_down_ref,
    x_s, g_s, sum_first_s, sum_down_s, ready_s, pick_s, routed_s, back_s, sem,
):
    tile, expert = pl.program_id(0), pl.program_id(1)
    last = pl.num_programs(0) - 1
    hidden = down_ref.shape[1]
    slots = x_s.shape[0] // TILE
    tokens = rank_ref.shape[2]
    chosen, gates = [], []
    number = lax.broadcasted_iota(jnp.int32, (slots, tokens), 0).astype(jnp.float32)
    for at in range(TILE):
        rows = pl.ds(at * slots, slots)
        own = rank_ref[at, pl.ds(expert, 1), :] == number
        chosen.append(own)
        gates.append(jnp.sum(jnp.where(own, gate_ref[at, pl.ds(expert, 1), :], 0.0), axis=1, keepdims=True))
        picker = half(own.astype(jnp.float32))
        x_s[rows, :] = half(mul_nn(picker, rows_ref[at]))
        g_s[rows, :] = half(mul_nn(picker, grads_ref[at]))
    gate = jnp.concatenate(gates, axis=0)
    x, grad = x_s[...], g_s[...].astype(jnp.float32)
    both = mul_nn(x, first_ref[0])
    hg, hu = both[:, :hidden], both[:, hidden:]
    squashed = jax.nn.sigmoid(hg)
    act = half(hg * squashed * hu)
    out = half(mul_nn(act, down_ref[0]))
    out_f = out.astype(jnp.float32)
    dgate = jnp.sum(grad * out_f, axis=1, keepdims=True)
    routed = half(gate * out_f)
    grad_out = half(gate * grad)
    grad_act = mul_nt(grad_out, down_ref[0])
    grad_hg = half(grad_act * hu * (squashed * (1.0 + hg * (1.0 - squashed))))
    grad_hu = half(grad_act * hg * squashed)
    grad_both = jnp.concatenate([grad_hg, grad_hu], axis=1)
    back = half(mul_nt(grad_both, first_ref[0]))

    @pl.when(tile == 0)
    def _():
        sum_first_s[expert] = jnp.zeros(sum_first_s.shape[1:], jnp.float32)
        sum_down_s[expert] = jnp.zeros(sum_down_s.shape[1:], jnp.float32)

    @pl.loop(0, x_s.shape[1] // 256)
    def _(at):
        some = pl.ds(pl.multiple_of(at * 256, 256), 256)
        sum_first_s[expert, some, :] += mul_tn(x_s[:, some], grad_both)

    sum_down_s[expert] += mul_tn(act, grad_out)
    for at in range(TILE):
        rows = slice(at * slots, (at + 1) * slots)
        some = pl.ds(pl.multiple_of(expert * slots, slots), slots)
        pick_s[at, some, :] = half(chosen[at].astype(jnp.float32))
        routed_s[at, some, :] = routed[rows]
        back_s[at, some, :] = back[rows]
        dgate_ref[at, pl.ds(expert, 1), :] = jnp.sum(
            jnp.where(chosen[at], dgate[rows], 0.0), axis=0, keepdims=True
        )

    @pl.when(expert == pl.num_programs(1) - 1)
    def _():
        for at in range(TILE):
            routed_ref[at] = half(mul_tn(pick_s[at], routed_s[at]))
            back_ref[at] = half(mul_tn(pick_s[at], back_s[at]))

    @pl.when(tile == last)
    def _():
        height = ready_s.shape[0]
        for sums, target in ((sum_first_s, grad_first_ref), (sum_down_s, grad_down_ref)):
            width = sums.shape[2]
            for at in range(sums.shape[1] // height):
                some = pl.ds(at * height, height)
                ready_s[:, :width] = half(sums[expert, some, :])
                copy = pltpu.make_async_copy(
                    ready_s.at[:, pl.ds(0, width)], target.at[expert, some, :], sem
                )
                copy.start()
                copy.wait()


def routed_experts(rank, gate, rows, grads, first, down, slots):
    blocks, held, tokens = rank.shape
    features, hidden = first.shape[1], down.shape[1]
    some = lambda t, e: (t, 0, 0)
    table = pl.BlockSpec((TILE, held, tokens), some)
    wide = pl.BlockSpec((TILE, tokens, features), some)
    once = pl.BlockSpec((TILE, tokens, features), some, pipeline_mode=pl.Buffered(1))
    anywhere = pl.BlockSpec(memory_space=pl.ANY)
    return pl.pallas_call(
        experts_kernel,
        grid=(blocks // TILE, held),
        in_specs=[
            table,
            table,
            once,
            once,
            pl.BlockSpec((1, features, 2 * hidden), lambda t, e: (e, 0, 0)),
            pl.BlockSpec((1, hidden, features), lambda t, e: (e, 0, 0)),
        ],
        out_specs=[wide, wide, table, anywhere, anywhere],
        out_shape=[
            bf16_out(blocks, tokens, features),
            bf16_out(blocks, tokens, features),
            f32_out(blocks, held, tokens),
            bf16_out(held, features, 2 * hidden),
            bf16_out(held, hidden, features),
        ],
        scratch_shapes=[
            pltpu.VMEM((TILE * slots, features), jnp.bfloat16),
            pltpu.VMEM((TILE * slots, features), jnp.bfloat16),
            pltpu.VMEM((held, features, 2 * hidden), jnp.float32),
            pltpu.VMEM((held, hidden, features), jnp.float32),
            pltpu.VMEM((256, features), jnp.bfloat16),
            pltpu.VMEM((TILE, held * slots, tokens), jnp.bfloat16),
            pltpu.VMEM((TILE, held * slots, features), jnp.bfloat16),
            pltpu.VMEM((TILE, held * slots, features), jnp.bfloat16),
            pltpu.SemaphoreType.DMA,
        ],
        cost_estimate=BRIEF,
        compiler_params=pltpu.CompilerParams(
            vmem_limit_bytes=62 * 1024 * 1024, dimension_semantics=("arbitrary", "arbitrary")
        ),
    )(rank, gate, rows, grads, first, down)


def on_device(
    layer_in,
    seg_ids,
    route_ids,
    out_grad,
    norm_in,
    w_in,
    conv_w,
    conv_b,
    dt_bias,
    a_log,
    d_skip,
    norm_gate,
    w_out,
    norm_mid,
    w_router,
    w_sgate,
    w_sup,
    w_sdown,
    e_gate,
    e_up,
    e_down,
):
    f32, bf16 = jnp.float32, jnp.bfloat16
    row_count, d_model = layer_in.shape[1:]
    devices = lax.axis_size("dp") * lax.axis_size("ctx")
    ctx_place = lax.axis_index("ctx")
    held = EXP_DEV // 2
    first_expert = lax.axis_index("dp") * EXP_DEV + lax.div(ctx_place, 2) * held
    blocks = lax.axis_size("dp") * 2
    expert_count = EXP_DEV * lax.axis_size("dp")
    capacity = row_count * TOP * 5 // (expert_count * 4)
    slots = -(-capacity // 64) * 64
    tap_count = conv_w.shape[0]
    halo = 8

    small_parts = (norm_in, conv_w, conv_b, norm_gate, norm_mid, w_router)
    small_flat = jnp.concatenate([part.reshape(-1) for part in small_parts])
    small_flat = jnp.pad(small_flat, (0, 4096 - small_flat.shape[0])).reshape(32, 128)
    edge_rows = layer_in[0, row_count - halo :].reshape(-1, 128)
    width, hidden = e_gate.shape[1:]
    first_strips, down_strips = strips(width), strips(hidden)
    w_in_all, w_out_all, small_all, expert_first, expert_down = pallas_gather(
        [w_in, w_out, jnp.concatenate([small_flat, edge_rows])],
        [(16, 1664), (16, 1536), (128, 128)],
        1,
        ahead=6,
        more=[e_gate, e_up, e_down],
        more_shapes=[(held, d_model, 2 * hidden), (held, hidden, d_model)],
        moves=[
            (part, 0, half_strip(True, start), columns(quarter(1, width, 0, start), part * hidden, hidden), 2)
            for start in first_strips
            for part in range(2)
        ]
        + [(2, 1, half_strip(True, start), quarter(2, width, 0, start), 2) for start in down_strips],
    )
    pair_at = lax.div(ctx_place, 2)
    sent = nothing(w_in_all)
    shared_all = lax.all_gather(
        (jnp.concatenate([w_sgate, w_sup], axis=1).astype(f32) + sent).astype(bf16), BOTH, axis=0
    )
    sdown_all = lax.all_gather((w_sdown.astype(f32) + sent).astype(bf16), BOTH, axis=0)
    own_first = jnp.concatenate([held_experts(e_gate, False), held_experts(e_up, False)], axis=2)
    expert_first = with_quarter(expert_first, own_first, 1)
    expert_down = with_quarter(expert_down, held_experts(e_down, False), 2)
    edge_all = small_all[:, small_flat.shape[0] :].reshape(devices, halo, d_model)
    small_all = small_all[:, : small_flat.shape[0]].reshape(devices, 4096)
    taken, pieces = 0, []
    for part in small_parts:
        pieces.append(small_all[:, taken : taken + part.size])
        taken += part.size
    gain_in = pieces[0].reshape(-1).astype(f32)
    conv_weight = jnp.moveaxis(pieces[1].reshape(devices, tap_count, -1), 0, 1).reshape(tap_count, CONV).astype(f32)
    conv_bias = pieces[2].reshape(-1).astype(f32)
    gain_gate = pieces[3].reshape(-1).astype(f32)
    gain_mid = pieces[4].reshape(-1).astype(f32)
    router_weight = pieces[5].reshape(d_model, expert_count)
    weight_in = w_in_all.reshape(d_model, PROJ)
    weight_out = w_out_all.reshape(DI, d_model)
    shared_weight = shared_all.reshape(d_model, -1)
    sdown_weight = sdown_all.reshape(-1, d_model)
    named, ranks = route_table(route_ids[0], expert_count)

    own_in = layer_in[0]
    place = lax.axis_index("dp") * lax.axis_size("ctx") + ctx_place
    edge_in = lax.dynamic_index_in_dim(edge_all, jnp.maximum(place - 1, 0), 0, keepdims=False)
    edge_in = jnp.where(ctx_place > 0, edge_in, jnp.zeros_like(edge_in))
    input_f = jnp.concatenate(
        [own_in, jnp.zeros((128 - halo, d_model), bf16), edge_in], axis=0
    ).astype(f32)
    normed = scaled_norm(input_f, gain_in).astype(bf16)
    projected = lax.dot_general(
        weight_in, normed, (((0,), (1,)), ((), ())), preferred_element_type=f32
    )
    seg_pad = jnp.concatenate([jnp.full((tap_count - 1,), -1, jnp.int32), seg_ids[0]])
    seg_window = lax.dynamic_slice_in_dim(
        seg_pad, ctx_place * row_count, row_count + tap_count - 1, 0
    )
    taps = jnp.concatenate(
        [conv_weight.T, conv_bias[:, None], jnp.zeros((CONV, 7 - tap_count), f32)], axis=1
    )
    dt_raw = projected[DI + CONV :, :row_count]
    dt_pos, decay, cumul, cumul_col, flags, seg_col, masks, through, skip_rows = mixer_rows(
        dt_raw, dt_bias, a_log, d_skip, seg_window, tap_count
    )
    bc_pre, pre, state_out = mixer_forward_states(projected, taps, masks, dt_pos, cumul, flags)
    passed = jnp.broadcast_to(jnp.repeat(through, HEAD)[:, None], (DI, 8))
    gain_col = jnp.broadcast_to(gain_gate[:, None], (DI, 8))
    y_heads, state_in, gated, gate_scale = mixer_forward(
        state_out, passed, pre, bc_pre, dt_pos, cumul, cumul_col, skip_rows, flags, seg_col, projected, gain_col, 7
    )

    mixed = times_rows(gated, weight_out)
    resid_mid = own_in.astype(f32) + mixed
    normed_mid_f, pull_mid = jax.vjp(scaled_norm, resid_mid, gain_mid)
    normed_mid = normed_mid_f.astype(bf16)
    logits = jnp.dot(normed_mid, router_weight, preferred_element_type=f32)
    top_logit = jnp.max(jnp.where(named, logits, -jnp.inf), axis=-1, keepdims=True)
    powers = jnp.where(named, jnp.exp(jnp.where(named, logits - top_logit, 0.0)), 0.0)
    gates = powers / jnp.sum(powers, axis=-1, keepdims=True)
    gate_high, gate_low = two_parts(gates)
    side = jnp.concatenate(
        [gate_high, gate_low, ranks.astype(bf16), jnp.zeros((row_count, 128 - 3 * expert_count), bf16)],
        axis=1,
    )
    token_rows, grad_rows, side_all, expert_first, expert_down = pallas_gather(
        [normed_mid, out_grad[0], side],
        [(16, 1536), (16, 1536), (128, 128)],
        3,
        line=(2,),
        ahead=4,
        more=[expert_first, expert_down],
        moves=[
            (part, part, quarter(axis, width, bits, start), quarter(axis, width, bits, start), 1)
            for bits in (0, 2)
            for part, axis, starts in ((0, 1, first_strips), (1, 2, down_strips))
            for start in starts
        ],
    )
    normed_later = (normed_mid.astype(f32) + nothing(token_rows)).astype(bf16)
    shared_hidden = jnp.dot(normed_later, shared_weight, preferred_element_type=f32)
    shared_gate, shared_up = jnp.split(shared_hidden, 2, axis=1)
    shared_act = (jax.nn.silu(shared_gate) * shared_up).astype(bf16)
    shared_out = jnp.dot(shared_act, sdown_weight, preferred_element_type=f32)

    def owned(grad):
        return grad.astype(bf16).reshape(devices, -1, grad.shape[-1])

    mine_of = partial(lax.dynamic_slice_in_dim, slice_size=held, axis=2)
    my_gate = mine_of(side_all, first_expert).astype(f32) + mine_of(
        side_all, first_expert + expert_count
    ).astype(f32)
    my_rank = mine_of(side_all, first_expert + 2 * expert_count).astype(f32)
    my_gate, my_rank = jnp.swapaxes(my_gate, 1, 2), jnp.swapaxes(my_rank, 1, 2)
    routed_rows, grad_slot_rows, token_dgate, grad_first, grad_down = routed_experts(
        my_rank, my_gate, token_rows, grad_rows, expert_first, expert_down, slots
    )
    experts = jnp.arange(held, dtype=jnp.int32)[:, None] + first_expert
    dgate_table = jnp.sum(
        token_dgate[..., None] * (jnp.arange(expert_count) == experts).astype(f32)[:, None, :], axis=1
    )
    dgate_high, dgate_low = two_parts(dgate_table)
    back_side = jnp.concatenate(
        [dgate_high, dgate_low, jnp.zeros((blocks, row_count, 128 - 2 * expert_count), bf16)], axis=-1
    )
    grad_shared_out = out_grad[0]
    grad_w_sdown = times_rows(shared_act, grad_shared_out)
    grad_shared_act = times_back(grad_shared_out, sdown_weight)
    grad_sgate = (grad_shared_act * shared_up * silu_slope(shared_gate)).astype(bf16)
    grad_sup = (grad_shared_act * jax.nn.silu(shared_gate)).astype(bf16)
    grad_shared = jnp.concatenate([grad_sgate, grad_sup], axis=1)
    grad_w_shared = times_rows(normed_mid, grad_shared)
    back_rows, back_side, sum_sdown, sum_shared, beside_first, beside_down, routed_rows = pallas_reduce(
        [grad_slot_rows, back_side, owned(grad_w_sdown), owned(grad_w_shared)],
        [(16, 1536), (128, 128), (16, 1536), (16, 1024)],
        4,
        lines=[(2,), (2,), (1, 2, 3), (1, 2, 3)],
        more=[grad_first, grad_down, routed_rows],
        more_shapes=[(held, width, 2 * hidden), (held, hidden, width), routed_rows.shape],
        same=(2,),
        moves=[
            (part, part, quarter(axis, width, 3, start), strip(start), 1)
            for part, axis, starts in ((0, 1, first_strips), (1, 2, down_strips))
            for start in starts
        ],
    )
    routed = lax.psum_scatter(
        routed_rows.reshape(-1, 2, row_count, d_model), "dp", scatter_dimension=0
    )
    routed = with_layout_constraint(routed, Layout(major_to_minor=(0, 1, 2)))
    routed_own = lax.dynamic_index_in_dim(routed, pair_at, 0, keepdims=False)
    routed_far = lax.dynamic_index_in_dim(routed, 1 - pair_at, 0, keepdims=False)
    grad_top = out_grad[0].astype(f32)
    grad_mid_shared = times_back(grad_shared, shared_weight)
    grad_gates = back_side[:, :expert_count] + back_side[:, expert_count : 2 * expert_count]
    grad_pick = gates * (grad_gates - jnp.sum(gates * grad_gates, axis=-1, keepdims=True))
    grad_logits = grad_pick.astype(bf16)
    grad_w_router = times_rows(normed_mid, grad_logits)
    grad_mid = (
        back_rows + grad_mid_shared + times_back(grad_logits, router_weight)
    )
    grad_resid_part, grad_gain_mid = pull_mid(grad_mid)
    grad_resid = grad_top + grad_resid_part
    grad_mixed = grad_resid.astype(bf16)

    grad_w_out = jnp.dot(gated, grad_mixed, preferred_element_type=f32)
    grad_gated = times_back(weight_out, grad_mixed)
    scaled_u = y_heads * jax.nn.silu(projected[:DI, :row_count])
    scale_row = gate_scale[:1]
    along = jnp.sum(grad_gated * gain_gate[:, None] * scaled_u, axis=0, keepdims=True)
    grad_gain_gate = jnp.sum(grad_gated * scaled_u * scale_row, axis=1)
    gate_rows = jnp.concatenate(
        [scale_row, scale_row * scale_row * scale_row * along * (1.0 / DI), jnp.zeros((6, row_count), f32)]
    )
    grad_y, grad_z, grad_state_local = mixer_back_gate(
        y_heads, projected, grad_gated, gain_col, gate_rows, bc_pre, cumul, flags
    )
    grad_scaled, grad_state_out, grad_cum_inner, grad_skip, grad_bc_inner = mixer_back_inner(
        grad_state_local, passed, pre, grad_y, bc_pre, dt_pos, cumul, cumul_col, flags, seg_col, 8
    )
    far_first, far_down = (
        half(own_quarter(whole, axis, 2).astype(f32) + beside.astype(f32))
        for whole, beside, axis in ((grad_first, beside_first, 1), (grad_down, beside_down, 2))
    )
    grad_x, grad_taps_x, grad_dt, grad_cum_join, grad_last, grad_bc_join = mixer_back_join(
        grad_scaled, grad_y, pre, projected, taps, masks, state_in, grad_state_out,
        bc_pre, dt_pos, cumul, skip_rows, flags,
    )
    grad_bc, grad_taps_bc = mixer_back_conv(
        grad_bc_inner + grad_bc_join, bc_pre, projected, taps, masks
    )
    grad_cum = grad_cum_inner + grad_cum_join
    grad_last = grad_last[:, 0] + through * grad_last[:, 1]
    lower = jnp.tril(jnp.ones((row_count, row_count), f32))
    grad_decay = jnp.dot(grad_cum, lower, precision=lax.Precision.HIGHEST) + grad_last[:, None]
    grad_dt = grad_dt - jnp.exp(a_log)[:, None] * grad_decay
    grad_raw = grad_dt * jax.nn.sigmoid(dt_raw + dt_bias[:, None])
    grad_taps = jnp.concatenate([grad_taps_x, grad_taps_bc])
    grad_conv_w, grad_conv_b = grad_taps[:, :tap_count].T, grad_taps[:, tap_count]
    head_sums_all = jnp.concatenate(
        [jnp.sum(grad_raw, axis=1), jnp.sum(decay * grad_decay, axis=1), jnp.sum(grad_skip, axis=1)]
    )
    grad_rest = jnp.concatenate(
        [
            grad_bc,
            jnp.pad(grad_raw.astype(bf16), ((0, WIDE - 2 * STATE - HEADS), (0, 128))),
        ]
    )
    normed_t = normed.T
    grad_w_in, grad_normed, routed_far = proj_back(
        normed_t, weight_in, grad_z, grad_x, grad_rest, routed_far, 9
    )
    grad_normed = grad_normed.T
    edge_grad = from_behind(grad_normed[row_count + 128 - halo :], "ctx", -1)
    grad_normed = jnp.concatenate(
        [grad_normed[: row_count - halo], grad_normed[row_count - halo : row_count] + edge_grad],
        axis=0,
    )
    _, pull_in = jax.vjp(scaled_norm, own_in.astype(f32), gain_in)
    grad_input_part, grad_gain_in = pull_in(grad_normed)
    grad_in = (grad_resid + grad_input_part)[None]

    small_grads = jnp.concatenate(
        [
            grad_gain_in.reshape(devices, -1),
            jnp.moveaxis(grad_conv_w.reshape(tap_count, devices, -1), 1, 0).reshape(devices, -1),
            grad_conv_b.reshape(devices, -1),
            grad_gain_gate.reshape(devices, -1),
            grad_gain_mid.reshape(devices, -1),
            grad_w_router.reshape(devices, -1),
            jnp.broadcast_to(head_sums_all, (devices, 3 * HEADS)),
        ],
        axis=1,
    )
    small_grads = jnp.pad(small_grads, ((0, 0), (0, 3072 - small_grads.shape[1])))
    sum_in, sum_out, sum_small, far_first, far_down, beside_first, beside_down = pallas_reduce(
        [owned(grad_w_in), owned(grad_w_out), small_grads.reshape(devices, 24, 128)],
        [(16, 1664), (16, 1536), (24, 128)],
        6,
        ahead=3,
        more=[far_first, far_down, grad_first, grad_down],
        more_shapes=[far_first.shape, far_down.shape] * 2,
        moves=[
            move
            for part, axis, starts in ((0, 1, first_strips), (1, 2, down_strips))
            for start in starts
            for move in (
                (part, part, strip(start), strip(start), 2),
                (2 + part, 2 + part, quarter(axis, width, 1, start), strip(start), 1),
            )
        ],
    )
    near_first, near_down = (
        own_quarter(whole, axis, 0).astype(f32) + beside.astype(f32)
        for whole, beside, axis in ((grad_first, beside_first, 1), (grad_down, beside_down, 2))
    )
    layer_out = (resid_mid + shared_out + routed_own.astype(f32) + routed_far.astype(f32)).astype(bf16)[None]
    sum_sgate, sum_sup = jnp.split(sum_shared, 2, axis=1)
    grad_e_gate = expert_owners(near_first[..., :hidden], far_first[..., :hidden])
    grad_e_up = expert_owners(near_first[..., hidden:], far_first[..., hidden:])
    grad_e_down = expert_owners(near_down, far_down)
    sum_small = sum_small.reshape(-1)
    taken, mine = 0, []
    for part in small_parts:
        mine.append(sum_small[taken : taken + part.size].reshape(part.shape))
        taken += part.size
    return (
        layer_out,
        grad_in,
        mine[0],
        sum_in,
        mine[1],
        mine[2],
        sum_small[taken : taken + HEADS],
        sum_small[taken + HEADS : taken + 2 * HEADS],
        sum_small[taken + 2 * HEADS : taken + 3 * HEADS],
        mine[3],
        sum_out,
        mine[4],
        mine[5],
        sum_sgate,
        sum_sup,
        sum_sdown,
        grad_e_gate,
        grad_e_up,
        grad_e_down,
    )


def solution(mesh):
    in_specs = (
        P("dp", "ctx", None),
        P("dp", None),
        P("dp", "ctx", None),
        P("dp", "ctx", None),
        P(("dp", "ctx")),
        P(("dp", "ctx"), None),
        P(None, ("dp", "ctx")),
        P(("dp", "ctx")),
        P(),
        P(),
        P(),
        P(("dp", "ctx")),
        P(("dp", "ctx"), None),
        P(("dp", "ctx")),
        P(("dp", "ctx"), None),
        P(("dp", "ctx"), None),
        P(("dp", "ctx"), None),
        P(("dp", "ctx"), None),
        P("dp", "ctx", None),
        P("dp", "ctx", None),
        P("dp", None, "ctx"),
    )
    out_specs = (
        P("dp", "ctx", None),
        P("dp", "ctx", None),
        P(("dp", "ctx")),
        P(("dp", "ctx"), None),
        P(None, ("dp", "ctx")),
        P(("dp", "ctx")),
        P(),
        P(),
        P(),
        P(("dp", "ctx")),
        P(("dp", "ctx"), None),
        P(("dp", "ctx")),
        P(("dp", "ctx"), None),
        P(("dp", "ctx"), None),
        P(("dp", "ctx"), None),
        P(("dp", "ctx"), None),
        P("dp", "ctx", None),
        P("dp", "ctx", None),
        P("dp", None, "ctx"),
    )
    one_each = mesh.shape["ctx"] == EXP_DEV and mesh.shape["dp"] == 8
    return jax.shard_map(
        on_device if one_each else on_device_general, mesh=mesh, in_specs=in_specs, out_specs=out_specs, check_vma=False
    )
```

```python
from functools import partial

import jax
import jax.numpy as jnp
from jax import lax
from jax.experimental import pallas as pl
from jax.experimental.layout import Layout, with_layout_constraint
from jax.experimental.pallas import tpu as pltpu
from jax.sharding import PartitionSpec as P

HEADS = 48
HEAD = 64
STATE = 128
TOP = 6
EXP_DEV = 4
DI = 3072
CONV = 3328
PROJ = 6448


def from_behind(value, axis, steps):
    count = lax.axis_size(axis)
    leading, last = (max(0, -steps), min(count, count - steps))
    return lax.ppermute(value, axis, [(source, source + steps) for source in range(leading, last)])


def carried_in_2(x, axis, combine, identity):
    count, mine = (lax.axis_size(axis), lax.axis_index(axis))
    everything = jax.tree.map(
        lambda part, kind: lax.all_gather(part.astype(kind), axis), x, (jnp.bfloat16, jnp.bfloat16)
    )
    start = jax.tree.map(
        lambda part, zero: jnp.broadcast_to(jnp.asarray(zero, part.dtype), part.shape), x, identity
    )

    def lap(k, before):
        reached = k < mine
        new = combine(
            before, jax.tree.map(lambda part, own: part[k].astype(own.dtype), everything, x)
        )
        return jax.tree.map(lambda a, b: jnp.where(reached, a, b), new, before)

    return lax.fori_loop(0, count, lap, start)


def carried_in_3(x, axis, combine, identity):
    count, mine = (lax.axis_size(axis), lax.axis_index(axis))
    everything = jax.tree.map(
        lambda part, kind: lax.all_gather(part.astype(kind), axis),
        x,
        jax.tree.map(lambda a: jnp.bfloat16 if a.dtype == jnp.float32 else a.dtype, x),
    )
    start = jax.tree.map(
        lambda part, zero: jnp.broadcast_to(jnp.asarray(zero, part.dtype), part.shape), x, identity
    )

    def lap(k, before):
        at = count - 1 - k
        reached = at > mine
        new = combine(
            before, jax.tree.map(lambda part, own: part[at].astype(own.dtype), everything, x)
        )
        return jax.tree.map(lambda a, b: jnp.where(reached, a, b), new, before)

    return lax.fori_loop(0, count, lap, start)


def for_sending(x):
    return jax.tree.map(lambda a: a.astype(jnp.bfloat16) if a.dtype == jnp.float32 else a, x)


def normalize(value):
    return value * lax.rsqrt(jnp.mean(value * value, axis=-1, keepdims=True) + 1e-05)


def scaled_norm(value, gain):
    return normalize(value) * gain


def gate_norm(y_heads, z_part, gain):
    joined = y_heads.reshape(z_part.shape) * jax.nn.silu(z_part)
    return normalize(joined) * gain


def silu_slope(value):
    squashed = jax.nn.sigmoid(value)
    return squashed * (1.0 + value * (1.0 - squashed))


def conv_apply(padded, weight, bias, seg_pad):
    tap_count = weight.shape[0]
    length = padded.shape[1] - tap_count + 1
    current = seg_pad[:, tap_count - 1 :]
    summed = bias + jnp.zeros(padded[:, tap_count - 1 :].shape, jnp.float32)
    for offset in range(tap_count):
        matches = (seg_pad[:, offset : offset + length] == current).astype(jnp.float32)
        summed = summed + weight[offset] * padded[:, offset : offset + length] * matches[..., None]
    return jax.nn.silu(summed)


def split_blocks(value, count):
    shaped = value.reshape((value.shape[0], count, value.shape[1] // count) + value.shape[2:])
    return jnp.moveaxis(shaped, 1, 0)


def block_step(carried_in, pieces):
    memory, previous = carried_in
    x_heads, b_mat, c_mat, dt_pos, decay, segment_ids = pieces
    cumul = jnp.cumsum(decay, axis=1)
    places = jnp.arange(segment_ids.shape[1])
    causal = places[:, None] >= places[None, :]
    linked = ((segment_ids[:, :, None] == segment_ids[:, None, :]) & causal[None])[..., None]
    spread = cumul[:, :, None, :] - cumul[:, None, :, :]
    weights = jnp.where(linked, jnp.exp(jnp.where(linked, spread, 0.0)), 0.0)
    inner = jnp.einsum("gtn,gsn->gts", c_mat, b_mat, precision=lax.Precision.HIGHEST)
    weights = weights * inner[..., None] * dt_pos[:, None, :, :]
    output = jnp.einsum("gtsh,gshp->gthp", weights, x_heads, precision=lax.Precision.HIGHEST)
    keeps = (segment_ids == previous[:, None]).astype(jnp.float32)
    reach = jnp.exp(cumul) * keeps[..., None]
    output = (
        output
        + jnp.einsum("gtn,ghpn->gthp", c_mat, memory, precision=lax.Precision.HIGHEST)
        * reach[..., None]
    )
    latest = segment_ids[:, -1]
    tails = (
        jnp.exp(cumul[:, -1:, :] - cumul)
        * (segment_ids == latest[:, None]).astype(jnp.float32)[..., None]
        * dt_pos
    )
    through = jnp.exp(cumul[:, -1, :]) * (latest == previous).astype(jnp.float32)[:, None]
    memory = memory * through[..., None, None] + jnp.einsum(
        "gsh,gshp,gsn->ghpn", tails, x_heads, b_mat, precision=lax.Precision.HIGHEST
    )
    return ((memory, latest), output)


def scan_blocks(x_heads, b_mat, c_mat, dt_pos, decay, segment_ids, memory, previous):
    length = segment_ids.shape[1]
    count = length // min(128, length)
    inputs = tuple(
        (
            split_blocks(value, count)
            for value in (x_heads, b_mat, c_mat, dt_pos, decay, segment_ids)
        )
    )
    (memory, latest), outputs = lax.scan(jax.checkpoint(block_step), (memory, previous), inputs)
    return (jnp.moveaxis(outputs, 0, 1).reshape(x_heads.shape), memory)


def part_local(x_heads, b_mat, c_mat, dt_raw, dt_bias, a_log, d_skip, segment_ids, previous):
    dt_pos = jax.nn.softplus(dt_raw + dt_bias)
    decay = -jnp.exp(a_log) * dt_pos
    zero_state = jnp.zeros((x_heads.shape[0], HEADS, HEAD, STATE), jnp.float32)
    mixed_heads, final_state = scan_blocks(
        x_heads, b_mat, c_mat, dt_pos, decay, segment_ids, zero_state, previous
    )
    y_local = mixed_heads + d_skip[:, None] * x_heads
    through = (
        jnp.exp(jnp.sum(decay, axis=1))
        * (segment_ids[:, -1] == previous).astype(jnp.float32)[:, None]
    )
    return (y_local, final_state, through)


def part_carry(c_mat, dt_raw, dt_bias, a_log, state_in, segment_ids, previous):
    dt_pos = jax.nn.softplus(dt_raw + dt_bias)
    cumul = jnp.cumsum(-jnp.exp(a_log) * dt_pos, axis=1)
    keeps = (segment_ids == previous[:, None]).astype(jnp.float32)
    reach = jnp.exp(cumul) * keeps[..., None]
    return (
        jnp.einsum("gtn,ghpn->gthp", c_mat, state_in, precision=lax.Precision.HIGHEST)
        * reach[..., None]
    )


def carry_forward(earlier, later):
    return (earlier[0] * later[0], later[0][..., None, None] * earlier[1] + later[1])


def carry_backward(earlier, later):
    return (earlier[0] * later[0], later[1] + later[0][..., None, None] * earlier[1])


def route_slots(flat_routes, expert_count, capacity):
    blocks = flat_routes.shape[0]
    onehot = (flat_routes[..., None] == jnp.arange(expert_count, dtype=jnp.int32)).astype(jnp.int32)
    ranks = jnp.sum((jnp.cumsum(onehot, axis=1) - onehot) * onehot, axis=-1)
    spots = (
        flat_routes * (blocks * capacity)
        + jnp.arange(blocks, dtype=jnp.int32)[:, None] * capacity
        + ranks
    )
    return spots


def times_rows(left, right):
    return lax.dot_general(
        left, right, (((0,), (0,)), ((), ())), preferred_element_type=jnp.float32
    )


def times_back(left, right):
    return lax.dot_general(
        left, right, (((1,), (1,)), ((), ())), preferred_element_type=jnp.float32
    )


def on_device_general(
    layer_in,
    seg_ids,
    route_ids,
    out_grad,
    norm_in,
    w_in,
    conv_w,
    conv_b,
    dt_bias,
    a_log,
    d_skip,
    norm_gate,
    w_out,
    norm_mid,
    w_router,
    w_sgate,
    w_sup,
    w_sdown,
    e_gate,
    e_up,
    e_down,
):
    seq_count, row_count, d_model = layer_in.shape
    token_count = seq_count * row_count
    tap_count = conv_w.shape[0]
    ctx_place = lax.axis_index("ctx")
    expert_count = EXP_DEV * lax.axis_size("dp")
    capacity = row_count * TOP * 5 // (expert_count * 4)
    dense_set = (
        lax.all_gather(norm_in, ("dp", "ctx"), axis=0, tiled=True),
        lax.all_gather(w_in, ("dp", "ctx"), axis=0, tiled=True),
        lax.all_gather(conv_w, ("dp", "ctx"), axis=1, tiled=True),
        lax.all_gather(conv_b, ("dp", "ctx"), axis=0, tiled=True),
        lax.all_gather(norm_gate, ("dp", "ctx"), axis=0, tiled=True),
        lax.all_gather(w_out, ("dp", "ctx"), axis=0, tiled=True),
        lax.all_gather(norm_mid, ("dp", "ctx"), axis=0, tiled=True),
        lax.all_gather(w_router, ("dp", "ctx"), axis=0, tiled=True),
        lax.all_gather(w_sgate, ("dp", "ctx"), axis=0, tiled=True),
        lax.all_gather(w_sup, ("dp", "ctx"), axis=0, tiled=True),
        lax.all_gather(w_sdown, ("dp", "ctx"), axis=0, tiled=True),
    )
    (
        gain_in,
        weight_in,
        conv_weight,
        conv_bias,
        gain_gate,
        weight_out,
        gain_mid,
        router_weight,
        sgate_weight,
        sup_weight,
        sdown_weight,
    ) = dense_set
    expert_gate, expert_up, expert_down = (
        lax.all_gather(e_gate, "ctx", axis=1, tiled=True),
        lax.all_gather(e_up, "ctx", axis=1, tiled=True),
        lax.all_gather(e_down, "ctx", axis=2, tiled=True),
    )
    input_f = layer_in.astype(jnp.float32)
    normed_f, pull_in = jax.vjp(scaled_norm, input_f, gain_in.astype(jnp.float32))
    normed = normed_f.astype(jnp.bfloat16).reshape(token_count, d_model)
    projected = jnp.dot(normed, weight_in, preferred_element_type=jnp.float32).reshape(
        seq_count, row_count, PROJ
    )
    z_part = projected[..., :DI]
    xbc_part = projected[..., DI : DI + CONV]
    dt_raw = projected[..., DI + CONV :]
    edge_rows = from_behind(
        xbc_part[:, row_count - tap_count + 1 :, :].astype(jnp.bfloat16), "ctx", 1
    ).astype(jnp.float32)
    seg_pad = jnp.concatenate(
        [jnp.full((seq_count, tap_count - 1), -1, jnp.int32), seg_ids], axis=1
    )
    seg_window = lax.dynamic_slice_in_dim(
        seg_pad, ctx_place * row_count, row_count + tap_count - 1, 1
    )
    seg_now = seg_window[:, tap_count - 1 :]
    seg_before = seg_window[:, tap_count - 2]
    padded = jnp.concatenate([edge_rows, xbc_part], axis=1)
    conv_out, pull_conv = jax.vjp(
        partial(conv_apply, seg_pad=seg_window),
        padded,
        conv_weight.astype(jnp.float32),
        conv_bias.astype(jnp.float32),
    )
    x_heads = conv_out[..., :DI].reshape(seq_count, row_count, HEADS, HEAD)
    b_mat = conv_out[..., DI : DI + STATE]
    c_mat = conv_out[..., DI + STATE :]
    local_piece = partial(part_local, segment_ids=seg_now, previous=seg_before)
    (y_local, state_out, through), pull_local = jax.vjp(
        local_piece, x_heads, b_mat, c_mat, dt_raw, dt_bias, a_log, d_skip
    )
    carried = carried_in_2(
        (through, state_out),
        "ctx",
        carry_forward,
        (jnp.ones_like(through), jnp.zeros_like(state_out)),
    )
    state_in = carried[1]
    carry_piece = partial(part_carry, segment_ids=seg_now, previous=seg_before)
    y_carry, pull_carry = jax.vjp(carry_piece, c_mat, dt_raw, dt_bias, a_log, state_in)
    gated_f, pull_gate = jax.vjp(
        gate_norm, y_local + y_carry, z_part, gain_gate.astype(jnp.float32)
    )
    gated = gated_f.astype(jnp.bfloat16).reshape(token_count, DI)
    mixed = jnp.dot(gated, weight_out, preferred_element_type=jnp.float32)
    resid_mid = input_f.reshape(token_count, d_model) + mixed
    normed_mid_f, pull_mid = jax.vjp(scaled_norm, resid_mid, gain_mid.astype(jnp.float32))
    normed_mid = normed_mid_f.astype(jnp.bfloat16)
    logits = jnp.dot(normed_mid, router_weight, preferred_element_type=jnp.float32)
    route_flat = route_ids.reshape(token_count, TOP)
    gates = jax.nn.softmax(jnp.take_along_axis(logits, route_flat, axis=1), axis=-1)
    shared_gate = jnp.dot(normed_mid, sgate_weight, preferred_element_type=jnp.float32)
    shared_up = jnp.dot(normed_mid, sup_weight, preferred_element_type=jnp.float32)
    shared_act = (jax.nn.silu(shared_gate) * shared_up).astype(jnp.bfloat16)
    shared_out = jnp.dot(shared_act, sdown_weight, preferred_element_type=jnp.float32)
    slot_ids = route_slots(route_ids.reshape(seq_count, row_count * TOP), expert_count, capacity)
    assigned = jnp.arange(token_count * TOP, dtype=jnp.int32)
    owners = (
        jnp.full((expert_count * seq_count * capacity,), token_count * TOP, jnp.int32)
        .at[slot_ids.reshape(-1)]
        .set(assigned)
    )
    token_of = owners // TOP
    rows_pad = jnp.concatenate([normed_mid, jnp.zeros((1, d_model), jnp.bfloat16)], axis=0)
    outgoing = rows_pad[token_of].reshape(expert_count, seq_count * capacity, d_model)
    incoming = lax.all_to_all(outgoing, "dp", split_axis=0, concat_axis=1, tiled=True)
    hidden_gate = jnp.einsum(
        "erd,edf->erf", incoming, expert_gate, preferred_element_type=jnp.float32
    )
    hidden_up = jnp.einsum("erd,edf->erf", incoming, expert_up, preferred_element_type=jnp.float32)
    hidden_act = (jax.nn.silu(hidden_gate) * hidden_up).astype(jnp.bfloat16)
    expert_out = jnp.einsum(
        "erf,efd->erd", hidden_act, expert_down, preferred_element_type=jnp.float32
    ).astype(jnp.bfloat16)
    returned = lax.all_to_all(expert_out, "dp", split_axis=1, concat_axis=0, tiled=True)
    slot_flat = slot_ids.reshape(token_count, TOP)
    picked = returned.reshape(-1, d_model)[slot_flat]
    routed = jnp.sum(gates[..., None] * picked, axis=1)
    layer_out = (
        (resid_mid + shared_out + routed)
        .astype(jnp.bfloat16)
        .reshape(seq_count, row_count, d_model)
    )
    grad_top = out_grad.astype(jnp.float32).reshape(token_count, d_model)
    grad_gates = jnp.sum(picked * grad_top[:, None, :], axis=-1)
    grad_pick = gates * (grad_gates - jnp.sum(gates * grad_gates, axis=-1, keepdims=True))
    expert_ids = jnp.arange(expert_count, dtype=jnp.int32)
    grad_logits = jnp.sum(
        grad_pick[..., None] * (route_flat[..., None] == expert_ids).astype(jnp.float32), axis=1
    ).astype(jnp.bfloat16)
    gates_pad = jnp.concatenate([gates.reshape(-1), jnp.zeros((1,), jnp.float32)])
    grad_pad = jnp.concatenate([grad_top, jnp.zeros((1, d_model), jnp.float32)], axis=0)
    grad_slots = (
        (gates_pad[owners][:, None] * grad_pad[token_of])
        .astype(jnp.bfloat16)
        .reshape(expert_count, seq_count * capacity, d_model)
    )
    grad_arrived = lax.all_to_all(grad_slots, "dp", split_axis=0, concat_axis=1, tiled=True)
    grad_act = jnp.einsum(
        "erd,efd->erf", grad_arrived, expert_down, preferred_element_type=jnp.float32
    )
    grad_e_down = jnp.einsum(
        "erf,erd->efd", hidden_act, grad_arrived, preferred_element_type=jnp.float32
    )
    grad_hgate = (grad_act * hidden_up * silu_slope(hidden_gate)).astype(jnp.bfloat16)
    grad_hup = (grad_act * jax.nn.silu(hidden_gate)).astype(jnp.bfloat16)
    grad_e_gate = jnp.einsum(
        "erd,erf->edf", incoming, grad_hgate, preferred_element_type=jnp.float32
    )
    grad_e_up = jnp.einsum("erd,erf->edf", incoming, grad_hup, preferred_element_type=jnp.float32)
    grad_incoming = jnp.einsum(
        "erf,edf->erd", grad_hgate, expert_gate, preferred_element_type=jnp.float32
    )
    grad_incoming = (
        grad_incoming
        + jnp.einsum("erf,edf->erd", grad_hup, expert_up, preferred_element_type=jnp.float32)
    ).astype(jnp.bfloat16)
    grad_returned = lax.all_to_all(grad_incoming, "dp", split_axis=1, concat_axis=0, tiled=True)
    grad_routed = jnp.sum(grad_returned.reshape(-1, d_model)[slot_flat], axis=1, dtype=jnp.float32)
    dense_set = (
        lax.all_gather(norm_in, ("dp", "ctx"), axis=0, tiled=True),
        lax.all_gather(w_in, ("dp", "ctx"), axis=0, tiled=True),
        lax.all_gather(conv_w, ("dp", "ctx"), axis=1, tiled=True),
        lax.all_gather(conv_b, ("dp", "ctx"), axis=0, tiled=True),
        lax.all_gather(norm_gate, ("dp", "ctx"), axis=0, tiled=True),
        lax.all_gather(w_out, ("dp", "ctx"), axis=0, tiled=True),
        lax.all_gather(norm_mid, ("dp", "ctx"), axis=0, tiled=True),
        lax.all_gather(w_router, ("dp", "ctx"), axis=0, tiled=True),
        lax.all_gather(w_sgate, ("dp", "ctx"), axis=0, tiled=True),
        lax.all_gather(w_sup, ("dp", "ctx"), axis=0, tiled=True),
        lax.all_gather(w_sdown, ("dp", "ctx"), axis=0, tiled=True),
    )
    (
        gain_in,
        weight_in,
        conv_weight,
        conv_bias,
        gain_gate,
        weight_out,
        gain_mid,
        router_weight,
        sgate_weight,
        sup_weight,
        sdown_weight,
    ) = dense_set
    grad_w_router = times_rows(normed_mid, grad_logits)
    grad_shared_out = grad_top.astype(jnp.bfloat16)
    grad_w_sdown = times_rows(shared_act, grad_shared_out)
    grad_shared_act = times_back(grad_shared_out, sdown_weight)
    grad_sgate = (grad_shared_act * shared_up * silu_slope(shared_gate)).astype(jnp.bfloat16)
    grad_sup = (grad_shared_act * jax.nn.silu(shared_gate)).astype(jnp.bfloat16)
    grad_w_sgate = times_rows(normed_mid, grad_sgate)
    grad_w_sup = times_rows(normed_mid, grad_sup)
    grad_mid = (
        grad_routed
        + times_back(grad_logits, router_weight)
        + times_back(grad_sgate, sgate_weight)
        + times_back(grad_sup, sup_weight)
    )
    grad_resid_part, grad_gain_mid = pull_mid(grad_mid)
    grad_resid = grad_top + grad_resid_part
    grad_mixed = grad_resid.astype(jnp.bfloat16)
    grad_w_out = times_rows(gated, grad_mixed)
    grad_gated = times_back(grad_mixed, weight_out).reshape(seq_count, row_count, DI)
    grad_y, grad_z, grad_gain_gate = pull_gate(grad_gated)
    grad_cmat_carry, grad_dt_carry, grad_bias_carry, grad_alog_carry, grad_state_in = pull_carry(
        grad_y
    )
    back_scan = carried_in_3(
        (through, grad_state_in),
        "ctx",
        carry_backward,
        (jnp.ones_like(through), jnp.zeros_like(grad_state_in)),
    )
    grad_state_out = back_scan[1]
    grad_through = jnp.sum(state_in * grad_state_out, axis=(2, 3))
    (
        grad_xheads,
        grad_bmat,
        grad_cmat,
        grad_dt_local,
        grad_bias_local,
        grad_alog_local,
        grad_dskip,
    ) = pull_local((grad_y, grad_state_out, grad_through))
    grad_conv_out = jnp.concatenate(
        [grad_xheads.reshape(seq_count, row_count, DI), grad_bmat, grad_cmat + grad_cmat_carry],
        axis=-1,
    )
    grad_padded, grad_conv_w, grad_conv_b = pull_conv(grad_conv_out)
    edge_grad = from_behind(for_sending(grad_padded[:, : tap_count - 1, :]), "ctx", -1)
    grad_xbc = grad_padded[:, tap_count - 1 :, :]
    grad_xbc = jnp.concatenate(
        [
            grad_xbc[:, : row_count - tap_count + 1],
            grad_xbc[:, row_count - tap_count + 1 :] + edge_grad,
        ],
        axis=1,
    )
    grad_proj = (
        jnp.concatenate([grad_z, grad_xbc, grad_dt_local + grad_dt_carry], axis=-1)
        .astype(jnp.bfloat16)
        .reshape(token_count, PROJ)
    )
    grad_w_in = times_rows(normed, grad_proj)
    grad_normed = times_back(grad_proj, weight_in).reshape(seq_count, row_count, d_model)
    grad_input_part, grad_gain_in = pull_in(grad_normed)
    grad_in = grad_resid.reshape(seq_count, row_count, d_model) + grad_input_part
    dense_grads = (
        lax.psum_scatter(grad_gain_in, ("dp", "ctx"), scatter_dimension=0, tiled=True),
        lax.psum_scatter(grad_w_in, ("dp", "ctx"), scatter_dimension=0, tiled=True),
        lax.psum_scatter(grad_conv_w, ("dp", "ctx"), scatter_dimension=1, tiled=True),
        lax.psum_scatter(grad_conv_b, ("dp", "ctx"), scatter_dimension=0, tiled=True),
        lax.psum_scatter(grad_gain_gate, ("dp", "ctx"), scatter_dimension=0, tiled=True),
        lax.psum_scatter(grad_w_out, ("dp", "ctx"), scatter_dimension=0, tiled=True),
        lax.psum_scatter(grad_gain_mid, ("dp", "ctx"), scatter_dimension=0, tiled=True),
        lax.psum_scatter(grad_w_router, ("dp", "ctx"), scatter_dimension=0, tiled=True),
        lax.psum_scatter(grad_w_sgate, ("dp", "ctx"), scatter_dimension=0, tiled=True),
        lax.psum_scatter(grad_w_sup, ("dp", "ctx"), scatter_dimension=0, tiled=True),
        lax.psum_scatter(grad_w_sdown, ("dp", "ctx"), scatter_dimension=0, tiled=True),
    )
    expert_grads = (
        lax.psum_scatter(
            grad_e_gate.astype(jnp.bfloat16), "ctx", scatter_dimension=1, tiled=True
        ).astype(jnp.float32),
        lax.psum_scatter(
            grad_e_up.astype(jnp.bfloat16), "ctx", scatter_dimension=1, tiled=True
        ).astype(jnp.float32),
        lax.psum_scatter(
            grad_e_down.astype(jnp.bfloat16), "ctx", scatter_dimension=2, tiled=True
        ).astype(jnp.float32),
    )
    head_grads = lax.psum(
        (grad_bias_local + grad_bias_carry, grad_alog_local + grad_alog_carry, grad_dskip),
        ("dp", "ctx"),
    )
    return (
        layer_out,
        grad_in,
        dense_grads[0],
        dense_grads[1],
        dense_grads[2],
        dense_grads[3],
        head_grads[0],
        head_grads[1],
        head_grads[2],
        dense_grads[4],
        dense_grads[5],
        dense_grads[6],
        dense_grads[7],
        dense_grads[8],
        dense_grads[9],
        dense_grads[10],
        expert_grads[0],
        expert_grads[1],
        expert_grads[2],
    )


GROUP = 8
WIDE = GROUP * HEAD
VMEM_MOST = 56 * 1024 * 1024
BRIEF = pl.CostEstimate(flops=1024, bytes_accessed=1024, transcendentals=0)


def spread_rows(rows):
    count, width = rows.shape
    return jnp.broadcast_to(rows[:, None, :], (count, HEAD, width)).reshape(count * HEAD, width)


def head_sums(value):
    return jnp.sum(value.reshape(GROUP, HEAD, value.shape[-1]), axis=1)


def mul_nn(left, right):
    return lax.dot_general(
        left, right, (((1,), (0,)), ((), ())), preferred_element_type=jnp.float32
    )


def mul_nt(left, right):
    return lax.dot_general(
        left, right, (((1,), (1,)), ((), ())), preferred_element_type=jnp.float32
    )


def mul_tn(left, right):
    return lax.dot_general(
        left, right, (((0,), (0,)), ((), ())), preferred_element_type=jnp.float32
    )


def half(value):
    return value.astype(jnp.bfloat16)


def call_steps(kernel, steps, ins, in_specs, outs, out_specs, scratch=(), name_id=None, micros=0):
    return pl.pallas_call(
        kernel,
        grid=(steps,),
        in_specs=in_specs,
        out_specs=out_specs,
        out_shape=outs,
        scratch_shapes=list(scratch),
        cost_estimate=pl.CostEstimate(flops=1024 + micros * 10**9, bytes_accessed=1024, transcendentals=0),
        compiler_params=pltpu.CompilerParams(
            vmem_limit_bytes=VMEM_MOST,
            dimension_semantics=("arbitrary",),
            collective_id=name_id,
            has_side_effects=name_id is not None,
        ),
    )(*ins)


def block(shape, index):
    return pl.BlockSpec(shape, index)


def whole(array):
    return pl.BlockSpec(array.shape, lambda i: (0,) * array.ndim)


def f32_out(*shape):
    return jax.ShapeDtypeStruct(shape, jnp.float32)


def bf16_out(*shape):
    return jax.ShapeDtypeStruct(shape, jnp.bfloat16)


def conv_steps(x, taps, masks):
    total = taps[:, 4:5] + taps[:, 3:4] * x * masks[0:1]
    for back in (1, 2, 3):
        total = total + taps[:, 3 - back : 4 - back] * pltpu.roll(x, back, 1) * masks[back : back + 1]
    return total


def conv_kernel(x_ref, taps_ref, masks_ref, pre_ref):
    tokens = pre_ref.shape[1]
    pre_ref[...] = conv_steps(x_ref[...], taps_ref[...], masks_ref[...])[:, :tokens]


def conv_adjoint(grad_pre, x, taps, masks):
    width = x.shape[1]
    grad_x = jnp.zeros_like(x)
    columns = []
    for back in (3, 2, 1, 0):
        part = grad_pre * masks[back : back + 1]
        moved = x if back == 0 else pltpu.roll(x, back, 1)
        columns.append(jnp.sum(part * moved, axis=1, keepdims=True))
        tap = taps[:, 3 - back : 4 - back]
        grad_x = grad_x + tap * (part if back == 0 else pltpu.roll(part, width - back, 1))
    columns.append(jnp.sum(grad_pre, axis=1, keepdims=True))
    lane = lax.broadcasted_iota(jnp.int32, (x.shape[0], 8), 1)
    packed = jnp.zeros((x.shape[0], 8), jnp.float32)
    for place, column in enumerate(columns):
        packed = jnp.where(lane == place, column, packed)
    return grad_x, packed


def conv_back_kernel(grad_ref, pre_ref, x_ref, taps_ref, masks_ref, grad_x_ref, taps_out_ref):
    grad_pre = grad_ref[...] * silu_slope(pre_ref[...])
    rest = x_ref.shape[1] - grad_pre.shape[1]
    grad_pre = jnp.concatenate([grad_pre, jnp.zeros((grad_pre.shape[0], rest), jnp.float32)], axis=1)
    grad_x, packed = conv_adjoint(grad_pre, x_ref[...], taps_ref[...], masks_ref[...])
    grad_x_ref[...] = grad_x.astype(grad_x_ref.dtype)
    taps_out_ref[...] = packed


def link_mask(seg_row, seg_col):
    count = seg_row.shape[1]
    source = lax.broadcasted_iota(jnp.int32, (count, count), 0)
    target = lax.broadcasted_iota(jnp.int32, (count, count), 1)
    linked = jnp.logical_and(source <= target, seg_row == seg_col)
    return jnp.where(linked, 0.0, -1e30)


def state_kernel(x_ref, taps_ref, masks_ref, bc_ref, dt_ref, cum_ref, flags_ref, pre_ref, state_ref):
    tokens = pre_ref.shape[1]
    pre = conv_steps(x_ref[...], taps_ref[...], masks_ref[...])[:, :tokens]
    pre_ref[...] = pre
    b_t = half(jax.nn.silu(bc_ref[:STATE, :]))
    cum = cum_ref[...]
    tail = jnp.exp(cum[:, tokens - 1 :] - cum) * flags_ref[1:2, :] * dt_ref[...]
    scaled = half(jax.nn.silu(pre) * spread_rows(tail))
    state_ref[...] = half(mul_nt(scaled, b_t))


def gate_back_kernel(
    y_ref, z_ref, grad_ref, gain_ref, rows_ref, bc_ref, cum_ref, flags_ref, grad_y_ref, grad_z_ref, grad_state_ref
):
    y, z, gain = y_ref[...], z_ref[...], gain_ref[:, 0:1]
    squashed = jax.nn.sigmoid(z)
    u = y * z * squashed
    grad_u = gain * rows_ref[0:1, :] * grad_ref[...] - u * rows_ref[1:2, :]
    grad_y = grad_u * z * squashed
    grad_y_ref[...] = grad_y
    grad_z_ref[...] = half(grad_u * y * (squashed * (1.0 + z * (1.0 - squashed))))
    c_t = half(jax.nn.silu(bc_ref[STATE:, :]))
    reach = jnp.exp(cum_ref[...]) * flags_ref[0:1, :]
    grad_state_ref[...] = half(mul_nt(half(grad_y * spread_rows(reach)), c_t))


def inner_back_kernel(
    local_ref, passed_ref, pre_ref, grad_y_ref, bc_ref, dt_ref, cum_ref, cum_col_ref, flags_ref, seg_col_ref,
    grad_x_ref, grad_state_ref, grad_cum_ref, grad_skip_ref, grad_bc_ref, mask_s, inner_s, total_s, *chain,
):
    step = pl.program_id(0)
    first, last, device = chain_places(step, False)

    @pl.when(step == 0)
    def _():
        mask_s[...] = link_mask(flags_ref[2:3, :], seg_col_ref[:, 0:1])
        bc = half(jax.nn.silu(bc_ref[...]))
        inner_s[...] = mul_tn(bc[:STATE], bc[STATE:])
        total_s[...] = jnp.zeros_like(total_s)

    grad_state_ref[...] = chain_step(step, first, last, device, local_ref, passed_ref, *chain)
    x = jax.nn.silu(pre_ref[...])
    grad_y = grad_y_ref[...]
    grad_skip_ref[...] = head_sums(x * grad_y)
    scaled = half(x * spread_rows(dt_ref[...]))
    grad_half = half(grad_y)
    cum, cum_col = cum_ref[...], cum_col_ref[0]
    ones = jnp.ones((8, cum.shape[1]), jnp.bfloat16)
    for head in range(GROUP):
        rows = slice(head * HEAD, (head + 1) * HEAD)
        decay = jnp.exp(cum[head : head + 1, :] - cum_col[:, head : head + 1] + mask_s[...])
        weights = decay * inner_s[...]
        grad_x_ref[rows, :] = mul_nt(grad_half[rows], half(weights))
        grad_weights = mul_tn(scaled[rows], grad_half[rows])
        total_s[...] += grad_weights * decay
        moved = half(grad_weights * weights)
        sums = mul_nn(ones, moved) - mul_nt(ones, moved)
        grad_cum_ref[head : head + 1, :] = sums[0:1]

    @pl.when(step == pl.num_programs(0) - 1)
    def _():
        bc = half(jax.nn.silu(bc_ref[...]))
        total = half(total_s[...])
        grad_bc_ref[:STATE, :] = mul_nt(bc[STATE:], total)
        grad_bc_ref[STATE:, :] = mul_nn(bc[:STATE], total)
        chain_end(chain[0].shape[0], last, device, *chain)


def join_back_kernel(
    grad_in_ref, grad_y_ref, pre_ref, x_ref, taps_ref, masks_ref, state_ref, grad_state_ref,
    bc_ref, dt_ref, cum_ref, skip_ref, flags_ref,
    grad_x_ref, taps_out_ref, grad_dt_ref, grad_cum_ref, grad_last_ref, grad_bc_ref,
):
    step = pl.program_id(0)

    @pl.when(step == 0)
    def _():
        grad_bc_ref[...] = jnp.zeros_like(grad_bc_ref)

    bc = half(jax.nn.silu(bc_ref[...]))
    b_t, c_t = bc[:STATE], bc[STATE:]
    pre, grad_y, cum, dt = pre_ref[...], grad_y_ref[...], cum_ref[...], dt_ref[...]
    tokens = pre.shape[1]
    state, grad_state = state_ref[...], grad_state_ref[...]
    x = jax.nn.silu(pre)
    reached = grad_y * spread_rows(jnp.exp(cum) * flags_ref[0:1, :])
    grad_cum = head_sums(reached * mul_nn(state, c_t))
    grad_bc_ref[STATE:, :] += mul_tn(state, half(reached))
    tail = spread_rows(jnp.exp(cum[:, tokens - 1 :] - cum) * flags_ref[1:2, :])
    dt_wide = spread_rows(dt)
    scaled = x * dt_wide
    from_state = mul_nn(grad_state, b_t) * tail
    grad_bc_ref[:STATE, :] += mul_tn(grad_state, half(scaled * tail))
    tails = head_sums(scaled * from_state)
    grad_cum_ref[...] = grad_cum - tails
    last = jnp.sum(tails, axis=1, keepdims=True)
    through = jnp.sum(
        head_sums(state.astype(jnp.float32) * grad_state.astype(jnp.float32)), axis=1, keepdims=True
    )
    lane = lax.broadcasted_iota(jnp.int32, (GROUP, 128), 1)
    grad_last_ref[...] = jnp.where(lane == 0, last, jnp.where(lane == 1, through, 0.0))
    grad_scaled = grad_in_ref[...] + from_state
    grad_dt_ref[...] = head_sums(grad_scaled * x)
    grad_pre = (grad_scaled * dt_wide + grad_y * spread_rows(skip_ref[...])) * silu_slope(pre)
    rest = x_ref.shape[1] - tokens
    grad_pre = jnp.concatenate([grad_pre, jnp.zeros((grad_pre.shape[0], rest), jnp.float32)], axis=1)
    grad_x, packed = conv_adjoint(grad_pre, x_ref[...], taps_ref[...], masks_ref[...])
    grad_x_ref[...] = half(grad_x)
    taps_out_ref[...] = packed


def mixer_rows(dt_raw, dt_bias, a_log, d_skip, seg_window, taps):
    tokens = dt_raw.shape[1]
    dt = jax.nn.softplus(dt_raw + dt_bias[:, None])
    decay = -jnp.exp(a_log)[:, None] * dt
    upper = jnp.triu(jnp.ones((tokens, tokens), jnp.float32))
    cum = jnp.dot(decay, upper, precision=lax.Precision.HIGHEST)
    cum_col = jnp.swapaxes(cum.reshape(-1, GROUP, tokens), 1, 2)
    seg_now = seg_window[taps - 1 :]
    before = seg_window[taps - 2]
    reach = (seg_now == before).astype(jnp.float32)
    tail = (seg_now == seg_now[-1]).astype(jnp.float32)
    none = jnp.zeros((5, tokens), jnp.float32)
    flags = jnp.concatenate([jnp.stack([reach, tail, seg_now.astype(jnp.float32)]), none])
    seg_col = jnp.broadcast_to(seg_now.astype(jnp.float32)[:, None], (tokens, 8))
    masks = [
        (seg_window[taps - 1 - back : taps - 1 - back + tokens] == seg_now).astype(jnp.float32)
        for back in range(taps)
    ]
    masks = jnp.pad(jnp.stack(masks), ((0, 8 - taps), (0, 128)))
    through = jnp.exp(cum[:, -1]) * (seg_now[-1] == before).astype(jnp.float32)
    skip = jnp.broadcast_to(d_skip[:, None], dt.shape)
    return dt, decay, cum, cum_col, flags, seg_col, masks, through, skip


def mixer_forward_states(proj, taps, masks, dt, cum, flags):
    tokens, groups = dt.shape[1], HEADS // GROUP
    wide = proj.shape[1]
    bc_pre = call_steps(
        conv_kernel, 1, (proj, taps, masks),
        [block((2 * STATE, wide), lambda i: (DI // STATE, 0)),
         block((2 * STATE, 8), lambda i: (DI // (2 * STATE), 0)), whole(masks)],
        f32_out(2 * STATE, tokens), block((2 * STATE, tokens), lambda i: (0, 0)),
    )
    rows = block((GROUP, tokens), lambda i: (i, 0))
    pre, state = call_steps(
        state_kernel, groups, (proj, taps, masks, bc_pre, dt, cum, flags),
        [block((WIDE, wide), lambda i: (i + groups, 0)), block((WIDE, 8), lambda i: (i, 0)), whole(masks),
         whole(bc_pre), rows, rows, whole(flags)],
        [f32_out(DI, tokens), bf16_out(DI, STATE)],
        [block((WIDE, tokens), lambda i: (i, 0)), block((WIDE, STATE), lambda i: (i, 0))],
    )
    return bc_pre, pre, state


def mixer_back_gate(y, proj, grad_gated, gain_col, gate_rows, bc_pre, cum, flags):
    tokens, groups = y.shape[1], HEADS // GROUP
    wide = block((WIDE, tokens), lambda i: (i, 0))
    return call_steps(
        gate_back_kernel, groups, (y, proj, grad_gated, gain_col, gate_rows, bc_pre, cum, flags),
        [wide, wide, wide, block((WIDE, 8), lambda i: (i, 0)), whole(gate_rows), whole(bc_pre),
         block((GROUP, tokens), lambda i: (i, 0)), whole(flags)],
        [f32_out(DI, tokens), bf16_out(DI, tokens), bf16_out(DI, STATE)],
        [wide, wide, block((WIDE, STATE), lambda i: (i, 0))], micros=9,
    )


def mixer_back_inner(local, passed, pre, grad_y, bc_pre, dt, cum, cum_col, flags, seg_col, name_id):
    tokens, groups = dt.shape[1], HEADS // GROUP
    rows = block((GROUP, tokens), lambda i: (i, 0))
    wide = block((WIDE, tokens), lambda i: (i, 0))
    states = block((WIDE, STATE), lambda i: (i, 0))
    square = pltpu.VMEM((tokens, tokens), jnp.float32)
    return call_steps(
        inner_back_kernel, groups, (local, passed, pre, grad_y, bc_pre, dt, cum, cum_col, flags, seg_col),
        [states, block((WIDE, 8), lambda i: (i, 0)), wide, wide, whole(bc_pre), rows, rows, block((1, tokens, GROUP), lambda i: (i, 0, 0)),
         whole(flags), whole(seg_col)],
        [f32_out(DI, tokens), bf16_out(DI, STATE), f32_out(HEADS, tokens), f32_out(HEADS, tokens),
         f32_out(2 * STATE, tokens)],
        [wide, states, rows, rows, block((2 * STATE, tokens), lambda i: (0, 0))],
        (square, square, square) + chain_room(groups), name_id=name_id, micros=35,
    )


def mixer_back_join(grad_scaled, grad_y, pre, proj, taps, masks, state_in, grad_state, bc_pre, dt, cum, skip, flags):
    tokens, groups = dt.shape[1], HEADS // GROUP
    rows = block((GROUP, tokens), lambda i: (i, 0))
    wide = block((WIDE, tokens), lambda i: (i, 0))
    longer = block((WIDE, proj.shape[1]), lambda i: (i, 0))
    later = block((WIDE, proj.shape[1]), lambda i: (i + groups, 0))
    states = block((WIDE, STATE), lambda i: (i, 0))
    narrow = block((WIDE, 8), lambda i: (i, 0))
    return call_steps(
        join_back_kernel, groups,
        (grad_scaled, grad_y, pre, proj, taps, masks, state_in, grad_state, bc_pre, dt, cum, skip, flags),
        [wide, wide, wide, later, narrow, whole(masks), states, states, whole(bc_pre), rows, rows, rows,
         whole(flags)],
        [bf16_out(DI, proj.shape[1]), f32_out(DI, 8), f32_out(HEADS, tokens), f32_out(HEADS, tokens),
         f32_out(HEADS, 128), f32_out(2 * STATE, tokens)],
        [longer, narrow, rows, rows, block((GROUP, 128), lambda i: (i, 0)),
         block((2 * STATE, tokens), lambda i: (0, 0))], micros=19,
    )


def mixer_back_conv(grad_bc, bc_pre, proj, taps, masks):
    place = DI // (2 * STATE)
    wide = proj.shape[1]
    return call_steps(
        conv_back_kernel, 1, (grad_bc, bc_pre, proj, taps, masks),
        [whole(grad_bc), whole(bc_pre), block((2 * STATE, wide), lambda i: (2 * place, 0)),
         block((2 * STATE, 8), lambda i: (place, 0)), whole(masks)],
        [bf16_out(2 * STATE, wide), f32_out(2 * STATE, 8)],
        [block((2 * STATE, wide), lambda i: (0, 0)), block((2 * STATE, 8), lambda i: (0, 0))],
    )


def cut(array_index, rows, columns, row_step, column_step):
    found = []
    for row in range(0, rows, row_step):
        for column in range(0, columns, column_step):
            found.append(
                (array_index, row, min(row_step, rows - row), column, min(column_step, columns - column))
            )
    return found


def flipped(z, bits):
    if bits & 1:
        z = z + 1 - 2 * lax.rem(z, 2)
    return lax.rem(z + (bits & 2), 4)


def places(line):
    dp, z = lax.axis_index("dp"), lax.axis_index("ctx")
    y, x, core = lax.div(dp, 4), lax.rem(lax.div(dp, 2), 2), lax.rem(dp, 2)
    others = {
        "x": (dp + 2 - 4 * x, z),
        "y": (dp + 4 - 8 * y, z),
        "core": (dp + 1 - 2 * core, z),
    }
    for away in line:
        others[away] = (dp, lax.rem(z + away, 4))
    others["beside"] = (dp, flipped(z, 1))
    others["across"] = (dp, 3 - z)
    return y, x, core, z, others


def moved(moves, refs_in, refs_out, z, others, sems):
    copies = []
    for at, (source, target, take, put, bits) in enumerate(moves):
        source, target = refs_in[source], refs_out[target]
        source, target = source.at[take(z)], target.at[put(z)]
        copies.append(
            pltpu.make_async_remote_copy(
                src_ref=source,
                dst_ref=target,
                send_sem=sems[0].at[at],
                recv_sem=sems[1].at[at],
                device_id=others["beside" if bits == 1 else 2],
                device_id_type=pl.DeviceIdType.MESH,
            )
        )
    return copies


def greet(others):
    barrier = pltpu.get_barrier_semaphore()
    for device in others.values():
        pl.semaphore_signal(
            barrier, inc=1, device_id=device, device_id_type=pl.DeviceIdType.MESH
        )
    pl.semaphore_wait(barrier, len(others))


def send(source, target, sems, piece, leg, device):
    return pltpu.make_async_remote_copy(
        src_ref=source,
        dst_ref=target,
        send_sem=sems[0].at[piece, leg],
        recv_sem=sems[1].at[piece, leg],
        device_id=device,
        device_id_type=pl.DeviceIdType.MESH,
    )


def gather_kernel(pieces, ahead, count, line, moves, sizes, *refs):
    ins, more_in = refs[:count], refs[count : count + sizes[0]]
    refs = refs[count + sizes[0] :]
    outs, more_out = refs[:count], refs[count : count + sizes[1]]
    sent, came, kept, *more_sems = refs[count + sizes[1] :]
    y, x, core, z, others = places(line)
    deep = len(line) + 1
    slot = z if deep == 4 else lax.div(z, 2)
    inner = jnp.logical_and(z > 0, z < 3)
    greet(others)
    sems = (sent, came)

    def extra():
        return moved(moves, more_in if sizes[2] else more_out, more_out, z, others, more_sems) if moves else []

    def extra_turn(turn, turns):
        share = -(-len(moves) // turns)
        if turn < turns:
            for copy in extra()[share * turn : share * (turn + 1)]:
                copy.start()

    def legs(number):
        array, row, rows, column, columns = pieces[number]
        area = (pl.ds(row, rows), pl.ds(column, columns))
        out = outs[array]
        first, second = ("x", "y") if number % 2 == 0 else ("y", "x")
        rest = ((slice(None),) if line else ()) + area
        own = ins[array].at[area]
        mine = out.at[(y, x, core) + ((slot,) if line else ()) + area]
        lane = out.at[(y, x, core) + rest]
        at_pair = lax.div(z, 2)
        pair = out.at[(y, x, core, pl.ds(2 * at_pair, 2)) + area] if deep == 4 else None
        rest_pair = out.at[(y, x, core, pl.ds(2 - 2 * at_pair, 2)) + area] if deep == 4 else None
        if first == "x":
            plane = out.at[(y, slice(None), core) + rest]
        else:
            plane = out.at[(slice(None), x, core) + rest]
        every = out.at[(slice(None), slice(None), core) + rest]
        return {
            "keep": lambda: pltpu.make_async_copy(own, mine, kept.at[number]),
            "line": lambda: [send(own, mine, sems, number, 0, others["beside" if deep == 4 else 2])],
            "across": lambda: send(pair, pair, sems, number, 1, others["across"]),
            "outward": lambda: send(rest_pair, rest_pair, sems, number, 2, others["beside"]),
            "first": lambda: send(lane if line else own, lane, sems, number, 3, others[first]),
            "second": lambda: send(plane, plane, sems, number, 4, others[second]),
            "core": lambda: send(every, every, sems, number, 5, others["core"]),
        }

    def begin(number):
        if number < len(pieces):
            leg = legs(number)
            leg["keep"]().start()
            for copy in leg["line"]():
                copy.start()

    def advance(number, stage):
        if not 0 <= number < len(pieces):
            return
        leg = legs(number)
        if stage < 2 and deep < 4:
            return
        if stage == 0:
            leg["keep"]().wait()
            leg["line"]()[0].wait_recv()

            @pl.when(inner)
            def _():
                leg["across"]().start()
        elif stage == 1:

            @pl.when(inner)
            def _():
                leg["across"]().wait_recv()
                leg["outward"]().start()
        elif stage == 2:
            if deep == 4:

                @pl.when(jnp.logical_not(inner))
                def _():
                    leg["outward"]().wait_recv()
            else:
                leg["keep"]().wait()
                leg["line"]()[0].wait_recv()
            leg["first"]().start()
        elif stage == 3:
            leg["first"]().wait_recv()
            leg["second"]().start()
        elif stage == 4:
            leg["second"]().wait_recv()
            leg["core"]().start()
        else:
            leg["core"]().wait_recv()

    for number in range(2 * ahead):
        begin(number)
    pairs = -(-len(pieces) // 2)
    early = 0 if deep == 4 else 2
    for turn in range(pairs + 5 - early):
        extra_turn(turn, pairs)
        for stage in range(early, 6):
            for number in (2 * (turn - stage + early), 2 * (turn - stage + early) + 1):
                advance(number, stage)
                if stage == early and number < len(pieces):
                    begin(number + 2 * ahead)
    for number in range(len(pieces)):
        leg = legs(number)
        for copy in leg["line"]() + [leg["first"](), leg["second"](), leg["core"]()]:
            copy.wait_send()
        if deep == 4:

            @pl.when(inner)
            def _():
                leg["across"]().wait_send()
                leg["outward"]().wait_send()
    for copy in extra():
        copy.wait()


def move_room(moves):
    if not moves:
        return []
    return [pltpu.SemaphoreType.DMA((len(moves),))] * 2


def pallas_gather(parts, steps, name_id, line=(1, 2, 3), ahead=2, more=(), more_shapes=(), moves=()):
    pieces = []
    for index, (part, (row_step, column_step)) in enumerate(zip(parts, steps)):
        pieces += cut(index, part.shape[0], part.shape[1], row_step, column_step)
    count = len(parts)
    made = more_shapes or [part.shape for part in more]
    lead = (2, 2, 2) + ((len(line) + 1,) if line else ())
    anywhere = pl.BlockSpec(memory_space=pl.ANY)
    outs = pl.pallas_call(
        partial(gather_kernel, pieces, ahead, count, line, moves, (len(more), len(made), bool(more_shapes))),
        in_specs=[anywhere] * (count + len(more)),
        out_specs=[anywhere] * (count + len(made)),
        out_shape=[jax.ShapeDtypeStruct(lead + part.shape, part.dtype) for part in parts]
        + [bf16_out(*shape) for shape in made],
        scratch_shapes=[
            pltpu.SemaphoreType.DMA((len(pieces), 6)),
            pltpu.SemaphoreType.DMA((len(pieces), 6)),
            pltpu.SemaphoreType.DMA((len(pieces),)),
        ]
        + move_room(moves),
        input_output_aliases={} if more_shapes else {count + at: count + at for at in range(len(more))},
        cost_estimate=BRIEF,
        compiler_params=pltpu.CompilerParams(collective_id=name_id, has_side_effects=True),
    )(*parts, *more)
    return [out.reshape((-1,) + part.shape) for out, part in zip(outs, parts)] + list(outs[count:])


def reduce_kernel(pieces, ahead, count, lines, moves, sizes, *refs):
    ins, more_in = refs[:count], refs[count : count + sizes[0]]
    refs = refs[count + sizes[0] :]
    outs, more_out = refs[:count], refs[count : count + sizes[1]]
    sent, came, kept, put = refs[count + sizes[1] : count + sizes[1] + 4]
    room = refs[count + sizes[1] + 4 :]
    if moves:
        more_sems, room = room[:2], room[2:]
    y, x, core, z, others = places(max(lines, key=len))
    greet(others)
    sems = (sent, came)
    amount = len(pieces)

    def extra():
        return moved(moves, more_in, more_out, z, others, more_sems) if moves else []

    def extra_turn(turn, turns):
        share = -(-len(moves) // turns)
        if turn < turns:
            for copy in extra()[share * turn : share * (turn + 1)]:
                copy.start()

    def held(number):
        return room[6 * number : 6 * number + 6]

    def legs(number):
        array, row, rows, column, columns = pieces[number]
        area = (pl.ds(row, rows), pl.ds(column, columns))
        total, from_core, from_first, from_second, from_line, result = held(number)
        every = (slice(None), slice(None))
        line = lines[array]
        deep = len(line) + 1
        slot = z if deep == 4 else lax.div(z, 2)
        rest = ((slice(None),) if line else ()) + area
        side = number % 2 == 0
        return {
            "load": lambda: pltpu.make_async_copy(
                ins[array].at[every + (core,) + rest], total, kept.at[number]
            ),
            "core": lambda: send(
                ins[array].at[every + (1 - core,) + rest],
                from_core, sems, number, 0, others["core"],
            ),
            "first": lambda: send(
                total.at[:, 1 - x] if side else total.at[1 - y],
                from_first, sems, number, 1, others["x" if side else "y"],
            ),
            "second": lambda: send(
                total.at[1 - y, x] if side else total.at[y, 1 - x],
                from_second, sems, number, 2, others["y" if side else "x"],
            ),
            "line": lambda: [
                send(
                    total.at[y, x, lax.rem(z + away, 4) if deep == 4 else 1 - slot],
                    from_line.at[away - line[0]], sems, number, 2 + away, others[away],
                )
                for away in line
            ],
            "store": lambda: pltpu.make_async_copy(result, outs[array].at[area], put.at[number]),
        }

    def begin(number):
        if number < amount:
            leg = legs(number)
            leg["load"]().start()
            leg["core"]().start()

    def advance(number, stage):
        if not 0 <= number < amount:
            return
        leg = legs(number)
        total, from_core, from_first, from_second, from_line, result = held(number)
        line = lines[pieces[number][0]]
        deep = len(line) + 1
        slot = z if deep == 4 else lax.div(z, 2)

        def place(at, *lead):
            return lead + ((lax.rem(at, deep),) if line else ())

        if stage == 0:
            leg["load"]().wait()
            leg["core"]().wait_recv()

            @pl.loop(0, 4 * deep)
            def _(at):
                here = place(at, lax.div(at, 2 * deep), lax.rem(lax.div(at, deep), 2))
                total[here] = total[here] + from_core[here]

            leg["first"]().start()
        elif stage == 1:
            leg["first"]().wait_recv()

            @pl.loop(0, 2 * deep)
            def _(at):
                outer = lax.div(at, deep)
                here = place(at, outer, x) if number % 2 == 0 else place(at, y, outer)
                total[here] = total[here] + from_first[place(at, outer)]

            leg["second"]().start()
        elif stage == 2:
            leg["second"]().wait_recv()
            if line:

                @pl.loop(0, deep)
                def _(at):
                    total[y, x, at] = total[y, x, at] + from_second[at]

                for copy in leg["line"]():
                    copy.start()
            else:
                result[...] = total[y, x].astype(jnp.float32) + from_second[...].astype(jnp.float32)
                leg["store"]().start()
        elif line:
            for copy in leg["line"]():
                copy.wait_recv()
            summed = total[y, x, slot].astype(jnp.float32)
            for away in range(len(line)):
                summed = summed + from_line[away].astype(jnp.float32)
            result[...] = summed
            leg["store"]().start()

    for number in range(2 * ahead):
        begin(number)
    pairs = -(-amount // 2)
    for turn in range(pairs + 3):
        extra_turn(turn, pairs)
        for stage in range(4):
            for number in (2 * (turn - stage), 2 * (turn - stage) + 1):
                advance(number, stage)
                if stage == 0 and number >= 0:
                    begin(number + 2 * ahead)
    for number in range(amount):
        leg = legs(number)
        for copy in [leg["core"](), leg["first"](), leg["second"]()] + leg["line"]():
            copy.wait_send()
        leg["store"]().wait()
    for copy in extra():
        copy.wait()


def pallas_reduce(parts, steps, name_id, lines=None, ahead=2, more=(), more_shapes=(), moves=(), same=()):
    lines = lines or [(1, 2, 3)] * len(parts)
    shapes = [part.shape[1:] for part in parts]
    pieces = []
    for index, (shape, (row_step, column_step)) in enumerate(zip(shapes, steps)):
        pieces += cut(index, shape[0], shape[1], row_step, column_step)
    count, amount = len(parts), len(pieces)
    anywhere = pl.BlockSpec(memory_space=pl.ANY)
    room = []
    for array, _, rows, _, columns in pieces:
        kind, line = parts[array].dtype, lines[array]
        deep = (len(line) + 1,) if line else ()
        for lead in ((2, 2) + deep, (2, 2) + deep, (2,) + deep, deep, (max(len(line), 1),)):
            room.append(pltpu.VMEM(lead + (rows, columns), kind))
        room.append(pltpu.VMEM((rows, columns), jnp.float32))
    return pl.pallas_call(
        partial(reduce_kernel, pieces, ahead, count, lines, moves, (len(more), len(more_shapes))),
        in_specs=[anywhere] * (count + len(more)),
        out_specs=[anywhere] * (count + len(more_shapes)),
        out_shape=[jax.ShapeDtypeStruct(shape, jnp.float32) for shape in shapes]
        + [bf16_out(*shape) for shape in more_shapes],
        scratch_shapes=[
            pltpu.SemaphoreType.DMA((amount, 6)),
            pltpu.SemaphoreType.DMA((amount, 6)),
            pltpu.SemaphoreType.DMA((amount,)),
            pltpu.SemaphoreType.DMA((amount,)),
        ]
        + move_room(moves)
        + room,
        input_output_aliases={count + at: count + at for at in same},
        cost_estimate=BRIEF,
        compiler_params=pltpu.CompilerParams(
            collective_id=name_id, has_side_effects=True, vmem_limit_bytes=VMEM_MOST
        ),
        )(*[part.reshape((2, 2, 2) + ((len(line) + 1,) if line else ()) + shape) for part, shape, line in zip(parts, shapes, lines)], *more)


def proj_back_kernel(
    normed_ref, weight_ref, grad_z_ref, grad_x_ref, grad_rest_ref, rows_ref,
    grad_weight_ref, grad_normed_ref, came_ref, sent, came,
):
    step, groups = pl.program_id(0), DI // WIDE
    tokens = grad_z_ref.shape[1]
    dp, z = lax.axis_index("dp"), lax.axis_index("ctx")
    far = (dp, lax.rem(z + 2, 4))

    def exchange():
        return pltpu.make_async_remote_copy(
            src_ref=rows_ref,
            dst_ref=came_ref,
            send_sem=sent,
            recv_sem=came,
            device_id=far,
            device_id_type=pl.DeviceIdType.MESH,
        )

    @pl.when(step == 0)
    def _():
        grad_normed_ref[...] = jnp.zeros_like(grad_normed_ref)
        greet({"far": far})
        exchange().start()

    @pl.when(step == 2 * groups)
    def _():
        exchange().wait()

    @pl.when(step < groups)
    def _():
        grad_weight_ref[...] = half(mul_nt(normed_ref[:, :tokens], grad_z_ref[...]))
        grad_normed_ref[:, :tokens] += mul_nn(weight_ref[...], grad_z_ref[...])

    @pl.when(jnp.logical_and(step >= groups, step < 2 * groups))
    def _():
        grad_weight_ref[...] = half(mul_nt(normed_ref[...], grad_x_ref[...]))
        grad_normed_ref[...] += mul_nn(weight_ref[...], grad_x_ref[...])

    @pl.when(step == 2 * groups)
    def _():
        lane = lax.broadcasted_iota(jnp.int32, weight_ref.shape, 1)
        weight = jnp.where(lane < PROJ - 2 * DI, weight_ref[...], jnp.zeros_like(weight_ref))
        grad_weight_ref[...] = half(mul_nt(normed_ref[...], grad_rest_ref[...]))
        grad_normed_ref[...] += mul_nn(weight, grad_rest_ref[...])


def proj_back(normed_t, weight, grad_z, grad_x, grad_rest, rows, name_id):
    features, tokens = normed_t.shape
    groups = DI // WIDE
    return call_steps(
        proj_back_kernel, 2 * groups + 1, (normed_t, weight, grad_z, grad_x, grad_rest, rows),
        [whole(normed_t), block((features, WIDE), lambda i: (0, i)),
         block((WIDE, grad_z.shape[1]), lambda i: (jnp.minimum(i, groups - 1), 0)),
         block((WIDE, tokens), lambda i: (jnp.clip(i - groups, 0, groups - 1), 0)), whole(grad_rest),
         pl.BlockSpec(memory_space=pl.ANY)],
        [bf16_out(features, PROJ), f32_out(features, tokens), bf16_out(*rows.shape)],
        [block((features, WIDE), lambda i: (0, i)), block((features, tokens), lambda i: (0, 0)),
         pl.BlockSpec(memory_space=pl.ANY)],
        (pltpu.SemaphoreType.DMA, pltpu.SemaphoreType.DMA), name_id=name_id, micros=27,
    )


def hop(group, leaving, arrived, sent, came, device):
    return pltpu.make_async_remote_copy(
        src_ref=leaving.at[group],
        dst_ref=arrived.at[group],
        send_sem=sent.at[group],
        recv_sem=came.at[group],
        device_id=device,
        device_id_type=pl.DeviceIdType.MESH,
    )


def chain_places(step, forward):
    dp, z = lax.axis_index("dp"), lax.axis_index("ctx")
    others = {"left": (dp, lax.rem(z + 3, 4)), "right": (dp, lax.rem(z + 1, 4))}

    @pl.when(step == 0)
    def _():
        greet(others)

    if forward:
        return z == 0, z == 3, others["right"]
    return z == 3, z == 0, others["left"]


def chain_step(step, first, last, device, local_ref, passed_ref, leaving, arrived, sent, came):
    @pl.when(first)
    def _():
        arrived[step] = jnp.zeros(arrived.shape[1:], arrived.dtype)

    @pl.when(jnp.logical_not(first))
    def _():
        hop(step, leaving, arrived, sent, came, device).wait_recv()

    here = arrived[step]
    leaving[step] = half(here.astype(jnp.float32) * passed_ref[:, 0:1] + local_ref[...].astype(jnp.float32))

    @pl.when(jnp.logical_not(last))
    def _():
        hop(step, leaving, arrived, sent, came, device).start()

    return here


def chain_end(groups, last, device, leaving, arrived, sent, came):
    @pl.when(jnp.logical_not(last))
    def _():
        for group in range(groups):
            hop(group, leaving, arrived, sent, came, device).wait_send()


def chain_room(groups):
    slots = pltpu.VMEM((groups, WIDE, STATE), jnp.bfloat16)
    sems = pltpu.SemaphoreType.DMA((groups,))
    return (slots, slots, sems, sems)


def forward_kernel(
    local_ref, passed_ref, pre_ref, bc_ref, dt_ref, cum_ref, cum_col_ref, skip_ref, flags_ref, seg_col_ref,
    z_ref, gain_ref, y_ref, state_ref, gated_ref, scale_ref, mask_s, inner_s, u_s, sum_s, *chain,
):
    step, groups = pl.program_id(0), u_s.shape[0]
    first, last, device = chain_places(step, True)

    @pl.when(step == 0)
    def _():
        mask_s[...] = link_mask(flags_ref[2:3, :], seg_col_ref[:, 0:1])
        bc = half(jax.nn.silu(bc_ref[...]))
        inner_s[...] = mul_tn(bc[:STATE], bc[STATE:])
        sum_s[...] = jnp.zeros_like(sum_s)

    @pl.when(step < groups)
    def _():
        here = chain_step(step, first, last, device, local_ref, passed_ref, *chain)
        state_ref[...] = here
        cum, cum_col = cum_ref[...], cum_col_ref[0]
        c_t = half(jax.nn.silu(bc_ref[STATE:, :]))
        x = jax.nn.silu(pre_ref[...])
        scaled = half(x * spread_rows(dt_ref[...]))
        reach = jnp.exp(cum) * flags_ref[0:1, :]
        y_ref[...] = mul_nn(here, c_t) * spread_rows(reach) + x * spread_rows(skip_ref[...])
        for head in range(GROUP):
            rows = slice(head * HEAD, (head + 1) * HEAD)
            spread = cum[head : head + 1, :] - cum_col[:, head : head + 1] + mask_s[...]
            y_ref[rows, :] += mul_nn(scaled[rows], half(jnp.exp(spread) * inner_s[...]))
        u = y_ref[...] * jax.nn.silu(z_ref[...])
        u_s[step] = u
        sum_s[...] += jnp.sum(u * u, axis=0, keepdims=True)

    @pl.when(step >= groups)
    def _():
        scale = lax.rsqrt(sum_s[0:1, :] * (1.0 / DI) + 1e-05)
        gated_ref[...] = half(u_s[step - groups] * scale * gain_ref[:, 0:1])
        scale_ref[...] = jnp.broadcast_to(scale, scale_ref.shape)

    @pl.when(step == 2 * groups - 1)
    def _():
        chain_end(groups, last, device, *chain)


def mixer_forward(local, passed, pre, bc_pre, dt, cum, cum_col, skip, flags, seg_col, proj, gain_col, name_id):
    tokens, groups = dt.shape[1], HEADS // GROUP
    first = lambda i: (jnp.minimum(i, groups - 1), 0)
    second = lambda i: (jnp.maximum(i - groups, 0), 0)
    rows, wide = block((GROUP, tokens), first), block((WIDE, tokens), first)
    states = block((WIDE, STATE), first)
    square = pltpu.VMEM((tokens, tokens), jnp.float32)
    return call_steps(
        forward_kernel, 2 * groups,
        (local, passed, pre, bc_pre, dt, cum, cum_col, skip, flags, seg_col, proj, gain_col),
        [states, block((WIDE, 8), first), wide, whole(bc_pre), rows, rows,
         block((1, tokens, GROUP), lambda i: (jnp.minimum(i, groups - 1), 0, 0)), rows, whole(flags),
         whole(seg_col), wide, block((WIDE, 8), second)],
        [f32_out(DI, tokens), bf16_out(DI, STATE), bf16_out(DI, tokens), f32_out(8, tokens)],
        [wide, states, block((WIDE, tokens), second), block((8, tokens), lambda i: (0, 0))],
        (square, square, pltpu.VMEM((groups, WIDE, tokens), jnp.float32), pltpu.VMEM((8, tokens), jnp.float32))
        + chain_room(groups),
        name_id=name_id,
    )


BOTH = ("dp", "ctx")


def nothing(value):
    first = value[(0,) * value.ndim].astype(jnp.float32)
    return jnp.minimum(jnp.abs(first), 0.0)


def no_step(value):
    return nothing(value).astype(jnp.int32)


def two_parts(value):
    high = value.astype(jnp.bfloat16)
    low = (value - high.astype(jnp.float32)).astype(jnp.bfloat16)
    return high, low


def route_table(routes, expert_count):
    named = jnp.any(
        routes[:, :, None] == jnp.arange(expert_count, dtype=jnp.int32), axis=1
    )
    rows = routes.shape[0]
    earlier = jnp.tril(jnp.ones((rows, rows), jnp.bfloat16), -1)
    ranks = jnp.dot(earlier, named.astype(jnp.bfloat16), preferred_element_type=jnp.float32)
    return named, jnp.where(named, ranks, -1.0)


def swap(value, bits):
    count = lax.axis_size("ctx")
    return lax.ppermute(value, "ctx", [(source, source ^ bits) for source in range(count)])


def half_strip(other, start):
    def at(z):
        own = lax.div(z, 2)
        first = EXP_DEV // 2 * (1 - own if other else own)
        return (pl.ds(first, EXP_DEV // 2), pl.ds(start, STRIP))

    return at


def columns(place, start, size):
    return lambda z: place(z) + (pl.ds(start, size),)


def held_experts(shard, other):
    held = EXP_DEV // 2
    half_at = lax.div(lax.axis_index("ctx"), 2)
    return lax.dynamic_slice_in_dim(shard, held * (1 - half_at if other else half_at), held, 0)


STRIP = 64


def quarter(axis, width, bits, start):
    def at(z):
        first = flipped(z, bits) * width
        if axis == 1:
            return (slice(None), pl.ds(pl.multiple_of(first + start, STRIP), STRIP))
        return (slice(None), pl.ds(start, STRIP), pl.ds(pl.multiple_of(first, 128), width))

    return at


def strip(start, *lead):
    return lambda z: lead + (slice(None), pl.ds(start, STRIP))


def strips(rows):
    return range(0, rows, STRIP)


def with_quarter(whole, own, axis):
    place = lax.axis_index("ctx") * own.shape[axis]
    return lax.dynamic_update_slice_in_dim(whole, own, place, axis)


def own_quarter(whole, axis, bits):
    width = whole.shape[axis] // 4
    return lax.dynamic_slice_in_dim(whole, flipped(lax.axis_index("ctx"), bits) * width, width, axis)


def expert_owners(near, far):
    far = far.astype(jnp.float32)
    low = lax.div(lax.axis_index("ctx"), 2) == 0
    return jnp.concatenate([jnp.where(low, near, far), jnp.where(low, far, near)], axis=0)


TILE = 4


def experts_kernel(
    rank_ref, gate_ref, rows_ref, grads_ref, first_ref, down_ref,
    routed_ref, back_ref, side_ref, grad_first_ref, grad_down_ref,
    x_s, g_s, sum_first_s, sum_down_s, ready_s, pick_s, routed_s, back_s, side_s, sem,
):
    tile, expert = pl.program_id(0), pl.program_id(1)
    last = pl.num_programs(0) - 1
    hidden = down_ref.shape[1]
    held, slots = x_s.shape[0], x_s.shape[1] // TILE
    tokens = rank_ref.shape[2]
    gates = []
    number = lax.broadcasted_iota(jnp.int32, (slots, tokens), 0).astype(jnp.float32)
    @pl.when(expert == 0)
    def _():
        for at in range(TILE):
            rows = pl.ds(at * slots, slots)
            for one in range(held):
                own = rank_ref[at, one : one + 1, :] == number
                pick_s[at, one * slots : (one + 1) * slots, :] = half(own.astype(jnp.float32))
            x_rows = half(mul_nn(pick_s[at], rows_ref[at]))
            g_rows = half(mul_nn(pick_s[at], grads_ref[at]))
            for one in range(held):
                x_s[one, rows, :] = x_rows[one * slots : (one + 1) * slots]
                g_s[one, rows, :] = g_rows[one * slots : (one + 1) * slots]

    for at in range(TILE):
        own = rank_ref[at, pl.ds(expert, 1), :] == number
        gates.append(jnp.sum(jnp.where(own, gate_ref[at, pl.ds(expert, 1), :], 0.0), axis=1, keepdims=True))
    gate = jnp.concatenate(gates, axis=0)
    x, grad = x_s[expert], g_s[expert].astype(jnp.float32)
    both = mul_nn(x, first_ref[0])
    hg, hu = both[:, :hidden], both[:, hidden:]
    squashed = jax.nn.sigmoid(hg)
    act = half(hg * squashed * hu)
    out = half(mul_nn(act, down_ref[0]))
    out_f = out.astype(jnp.float32)
    dgate = jnp.sum(grad * out_f, axis=1, keepdims=True)
    routed = half(gate * out_f)
    grad_out = half(gate * grad)
    grad_act = mul_nt(grad_out, down_ref[0])
    grad_hg = half(grad_act * hu * (squashed * (1.0 + hg * (1.0 - squashed))))
    grad_hu = half(grad_act * hg * squashed)
    grad_both = jnp.concatenate([grad_hg, grad_hu], axis=1)
    back = half(mul_nt(grad_both, first_ref[0]))

    @pl.when(tile == 0)
    def _():
        sum_first_s[expert] = jnp.zeros(sum_first_s.shape[1:], jnp.float32)
        sum_down_s[expert] = jnp.zeros(sum_down_s.shape[1:], jnp.float32)

    @pl.loop(0, x_s.shape[2] // 256)
    def _(at):
        some = pl.ds(pl.multiple_of(at * 256, 256), 256)
        sum_first_s[expert, some, :] += mul_tn(x_s[expert, :, some], grad_both)

    sum_down_s[expert] += mul_tn(act, grad_out)
    count = EXP_DEV * lax.axis_size("dp")
    column = lax.axis_index("dp") * EXP_DEV + lax.div(lax.axis_index("ctx"), 2) * held + expert
    lane = lax.broadcasted_iota(jnp.int32, (slots, side_s.shape[2]), 1)
    high = half(dgate).astype(jnp.float32)
    for at in range(TILE):
        rows = slice(at * slots, (at + 1) * slots)
        some = pl.ds(pl.multiple_of(expert * slots, slots), slots)
        routed_s[at, some, :] = routed[rows]
        back_s[at, some, :] = back[rows]
        side_s[at, some, :] = half(
            jnp.where(lane == column, high[rows], jnp.where(lane == column + count, dgate[rows] - high[rows], 0.0))
        )

    @pl.when(expert == pl.num_programs(1) - 1)
    def _():
        for at in range(TILE):
            routed_ref[at] = half(mul_tn(pick_s[at], routed_s[at]))
            back_ref[at] = half(mul_tn(pick_s[at], back_s[at]))
            side_ref[at] = half(mul_tn(pick_s[at], side_s[at]))

    @pl.when(tile == last)
    def _():
        height = ready_s.shape[0]
        for sums, target in ((sum_first_s, grad_first_ref), (sum_down_s, grad_down_ref)):
            width = sums.shape[2]
            for at in range(sums.shape[1] // height):
                some = pl.ds(at * height, height)
                ready_s[:, :width] = half(sums[expert, some, :])
                copy = pltpu.make_async_copy(
                    ready_s.at[:, pl.ds(0, width)], target.at[expert, some, :], sem
                )
                copy.start()
                copy.wait()


def routed_experts(rank, gate, rows, grads, first, down, slots):
    blocks, held, tokens = rank.shape
    features, hidden = first.shape[1], down.shape[1]
    some = lambda t, e: (t, 0, 0)
    table = pl.BlockSpec((TILE, held, tokens), some)
    wide = pl.BlockSpec((TILE, tokens, features), some)
    once = pl.BlockSpec((TILE, tokens, features), some, pipeline_mode=pl.Buffered(1))
    anywhere = pl.BlockSpec(memory_space=pl.ANY)
    return pl.pallas_call(
        experts_kernel,
        grid=(blocks // TILE, held),
        in_specs=[
            table,
            table,
            once,
            once,
            pl.BlockSpec((1, features, 2 * hidden), lambda t, e: (e, 0, 0)),
            pl.BlockSpec((1, hidden, features), lambda t, e: (e, 0, 0)),
        ],
        out_specs=[wide, wide, pl.BlockSpec((TILE, tokens, 128), some), anywhere, anywhere],
        out_shape=[
            bf16_out(blocks, tokens, features),
            bf16_out(blocks, tokens, features),
            bf16_out(blocks, tokens, 128),
            bf16_out(held, features, 2 * hidden),
            bf16_out(held, hidden, features),
        ],
        scratch_shapes=[
            pltpu.VMEM((held, TILE * slots, features), jnp.bfloat16),
            pltpu.VMEM((held, TILE * slots, features), jnp.bfloat16),
            pltpu.VMEM((held, features, 2 * hidden), jnp.float32),
            pltpu.VMEM((held, hidden, features), jnp.float32),
            pltpu.VMEM((256, features), jnp.bfloat16),
            pltpu.VMEM((TILE, held * slots, tokens), jnp.bfloat16),
            pltpu.VMEM((TILE, held * slots, features), jnp.bfloat16),
            pltpu.VMEM((TILE, held * slots, features), jnp.bfloat16),
            pltpu.VMEM((TILE, held * slots, 128), jnp.bfloat16),
            pltpu.SemaphoreType.DMA,
        ],
        cost_estimate=BRIEF,
        compiler_params=pltpu.CompilerParams(
            vmem_limit_bytes=62 * 1024 * 1024, dimension_semantics=("arbitrary", "arbitrary")
        ),
    )(rank, gate, rows, grads, first, down)


def on_device(
    layer_in,
    seg_ids,
    route_ids,
    out_grad,
    norm_in,
    w_in,
    conv_w,
    conv_b,
    dt_bias,
    a_log,
    d_skip,
    norm_gate,
    w_out,
    norm_mid,
    w_router,
    w_sgate,
    w_sup,
    w_sdown,
    e_gate,
    e_up,
    e_down,
):
    f32, bf16 = jnp.float32, jnp.bfloat16
    row_count, d_model = layer_in.shape[1:]
    devices = lax.axis_size("dp") * lax.axis_size("ctx")
    ctx_place = lax.axis_index("ctx")
    held = EXP_DEV // 2
    first_expert = lax.axis_index("dp") * EXP_DEV + lax.div(ctx_place, 2) * held
    blocks = lax.axis_size("dp") * 2
    expert_count = EXP_DEV * lax.axis_size("dp")
    capacity = row_count * TOP * 5 // (expert_count * 4)
    slots = -(-capacity // 64) * 64
    tap_count = conv_w.shape[0]
    halo = 8

    small_parts = (norm_in, conv_w, conv_b, norm_gate, norm_mid, w_router)
    small_flat = jnp.concatenate([part.reshape(-1) for part in small_parts])
    small_flat = jnp.pad(small_flat, (0, 4096 - small_flat.shape[0])).reshape(32, 128)
    edge_rows = layer_in[0, row_count - halo :].reshape(-1, 128)
    width, hidden = e_gate.shape[1:]
    first_strips, down_strips = strips(width), strips(hidden)
    w_in_all, w_out_all, small_all, expert_first, expert_down = pallas_gather(
        [w_in, w_out, jnp.concatenate([small_flat, edge_rows])],
        [(16, 1664), (16, 1536), (128, 128)],
        1,
        ahead=6,
        more=[e_gate, e_up, e_down],
        more_shapes=[(held, d_model, 2 * hidden), (held, hidden, d_model)],
        moves=[
            (part, 0, half_strip(True, start), columns(quarter(1, width, 0, start), part * hidden, hidden), 2)
            for start in first_strips
            for part in range(2)
        ]
        + [(2, 1, half_strip(True, start), quarter(2, width, 0, start), 2) for start in down_strips],
    )
    pair_at = lax.div(ctx_place, 2)
    sent = nothing(w_in_all)
    shared_all = lax.all_gather(
        (jnp.concatenate([w_sgate, w_sup], axis=1).astype(f32) + sent).astype(bf16), BOTH, axis=0
    )
    sdown_all = lax.all_gather((w_sdown.astype(f32) + sent).astype(bf16), BOTH, axis=0)
    own_first = jnp.concatenate([held_experts(e_gate, False), held_experts(e_up, False)], axis=2)
    expert_first = with_quarter(expert_first, own_first, 1)
    expert_down = with_quarter(expert_down, held_experts(e_down, False), 2)
    edge_all = small_all[:, small_flat.shape[0] :].reshape(devices, halo, d_model)
    small_all = small_all[:, : small_flat.shape[0]].reshape(devices, 4096)
    taken, pieces = 0, []
    for part in small_parts:
        pieces.append(small_all[:, taken : taken + part.size])
        taken += part.size
    gain_in = pieces[0].reshape(-1).astype(f32)
    conv_weight = jnp.moveaxis(pieces[1].reshape(devices, tap_count, -1), 0, 1).reshape(tap_count, CONV).astype(f32)
    conv_bias = pieces[2].reshape(-1).astype(f32)
    gain_gate = pieces[3].reshape(-1).astype(f32)
    gain_mid = pieces[4].reshape(-1).astype(f32)
    router_weight = pieces[5].reshape(d_model, expert_count)
    weight_in = w_in_all.reshape(d_model, PROJ)
    weight_out = w_out_all.reshape(DI, d_model)
    shared_weight = shared_all.reshape(d_model, -1)
    sdown_weight = sdown_all.reshape(-1, d_model)
    named, ranks = route_table(route_ids[0], expert_count)

    own_in = layer_in[0]
    place = lax.axis_index("dp") * lax.axis_size("ctx") + ctx_place
    edge_in = lax.dynamic_index_in_dim(edge_all, jnp.maximum(place - 1, 0), 0, keepdims=False)
    edge_in = jnp.where(ctx_place > 0, edge_in, jnp.zeros_like(edge_in))
    input_f = jnp.concatenate(
        [own_in, jnp.zeros((128 - halo, d_model), bf16), edge_in], axis=0
    ).astype(f32)
    normed = scaled_norm(input_f, gain_in).astype(bf16)
    projected = lax.dot_general(
        weight_in, normed, (((0,), (1,)), ((), ())), preferred_element_type=f32
    )
    seg_pad = jnp.concatenate([jnp.full((tap_count - 1,), -1, jnp.int32), seg_ids[0]])
    seg_window = lax.dynamic_slice_in_dim(
        seg_pad, ctx_place * row_count, row_count + tap_count - 1, 0
    )
    taps = jnp.concatenate(
        [conv_weight.T, conv_bias[:, None], jnp.zeros((CONV, 7 - tap_count), f32)], axis=1
    )
    dt_raw = projected[DI + CONV :, :row_count]
    dt_pos, decay, cumul, cumul_col, flags, seg_col, masks, through, skip_rows = mixer_rows(
        dt_raw, dt_bias, a_log, d_skip, seg_window, tap_count
    )
    bc_pre, pre, state_out = mixer_forward_states(projected, taps, masks, dt_pos, cumul, flags)
    passed = jnp.broadcast_to(jnp.repeat(through, HEAD)[:, None], (DI, 8))
    gain_col = jnp.broadcast_to(gain_gate[:, None], (DI, 8))
    y_heads, state_in, gated, gate_scale = mixer_forward(
        state_out, passed, pre, bc_pre, dt_pos, cumul, cumul_col, skip_rows, flags, seg_col, projected, gain_col, 7
    )

    mixed = times_rows(gated, weight_out)
    resid_mid = own_in.astype(f32) + mixed
    normed_mid_f, pull_mid = jax.vjp(scaled_norm, resid_mid, gain_mid)
    normed_mid = normed_mid_f.astype(bf16)
    logits = jnp.dot(normed_mid, router_weight, preferred_element_type=f32)
    top_logit = jnp.max(jnp.where(named, logits, -jnp.inf), axis=-1, keepdims=True)
    powers = jnp.where(named, jnp.exp(jnp.where(named, logits - top_logit, 0.0)), 0.0)
    gates = powers / jnp.sum(powers, axis=-1, keepdims=True)
    gate_high, gate_low = two_parts(gates)
    side = jnp.concatenate(
        [gate_high, gate_low, ranks.astype(bf16), jnp.zeros((row_count, 128 - 3 * expert_count), bf16)],
        axis=1,
    )
    token_rows, grad_rows, side_all, expert_first, expert_down = pallas_gather(
        [normed_mid, out_grad[0], side],
        [(16, 1536), (16, 1536), (128, 128)],
        3,
        line=(2,),
        ahead=4,
        more=[expert_first, expert_down],
        moves=[
            (part, part, quarter(axis, width, bits, start), quarter(axis, width, bits, start), 1)
            for bits in (0, 2)
            for part, axis, starts in ((0, 1, first_strips), (1, 2, down_strips))
            for start in starts
        ],
    )
    normed_later = (normed_mid.astype(f32) + nothing(token_rows)).astype(bf16)
    shared_hidden = jnp.dot(normed_later, shared_weight, preferred_element_type=f32)
    shared_gate, shared_up = jnp.split(shared_hidden, 2, axis=1)
    shared_act = (jax.nn.silu(shared_gate) * shared_up).astype(bf16)
    shared_out = jnp.dot(shared_act, sdown_weight, preferred_element_type=f32)

    def owned(grad):
        return grad.astype(bf16).reshape(devices, -1, grad.shape[-1])

    mine_of = partial(lax.dynamic_slice_in_dim, slice_size=held, axis=2)
    my_gate = mine_of(side_all, first_expert).astype(f32) + mine_of(
        side_all, first_expert + expert_count
    ).astype(f32)
    my_rank = mine_of(side_all, first_expert + 2 * expert_count).astype(f32)
    my_gate, my_rank = jnp.swapaxes(my_gate, 1, 2), jnp.swapaxes(my_rank, 1, 2)
    routed_rows, grad_slot_rows, back_side, grad_first, grad_down = routed_experts(
        my_rank, my_gate, token_rows, grad_rows, expert_first, expert_down, slots
    )
    grad_shared_out = out_grad[0]
    grad_w_sdown = times_rows(shared_act, grad_shared_out)
    grad_shared_act = times_back(grad_shared_out, sdown_weight)
    grad_sgate = (grad_shared_act * shared_up * silu_slope(shared_gate)).astype(bf16)
    grad_sup = (grad_shared_act * jax.nn.silu(shared_gate)).astype(bf16)
    grad_shared = jnp.concatenate([grad_sgate, grad_sup], axis=1)
    grad_w_shared = times_rows(normed_mid, grad_shared)
    back_rows, back_side, sum_sdown, sum_shared, beside_first, beside_down, routed_rows = pallas_reduce(
        [grad_slot_rows, back_side, owned(grad_w_sdown), owned(grad_w_shared)],
        [(16, 1536), (128, 128), (16, 1536), (16, 1024)],
        4,
        lines=[(2,), (2,), (1, 2, 3), (1, 2, 3)],
        more=[grad_first, grad_down, routed_rows],
        more_shapes=[(held, width, 2 * hidden), (held, hidden, width), routed_rows.shape],
        same=(2,),
        moves=[
            (part, part, quarter(axis, width, 3, start), strip(start), 1)
            for part, axis, starts in ((0, 1, first_strips), (1, 2, down_strips))
            for start in starts
        ],
    )
    routed = lax.psum_scatter(
        routed_rows.reshape(-1, 2, row_count, d_model), "dp", scatter_dimension=0
    )
    routed = with_layout_constraint(routed, Layout(major_to_minor=(0, 1, 2)))
    routed_own = lax.dynamic_index_in_dim(routed, pair_at, 0, keepdims=False)
    routed_far = lax.dynamic_index_in_dim(routed, 1 - pair_at, 0, keepdims=False)
    grad_top = out_grad[0].astype(f32)
    grad_mid_shared = times_back(grad_shared, shared_weight)
    grad_gates = back_side[:, :expert_count] + back_side[:, expert_count : 2 * expert_count]
    grad_pick = gates * (grad_gates - jnp.sum(gates * grad_gates, axis=-1, keepdims=True))
    grad_logits = grad_pick.astype(bf16)
    grad_w_router = times_rows(normed_mid, grad_logits)
    grad_mid = (
        back_rows + grad_mid_shared + times_back(grad_logits, router_weight)
    )
    grad_resid_part, grad_gain_mid = pull_mid(grad_mid)
    grad_resid = grad_top + grad_resid_part
    grad_mixed = grad_resid.astype(bf16)

    grad_w_out = jnp.dot(gated, grad_mixed, preferred_element_type=f32)
    grad_gated = times_back(weight_out, grad_mixed)
    scaled_u = y_heads * jax.nn.silu(projected[:DI, :row_count])
    scale_row = gate_scale[:1]
    along = jnp.sum(grad_gated * gain_gate[:, None] * scaled_u, axis=0, keepdims=True)
    grad_gain_gate = jnp.sum(grad_gated * scaled_u * scale_row, axis=1)
    gate_rows = jnp.concatenate(
        [scale_row, scale_row * scale_row * scale_row * along * (1.0 / DI), jnp.zeros((6, row_count), f32)]
    )
    grad_y, grad_z, grad_state_local = mixer_back_gate(
        y_heads, projected, grad_gated, gain_col, gate_rows, bc_pre, cumul, flags
    )
    grad_scaled, grad_state_out, grad_cum_inner, grad_skip, grad_bc_inner = mixer_back_inner(
        grad_state_local, passed, pre, grad_y, bc_pre, dt_pos, cumul, cumul_col, flags, seg_col, 8
    )
    far_first, far_down = (
        half(own_quarter(whole, axis, 2).astype(f32) + beside.astype(f32))
        for whole, beside, axis in ((grad_first, beside_first, 1), (grad_down, beside_down, 2))
    )
    grad_x, grad_taps_x, grad_dt, grad_cum_join, grad_last, grad_bc_join = mixer_back_join(
        grad_scaled, grad_y, pre, projected, taps, masks, state_in, grad_state_out,
        bc_pre, dt_pos, cumul, skip_rows, flags,
    )
    grad_bc, grad_taps_bc = mixer_back_conv(
        grad_bc_inner + grad_bc_join, bc_pre, projected, taps, masks
    )
    grad_cum = grad_cum_inner + grad_cum_join
    grad_last = grad_last[:, 0] + through * grad_last[:, 1]
    lower = jnp.tril(jnp.ones((row_count, row_count), f32))
    grad_decay = jnp.dot(grad_cum, lower, precision=lax.Precision.HIGHEST) + grad_last[:, None]
    grad_dt = grad_dt - jnp.exp(a_log)[:, None] * grad_decay
    grad_raw = grad_dt * jax.nn.sigmoid(dt_raw + dt_bias[:, None])
    grad_taps = jnp.concatenate([grad_taps_x, grad_taps_bc])
    grad_conv_w, grad_conv_b = grad_taps[:, :tap_count].T, grad_taps[:, tap_count]
    head_sums_all = jnp.concatenate(
        [jnp.sum(grad_raw, axis=1), jnp.sum(decay * grad_decay, axis=1), jnp.sum(grad_skip, axis=1)]
    )
    grad_rest = jnp.concatenate(
        [
            grad_bc,
            jnp.pad(grad_raw.astype(bf16), ((0, WIDE - 2 * STATE - HEADS), (0, 128))),
        ]
    )
    normed_t = normed.T
    grad_w_in, grad_normed, routed_far = proj_back(
        normed_t, weight_in, grad_z, grad_x, grad_rest, routed_far, 9
    )
    grad_normed = grad_normed.T
    edge_grad = from_behind(grad_normed[row_count + 128 - halo :], "ctx", -1)
    grad_normed = jnp.concatenate(
        [grad_normed[: row_count - halo], grad_normed[row_count - halo : row_count] + edge_grad],
        axis=0,
    )
    _, pull_in = jax.vjp(scaled_norm, own_in.astype(f32), gain_in)
    grad_input_part, grad_gain_in = pull_in(grad_normed)
    grad_in = (grad_resid + grad_input_part)[None]

    small_grads = jnp.concatenate(
        [
            grad_gain_in.reshape(devices, -1),
            jnp.moveaxis(grad_conv_w.reshape(tap_count, devices, -1), 1, 0).reshape(devices, -1),
            grad_conv_b.reshape(devices, -1),
            grad_gain_gate.reshape(devices, -1),
            grad_gain_mid.reshape(devices, -1),
            grad_w_router.reshape(devices, -1),
            jnp.broadcast_to(head_sums_all, (devices, 3 * HEADS)),
        ],
        axis=1,
    )
    small_grads = jnp.pad(small_grads, ((0, 0), (0, 3072 - small_grads.shape[1])))
    sum_in, sum_out, sum_small, far_first, far_down, beside_first, beside_down = pallas_reduce(
        [owned(grad_w_in), owned(grad_w_out), small_grads.reshape(devices, 24, 128)],
        [(16, 1664), (16, 1536), (24, 128)],
        6,
        ahead=3,
        more=[far_first, far_down, grad_first, grad_down],
        more_shapes=[far_first.shape, far_down.shape] * 2,
        moves=[
            move
            for part, axis, starts in ((0, 1, first_strips), (1, 2, down_strips))
            for start in starts
            for move in (
                (part, part, strip(start), strip(start), 2),
                (2 + part, 2 + part, quarter(axis, width, 1, start), strip(start), 1),
            )
        ],
    )
    near_first, near_down = (
        own_quarter(whole, axis, 0).astype(f32) + beside.astype(f32)
        for whole, beside, axis in ((grad_first, beside_first, 1), (grad_down, beside_down, 2))
    )
    layer_out = (resid_mid + shared_out + routed_own.astype(f32) + routed_far.astype(f32)).astype(bf16)[None]
    sum_sgate, sum_sup = jnp.split(sum_shared, 2, axis=1)
    grad_e_gate = expert_owners(near_first[..., :hidden], far_first[..., :hidden])
    grad_e_up = expert_owners(near_first[..., hidden:], far_first[..., hidden:])
    grad_e_down = expert_owners(near_down, far_down)
    sum_small = sum_small.reshape(-1)
    taken, mine = 0, []
    for part in small_parts:
        mine.append(sum_small[taken : taken + part.size].reshape(part.shape))
        taken += part.size
    return (
        layer_out,
        grad_in,
        mine[0],
        sum_in,
        mine[1],
        mine[2],
        sum_small[taken : taken + HEADS],
        sum_small[taken + HEADS : taken + 2 * HEADS],
        sum_small[taken + 2 * HEADS : taken + 3 * HEADS],
        mine[3],
        sum_out,
        mine[4],
        mine[5],
        sum_sgate,
        sum_sup,
        sum_sdown,
        grad_e_gate,
        grad_e_up,
        grad_e_down,
    )


def solution(mesh):
    in_specs = (
        P("dp", "ctx", None),
        P("dp", None),
        P("dp", "ctx", None),
        P("dp", "ctx", None),
        P(("dp", "ctx")),
        P(("dp", "ctx"), None),
        P(None, ("dp", "ctx")),
        P(("dp", "ctx")),
        P(),
        P(),
        P(),
        P(("dp", "ctx")),
        P(("dp", "ctx"), None),
        P(("dp", "ctx")),
        P(("dp", "ctx"), None),
        P(("dp", "ctx"), None),
        P(("dp", "ctx"), None),
        P(("dp", "ctx"), None),
        P("dp", "ctx", None),
        P("dp", "ctx", None),
        P("dp", None, "ctx"),
    )
    out_specs = (
        P("dp", "ctx", None),
        P("dp", "ctx", None),
        P(("dp", "ctx")),
        P(("dp", "ctx"), None),
        P(None, ("dp", "ctx")),
        P(("dp", "ctx")),
        P(),
        P(),
        P(),
        P(("dp", "ctx")),
        P(("dp", "ctx"), None),
        P(("dp", "ctx")),
        P(("dp", "ctx"), None),
        P(("dp", "ctx"), None),
        P(("dp", "ctx"), None),
        P(("dp", "ctx"), None),
        P("dp", "ctx", None),
        P("dp", "ctx", None),
        P("dp", None, "ctx"),
    )
    one_each = mesh.shape["ctx"] == EXP_DEV and mesh.shape["dp"] == 8
    return jax.shard_map(
        on_device if one_each else on_device_general, mesh=mesh, in_specs=in_specs, out_specs=out_specs, check_vma=False
    )
```
